128 devices in a mesh: dp: 16 (over z, y_lo, core), tensor: 8 (over y_hi, x).
Axes of the slice: x: 4, y: 4 (y_hi: 2, y_lo: 2; y = y_hi * 2 + y_lo), z: 4, core: 2. Of those that a mesh axis runs over, the one named last changes fastest.
Arguments:
- tokens: bfloat16 [16384, 2048], P(('dp', 'tensor')), may hold values from -6 to 6
- cotangent: bfloat16 [16384, 2048], P(('dp', 'tensor')), may hold values from -6 to 6
- doc_lengths: int32 [16, 4], P('dp'), may hold values from 1 to 1021, as said below
- query_weight: float32 [2048, 2048], P('dp', 'tensor'), may hold values from -0.125 to 0.125
- key_value_weight: float32 [2, 2048, 1024], P(None, 'dp', 'tensor'), may hold values from -0.125 to 0.125
- output_weight: float32 [2048, 2048], P('tensor', 'dp'), may hold values from -1.5 to 1.5
- gateup_weight: float32 [2, 2048, 6144], P(None, 'dp', 'tensor'), may hold values from -0.125 to 0.125
- down_weight: float32 [6144, 2048], P('tensor', 'dp'), may hold values from -0.078125 to 0.078125
- norm_gains: float32 [4352], P(('dp', 'tensor')), may hold values from 0.5 to 1.5
- query_momentum: float32 [2048, 2048], P('dp', 'tensor')
- keyval_momentum: float32 [2, 2048, 1024], P(None, 'dp', 'tensor')
- output_momentum: float32 [2048, 2048], P('tensor', 'dp')
- gateup_momentum: float32 [2, 2048, 6144], P(None, 'dp', 'tensor')
- down_momentum: float32 [6144, 2048], P('tensor', 'dp')
- gains_momentum: float32 [4352], P(('dp', 'tensor'))
- query_average: float32 [2048, 2048], P('dp', 'tensor'), may hold values from -0.125 to 0.125
- key_value_mean: float32 [2, 2048, 1024], P(None, 'dp', 'tensor'), may hold values from -0.125 to 0.125
- output_average: float32 [2048, 2048], P('tensor', 'dp'), may hold values from -1.5 to 1.5
- gateup_average: float32 [2, 2048, 6144], P(None, 'dp', 'tensor'), may hold values from -0.125 to 0.125
- down_average: float32 [6144, 2048], P('tensor', 'dp'), may hold values from -0.078125 to 0.078125
- gains_average: float32 [4352], P(('dp', 'tensor')), may hold values from 0.2 to 1.8
Outputs:
- block_out: bfloat16 [16384, 2048], P(('dp', 'tensor'))
- input_grad: bfloat16 [16384, 2048], P(('dp', 'tensor'))
- query_updated: float32 [2048, 2048], P('dp', 'tensor')
- keyval_updated: float32 [2, 2048, 1024], P(None, 'dp', 'tensor')
- output_updated: float32 [2048, 2048], P('tensor', 'dp')
- gateup_updated: float32 [2, 2048, 6144], P(None, 'dp', 'tensor')
- down_updated: float32 [6144, 2048], P('tensor', 'dp')
- gains_updated: float32 [4352], P(('dp', 'tensor'))
- query_velocity: float32 [2048, 2048], P('dp', 'tensor')
- keyval_velocity: float32 [2, 2048, 1024], P(None, 'dp', 'tensor')
- output_velocity: float32 [2048, 2048], P('tensor', 'dp')
- gateup_velocity: float32 [2, 2048, 6144], P(None, 'dp', 'tensor')
- down_velocity: float32 [6144, 2048], P('tensor', 'dp')
- gains_velocity: float32 [4352], P(('dp', 'tensor'))
- query_smoothed: float32 [2048, 2048], P('dp', 'tensor')
- keyval_smoothed: float32 [2, 2048, 1024], P(None, 'dp', 'tensor')
- output_smoothed: float32 [2048, 2048], P('tensor', 'dp')
- gateup_smoothed: float32 [2, 2048, 6144], P(None, 'dp', 'tensor')
- down_smoothed: float32 [6144, 2048], P('tensor', 'dp')
- gains_smoothed: float32 [4352], P(('dp', 'tensor'))
The draws below stay inside these ranges and needn't reach their ends.
Inputs may be any that keep to these rules, and one draw needn't show every extreme that they name: `doc_lengths`: row g holds the lengths of group g's 4 documents in order, summing to 1024; the first, third and fourth are each at least 1 and under 1024 // 8, the third and fourth together under 1024 // 8.
All inputs are finite; a program needn't handle non-finite values.
Results may differ from the reference program's by a relative error of at most 0.02.
Values may be sent and summed in bfloat16 or wider, within the bound.
A program may use at most 192 MiB of HBM per device.

```python
import math
import jax
import jax.numpy as jnp
from jax import lax

MODEL_WIDTH = 2048
QUERY_HEADS = 16
KEY_VALUE_HEADS = 8
HEAD_SIZE = 128
FF = 6144
GROUP_TOK = 1024
GROUPS = 16
TOKENS = 16384
GAINS = 4352


def moment_buffer(key, field_shape, spread):
    return spread * math.sqrt(TOKENS) * jnp.clip(jax.random.normal(key, field_shape, jnp.float32), -6.0, 6.0)


def draw_doc_lengths(key, part):
    key = jax.random.fold_in(key, 11)
    edge = GROUP_TOK // 8
    split_keys = jax.random.split(key, 4)
    head_len = jax.random.randint(split_keys[0], (GROUPS,), 1, edge)
    tail_total = jax.random.randint(split_keys[1], (GROUPS,), 2, edge)
    third_len = jax.random.randint(split_keys[2], (GROUPS,), 1, tail_total)
    chosen = jax.random.randint(split_keys[3], (), 0, GROUPS)
    marked = jnp.arange(GROUPS) == chosen
    head_len = jnp.where(marked, 1, head_len)
    tail_total = jnp.where(marked, 2, tail_total)
    third_len = jnp.where(marked, 1, third_len)
    fourth_len = tail_total - third_len
    long_len = GROUP_TOK - head_len - tail_total
    return jnp.stack([head_len, long_len, third_len, fourth_len], axis=1).astype(jnp.int32)


def draw_query_momentum(key, part):
    key = jax.random.fold_in(key, 21)
    return moment_buffer(key, (MODEL_WIDTH, QUERY_HEADS * HEAD_SIZE), 1.0)


def draw_keyval_momentum(key, part):
    key = jax.random.fold_in(key, 22)
    return moment_buffer(key, (2, MODEL_WIDTH, KEY_VALUE_HEADS * HEAD_SIZE), 1.0)


def draw_output_momentum(key, part):
    key = jax.random.fold_in(key, 23)
    return moment_buffer(key, (QUERY_HEADS * HEAD_SIZE, MODEL_WIDTH), 0.12)


def draw_gateup_momentum(key, part):
    key = jax.random.fold_in(key, 24)
    return moment_buffer(key, (2, MODEL_WIDTH, FF), 0.35)


def draw_down_momentum(key, part):
    key = jax.random.fold_in(key, 25)
    return moment_buffer(key, (FF, MODEL_WIDTH), 0.6)


def draw_gains_momentum(key, part):
    key = jax.random.fold_in(key, 26)
    return moment_buffer(key, (GAINS,), 1.5)


def block_scale(own_key, shape, cuts, smallest, high):
    level = 1.0
    for dim, shards_of in cuts:
        draws = jax.random.uniform(jax.random.fold_in(jax.random.fold_in(own_key, 6), dim), (shards_of,), jnp.float32, smallest / len(cuts), high / len(cuts))
        level = level * jnp.repeat(jnp.exp(draws), shape[dim] // shards_of).reshape((-1,) + (1,) * (len(shape) - 1 - dim))
    return level


def gaussian(own_key, shape, deviation, reach, cuts=(), kind=jnp.bfloat16):
    array = deviation * jax.random.normal(own_key, shape, jnp.float32)
    if cuts:
        array = array * block_scale(own_key, shape, cuts, -0.22, 0.18)
    return jnp.clip(array, -reach, reach).astype(kind)


def setup_inputs(seed: int = 0) -> dict:
    arg_keys = jax.random.split(jax.random.key(seed), 22)
    tokens = gaussian(arg_keys[0], (TOKENS, MODEL_WIDTH), 1.0, 6.0, ((0, 128),))
    cotangent = gaussian(arg_keys[1], (TOKENS, MODEL_WIDTH), 1.0, 6.0, ((0, 128),))
    doc_lengths = draw_doc_lengths(jax.random.fold_in(arg_keys[21], 71), 0)
    query_weight = gaussian(arg_keys[3], (MODEL_WIDTH, QUERY_HEADS * HEAD_SIZE), MODEL_WIDTH ** -0.5, 0.125, ((0, 16), (1, 8)), jnp.float32)
    key_value_weight = gaussian(arg_keys[4], (2, MODEL_WIDTH, KEY_VALUE_HEADS * HEAD_SIZE), MODEL_WIDTH ** -0.5, 0.125, ((1, 16), (2, 8)), jnp.float32)
    output_weight = gaussian(arg_keys[5], (QUERY_HEADS * HEAD_SIZE, MODEL_WIDTH), (QUERY_HEADS * HEAD_SIZE // 128) ** -0.5, 1.5, ((0, 8), (1, 16)), jnp.float32)
    gateup_weight = gaussian(arg_keys[6], (2, MODEL_WIDTH, FF), MODEL_WIDTH ** -0.5, 0.125, ((1, 16), (2, 8)), jnp.float32)
    down_weight = gaussian(arg_keys[7], (FF, MODEL_WIDTH), FF ** -0.5, 0.078125, ((0, 8), (1, 16)), jnp.float32)
    norm_gains = jnp.clip(1.0 + 0.1 * jax.random.normal(arg_keys[8], (GAINS,), jnp.float32), 0.5, 1.5)
    query_momentum = draw_query_momentum(jax.random.fold_in(arg_keys[21], 71), 0)
    keyval_momentum = draw_keyval_momentum(jax.random.fold_in(arg_keys[21], 71), 0)
    output_momentum = draw_output_momentum(jax.random.fold_in(arg_keys[21], 71), 0)
    gateup_momentum = draw_gateup_momentum(jax.random.fold_in(arg_keys[21], 71), 0)
    down_momentum = draw_down_momentum(jax.random.fold_in(arg_keys[21], 71), 0)
    gains_momentum = draw_gains_momentum(jax.random.fold_in(arg_keys[21], 71), 0)
    query_average = gaussian(arg_keys[15], (MODEL_WIDTH, QUERY_HEADS * HEAD_SIZE), MODEL_WIDTH ** -0.5, 0.125, ((0, 16), (1, 8)), jnp.float32)
    key_value_mean = gaussian(arg_keys[16], (2, MODEL_WIDTH, KEY_VALUE_HEADS * HEAD_SIZE), MODEL_WIDTH ** -0.5, 0.125, ((1, 16), (2, 8)), jnp.float32)
    output_average = gaussian(arg_keys[17], (QUERY_HEADS * HEAD_SIZE, MODEL_WIDTH), (QUERY_HEADS * HEAD_SIZE // 128) ** -0.5, 1.5, ((0, 8), (1, 16)), jnp.float32)
    gateup_average = gaussian(arg_keys[18], (2, MODEL_WIDTH, FF), MODEL_WIDTH ** -0.5, 0.125, ((1, 16), (2, 8)), jnp.float32)
    down_average = gaussian(arg_keys[19], (FF, MODEL_WIDTH), FF ** -0.5, 0.078125, ((0, 8), (1, 16)), jnp.float32)
    gains_average = jnp.clip(0.2 + 1.5999999 * jax.random.uniform(arg_keys[20], (GAINS,), jnp.float32) ** block_scale(arg_keys[20], (GAINS,), ((0, 128),), -0.2, 0.2), 0.2, 1.8)
    return dict(tokens=tokens, cotangent=cotangent, doc_lengths=doc_lengths, query_weight=query_weight, key_value_weight=key_value_weight, output_weight=output_weight, gateup_weight=gateup_weight, down_weight=down_weight, norm_gains=norm_gains, query_momentum=query_momentum, keyval_momentum=keyval_momentum, output_momentum=output_momentum, gateup_momentum=gateup_momentum, down_momentum=down_momentum, gains_momentum=gains_momentum, query_average=query_average, key_value_mean=key_value_mean, output_average=output_average, gateup_average=gateup_average, down_average=down_average, gains_average=gains_average)


EPSILON = 1e-06
MOMENTUM = 0.9
AVERAGING = 0.5
ROPE_BASE = 1000000.0

@jax.custom_vjp
def reduced_precision(v):
    return lax.optimization_barrier(v.astype(jnp.bfloat16)).astype(jnp.float32)

@jax.custom_vjp
def low_back(v):
    return v

def low_keep(v):
    return (reduced_precision(v), None)

def low_pass(kept, grad):
    return (grad,)

def back_keep(v):
    return (v, None)

def back_low(kept, grad):
    return (reduced_precision(grad),)
reduced_precision.defvjp(low_keep, low_pass)
low_back.defvjp(back_keep, back_low)

def dense(left, right):
    return jnp.dot(left, right, precision=lax.Precision.HIGHEST, preferred_element_type=jnp.float32)

def root_mean_norm(value_vectors, scaling):
    return value_vectors * lax.rsqrt(lax.optimization_barrier(jnp.mean(value_vectors * value_vectors, axis=-1, keepdims=True)) + EPSILON) * scaling

def rotary_embed(value_vectors, cosine_table, sine_table):
    middle = value_vectors.shape[-1] // 2
    turned = jnp.concatenate([-value_vectors[..., middle:], value_vectors[..., :middle]], axis=-1)
    return value_vectors * cosine_table + turned * sine_table

def doc_layout(length_row, row_total_count):
    doc_ends = jnp.cumsum(length_row).astype(jnp.int32)
    places = jnp.arange(row_total_count, dtype=jnp.int32)
    passed = places[:, None] >= doc_ends[None, :]
    segment = lax.optimization_barrier(jnp.sum(passed.astype(jnp.int32), axis=1))
    starts = lax.optimization_barrier(jnp.sum(jnp.where(passed, length_row[None, :], 0), axis=1)).astype(jnp.int32)
    position = places - starts
    halves = jnp.arange(HEAD_SIZE // 2, dtype=jnp.float32)
    inverse = ROPE_BASE ** (-2.0 * halves / HEAD_SIZE)
    angles = position.astype(jnp.float32)[:, None] * inverse[None, :]
    angles = jnp.concatenate([angles, angles], axis=-1)
    return (segment, places, jnp.cos(angles), jnp.sin(angles))

def step_rates(total_tokens):
    root_tokens = math.sqrt(total_tokens)
    narrow = MODEL_WIDTH ** (-0.5)
    return (narrow / (2.0 * root_tokens), narrow / (2.0 * root_tokens), (QUERY_HEADS * HEAD_SIZE // 128) ** (-0.5) / (0.24 * root_tokens), narrow / (0.7 * root_tokens), FF ** (-0.5) / (1.2 * root_tokens), 0.025 / root_tokens)

def attend_block(query_tile_block, segment_block, place_block, key_vectors, value_vectors, segment, places):
    block_row_span = query_tile_block.shape[0]
    grouped_heads = query_tile_block.reshape(block_row_span, KEY_VALUE_HEADS, QUERY_HEADS // KEY_VALUE_HEADS, HEAD_SIZE)
    scores = jnp.einsum('qkgd,skd->kgqs', grouped_heads, key_vectors, precision=lax.Precision.HIGHEST) * HEAD_SIZE ** (-0.5)
    scores = low_back(scores)
    allowed = (segment_block[:, None] == segment[None, :]) & (places[None, :] <= place_block[:, None])
    scores = jnp.where(allowed, scores, -1e+30)
    highest = lax.optimization_barrier(jnp.max(scores, axis=-1, keepdims=True))
    weights = jnp.exp(scores - highest)
    probability = reduced_precision(weights / lax.optimization_barrier(jnp.sum(weights, axis=-1, keepdims=True)))
    blended = jnp.einsum('kgqs,skd->qkgd', probability, value_vectors, precision=lax.Precision.HIGHEST)
    return blended.reshape(block_row_span, QUERY_HEADS * HEAD_SIZE)

def layer(inputs, query_matrix, keyval_matrix, output_matrix, gateup_matrix, down_matrix, gains, segment, places, cosine_table, sine_table):
    row_total_count = inputs.shape[0]
    gain_first = gains[:MODEL_WIDTH]
    gain_second = gains[MODEL_WIDTH:2 * MODEL_WIDTH]
    gain_query = gains[2 * MODEL_WIDTH:2 * MODEL_WIDTH + HEAD_SIZE]
    key_norm_gain = gains[2 * MODEL_WIDTH + HEAD_SIZE:]
    first_low = reduced_precision(root_mean_norm(inputs, gain_first))
    query_part = low_back(dense(first_low, reduced_precision(query_matrix)))
    key_slice = low_back(dense(first_low, reduced_precision(keyval_matrix[0])))
    value_slice = low_back(reduced_precision(dense(first_low, reduced_precision(keyval_matrix[1]))))
    queries = reduced_precision(rotary_embed(root_mean_norm(query_part.reshape(row_total_count, QUERY_HEADS, HEAD_SIZE), gain_query), cosine_table[:, None, :], sine_table[:, None, :]))
    key_vectors = reduced_precision(rotary_embed(root_mean_norm(key_slice.reshape(row_total_count, KEY_VALUE_HEADS, HEAD_SIZE), key_norm_gain), cosine_table[:, None, :], sine_table[:, None, :]))
    value_vectors = value_slice.reshape(row_total_count, KEY_VALUE_HEADS, HEAD_SIZE)
    block_row_span = min(512, row_total_count)
    blocks = row_total_count // block_row_span
    checked = jax.checkpoint(attend_block)

    def one_block(element):
        return checked(element[0], element[1], element[2], key_vectors, value_vectors, segment, places)
    attended = lax.map(one_block, (queries.reshape(blocks, block_row_span, QUERY_HEADS, HEAD_SIZE), segment.reshape(blocks, block_row_span), places.reshape(blocks, block_row_span)))
    attended = low_back(reduced_precision(attended.reshape(row_total_count, QUERY_HEADS * HEAD_SIZE)))
    attention_out = low_back(dense(attended, reduced_precision(output_matrix)))
    residual = inputs + attention_out
    second_low = reduced_precision(root_mean_norm(residual, gain_second))
    gate_value = low_back(dense(second_low, reduced_precision(gateup_matrix[0])))
    upward = low_back(dense(second_low, reduced_precision(gateup_matrix[1])))
    hidden = reduced_precision(jax.nn.silu(gate_value) * upward)
    return residual + low_back(dense(hidden, reduced_precision(down_matrix)))

def reference(tokens, cotangent, doc_lengths, query_weight, key_value_weight, output_weight, gateup_weight, down_weight, norm_gains, query_momentum, keyval_momentum, output_momentum, gateup_momentum, down_momentum, gains_momentum, query_average, key_value_mean, output_average, gateup_average, down_average, gains_average):
    masters = (query_weight, key_value_weight, output_weight, gateup_weight, down_weight, norm_gains)
    inputs_all = tokens.astype(jnp.float32).reshape(GROUPS, GROUP_TOK, MODEL_WIDTH)
    upstream_all = cotangent.astype(jnp.float32).reshape(GROUPS, GROUP_TOK, MODEL_WIDTH)

    def one_group(running, element):
        inputs, upstream, length_row = element
        segment, places, cosine_table, sine_table = doc_layout(length_row, GROUP_TOK)

        def forward(values_in, query_matrix, keyval_matrix, output_matrix, gateup_matrix, down_matrix, gains):
            return layer(values_in, query_matrix, keyval_matrix, output_matrix, gateup_matrix, down_matrix, gains, segment, places, cosine_table, sine_table)
        result, pullback = jax.vjp(forward, inputs, *masters)
        pulled = pullback(upstream)
        running = tuple((accum + part_grad for accum, part_grad in zip(running, pulled[1:])))
        return (running, (result, pulled[0]))
    zeros = tuple((jnp.zeros(master.shape, jnp.float32) for master in masters))
    summed, (outputs, input_grads) = lax.scan(one_group, zeros, (inputs_all, upstream_all, doc_lengths))
    block_out = outputs.reshape(TOKENS, MODEL_WIDTH).astype(jnp.bfloat16)
    input_grad = input_grads.reshape(TOKENS, MODEL_WIDTH).astype(jnp.bfloat16)
    rates = step_rates(TOKENS)
    moments = (query_momentum, keyval_momentum, output_momentum, gateup_momentum, down_momentum, gains_momentum)
    averages = (query_average, key_value_mean, output_average, gateup_average, down_average, gains_average)
    updated = []
    velocity = []
    smoothed = []
    for master, gradient, moment, average, rate in zip(masters, summed, moments, averages, rates):
        moment_next = MOMENTUM * moment + gradient
        master_next = master - rate * (gradient + MOMENTUM * moment_next)
        updated.append(master_next)
        velocity.append(moment_next)
        smoothed.append(AVERAGING * average + (1.0 - AVERAGING) * master_next)
    return (block_out, input_grad, updated[0], updated[1], updated[2], updated[3], updated[4], updated[5], velocity[0], velocity[1], velocity[2], velocity[3], velocity[4], velocity[5], smoothed[0], smoothed[1], smoothed[2], smoothed[3], smoothed[4], smoothed[5])
```

```python
import math

import jax
import jax.numpy as jnp
from jax import lax
from jax.experimental import pallas as pl
from jax.experimental.pallas import tpu as pltpu
from jax.sharding import Mesh
from jax.sharding import PartitionSpec as P

MODEL_WIDTH = 2048
QUERY_HEADS = 16
HEAD_SIZE = 128
FF = 6144
EPSILON = 1e-06
MOMENTUM = 0.9
AVERAGING = 0.5
ROPE_BASE = 1000000.0

AXES = ("z", "ylo", "core", "yhi", "x")
GRID = (4, 2, 2, 2, 4)
RING = 4
BF16 = jnp.bfloat16
F32 = jnp.float32


class Place:
    def __init__(self):
        self.x = lax.axis_index("x")
        self.z = lax.axis_index("z")
        self.core = lax.axis_index("core")
        self.yhi = lax.axis_index("yhi")
        self.ylo = lax.axis_index("ylo")
        self.y = self.yhi * 2 + self.ylo

    def at(self, axis):
        return self.x if axis == "x" else self.y if axis == "y" else self.z

    def step(self, axis, by):
        return lax.rem(self.at(axis) + (by + RING), RING)

    def device(self, axis, by=1):
        if axis == "core":
            return {"core": 1 - self.core}
        if axis == "turn":
            return {"core": 1 - self.core, "yhi": 1 - self.yhi}
        there = self.step(axis, by)
        if axis == "y":
            return {"yhi": lax.div(there, 2), "ylo": lax.rem(there, 2)}
        return {axis: there}

    def native(self):
        return self.core == self.yhi


class Net:
    def __init__(self, place, send_sems, recv_sems, local_sems):
        self.place = place
        self.send_sems, self.recv_sems, self.local_sems = send_sems, recv_sems, local_sems
        self.count = 0
        self.local_count = 0
        self.pending = []
        self.late = []

    def copy(self, source, target, index, axis, by=1):
        return pltpu.make_async_remote_copy(
            src_ref=source,
            dst_ref=target,
            send_sem=self.send_sems.at[index],
            recv_sem=self.recv_sems.at[index],
            device_id=self.place.device(axis, by),
            device_id_type=pl.DeviceIdType.MESH,
        )

    def number(self):
        self.count += 1
        return self.count - 1

    def send(self, source, target, axis, by=1):
        index = self.number()
        copy = self.copy(source, target, index, axis, by)
        copy.start()
        self.pending.append(copy)
        return index

    def arrive(self, index, target, axis, by=1):
        self.copy(target, target, index, axis, by).wait_recv()

    def local(self, source, target):
        copy = pltpu.make_async_copy(source, target, self.local_sems.at[self.local_count])
        self.local_count += 1
        copy.start()
        return copy

    def finish(self):
        for wait in self.late:
            wait()
        for copy in self.pending:
            copy.wait_send()


def greet(place, partners):
    barrier = pltpu.get_barrier_semaphore()
    for axis, by in partners:
        pl.semaphore_signal(
            barrier,
            inc=1,
            device_id=place.device(axis, by),
            device_id_type=pl.DeviceIdType.MESH,
        )
    pl.semaphore_wait(barrier, len(partners))


def drive(parts):
    parts = list(parts)
    while parts:
        for part in list(parts):
            try:
                next(part)
            except StopIteration:
                parts.remove(part)


def rows_gather(net, own, whole, rows):
    place = net.place
    half = rows // 2

    def block(core, x, part):
        start = pl.multiple_of((core * RING + x) * rows + part * half, half)
        return whole.at[pl.ds(start, half)]

    me, other = place.core, 1 - place.core
    right, left, far = place.step("x", 1), place.step("x", -1), place.step("x", 2)
    kept = net.local(own, whole.at[pl.ds(pl.multiple_of((me * RING + place.x) * rows, rows), rows)])
    piece = [own.at[pl.ds(part * half, half)] for part in range(2)]
    sent = {}
    for axis, by, part in (("x", 1, 0), ("x", -1, 1), ("x", 1, 1), ("x", -1, 0)):
        sent[by, part] = net.send(piece[part], block(me, place.x, part), axis, by)
    shared = []

    def share(x, part, source=None):
        there = block(me, x, part)
        shared.append((net.send(there if source is None else source, there, "core"), x, part))

    share(place.x, 0, piece[0])
    share(place.x, 1, piece[1])
    yield
    net.arrive(sent[1, 0], block(me, left, 0), "x", 1)
    passed_right = net.send(block(me, left, 0), block(me, left, 0), "x", 1)
    share(left, 0)
    net.arrive(sent[-1, 1], block(me, right, 1), "x", -1)
    passed_left = net.send(block(me, right, 1), block(me, right, 1), "x", -1)
    share(right, 1)
    yield
    net.arrive(sent[1, 1], block(me, left, 1), "x", 1)
    share(left, 1)
    net.arrive(sent[-1, 0], block(me, right, 0), "x", -1)
    share(right, 0)
    yield
    net.arrive(passed_right, block(me, far, 0), "x", 1)
    share(far, 0)
    net.arrive(passed_left, block(me, far, 1), "x", -1)
    share(far, 1)
    yield
    for index, x, part in shared:
        net.arrive(index, block(other, x, part), "core")
    kept.wait()


ROWS_GATHER_COPIES = 14


def ring_sum(net, axis, own, land, finish):
    through_left, through_right, sum_right, sum_left = land[0], land[1], land[2], land[3]
    from_left, from_right = (land[4], land[5]), (land[6], land[7])
    a = net.send(own(2, 0), through_left, axis, 1)
    b = net.send(own(2, 1), through_right, axis, -1)
    c = net.send(own(1, 1), from_left[1], axis, 1)
    d = net.send(own(-1, 0), from_right[0], axis, -1)
    yield
    net.arrive(a, through_left, axis, 1)
    sum_right[...] = through_left[...] + own(1, 0)[...]
    e = net.send(sum_right, from_left[0], axis, 1)
    net.arrive(b, through_right, axis, -1)
    sum_left[...] = through_right[...] + own(-1, 1)[...]
    f = net.send(sum_left, from_right[1], axis, -1)
    yield
    net.arrive(d, from_right[0], axis, -1)
    net.arrive(c, from_left[1], axis, 1)
    net.arrive(e, from_left[0], axis, 1)
    net.arrive(f, from_right[1], axis, -1)
    for part in range(2):
        total = own(0, part)[...].astype(F32) + from_left[part][...].astype(F32)
        finish(part, total + from_right[part][...].astype(F32))
    yield


RING_SUM_COPIES = 6


def rows_sum(net, whole, total, rows, landed, summed, land):
    place = net.place
    half = rows // 2

    def block(core, x, part):
        start = pl.multiple_of((core * RING + x) * rows + part * half, half)
        return whole.at[pl.ds(start, half)]

    me, other = place.core, 1 - place.core
    order = [(2, 0), (2, 1), (1, 1), (-1, 0), (1, 0), (-1, 1), (0, 0), (0, 1)]
    sent = [
        net.send(block(other, place.step("x", k), part), landed.at[k % RING, part], "core")
        for k, part in order
    ]
    yield
    def combine(at):
        k, part = order[at]
        net.arrive(sent[at], landed.at[k % RING, part], "core")
        summed[k % RING, part] = block(me, place.step("x", k), part)[...] + landed[k % RING, part]

    for at in range(4):
        combine(at)

    def own(k, part):
        return summed.at[k % RING, part]

    def finish(part, value):
        total[pl.ds(part * half, half)] = value

    ring = ring_sum(net, "x", own, [land.at[n] for n in range(8)], finish)
    next(ring)
    for at in range(4, 8):
        combine(at)
    yield
    yield from ring


ROWS_SUM_COPIES = 8 + RING_SUM_COPIES


def plane_gather(net, own, whole, rows, spot):
    place = net.place
    quarter = rows // 4

    def view(z, y, color, part):
        row, columns = spot(z, y)
        start = pl.multiple_of(row + (color * 2 + part) * quarter, quarter)
        return whole.at[pl.ds(start, quarter), columns]

    def one(color):
        first, second = ("z", "y") if color == 0 else ("y", "z")

        def at(i, j, part):
            z, y = (i, j) if color == 0 else (j, i)
            return view(z, y, color, part)

        def ring(axis, here, sources):
            sent = {}
            for by, part in ((1, 0), (-1, 1), (1, 1), (-1, 0)):
                source = sources[part] if sources is not None else here(place.at(axis), part)
                sent[by, part] = net.send(source, here(place.at(axis), part), axis, by)
            yield
            left, right, far = place.step(axis, -1), place.step(axis, 1), place.step(axis, 2)
            net.arrive(sent[1, 0], here(left, 0), axis, 1)
            go = net.send(here(left, 0), here(left, 0), axis, 1)
            net.arrive(sent[-1, 1], here(right, 1), axis, -1)
            back = net.send(here(right, 1), here(right, 1), axis, -1)
            net.arrive(sent[1, 1], here(left, 1), axis, 1)
            net.arrive(sent[-1, 0], here(right, 0), axis, -1)
            yield
            net.arrive(go, here(far, 0), axis, 1)
            net.arrive(back, here(far, 1), axis, -1)
            yield

        mine = [own.at[pl.ds((color * 2 + part) * quarter, quarter)] for part in range(2)]
        one_ring = ring(first, lambda i, part: at(i, place.at(second), part), mine)

        def second_ring(k):
            i = place.step(first, k)
            return ring(
                second, lambda j, part: at(i, j, part), mine if k == 0 else None
            )

        rings = [second_ring(0)]
        next(one_ring)
        next(rings[0])
        yield
        next(one_ring)
        for k in (1, -1):
            rings.append(second_ring(k))
            next(rings[-1])
        yield
        next(rings[0])
        next(one_ring)
        rings.append(second_ring(2))
        next(rings[-1])
        yield
        next(rings[1])
        next(rings[2])
        yield
        next(rings[3])
        yield
        for ring_ in rings:
            next(ring_)
        yield

    row, columns = spot(place.z, place.y)
    kept = net.local(own, whole.at[pl.ds(pl.multiple_of(row, rows), rows), columns])
    parts = [one(0), one(1)]
    for _ in range(6):
        for part in parts:
            next(part)
        yield
    kept.wait()


PLANE_GATHER_COPIES = 60


def plane_sum(net, whole, total, rows, spot, land, between):
    place = net.place
    quarter = rows // 4

    def view(z, y, color, part):
        row, columns = spot(z, y)
        start = pl.multiple_of(row + (color * 2 + part) * quarter, quarter)
        return whole.at[pl.ds(start, quarter), columns]

    def one(color):
        first, second = ("y", "z") if color == 0 else ("z", "y")

        def first_ring(k):
            def own(n, part):
                far, near = place.step(second, k), place.step(first, n)
                z, y = (far, near) if color == 0 else (near, far)
                return view(z, y, color, part)

            def keep(part, value):
                between[color, k % RING, part] = value.astype(BF16)

            slots = [land.at[color, k % RING, n] for n in range(8)]
            return ring_sum(net, first, own, slots, keep)

        rings = [first_ring(k) for k in (2, 1, -1, 0)]
        for ring in rings:
            next(ring)
        yield
        for ring in rings:
            next(ring)
        yield
        for ring in rings[:3]:
            next(ring)

        def done(part, value):
            start = (color * 2 + part) * quarter
            total[pl.ds(start, quarter)] = value.astype(total.dtype)

        last = ring_sum(
            net,
            second,
            lambda k, part: between.at[color, k % RING, part],
            [land.at[color, 4, n] for n in range(8)],
            done,
        )
        next(last)
        next(rings[3])
        yield
        next(last)
        yield
        next(last)
        yield

    parts = [one(0), one(1)]
    for _ in range(5):
        for part in parts:
            next(part)
        yield


PLANE_SUM_COPIES = 2 * 5 * RING_SUM_COPIES


def turned(net, pairs):
    place = net.place
    native = place.native()
    firsts = [(net.number(), net.number()) for _ in pairs]
    base = net.local_count
    net.local_count += len(pairs)

    def halves(ref):
        rows = ref.shape[0] // 2
        return [ref.at[pl.ds(part * rows, rows)] for part in range(2)]

    def copies():
        return [
            net.copy(source, target, index, "turn")
            for (whole_source, whole_target), indices in zip(pairs, firsts)
            for source, target, index in zip(halves(whole_source), halves(whole_target), indices)
        ]

    def kept():
        return [
            pltpu.make_async_copy(source, target, net.local_sems.at[base + k])
            for k, (source, target) in enumerate(pairs)
        ]

    @pl.when(jnp.logical_not(native))
    def _():
        for copy in copies():
            copy.start()

    @pl.when(native)
    def _():
        for copy in kept():
            copy.start()

    yield

    def wait_all():
        @pl.when(jnp.logical_not(native))
        def _():
            for copy in copies():
                copy.wait()

        @pl.when(native)
        def _():
            for copy in kept():
                copy.wait()

    net.late.append(wait_all)


def gains_gather(net, own, whole):
    place = net.place

    def rows(z, y, x, core, count):
        start = ((z * RING + y) * RING + x) * 2 + core
        return whole.at[pl.ds(start if count == 1 else pl.multiple_of(start, count), count)]

    kept = net.local(own, rows(place.z, place.y, place.x, place.core, 1))
    kept.wait()
    spots = {
        "core": lambda by: rows(place.z, place.y, place.x, (place.core + by) % 2, 1),
        "x": lambda by: rows(place.z, place.y, place.step("x", by), 0, 2),
        "y": lambda by: rows(place.z, place.step("y", by), 0, 0, 8),
        "z": lambda by: rows(place.step("z", by), 0, 0, 0, 32),
    }
    for axis in ("core", "x", "y", "z"):
        spot = spots[axis]
        steps = (1,) if axis == "core" else (1, -1, 2)
        sent = [net.send(spot(0), spot(0), axis, by) for by in steps]
        yield
        for index, by in zip(sent, steps):
            net.arrive(index, spot(-by), axis, by)
    yield


GAINS_COPIES = 10


def gains_sum(net, whole, total, land):
    place = net.place

    def rows(z, y, x, core, count):
        start = ((z * RING + y) * RING + x) * 2 + core
        return whole.at[pl.ds(start if count == 1 else pl.multiple_of(start, count), count)]

    spots = {
        "z": lambda by: rows(place.step("z", by), 0, 0, 0, 32),
        "y": lambda by: rows(place.z, place.step("y", by), 0, 0, 8),
        "x": lambda by: rows(place.z, place.y, place.step("x", by), 0, 2),
        "core": lambda by: rows(place.z, place.y, place.x, (place.core + by) % 2, 1),
    }
    first = 0
    for axis, count in (("z", 32), ("y", 8), ("x", 2), ("core", 1)):
        spot = spots[axis]
        steps = (1,) if axis == "core" else (1, -1, 2)
        sent = [
            net.send(spot(by), land.at[n, pl.ds(first, count)], axis, by)
            for n, by in enumerate(steps)
        ]
        yield
        value = spot(0)[...]
        for n, (index, by) in enumerate(zip(sent, steps)):
            net.arrive(index, land.at[n, pl.ds(first, count)], axis, by)
            value = value + land[n, pl.ds(first, count)]
        if axis == "core":
            total[...] = value
        else:
            spot(0)[...] = value
        first += count
    yield


class Kernel:
    def __init__(self, number, copies, locals_, partners):
        self.number, self.copies, self.locals_, self.partners = number, copies, locals_, partners

    def __call__(self, plan, arrays, outs, scratch=()):
        spaces = [pl.BlockSpec(memory_space=space) for _, space in arrays]
        n_in, n_out, n_scratch = len(arrays), len(outs), len(scratch)

        def kernel(*refs):
            ins, results = refs[:n_in], refs[n_in : n_in + n_out]
            work = refs[n_in + n_out : n_in + n_out + n_scratch]
            place = Place()
            net = Net(place, *refs[n_in + n_out + n_scratch :])
            greet(place, self.partners)
            drive(plan(net, ins, results, work))
            net.finish()

        return pl.pallas_call(
            kernel,
            out_shape=[shape for shape, _ in outs],
            in_specs=spaces,
            out_specs=[pl.BlockSpec(memory_space=space) for _, space in outs],
            scratch_shapes=[
                *scratch,
                pltpu.SemaphoreType.DMA((self.copies,)),
                pltpu.SemaphoreType.DMA((self.copies,)),
                pltpu.SemaphoreType.DMA((self.locals_,)),
            ],
            compiler_params=pltpu.CompilerParams(
                collective_id=self.number, has_side_effects=True, vmem_limit_bytes=48 * 2**20
            ),
            name="links_%d" % self.number,
        )(*[array for array, _ in arrays])


HBM = pl.ANY
VMEM = pltpu.VMEM
X_PARTNERS = (("x", 1), ("x", -1), ("core", 1))
PLANE_PARTNERS = (("y", 1), ("y", -1), ("z", 1), ("z", -1))
TURN_PARTNERS = (("turn", 1),)


def shape(dims, dtype=BF16):
    return jax.ShapeDtypeStruct(dims, dtype)


def attention_spot(z, y):
    piece = z * 4 + lax.rem(y, 2) * 2 + lax.div(y, 2)
    return piece * 128


def rows_spot(z, y):
    return attention_spot(z, y), pl.ds(0, 512)


def output_spot(z, y):
    return 0, pl.ds(pl.multiple_of(attention_spot(z, y), 128), 128)


def gateup_spot(z, y):
    columns = pl.ds(pl.multiple_of(lax.div(y, 2) * 384, 128), 384)
    return (z * 2 + lax.rem(y, 2)) * 256, columns


def down_spot(z, y):
    columns = pl.ds(pl.multiple_of((z * 2 + lax.rem(y, 2)) * 256, 128), 256)
    return lax.div(y, 2) * 384, columns


def enter(tokens, qkv, output, gains, lengths):
    def plan(net, ins, outs, work):
        tokens_, qkv_, output_, gains_, lengths_ = ins

        def swap_lengths():
            index = net.send(lengths_, outs[4], "core")
            yield
            net.arrive(index, outs[4], "core")

        return [
            gains_gather(net, gains_, outs[3]),
            turned(net, [(tokens_, outs[0]), (qkv_, outs[1]), (output_, outs[2])]),
            swap_lengths(),
        ]

    partners = X_PARTNERS + (("x", 2),) + PLANE_PARTNERS + (("y", 2), ("z", 2)) + TURN_PARTNERS
    return Kernel(0, GAINS_COPIES + 6 + 1, 4, partners)(
        plan,
        [(tokens, HBM), (qkv, HBM), (output, HBM), (gains, VMEM), (lengths, VMEM)],
        [
            (shape(tokens.shape), HBM),
            (shape(qkv.shape), HBM),
            (shape(output.shape), HBM),
            (shape((128, 1, 128), F32), VMEM),
            (shape((8, 128), jnp.int32), VMEM),
        ],
    )


def first_gather(first_low, qkv, output, cotangent, gate, up, down):
    def plan(net, ins, outs, work):
        first_, qkv_, output_, cotangent_, gate_, up_, down_ = ins
        place = net.place
        mine, theirs = place.core, 1 - place.core

        def halves():
            kept, sent = [], []
            for source, target in ((gate_, outs[4]), (up_, outs[5])):
                spot = target.at[pl.ds(pl.multiple_of(mine * 128, 128), 128)]
                there = target.at[pl.ds(pl.multiple_of(theirs * 128, 128), 128)]
                cut = lambda core: source.at[:, pl.ds(pl.multiple_of(core * 384, 128), 384)]
                kept.append(net.local(cut(mine), spot))
                sent.append((net.send(cut(theirs), spot, "core"), there))
            spot = outs[6].at[:, pl.ds(pl.multiple_of(mine * 128, 128), 128)]
            there = outs[6].at[:, pl.ds(pl.multiple_of(theirs * 128, 128), 128)]
            cut = lambda core: down_.at[pl.ds(pl.multiple_of(core * 384, 128), 384)]
            kept.append(net.local(cut(mine), spot))
            sent.append((net.send(cut(theirs), spot, "core"), there))
            yield
            for copy in kept:
                copy.wait()
            for index, there in sent:
                net.arrive(index, there, "core")

        return [
            rows_gather(net, first_, outs[0], 128),
            plane_gather(net, qkv_, outs[1], 128, rows_spot),
            plane_gather(net, output_, outs[2], 256, output_spot),
            turned(net, [(cotangent_, outs[3])]),
            halves(),
        ]

    return Kernel(
        1, ROWS_GATHER_COPIES + 2 * PLANE_GATHER_COPIES + 2 + 3, 1 + 2 + 1 + 3,
        X_PARTNERS + PLANE_PARTNERS + TURN_PARTNERS,
    )(
        plan,
        [(a, HBM) for a in (first_low, qkv, output, cotangent, gate, up, down)],
        [
            (shape((1024, 2048)), HBM),
            (shape((2048, 512)), HBM),
            (shape((256, 2048)), HBM),
            (shape((128, 2048)), HBM),
            (shape((256, 384)), HBM),
            (shape((256, 384)), HBM),
            (shape((384, 256)), HBM),
        ],
    )


def gather_and_weight(number, rows, piece, whole, spot):
    def plan(net, ins, outs, work):
        return [
            rows_gather(net, ins[0], outs[0], 128),
            plane_gather(net, ins[1], outs[1], piece.shape[0], spot),
        ]

    return Kernel(
        number, ROWS_GATHER_COPIES + PLANE_GATHER_COPIES, 2, X_PARTNERS + PLANE_PARTNERS
    )(
        plan,
        [(rows, HBM), (piece, HBM)],
        [(shape((1024, 2048)), HBM), (shape(whole), HBM)],
    )


SUM_SCRATCH = (
    pltpu.VMEM((4, 2, 64, 2048), BF16),
    pltpu.VMEM((4, 2, 64, 2048), BF16),
    pltpu.VMEM((8, 64, 2048), BF16),
)


def plane_scratch(rows, columns):
    return (
        pltpu.VMEM((2, 5, 8, rows // 4, columns), BF16),
        pltpu.VMEM((2, 4, 2, rows // 4, columns), BF16),
    )


def sum_and_weight(number, terms, piece, whole, spot):
    def plan(net, ins, outs, work):
        return [
            rows_sum(net, ins[0], outs[0], 128, *work),
            plane_gather(net, ins[1], outs[1], piece.shape[0], spot),
        ]

    return Kernel(
        number, ROWS_SUM_COPIES + PLANE_GATHER_COPIES, 1, X_PARTNERS + PLANE_PARTNERS
    )(
        plan,
        [(terms, VMEM), (piece, HBM)],
        [(shape((128, 2048), F32), VMEM), (shape(whole), HBM)],
        SUM_SCRATCH,
    )


def sum_and_gradient(number, terms, gradient, piece, spot):
    def plan(net, ins, outs, work):
        return [
            rows_sum(net, ins[0], outs[0], 128, *work[:3]),
            plane_sum(net, ins[1], outs[1], piece[0], spot, *work[3:]),
        ]

    return Kernel(
        number, ROWS_SUM_COPIES + PLANE_SUM_COPIES, 1, X_PARTNERS + PLANE_PARTNERS
    )(
        plan,
        [(terms, VMEM), (gradient, VMEM)],
        [(shape((128, 2048), F32), VMEM), (shape(piece), VMEM)],
        SUM_SCRATCH + plane_scratch(*piece),
    )


def gather_and_gradient(number, rows, gradient, piece, spot):
    def plan(net, ins, outs, work):
        return [
            rows_gather(net, ins[0], outs[0], 128),
            plane_sum(net, ins[1], outs[1], piece[0], spot, *work),
        ]

    return Kernel(
        number, ROWS_GATHER_COPIES + PLANE_SUM_COPIES, 1, X_PARTNERS + PLANE_PARTNERS
    )(
        plan,
        [(rows, HBM), (gradient, VMEM)],
        [(shape((1024, 2048)), HBM), (shape(piece), VMEM)],
        plane_scratch(*piece),
    )


def last_sums(terms, qkv_grad, output_grad, gains):
    def plan(net, ins, outs, work):
        return [
            rows_sum(net, ins[0], outs[0], 128, *work[:3]),
            plane_sum(net, ins[1], outs[1], 128, rows_spot, *work[3:5]),
            plane_sum(net, ins[2], outs[2], 256, output_spot, *work[5:7]),
            gains_sum(net, work[8], outs[3], work[7]),
        ]

    def with_gains(net, ins, outs, work):
        net.local(ins[3], work[8]).wait()
        return plan(net, ins, outs, work)

    return Kernel(
        8, ROWS_SUM_COPIES + 2 * PLANE_SUM_COPIES + GAINS_COPIES, 1,
        X_PARTNERS + (("x", 2),) + PLANE_PARTNERS + (("y", 2), ("z", 2)),
    )(
        with_gains,
        [(terms, VMEM), (qkv_grad, VMEM), (output_grad, VMEM), (gains, HBM)],
        [
            (shape((128, 2048), F32), VMEM),
            (shape((128, 512)), VMEM),
            (shape((256, 128)), VMEM),
            (shape((1, 1, 128), F32), VMEM),
        ],
        SUM_SCRATCH
        + plane_scratch(128, 512)
        + plane_scratch(256, 128)
        + (pltpu.VMEM((3, 64, 1, 128), F32), pltpu.VMEM((128, 1, 128), F32)),
    )


def leave(block_out, input_grad, qkv, output, gate, up, down):
    def plan(net, ins, outs, work):
        place = net.place
        mine, theirs = place.core, 1 - place.core

        def halves():
            kept, sent = [], []
            for source, target in ((ins[4], outs[4]), (ins[5], outs[5])):
                cut = lambda core: source.at[pl.ds(pl.multiple_of(core * 128, 128), 128)]
                spot = target.at[:, pl.ds(pl.multiple_of(mine * 384, 128), 384)]
                there = target.at[:, pl.ds(pl.multiple_of(theirs * 384, 128), 384)]
                kept.append(net.local(cut(mine), spot))
                sent.append((net.send(cut(theirs), spot, "core"), there))
            cut = lambda core: ins[6].at[:, pl.ds(pl.multiple_of(core * 128, 128), 128)]
            spot = outs[6].at[pl.ds(pl.multiple_of(mine * 384, 128), 384)]
            there = outs[6].at[pl.ds(pl.multiple_of(theirs * 384, 128), 384)]
            kept.append(net.local(cut(mine), spot))
            sent.append((net.send(cut(theirs), spot, "core"), there))
            yield
            for copy in kept:
                copy.wait()
            for index, there in sent:
                net.arrive(index, there, "core")

        return [turned(net, list(zip(ins[:4], outs[:4]))), halves()]

    return Kernel(9, 8 + 3, 4 + 3, (("core", 1),) + TURN_PARTNERS)(
        plan,
        [(a, HBM) for a in (block_out, input_grad, qkv, output, gate, up, down)],
        [
            (shape((128, 2048)), HBM),
            (shape((128, 2048)), HBM),
            (shape((128, 512)), HBM),
            (shape((256, 128)), HBM),
            (shape((128, 768)), HBM),
            (shape((128, 768)), HBM),
            (shape((768, 128)), HBM),
        ],
    )


def root_mean_norm(value_vectors, scaling):
    return (
        value_vectors
        * lax.rsqrt(jnp.mean(value_vectors * value_vectors, axis=-1, keepdims=True) + EPSILON)
        * scaling
    )


def rotary_embed(value_vectors, cosine_table, sine_table):
    middle = value_vectors.shape[-1] // 2
    turned = jnp.concatenate([-value_vectors[..., middle:], value_vectors[..., :middle]], axis=-1)
    return value_vectors * cosine_table + turned * sine_table


def doc_layout(length_row, row_total_count):
    doc_ends = jnp.cumsum(length_row)
    places = jnp.arange(row_total_count, dtype=jnp.int32)
    passed = places[:, None] >= doc_ends[None, :]
    segment = jnp.sum(passed.astype(jnp.int32), axis=1)
    starts = jnp.sum(jnp.where(passed, length_row[None, :], 0), axis=1)
    position = places - starts
    halves = jnp.arange(HEAD_SIZE // 2, dtype=jnp.float32)
    inverse = ROPE_BASE ** (-2.0 * halves / HEAD_SIZE)
    angles = position.astype(jnp.float32)[:, None] * inverse[None, :]
    angles = jnp.concatenate([angles, angles], axis=-1)
    return (segment, places, jnp.cos(angles), jnp.sin(angles))


def step_rates(total_tokens):
    root_tokens = math.sqrt(total_tokens)
    narrow = MODEL_WIDTH ** (-0.5)
    return (
        narrow / (2.0 * root_tokens),
        narrow / (2.0 * root_tokens),
        (QUERY_HEADS * HEAD_SIZE // 128) ** (-0.5) / (0.24 * root_tokens),
        narrow / (0.7 * root_tokens),
        FF ** (-0.5) / (1.2 * root_tokens),
        0.025 / root_tokens,
    )


def swiglu(gate_value, upward):
    return jax.nn.silu(gate_value) * upward


def head_turn(projected, scaling, cosine_table, sine_table):
    heads = projected.reshape(projected.shape[0], -1, HEAD_SIZE)
    return rotary_embed(
        root_mean_norm(heads, scaling), cosine_table[:, None, :], sine_table[:, None, :]
    )


def product(left, right):
    return jnp.dot(left, right, preferred_element_type=jnp.float32)


def contract_last(left, right):
    return lax.dot_general(
        left, right, (((1,), (1,)), ((), ())), preferred_element_type=jnp.float32
    )


def contract_first(left, right):
    return lax.dot_general(
        left, right, (((0,), (0,)), ((), ())), preferred_element_type=jnp.float32
    )


def scores_for(query_tile_block, key_vectors):
    return jnp.einsum(
        "qkgd,skd->kgqs", query_tile_block, key_vectors, preferred_element_type=jnp.float32
    ) * HEAD_SIZE ** (-0.5)


def mask_for(segment_block, place_block, segment, places):
    return (segment_block[:, None] == segment[None, :]) & (places[None, :] <= place_block[:, None])


def attend_forward(queries, key_vectors, value_vectors, segment, places, block_row_span):
    row_total_count = queries.shape[0]
    key_heads = key_vectors.shape[1]
    sharing = queries.shape[1] // key_heads
    blocks = row_total_count // block_row_span
    grouped_heads = queries.reshape(blocks, block_row_span, key_heads, sharing, HEAD_SIZE)

    def one_block(element):
        query_tile_block, segment_block, place_block = element
        allowed = mask_for(segment_block, place_block, segment, places)
        scores = jnp.where(allowed, scores_for(query_tile_block, key_vectors), -1e30)
        highest = jnp.max(scores, axis=-1, keepdims=True)
        weights = jnp.exp(scores - highest)
        summed = jnp.sum(weights, axis=-1, keepdims=True)
        probability = (weights / summed).astype(jnp.bfloat16)
        blended = jnp.einsum(
            "kgqs,skd->qkgd", probability, value_vectors, preferred_element_type=jnp.float32
        )
        return (blended.reshape(block_row_span, -1), highest + jnp.log(summed))

    return lax.map(
        one_block,
        (
            grouped_heads,
            segment.reshape(blocks, block_row_span),
            places.reshape(blocks, block_row_span),
        ),
    )


def attend_backward(
    queries, key_vectors, value_vectors, out_grad, log_totals, segment, places, block_row_span
):
    row_total_count = queries.shape[0]
    key_heads = key_vectors.shape[1]
    sharing = queries.shape[1] // key_heads
    blocks = row_total_count // block_row_span
    scaling = HEAD_SIZE ** (-0.5)
    grouped_heads = queries.reshape(blocks, block_row_span, key_heads, sharing, HEAD_SIZE)
    grad_grouped = out_grad.reshape(blocks, block_row_span, key_heads, sharing, HEAD_SIZE)

    def one_block(running, element):
        key_sum, value_sum = running
        query_tile_block, grad_block, log_block, segment_block, place_block = element
        allowed = mask_for(segment_block, place_block, segment, places)
        scores = scores_for(query_tile_block, key_vectors)
        probability = jnp.where(allowed, jnp.exp(scores - log_block), 0.0)
        probability_low = probability.astype(jnp.bfloat16)
        value_sum = value_sum + jnp.einsum(
            "kgqs,qkgd->skd", probability_low, grad_block, preferred_element_type=jnp.float32
        )
        prob_grad = jnp.einsum(
            "qkgd,skd->kgqs", grad_block, value_vectors, preferred_element_type=jnp.float32
        )
        centre = jnp.sum(probability * prob_grad, axis=-1, keepdims=True)
        score_grad = (probability * (prob_grad - centre)).astype(jnp.bfloat16)
        query_grad = (
            jnp.einsum(
                "kgqs,skd->qkgd", score_grad, key_vectors, preferred_element_type=jnp.float32
            )
            * scaling
        )
        key_sum = (
            key_sum
            + jnp.einsum(
                "kgqs,qkgd->skd", score_grad, query_tile_block, preferred_element_type=jnp.float32
            )
            * scaling
        )
        return ((key_sum, value_sum), query_grad.reshape(block_row_span, -1, HEAD_SIZE))

    empty = jnp.zeros(key_vectors.shape, jnp.float32)
    (key_grad, value_grad), query_grads = lax.scan(
        one_block,
        (empty, empty),
        (
            grouped_heads,
            grad_grouped,
            log_totals,
            segment.reshape(blocks, block_row_span),
            places.reshape(blocks, block_row_span),
        ),
    )
    return (query_grads.reshape(row_total_count, -1, HEAD_SIZE), key_grad, value_grad)


def body(
    tokens_own,
    cotangent_own,
    doc_lengths,
    query_weight,
    key_value_weight,
    output_weight,
    gateup_weight,
    down_weight,
    norm_gains,
    query_momentum,
    keyval_momentum,
    output_momentum,
    gateup_momentum,
    down_momentum,
    gains_momentum,
    query_average,
    key_value_mean,
    output_average,
    gateup_average,
    down_average,
    gains_average,
):
    group_rows = 1024
    block_row_span = 512
    rates = step_rates(16384)
    native = lax.axis_index("core") == lax.axis_index("yhi")
    qkv_own = jnp.concatenate(
        [query_weight, key_value_weight[0], key_value_weight[1]], axis=1
    ).astype(BF16)
    lengths = jnp.pad(doc_lengths, ((0, 7), (0, 124)))
    tokens, qkv_piece, output_piece, gains_rows, lengths_there = enter(
        tokens_own,
        qkv_own,
        output_weight.astype(BF16),
        jnp.pad(norm_gains, (0, 94)).reshape(1, 1, 128),
        lengths,
    )
    gains_full = (
        gains_rows.reshape(4, 2, 2, 4, 2, 128)[..., :34].transpose(0, 2, 4, 1, 3, 5).reshape(4352)
    )
    gain_first = gains_full[:MODEL_WIDTH]
    gain_second = gains_full[MODEL_WIDTH : 2 * MODEL_WIDTH]
    gain_query = gains_full[2 * MODEL_WIDTH : 2 * MODEL_WIDTH + HEAD_SIZE]
    key_norm_gain = gains_full[2 * MODEL_WIDTH + HEAD_SIZE :]
    length_row = jnp.where(native, doc_lengths[0], lengths_there[0, :4])
    segment, places, cosine_table, sine_table = doc_layout(length_row, group_rows)
    inputs = tokens.astype(jnp.float32)
    first_normed, first_pull = jax.vjp(root_mean_norm, inputs, gain_first)
    first_low = first_normed.astype(jnp.bfloat16)
    normed_all, qkv_full, output_full, cotangent, gate_piece, up_piece, down_piece = first_gather(
        first_low,
        qkv_piece,
        output_piece,
        cotangent_own,
        gateup_weight[0].astype(BF16),
        gateup_weight[1].astype(BF16),
        down_weight.astype(BF16),
    )
    parts = product(normed_all, qkv_full)
    query_part, key_slice, value_slice = parts[:, :256], parts[:, 256:384], parts[:, 384:]

    def turn_both(query_in, key_in, query_scale, key_scale):
        return (
            head_turn(query_in, query_scale, cosine_table, sine_table),
            head_turn(key_in, key_scale, cosine_table, sine_table),
        )

    (query_turned, key_turned), turn_pull = jax.vjp(
        turn_both, query_part, key_slice, gain_query, key_norm_gain
    )
    queries = query_turned.astype(jnp.bfloat16)
    key_vectors = key_turned.astype(jnp.bfloat16)
    value_vectors = value_slice.astype(jnp.bfloat16).reshape(group_rows, -1, HEAD_SIZE)
    attended, log_totals = attend_forward(
        queries, key_vectors, value_vectors, segment, places, block_row_span
    )
    attended_low = attended.reshape(group_rows, -1).astype(jnp.bfloat16)
    attention_out, gate_full = sum_and_weight(
        2, product(attended_low, output_full).astype(BF16), gate_piece, (2048, 768), gateup_spot
    )
    residual = inputs + attention_out
    second_normed, second_pull = jax.vjp(root_mean_norm, residual, gain_second)
    second_low = second_normed.astype(jnp.bfloat16)
    second_all, up_full = gather_and_weight(3, second_low, up_piece, (2048, 768), gateup_spot)
    upstream_all, down_full = gather_and_weight(4, cotangent, down_piece, (768, 2048), down_spot)
    gate_value = product(second_all, gate_full)
    upward = product(second_all, up_full)
    activated, swiglu_pull = jax.vjp(swiglu, gate_value, upward)
    hidden = activated.astype(jnp.bfloat16)
    mlp_terms = product(hidden, down_full).astype(BF16)
    hidden_grad = contract_last(upstream_all, down_full)
    down_grad = contract_first(hidden, upstream_all).astype(BF16)
    gate_grad, upward_grad = swiglu_pull(hidden_grad)
    gate_low = gate_grad.astype(jnp.bfloat16)
    upward_low = upward_grad.astype(jnp.bfloat16)
    gate_weight_grad = contract_first(second_all, gate_low).astype(BF16)
    up_weight_grad = contract_first(second_all, upward_low).astype(BF16)
    second_terms = (contract_last(gate_low, gate_full) + contract_last(upward_low, up_full)).astype(
        BF16
    )
    second_grad, down_total = sum_and_gradient(5, second_terms, down_grad, (384, 256), down_spot)
    residual_part, second_gain_grad = second_pull(second_grad)
    residual_grad = cotangent.astype(jnp.float32) + residual_part
    residual_low = residual_grad.astype(jnp.bfloat16)
    residual_all, gate_total = gather_and_gradient(
        6, residual_low, gate_weight_grad, (256, 384), gateup_spot
    )
    output_grad = contract_first(attended_low, residual_all).astype(BF16)
    attended_grad = contract_last(residual_all, output_full).astype(jnp.bfloat16)
    query_rot_grad, key_rot_grad, value_grad = attend_backward(
        queries,
        key_vectors,
        value_vectors,
        attended_grad,
        log_totals,
        segment,
        places,
        block_row_span,
    )
    query_part_grad, key_part_grad, query_gain_grad, key_gain_grad = turn_pull(
        (query_rot_grad, key_rot_grad)
    )
    parts_grad = jnp.concatenate(
        [query_part_grad, key_part_grad, value_grad.reshape(group_rows, -1)], axis=1
    ).astype(BF16)
    first_terms = contract_last(parts_grad, qkv_full).astype(BF16)
    first_grad, up_total = sum_and_gradient(
        7, first_terms, up_weight_grad, (256, 384), gateup_spot
    )
    qkv_grad = contract_first(normed_all, parts_grad).astype(BF16)
    input_part, first_gain_grad = first_pull(first_grad)
    input_grad = (residual_grad + input_part).astype(jnp.bfloat16)
    gain_terms = jnp.concatenate(
        [first_gain_grad, second_gain_grad, query_gain_grad, key_gain_grad]
    )
    gain_rows = jnp.pad(
        gain_terms.reshape(4, 2, 2, 2, 4, 34).transpose(0, 3, 1, 4, 2, 5).reshape(128, 1, 34),
        ((0, 0), (0, 0), (0, 94)),
    )
    mlp_out, qkv_total, output_total, gains_total = last_sums(
        mlp_terms, qkv_grad, output_grad, gain_rows
    )
    block_out = (residual + mlp_out).astype(jnp.bfloat16)
    block_out, input_grad, qkv_total, output_total, gate_total, up_total, down_total = leave(
        block_out, input_grad, qkv_total, output_total, gate_total, up_total, down_total
    )
    masters = (
        query_weight,
        key_value_weight,
        output_weight,
        gateup_weight,
        down_weight,
        norm_gains,
    )
    gradients = (
        qkv_total[:, :256].astype(F32),
        jnp.stack([qkv_total[:, 256:384], qkv_total[:, 384:]]).astype(F32),
        output_total.astype(F32),
        jnp.stack([gate_total, up_total]).astype(F32),
        down_total.astype(F32),
        gains_total.reshape(128)[:34],
    )
    moments = (
        query_momentum,
        keyval_momentum,
        output_momentum,
        gateup_momentum,
        down_momentum,
        gains_momentum,
    )
    averages = (
        query_average,
        key_value_mean,
        output_average,
        gateup_average,
        down_average,
        gains_average,
    )
    updated = []
    velocity = []
    smoothed = []
    for master, gradient, moment, average, rate in zip(
        masters, gradients, moments, averages, rates
    ):
        moment_next = MOMENTUM * moment + gradient
        master_next = master - rate * (gradient + MOMENTUM * moment_next)
        updated.append(master_next)
        velocity.append(moment_next)
        smoothed.append(AVERAGING * average + (1.0 - AVERAGING) * master_next)
    return (block_out, input_grad, *updated, *velocity, *smoothed)


def solution(mesh):
    parted = Mesh(mesh.devices.reshape(GRID), AXES)
    data = ("z", "ylo", "core")
    tensor = ("yhi", "x")
    rows = P(AXES, None)
    by_rows = P(data, tensor)
    pair = P(None, data, tensor)
    by_columns = P(tensor, data)
    flat = P(AXES)
    weights = (by_rows, pair, by_columns, pair, by_columns, flat)
    return jax.shard_map(
        body,
        mesh=parted,
        in_specs=(rows, rows, P(data, None)) + weights * 3,
        out_specs=(rows, rows) + weights * 3,
        check_vma=False,
    )
```

```python
import math

import jax
import jax.numpy as jnp
import numpy as np
from jax import lax
from jax.experimental import pallas as pl
from jax.experimental.pallas import tpu as pltpu
from jax.sharding import Mesh
from jax.sharding import PartitionSpec as P

MODEL_WIDTH = 2048
QUERY_HEADS = 16
HEAD_SIZE = 128
FF = 6144
GROUP_TOK = 1024
GAINS = 4352
OWN_GAINS = 34
EPSILON = 1e-06
MOMENTUM = 0.9
AVERAGING = 0.5
ROPE_BASE = 1000000.0
SCALE = HEAD_SIZE ** (-0.5)

AXES = ("z", "ylo", "core", "yhi", "x")
GRID = (4, 2, 2, 2, 4)
RING = 4
BF16 = jnp.bfloat16
F32 = jnp.float32
HBM = pl.ANY
VMEM = pltpu.VMEM


class Place:
    def __init__(self):
        self.x = lax.axis_index("x")
        self.z = lax.axis_index("z")
        self.core = lax.axis_index("core")
        self.yhi = lax.axis_index("yhi")
        self.ylo = lax.axis_index("ylo")
        self.y = self.yhi * 2 + self.ylo
        self.native = self.core == self.yhi

    def at(self, axis):
        return self.x if axis == "x" else self.y if axis == "y" else self.z

    def step(self, axis, by):
        return lax.rem(self.at(axis) + (by + RING), RING)

    def device(self, axis, by=1):
        if axis == "core":
            return {"core": 1 - self.core}
        if axis == "turn":
            return {"core": 1 - self.core, "yhi": 1 - self.yhi}
        there = self.step(axis, by)
        if axis == "y":
            return {"yhi": lax.div(there, 2), "ylo": lax.rem(there, 2)}
        return {axis: there}


class Net:
    def __init__(self, place, send_sems, recv_sems, local_sems):
        self.place = place
        self.send_sems, self.recv_sems, self.local_sems = send_sems, recv_sems, local_sems
        self.count = 0
        self.local_count = 0
        self.pending = {}

    def copy(self, source, target, index, axis, by=1):
        return pltpu.make_async_remote_copy(
            src_ref=source,
            dst_ref=target,
            send_sem=self.send_sems.at[index],
            recv_sem=self.recv_sems.at[index],
            device_id=self.place.device(axis, by),
            device_id_type=pl.DeviceIdType.MESH,
        )

    def number(self):
        self.count += 1
        return self.count - 1

    def local_number(self):
        self.local_count += 1
        return self.local_count - 1

    def send(self, source, target, axis, by=1):
        index = self.number()
        copy = self.copy(source, target, index, axis, by)
        copy.start()
        self.pending[index] = copy
        return index

    def arrive(self, index, target, axis, by=1):
        self.copy(target, target, index, axis, by).wait_recv()

    def local(self, source, target):
        copy = pltpu.make_async_copy(source, target, self.local_sems.at[self.local_number()])
        copy.start()
        return copy

    def sent(self, indices=None):
        for index in list(self.pending) if indices is None else indices:
            self.pending.pop(index).wait_send()


def greet(place, partners):
    barrier = pltpu.get_barrier_semaphore()
    for axis, by in partners:
        pl.semaphore_signal(
            barrier,
            inc=1,
            device_id=place.device(axis, by),
            device_id_type=pl.DeviceIdType.MESH,
        )
    pl.semaphore_wait(barrier, len(partners))


class RowsGather:
    COPIES, LOCALS = 14, 2

    def __init__(self, net, own, whole):
        self.net, self.own, self.whole = net, own, whole
        self.rows = own.shape[0]
        place = net.place
        self.me, self.other = place.core, 1 - place.core
        self.spots = {k: place.step("x", k) for k in (0, 1, -1, 2)}
        self.shared = {0: [], 1: [], -1: [], 2: []}

    def block(self, core, k, part):
        half = self.rows // 2
        start = (self.spots[k] * 2 + core) * self.rows + part * half
        return self.whole.at[pl.ds(pl.multiple_of(start, half), half)]

    def mine(self, k, part):
        return self.block(self.me, k, part)

    def share(self, k, part, source=None):
        there = self.mine(k, part)
        index = self.net.send(there if source is None else source, there, "core")
        self.shared[k].append((index, self.block(self.other, k, part)))

    def start(self):
        half = self.rows // 2
        piece = [self.own.at[pl.ds(part * half, half)] for part in range(2)]
        self.sent = {}
        for by, part in ((1, 0), (-1, 1), (1, 1), (-1, 0)):
            self.sent[by, part] = self.net.send(piece[part], self.mine(0, part), "x", by)
        for part in range(2):
            self.share(0, part, piece[part])
        self.kept = [self.net.local(piece[part], self.mine(0, part)) for part in range(2)]

    def near_first(self):
        net = self.net
        net.arrive(self.sent[1, 0], self.mine(-1, 0), "x", 1)
        self.passed_right = net.send(self.mine(-1, 0), self.mine(-1, 0), "x", 1)
        self.share(-1, 0)
        net.arrive(self.sent[-1, 1], self.mine(1, 1), "x", -1)
        self.passed_left = net.send(self.mine(1, 1), self.mine(1, 1), "x", -1)
        self.share(1, 1)

    def near_second(self):
        self.net.arrive(self.sent[1, 1], self.mine(-1, 1), "x", 1)
        self.share(-1, 1)
        self.net.arrive(self.sent[-1, 0], self.mine(1, 0), "x", -1)
        self.share(1, 0)

    def far(self):
        self.net.arrive(self.passed_right, self.mine(2, 0), "x", 1)
        self.share(2, 0)
        self.net.arrive(self.passed_left, self.mine(2, 1), "x", -1)
        self.share(2, 1)

    def out(self):
        shared = [index for k in (1, -1, 2) for index, _ in self.shared[k]]
        return [self.passed_right, self.passed_left] + shared

    def here(self, k):
        if k == 0:
            for copy in self.kept:
                copy.wait()
        for index, there in self.shared[k]:
            self.net.arrive(index, there, "core")


class RowsSum:
    COPIES = 14

    def __init__(self, net, whole, landed, land):
        self.net, self.whole, self.landed, self.land = net, whole, landed, land
        self.half = landed.shape[2]
        place = net.place
        self.me, self.other = place.core, 1 - place.core
        self.spots = {k: place.step("x", k) for k in (0, 1, -1, 2)}
        self.sent = {}

    def block(self, core, k, part):
        start = ((self.spots[k] * 2 + core) * 2 + part) * self.half
        return self.whole.at[pl.ds(pl.multiple_of(start, self.half), self.half)]

    def own(self, k, part):
        return self.landed.at[k % RING, part]

    def pass_over(self, k):
        for part in range(2):
            source = self.block(self.other, k, part)
            self.sent[k, part] = self.net.send(source, self.own(k, part), "core")

    def passed(self):
        return list(self.sent.values())

    def combine(self, k):
        for part in range(2):
            here = self.own(k, part)
            self.net.arrive(self.sent[k, part], here, "core")
            here[...] = here[...] + self.block(self.me, k, part)[...]

    def start_far(self):
        self.a = self.net.send(self.own(2, 0), self.land.at[0], "x", 1)
        self.b = self.net.send(self.own(2, 1), self.land.at[1], "x", -1)

    def start_right(self):
        self.c = self.net.send(self.own(1, 1), self.land.at[3], "x", 1)

    def start_left(self):
        self.d = self.net.send(self.own(-1, 0), self.land.at[4], "x", -1)

    def forward(self):
        net, land = self.net, self.land
        net.arrive(self.a, land.at[0], "x", 1)
        land[0] = land[0] + self.own(1, 0)[...]
        self.e = net.send(land.at[0], land.at[2], "x", 1)
        net.arrive(self.b, land.at[1], "x", -1)
        land[1] = land[1] + self.own(-1, 1)[...]
        self.f = net.send(land.at[1], land.at[5], "x", -1)

    def finish(self, keep):
        net, land = self.net, self.land
        net.arrive(self.d, land.at[4], "x", -1)
        net.arrive(self.c, land.at[3], "x", 1)
        net.arrive(self.e, land.at[2], "x", 1)
        net.arrive(self.f, land.at[5], "x", -1)
        for part in range(2):
            total = self.own(0, part)[...].astype(F32) + land[2 + part].astype(F32)
            keep(pl.ds(part * self.half, self.half), total + land[4 + part].astype(F32))


ROWS_SCRATCH = (pltpu.VMEM((4, 2, 64, 2048), BF16), pltpu.VMEM((6, 64, 2048), BF16))


class PlaneGather:
    COPIES, LOCALS = 38, 1

    def __init__(self, net, own, whole, spot):
        self.net, self.own, self.whole, self.spot = net, own, whole, spot
        self.rows = own.shape[0]
        self.half = self.rows // 2

    def view(self, color, i, j, part=None):
        place = self.net.place
        first, second = self.axes(color)
        a, b = place.step(first, i), place.step(second, j)
        row, columns = self.spot(a, b) if color == 0 else self.spot(b, a)
        start = row + color * self.half
        if part is None:
            return self.whole.at[pl.ds(pl.multiple_of(start, self.half), self.half), columns]
        size = self.half // 2
        return self.whole.at[pl.ds(pl.multiple_of(start + part * size, size), size), columns]

    @staticmethod
    def axes(color):
        return ("z", "y") if color == 0 else ("y", "z")

    def ring(self, color, i, source=None):
        here = self.view(color, i, 0)
        source = here if source is None else source
        axis = self.axes(color)[1]
        return [self.net.send(source, here, axis, by) for by in (1, -1)]

    def start(self):
        net = self.net
        self.first, self.rings, self.passed = {}, {}, {}
        mine = [self.own.at[pl.ds(color * self.half, self.half)] for color in range(2)]
        for color in range(2):
            axis = self.axes(color)[0]
            for by in (1, -1, 2):
                there = self.view(color, 0, 0)
                self.first[color, by] = net.send(mine[color], there, axis, by)
        for color in range(2):
            self.rings[color, 0] = self.ring(color, 0, mine[color])
        row, columns = self.spot(net.place.z, net.place.y)
        whole = self.whole.at[pl.ds(pl.multiple_of(row, self.rows), self.rows), columns]
        self.kept = net.local(self.own, whole)

    def spread(self):
        for by in (1, -1, 2):
            for color in range(2):
                axis = self.axes(color)[0]
                self.net.arrive(self.first[color, by], self.view(color, -by, 0), axis, by)
                self.rings[color, -by] = self.ring(color, -by)

    def forward(self, steps=(0, 1, -1, -2)):
        net = self.net
        for i in steps:
            for color in range(2):
                axis = self.axes(color)[1]
                right, left = self.rings[color, i]
                net.arrive(right, self.view(color, i, -1), axis, 1)
                passed = self.view(color, i, -1, 0)
                there = [net.send(passed, passed, axis, 1)]
                net.arrive(left, self.view(color, i, 1), axis, -1)
                passed = self.view(color, i, 1, 1)
                there.append(net.send(passed, passed, axis, -1))
                self.passed[color, i] = there

    def here(self):
        net = self.net
        for (color, i), (right, left) in self.passed.items():
            axis = self.axes(color)[1]
            net.arrive(right, self.view(color, i, 2, 0), axis, 1)
            net.arrive(left, self.view(color, i, 2, 1), axis, -1)
        self.kept.wait()


class PlaneSum:
    COPIES = 2 * (4 * 6 + 3 * 2)

    def __init__(self, net, whole, spot, land, last):
        self.net, self.whole, self.spot, self.land, self.last = net, whole, spot, land, last
        self.size = land.shape[3]

    @staticmethod
    def axes(color):
        return ("y", "z") if color == 0 else ("z", "y")

    def own(self, color, n, k, part):
        place = self.net.place
        first, second = self.axes(color)
        a, b = place.step(first, n), place.step(second, k)
        row, columns = self.spot(b, a) if color == 0 else self.spot(a, b)
        start = row + (color * 2 + part) * self.size
        return self.whole.at[pl.ds(pl.multiple_of(start, self.size), self.size), columns]

    def slot(self, color, k, n):
        return self.land.at[color, k % RING, n]

    def start(self):
        net = self.net
        self.sent, self.passed, self.ends = {}, {}, {}
        for k in (2, 1, -1, 0):
            for color in range(2):
                axis = self.axes(color)[0]
                self.sent[color, k] = (
                    net.send(self.own(color, 2, k, 0), self.slot(color, k, 0), axis, 1),
                    net.send(self.own(color, 2, k, 1), self.slot(color, k, 1), axis, -1),
                    net.send(self.own(color, 1, k, 1), self.slot(color, k, 3), axis, 1),
                    net.send(self.own(color, -1, k, 0), self.slot(color, k, 4), axis, -1),
                )

    def forward(self, steps=(2, 1, -1, 0)):
        net = self.net
        for k in steps:
            for color in range(2):
                axis = self.axes(color)[0]
                a, b, _, _ = self.sent[color, k]
                one, two = self.slot(color, k, 0), self.slot(color, k, 1)
                net.arrive(a, one, axis, 1)
                one[...] = one[...] + self.own(color, 1, k, 0)[...]
                e = net.send(one, self.slot(color, k, 2), axis, 1)
                net.arrive(b, two, axis, -1)
                two[...] = two[...] + self.own(color, -1, k, 1)[...]
                f = net.send(two, self.slot(color, k, 5), axis, -1)
                self.passed[color, k] = (e, f)

    def gather(self, steps=(2, 1, -1, 0)):
        net = self.net
        for k in steps:
            for color in range(2):
                axis, second = self.axes(color)
                _, _, c, d = self.sent[color, k]
                e, f = self.passed[color, k]
                net.arrive(e, self.slot(color, k, 2), axis, 1)
                net.arrive(c, self.slot(color, k, 3), axis, 1)
                net.arrive(d, self.slot(color, k, 4), axis, -1)
                net.arrive(f, self.slot(color, k, 5), axis, -1)
                for part in range(2):
                    here = self.slot(color, k, 2 + part)
                    total = self.own(color, 0, k, part)[...].astype(F32) + here[...].astype(F32)
                    total = total + self.slot(color, k, 4 + part)[...].astype(F32)
                    here[...] = total.astype(BF16)
                    if k != 0:
                        there = self.last.at[color, k % RING - 1, part]
                        self.ends[color, k, part] = net.send(here, there, second, k)

    def finish(self, total):
        net = self.net
        for color in range(2):
            second = self.axes(color)[1]
            for part in range(2):
                value = self.slot(color, 0, 2 + part)[...].astype(F32)
                for k in (1, -1, 2):
                    there = self.last.at[color, k % RING - 1, part]
                    net.arrive(self.ends[color, k, part], there, second, k)
                    value = value + there[...].astype(F32)
                start = (color * 2 + part) * self.size
                total[pl.ds(start, self.size)] = value.astype(total.dtype)


def plane_scratch(rows, columns):
    return (
        pltpu.VMEM((2, 4, 6, rows // 4, columns), BF16),
        pltpu.VMEM((2, 3, 2, rows // 4, columns), BF16),
    )


class Turn:
    def __init__(self, net, pairs, cuts=2):
        self.net = net
        self.remote, self.kept = [], []
        for source, target in pairs:
            rows = source.shape[0] // cuts
            for part in range(cuts):
                spot = pl.ds(part * rows, rows)
                self.remote.append((source.at[spot], target.at[spot], net.number()))
            self.kept.append((source, target, net.local_number()))

    def copies(self):
        return [self.net.copy(source, target, index, "turn") for source, target, index in self.remote]

    def locals(self):
        sems = self.net.local_sems
        return [pltpu.make_async_copy(a, b, sems.at[index]) for a, b, index in self.kept]

    def start(self):
        @pl.when(jnp.logical_not(self.net.place.native))
        def _():
            for copy in self.copies():
                copy.start()

        @pl.when(self.net.place.native)
        def _():
            for copy in self.locals():
                copy.start()

    def wait(self):
        @pl.when(jnp.logical_not(self.net.place.native))
        def _():
            for copy in self.copies():
                copy.wait()

        @pl.when(self.net.place.native)
        def _():
            for copy in self.locals():
                copy.wait()


class GainsGather:
    COPIES, LOCALS = 10, 1

    def __init__(self, net, own, whole):
        self.net, self.own, self.whole = net, own, whole

    def rows(self, z, y, x, core, count):
        start = ((z * RING + y) * RING + x) * 2 + core
        return self.whole.at[pl.ds(start if count == 1 else pl.multiple_of(start, count), count)]

    def steps(self):
        net, place = self.net, self.net.place
        net.local(self.own, self.rows(place.z, place.y, place.x, place.core, 1)).wait()
        spots = {
            "core": lambda by: self.rows(place.z, place.y, place.x, (place.core + by) % 2, 1),
            "x": lambda by: self.rows(place.z, place.y, place.step("x", by), 0, 2),
            "y": lambda by: self.rows(place.z, place.step("y", by), 0, 0, 8),
            "z": lambda by: self.rows(place.step("z", by), 0, 0, 0, 32),
        }
        for axis in ("core", "x", "y", "z"):
            spot = spots[axis]
            by_all = (1,) if axis == "core" else (1, -1, 2)
            sent = [net.send(spot(0), spot(0), axis, by) for by in by_all]
            yield
            for index, by in zip(sent, by_all):
                net.arrive(index, spot(-by), axis, by)
        yield


class GainsSum:
    COPIES = 10

    def __init__(self, net, whole, total, land):
        self.net, self.whole, self.total, self.land = net, whole, total, land

    rows = GainsGather.rows

    def steps(self):
        net, place, land = self.net, self.net.place, self.land
        spots = {
            "z": lambda by: self.rows(place.step("z", by), 0, 0, 0, 32),
            "y": lambda by: self.rows(place.z, place.step("y", by), 0, 0, 8),
            "x": lambda by: self.rows(place.z, place.y, place.step("x", by), 0, 2),
            "core": lambda by: self.rows(place.z, place.y, place.x, (place.core + by) % 2, 1),
        }
        first = 0
        for axis, count in (("z", 32), ("y", 8), ("x", 2), ("core", 1)):
            spot = spots[axis]
            by_all = (1,) if axis == "core" else (1, -1, 2)
            sent = [
                net.send(spot(by), land.at[n, pl.ds(first, count)], axis, by)
                for n, by in enumerate(by_all)
            ]
            yield
            value = spot(0)[...]
            for n, (index, by) in enumerate(zip(sent, by_all)):
                net.arrive(index, land.at[n, pl.ds(first, count)], axis, by)
                value = value + land[n, pl.ds(first, count)]
            if axis == "core":
                self.total[...] = value
            else:
                spot(0)[...] = value
            first += count
        yield


class Kernel:
    def __init__(self, number, copies, locals_, partners):
        self.number, self.copies, self.locals_, self.partners = number, copies, locals_, partners

    def __call__(self, body, arrays, outs, scratch=()):
        n_in, n_out, n_scratch = len(arrays), len(outs), len(scratch)

        def kernel(*refs):
            place = Place()
            net = Net(place, *refs[n_in + n_out + n_scratch :])
            greet(place, self.partners)
            body(
                net,
                refs[:n_in],
                refs[n_in : n_in + n_out],
                refs[n_in + n_out : n_in + n_out + n_scratch],
            )
            net.sent()

        return pl.pallas_call(
            kernel,
            out_shape=[shape for shape, _ in outs],
            in_specs=[pl.BlockSpec(memory_space=space) for _, space in arrays],
            out_specs=[pl.BlockSpec(memory_space=space) for _, space in outs],
            scratch_shapes=[
                *scratch,
                pltpu.SemaphoreType.DMA((self.copies,)),
                pltpu.SemaphoreType.DMA((self.copies,)),
                pltpu.SemaphoreType.DMA((self.locals_,)),
            ],
            compiler_params=pltpu.CompilerParams(
                collective_id=self.number, has_side_effects=True, vmem_limit_bytes=61 * 2**20
            ),
            name="links_%d" % self.number,
        )(*[array for array, _ in arrays])


CORE_PARTNER = (("core", 1),)
X_PARTNERS = (("x", 1), ("x", -1))
FAR_X = (("x", 2),)
PLANE_PARTNERS = (("y", 1), ("y", -1), ("y", 2), ("z", 1), ("z", -1), ("z", 2))
TURN_PARTNERS = (("turn", 1),)


def shape(dims, dtype=BF16):
    return jax.ShapeDtypeStruct(dims, dtype)


def attention_spot(z, y):
    piece = z * 4 + lax.rem(y, 2) * 2 + lax.div(y, 2)
    return piece * 128


def rows_spot(z, y):
    return attention_spot(z, y), pl.ds(0, 512)


def output_spot(z, y):
    return 0, pl.ds(pl.multiple_of(attention_spot(z, y), 128), 128)


def gateup_spot(z, y):
    columns = pl.ds(pl.multiple_of(lax.div(y, 2) * 384, 128), 384)
    return (z * 2 + lax.rem(y, 2)) * 256, columns


def down_spot(z, y):
    columns = pl.ds(pl.multiple_of((z * 2 + lax.rem(y, 2)) * 256, 128), 256)
    return lax.div(y, 2) * 384, columns


def nn(left, right):
    return lax.dot_general(left, right, (((1,), (0,)), ((), ())), preferred_element_type=F32)


def nt(left, right):
    return lax.dot_general(left, right, (((1,), (1,)), ((), ())), preferred_element_type=F32)


def tn(left, right):
    return lax.dot_general(left, right, (((0,), (0,)), ((), ())), preferred_element_type=F32)


def exact(left, right):
    return lax.dot_general(
        left, right, (((1,), (0,)), ((), ())),
        precision=lax.Precision.HIGHEST, preferred_element_type=F32,
    )


def inverse_root(rows):
    return lax.rsqrt(jnp.mean(rows * rows, axis=-1, keepdims=True) + EPSILON)


def norm_back(rows, gain, upstream):
    root = inverse_root(rows)
    weighted = upstream * gain
    meant = jnp.mean(weighted * rows, axis=-1, keepdims=True)
    return root * weighted - rows * (root * root * root * meant), upstream * rows * root


def rope_tables():
    halves = np.arange(HEAD_SIZE // 2, dtype=np.float64)
    angles = np.arange(GROUP_TOK)[:, None] * ROPE_BASE ** (-2.0 * halves / HEAD_SIZE)[None, :]
    angles = np.concatenate([angles, angles], axis=1)
    return np.cos(angles).astype(np.float32), np.sin(angles).astype(np.float32)


def owner_starts(dims, axis):
    row = lax.broadcasted_iota(jnp.int32, dims, axis)
    z, y, x, core = row >> 5, (row >> 3) & 3, (row >> 1) & 3, row & 1
    return (z * 32 + (y & 1) * 16 + core * 8 + (y >> 1) * 4 + x) * OWN_GAINS


def column_of(entry):
    return entry - jnp.floor((entry.astype(F32) + 0.5) * (1.0 / OWN_GAINS)).astype(jnp.int32) * OWN_GAINS


def gains_flat(rows):
    entry = lax.broadcasted_iota(jnp.int32, (128, GAINS), 1)
    past = entry - owner_starts((128, GAINS), 0)
    owner = ((past >= 0) & (past < OWN_GAINS)).astype(F32)
    columns = lax.dot_general(
        rows, owner, (((0,), (0,)), ((), ())),
        precision=lax.Precision.HIGHEST, preferred_element_type=F32,
    )
    place = lax.broadcasted_iota(jnp.int32, (128, GAINS), 0)
    return jnp.sum(jnp.where(column_of(entry) == place, columns, 0.0), axis=0, keepdims=True)


class Documents:
    def __init__(self, lengths):
        lengths = [lengths[0:1, n : n + 1] for n in range(4)]
        self.ends = [lengths[0], lengths[0] + lengths[1], lengths[0] + lengths[1] + lengths[2]]

    def pick(self, place, values):
        value = jnp.where(place >= self.ends[0], values[1], values[0])
        value = jnp.where(place >= self.ends[1], values[2], value)
        return jnp.where(place >= self.ends[2], values[3], value)

    def first(self, place):
        zero = jnp.zeros_like(self.ends[0])
        return self.pick(place, [zero] + self.ends)


def allowed_pairs(documents, first_row, rows, keys):
    query = lax.broadcasted_iota(jnp.int32, (rows, 1), 0) + first_row
    key = lax.broadcasted_iota(jnp.int32, (rows, keys), 1)
    return (key >= documents.first(query)) & (key <= query)


def attention_forward(
    tokens, cotangent, qkv, output, gains, lengths, cosine, sine, gate, up, down
):
    def body(net, ins, outs, work):
        (
            tokens_, cotangent_, qkv_, output_, gains_, lengths_, cosine_, sine_, gate_, up_, down_,
        ) = ins
        (
            residual_, tokens_here, cotangent_here, normed_, raw_, heads_, attended_, totals_,
            cosine_out, sine_out, qkv_out, output_out, gate_out, up_out, down_piece,
            cotangent_all, flat_, lengths_out,
        ) = outs
        (
            gathered, normed, qkv_w, output_w, qkv_piece, output_piece, gains_rows,
            lengths_there, gate_piece, up_piece, terms, landed, land,
        ) = work
        place = net.place
        mine, theirs = place.core, 1 - place.core

        weights = Turn(net, [(qkv_, qkv_piece), (output_, output_piece)])
        rows = Turn(net, [(tokens_, tokens_here)])
        upstream = Turn(net, [(cotangent_, cotangent_here)])
        weights.start()
        rows.start()
        length_copy = net.send(lengths_, lengths_there, "core")
        gains_steps = GainsGather(net, gains_, gains_rows).steps()
        next(gains_steps)

        halves = []

        def exchange(cut, source, there):
            halves.append((net.local(cut(source, mine), there(mine)), None, None))
            index = net.send(cut(source, theirs), there(mine), "core")
            halves.append((None, index, there(theirs)))

        def columns_half(source, core):
            return source.at[:, pl.ds(pl.multiple_of(core * 384, 128), 384)]

        def rows_half(source, core):
            return source.at[pl.ds(pl.multiple_of(core * 384, 128), 384)]

        for source, target in ((gate_, gate_piece), (up_, up_piece)):
            exchange(
                columns_half, source,
                lambda core, target=target: target.at[pl.ds(pl.multiple_of(core * 128, 128), 128)],
            )
        exchange(
            rows_half, down_,
            lambda core: down_piece.at[:, pl.ds(pl.multiple_of(core * 128, 128), 128)],
        )

        qkv_gather = PlaneGather(net, qkv_piece, qkv_w, rows_spot)
        output_gather = PlaneGather(net, output_piece, output_w, output_spot)
        gate_gather = PlaneGather(net, gate_piece, gate_out, gateup_spot)
        up_gather = PlaneGather(net, up_piece, up_out, gateup_spot)
        gather = RowsGather(net, tokens_here, gathered)
        later = RowsGather(net, cotangent_here, cotangent_all)

        weights.wait()
        qkv_gather.start()
        rows.wait()
        gather.start()
        upstream.start()
        output_gather.start()
        next(gains_steps)

        net.arrive(length_copy, lengths_there, "core")
        lengths_out[...] = jnp.where(place.native, lengths_[...], lengths_there[...])
        documents = Documents(lengths_out[...])
        zero = jnp.zeros((1, 1), jnp.int32)
        starts = [zero] + documents.ends
        everywhere = lax.broadcasted_iota(jnp.int32, (1, GROUP_TOK), 1)
        hits = jnp.concatenate(
            [(everywhere == start).astype(F32) for start in starts] * 2, axis=0
        )
        start_cosine = exact(hits, cosine_[...])
        start_sine = exact(hits, sine_[...])
        where = lax.broadcasted_iota(jnp.int32, (GROUP_TOK, 1), 0)
        cosine_by = documents.pick(where, [start_cosine[n : n + 1] for n in range(4)])
        sine_by = documents.pick(where, [start_sine[n : n + 1] for n in range(4)])
        cosine_out[...] = cosine_[...] * cosine_by + sine_[...] * sine_by
        sign = jnp.where(lax.broadcasted_iota(jnp.int32, (1, HEAD_SIZE), 1) < 64, -1.0, 1.0)
        sine_out[...] = (sine_[...] * cosine_by - cosine_[...] * sine_by) * sign

        next(gains_steps)
        qkv_gather.spread()
        next(gains_steps)
        gather.near_first()
        next(gains_steps)
        output_gather.spread()
        flat_[...] = gains_flat(gains_rows[...].reshape(128, 128))
        gain_first = flat_[0:1, 0:2048]
        gain_query = flat_[0:1, 4096:4224]
        gain_key = flat_[0:1, 4224:4352]
        qkv_gather.forward()

        def unit(k):
            return pl.ds(pl.multiple_of(place.step("x", k) * 256, 256), 256)

        stores = []

        def normalize(k):
            gather.here(k)
            rows_in = gathered[unit(k)].astype(F32)
            normed[unit(k)] = (rows_in * inverse_root(rows_in) * gain_first).astype(BF16)
            stores.append(net.local(normed.at[unit(k)], normed_.at[unit(k)]))

        normalize(0)
        gather.near_second()
        output_gather.forward()
        for copy, index, there in halves:
            if copy is not None:
                copy.wait()
            else:
                net.arrive(index, there, "core")
        gate_gather.start()
        normalize(-1)
        normalize(1)
        qkv_gather.here()
        stores.append(net.local(qkv_w, qkv_out))

        def true_rows(k, core):
            start = (core * RING + place.step("x", k)) * 128
            return pl.ds(pl.multiple_of(start, 128), 128)

        def project(k):
            parts = nn(normed[unit(k)], qkv_w[...])
            for core in range(2):
                spot = true_rows(k, core)
                part = parts[core * 128 : core * 128 + 128]
                raw_[spot] = part[:, 0:384]
                heads_[spot, 384:512] = part[:, 384:512].astype(BF16)
                for head in range(3):
                    columns = slice(head * 128, head * 128 + 128)
                    value = part[:, columns]
                    value = value * inverse_root(value) * (gain_key if head == 2 else gain_query)
                    turned = value * cosine_out[spot] + pltpu.roll(value, 64, 1) * sine_out[spot]
                    heads_[spot, columns] = turned.astype(BF16)

        project(0)
        gather.far()
        upstream.wait()
        later.start()
        gate_gather.spread()
        up_gather.start()
        project(-1)
        project(1)
        normalize(2)
        project(2)
        gate_gather.forward((0, 1))

        def attend(block):
            keys = 256 * (block + 1)
            spot = pl.ds(block * 256, 256)
            allowed = allowed_pairs(documents, block * 256, 256, keys)
            for head in range(2):
                columns = slice(head * 128, head * 128 + 128)
                scores = nt(heads_[spot, columns], heads_[0:keys, 256:384])
                scores = jnp.where(allowed, scores, -1e30)
                highest = jnp.max(scores, axis=-1, keepdims=True)
                weights_ = jnp.exp((scores - highest) * SCALE)
                summed = jnp.sum(weights_, axis=-1, keepdims=True)
                probability = (weights_ * (1.0 / summed)).astype(BF16)
                attended_[spot, columns] = nn(probability, heads_[0:keys, 384:512]).astype(BF16)
                totals_[spot, columns] = jnp.broadcast_to(
                    highest * SCALE + jnp.log(summed), (256, 128)
                )

        attend(0)
        later.near_first()
        attend(1)
        gate_gather.forward((-1, -2))
        attend(2)
        later.near_second()
        output_gather.here()
        stores.append(net.local(output_w, output_out))
        attend(3)
        up_gather.spread()
        sums = RowsSum(net, terms, landed, land)

        def out(k):
            own = jnp.concatenate(
                [attended_[true_rows(k, 0)], attended_[true_rows(k, 1)]], axis=0
            )
            terms[unit(k)] = nn(own, output_w[...]).astype(BF16)
            sums.pass_over(k)

        later.far()
        out(2)
        out(1)
        sums.combine(2)
        sums.start_far()
        out(-1)
        sums.combine(1)
        sums.start_right()
        out(0)
        sums.combine(-1)
        sums.start_left()
        gate_gather.here()
        up_gather.forward()
        sums.combine(0)
        sums.forward()
        for k in (0, 1, -1, 2):
            later.here(k)

        def keep(spot, value):
            residual_[spot] = value + tokens_here[spot].astype(F32)

        sums.finish(keep)
        up_gather.here()
        for store in stores:
            store.wait()

    copies = (
        4 + 2 + 2 + 1 + GainsGather.COPIES + 3
        + 4 * PlaneGather.COPIES + 2 * RowsGather.COPIES + RowsSum.COPIES
    )
    locals_ = 4 + 1 + 3 + 4 + 2 * 2 + 4 + 2
    return Kernel(
        0, copies, locals_, CORE_PARTNER + X_PARTNERS + FAR_X + PLANE_PARTNERS + TURN_PARTNERS
    )(
        body,
        [
            (tokens, HBM), (cotangent, HBM), (qkv, HBM), (output, HBM), (gains, VMEM),
            (lengths, VMEM), (cosine, VMEM), (sine, VMEM), (gate, HBM), (up, HBM), (down, HBM),
        ],
        [
            (shape((128, 2048), F32), VMEM),
            (shape((128, 2048)), VMEM),
            (shape((128, 2048)), VMEM),
            (shape((1024, 2048)), HBM),
            (shape((1024, 384), F32), VMEM),
            (shape((1024, 512)), VMEM),
            (shape((1024, 256)), VMEM),
            (shape((1024, 256), F32), VMEM),
            (shape((1024, 128), F32), VMEM),
            (shape((1024, 128), F32), VMEM),
            (shape((2048, 512)), HBM),
            (shape((256, 2048)), HBM),
            (shape((2048, 768)), HBM),
            (shape((2048, 768)), HBM),
            (shape((384, 256)), HBM),
            (shape((1024, 2048)), HBM),
            (shape((1, GAINS), F32), VMEM),
            (shape((8, 128), jnp.int32), VMEM),
        ],
        (
            pltpu.VMEM((1024, 2048), BF16),
            pltpu.VMEM((1024, 2048), BF16),
            pltpu.VMEM((2048, 512), BF16),
            pltpu.VMEM((256, 2048), BF16),
            pltpu.VMEM((128, 512), BF16),
            pltpu.VMEM((256, 128), BF16),
            pltpu.VMEM((128, 1, 128), F32),
            pltpu.VMEM((8, 128), jnp.int32),
            pltpu.VMEM((256, 384), BF16),
            pltpu.VMEM((256, 384), BF16),
            pltpu.VMEM((1024, 2048), BF16),
        )
        + ROWS_SCRATCH,
    )


def feed_forward(residual, cotangent, gains, cotangent_all, gate, up, down):
    def body(net, ins, outs, work):
        residual_, cotangent_, gains_, cotangent_all_, gate_, up_, down_ = ins
        back_, low_, gain_grad_, mlp_, gate_grad_, up_grad_, down_grad_ = outs
        (
            second_low, second, upstream, gate_w, up_w, down_w,
            hidden, gate_low, up_low, terms, staged, wide, landed, land,
        ) = work
        place = net.place
        down_gather = PlaneGather(net, down_, down_w, down_spot)
        down_gather.start()
        gain = gains_[0:1, 2048:4096]
        rows = residual_[...]
        second_low[...] = (rows * inverse_root(rows) * gain).astype(BF16)
        gather = RowsGather(net, second_low, second)
        gather.start()
        loads = [net.local(gate_, gate_w), net.local(up_, up_w), net.local(cotangent_all_, upstream)]
        sums = RowsSum(net, terms, landed, land)
        stores = []

        def unit(k):
            return pl.ds(pl.multiple_of(place.step("x", k) * 256, 256), 256)

        def forth(k):
            gather.here(k)
            gate_value = nn(second[unit(k)], gate_w[...])
            upward = nn(second[unit(k)], up_w[...])
            sigmoid = 1.0 / (1.0 + jnp.exp(-gate_value))
            active = gate_value * sigmoid
            hidden[unit(k)] = (active * upward).astype(BF16)
            gate_low[unit(k)] = (upward * (sigmoid + active * (1.0 - sigmoid))).astype(BF16)
            up_low[unit(k)] = active.astype(BF16)

        def back(k):
            hidden_grad = nt(upstream[unit(k)], down_w[...])
            gate_low[unit(k)] = (hidden_grad * gate_low[unit(k)].astype(F32)).astype(BF16)
            up_low[unit(k)] = (hidden_grad * up_low[unit(k)].astype(F32)).astype(BF16)
            terms[unit(k)] = (
                nt(gate_low[unit(k)], gate_w[...]) + nt(up_low[unit(k)], up_w[...])
            ).astype(BF16)
            sums.pass_over(k)

        loads[0].wait()
        loads[1].wait()
        forth(0)
        gather.near_first()
        down_gather.spread()
        down_gather.forward((0,))
        gather.near_second()
        forth(-1)
        down_gather.forward((1, -1, -2))
        gather.far()
        forth(1)
        forth(2)
        loads[2].wait()
        down_gather.here()
        back(2)
        back(1)
        sums.combine(2)
        sums.start_far()
        back(-1)
        sums.combine(1)
        sums.start_right()
        back(0)
        sums.combine(-1)
        sums.start_left()

        def mlp(k, slot):
            if slot >= 2:
                stores[slot - 2].wait()
            staged[slot % 2] = nn(hidden[unit(k)], down_w[...]).astype(BF16)
            stores.append(net.local(staged.at[slot % 2], mlp_.at[unit(k)]))

        mlp(2, 0)
        mlp(1, 1)
        sums.combine(0)
        mlp(-1, 2)
        mlp(0, 3)
        sums.forward()
        for n in range(3):
            spot = pl.ds(n * 256, 256)
            stores[2 + n].wait()
            staged[n % 2] = tn(hidden[:, spot], upstream[...]).astype(BF16)
            stores.append(net.local(staged.at[n % 2], down_grad_.at[spot]))
        first = len(stores)
        for which, (low, target) in enumerate(((gate_low, gate_grad_), (up_low, up_grad_))):
            for n in range(8):
                spot = pl.ds(n * 256, 256)
                slot = (which * 8 + n) % 4
                if which * 8 + n >= 4:
                    stores[first + which * 8 + n - 4].wait()
                wide[slot] = tn(second[:, spot], low[...]).astype(BF16)
                stores.append(net.local(wide.at[slot], target.at[spot]))

        def keep(spot, value):
            through, gain_part = norm_back(residual_[spot], gain, value)
            through = through + cotangent_[spot].astype(F32)
            back_[spot] = through
            low_[spot] = through.astype(BF16)
            gain_part = jnp.sum(gain_part, axis=0, keepdims=True)
            sums.gain = gain_part if sums.gain is None else sums.gain + gain_part

        sums.gain = None
        sums.finish(keep)
        gain_grad_[...] = sums.gain
        for store in stores[5:7] + stores[-4:]:
            store.wait()

    copies = RowsGather.COPIES + RowsSum.COPIES + PlaneGather.COPIES
    locals_ = 1 + 2 + 3 + 4 + 3 + 16
    return Kernel(1, copies, locals_, CORE_PARTNER + X_PARTNERS + PLANE_PARTNERS)(
        body,
        [
            (residual, VMEM), (cotangent, VMEM), (gains, VMEM),
            (cotangent_all, HBM), (gate, HBM), (up, HBM), (down, HBM),
        ],
        [
            (shape((128, 2048), F32), VMEM),
            (shape((128, 2048)), VMEM),
            (shape((1, 2048), F32), VMEM),
            (shape((1024, 2048)), HBM),
            (shape((2048, 768)), HBM),
            (shape((2048, 768)), HBM),
            (shape((768, 2048)), HBM),
        ],
        (
            pltpu.VMEM((128, 2048), BF16),
            pltpu.VMEM((1024, 2048), BF16),
            pltpu.VMEM((1024, 2048), BF16),
            pltpu.VMEM((2048, 768), BF16),
            pltpu.VMEM((2048, 768), BF16),
            pltpu.VMEM((768, 2048), BF16),
            pltpu.VMEM((1024, 768), BF16),
            pltpu.VMEM((1024, 768), BF16),
            pltpu.VMEM((1024, 768), BF16),
            pltpu.VMEM((1024, 2048), BF16),
            pltpu.VMEM((2, 256, 2048), BF16),
            pltpu.VMEM((4, 256, 768), BF16),
        )
        + ROWS_SCRATCH,
    )


def attention_backward(
    low, back, residual, tokens, gains, second_gain, heads, raw, attended, totals, cosine, sine,
    lengths, qkv, output, normed, mlp, gate, up, down,
):
    def body(net, ins, outs, work):
        (
            low_, back_, residual_, tokens_, gains_, second_gain_, heads_, raw_, attended_, totals_,
            cosine_, sine_, lengths_, qkv_, output_, normed_, mlp_, gate_, up_, down_,
        ) = ins
        (
            block_own, input_own, qkv_own, output_own, gate_own, up_own, down_own, gains_own,
        ) = outs
        (
            rows, terms, qkv_w, output_w, gate_g, up_g, down_g, qkv_g, output_g,
            attended_rows, attended_grad, key_sum, value_sum, parts,
            block_out, input_out, qkv_total, output_total, gate_total, up_total, down_total,
            gain_rows, gain_land,
            mlp_landed, mlp_land, first_landed, first_land,
            gate_land, gate_last, up_land, up_last, down_land, down_last,
            qkv_land, qkv_last, output_land, output_last,
        ) = work
        place = net.place
        mine, theirs = place.core, 1 - place.core

        def unit(k):
            return pl.ds(pl.multiple_of(place.step("x", k) * 256, 256), 256)

        def true_rows(k, core):
            start = (core * RING + place.step("x", k)) * 128
            return pl.ds(pl.multiple_of(start, 128), 128)

        gather = RowsGather(net, low_, rows)
        gather.start()
        loads = {
            name: net.local(source, target)
            for name, source, target in (
                ("gate", gate_, gate_g), ("output", output_, output_w), ("up", up_, up_g),
                ("mlp", mlp_, terms), ("down", down_, down_g), ("qkv", qkv_, qkv_w),
            )
        }
        gate_sum = PlaneSum(net, gate_g, gateup_spot, gate_land, gate_last)
        up_sum = PlaneSum(net, up_g, gateup_spot, up_land, up_last)
        down_sum = PlaneSum(net, down_g, down_spot, down_land, down_last)
        qkv_sum = PlaneSum(net, qkv_g, rows_spot, qkv_land, qkv_last)
        output_sum = PlaneSum(net, output_g, output_spot, output_land, output_last)
        mlp_sum = RowsSum(net, terms, mlp_landed, mlp_land)
        first_sum = RowsSum(net, terms, first_landed, first_land)
        loads["gate"].wait()
        gate_sum.start()
        for k in (0, 1, -1, 2):
            for core in range(2):
                start = pl.multiple_of(place.step("x", k) * 256 + core * 128, 128)
                attended_rows[pl.ds(start, 128)] = attended_[true_rows(k, core)]
        key_sum[...] = jnp.zeros_like(key_sum)
        value_sum[...] = jnp.zeros_like(value_sum)
        loads["output"].wait()

        def enter(k):
            gather.here(k)
            grad = nt(rows[unit(k)], output_w[...]).astype(BF16)
            for core in range(2):
                attended_grad[true_rows(k, core)] = grad[core * 128 : core * 128 + 128]

        enter(0)
        loads["mlp"].wait()
        for k in (2, 1, -1, 0):
            mlp_sum.pass_over(k)
        gather.near_first()
        loads["up"].wait()
        gate_sum.forward()
        up_sum.start()
        gather.near_second()
        enter(-1)
        enter(1)
        for k in (2, 1, -1, 0):
            mlp_sum.combine(k)
        gate_sum.gather()
        gather.far()
        mlp_sum.start_far()
        mlp_sum.start_right()
        mlp_sum.start_left()
        enter(2)
        for n in range(4):
            spot = pl.ds(n * 512, 512)
            output_g[:, spot] = tn(attended_rows[...], rows[:, spot]).astype(BF16)
        loads["down"].wait()
        up_sum.forward()
        down_sum.start()
        net.sent(gather.out())
        loads["normed"] = net.local(normed_, rows)

        documents = Documents(lengths_[...])
        gain_query, gain_key = gains_[0:1, 4096:4224], gains_[0:1, 4224:4352]
        gain_sums = {"query": 0.0, "key": 0.0}

        def through_rope(value, spot, raw_part, gain, which):
            value = value * cosine_[spot] + pltpu.roll(value * sine_[spot], 64, 1)
            through, gain_part = norm_back(raw_part, gain, value)
            gain_sums[which] = gain_sums[which] + jnp.sum(gain_part, axis=0, keepdims=True)
            return through.astype(BF16)

        def put(block, columns, value):
            for n in range(2):
                true = block * 2 + n
                start = ((true % RING) * 2 + true // RING) * 128
                parts[start : start + 128, columns] = value[n * 128 : n * 128 + 128]

        def attend(block):
            keys = 256 * (block + 1)
            spot = slice(block * 256, block * 256 + 256)
            allowed = allowed_pairs(documents, block * 256, 256, keys)
            for head in range(2):
                columns = slice(head * 128, head * 128 + 128)
                query, upstream = heads_[spot, columns], attended_grad[spot, columns]
                key, value = heads_[0:keys, 256:384], heads_[0:keys, 384:512]
                scores = nt(query, key) * SCALE
                total = totals_[spot, head * 128 : head * 128 + 1]
                probability = jnp.where(allowed, jnp.exp(scores - total), 0.0)
                prob_grad = nt(upstream, value)
                centre = jnp.sum(probability * prob_grad, axis=-1, keepdims=True)
                score_grad = (probability * (prob_grad - centre)).astype(BF16)
                value_sum[0:keys] += tn(probability.astype(BF16), upstream)
                key_sum[0:keys] += tn(score_grad, query)
                query_grad = nn(score_grad, key) * SCALE
                put(block, columns, through_rope(
                    query_grad, spot, raw_[spot, columns], gain_query, "query"
                ))

        attend(3)
        gate_sum.finish(gate_total)
        mlp_sum.forward()
        up_sum.gather()
        attend(2)
        attend(1)
        down_sum.forward()

        def keep_block(spot, value):
            block_out[spot] = (residual_[spot] + value).astype(BF16)

        mlp_sum.finish(keep_block)
        block_turn = Turn(net, [(block_out, block_own)])
        block_turn.start()
        attend(0)
        for block in range(4):
            spot = slice(block * 256, block * 256 + 256)
            put(block, slice(256, 384), through_rope(
                key_sum[spot] * SCALE, spot, raw_[spot, 256:384], gain_key, "key"
            ))
            put(block, slice(384, 512), value_sum[spot].astype(BF16))
        up_sum.finish(up_total)
        loads["qkv"].wait()
        net.sent(mlp_sum.passed())

        def out(k):
            terms[unit(k)] = nt(parts[unit(k)], qkv_w[...]).astype(BF16)
            first_sum.pass_over(k)

        out(2)
        out(1)
        first_sum.combine(2)
        first_sum.start_far()
        out(-1)
        first_sum.combine(1)
        first_sum.start_right()
        out(0)
        first_sum.combine(-1)
        first_sum.start_left()
        loads["normed"].wait()
        for n in range(8):
            spot = pl.ds(n * 256, 256)
            qkv_g[spot] = tn(rows[:, spot], parts[...]).astype(BF16)
        down_sum.gather()
        output_sum.start()
        qkv_sum.start()
        first_sum.combine(0)
        first_sum.forward()

        halves = []

        def exchange(source_cut, there):
            halves.append(net.local(source_cut(mine), there(mine)))
            index = net.send(source_cut(theirs), there(mine), "core")
            halves.append((index, there(theirs)))

        for source, target in ((gate_total, gate_own), (up_total, up_own)):
            exchange(
                lambda core, source=source: source.at[
                    pl.ds(pl.multiple_of(core * 128, 128), 128)
                ],
                lambda core, target=target: target.at[
                    :, pl.ds(pl.multiple_of(core * 384, 128), 384)
                ],
            )
        down_sum.finish(down_total)
        exchange(
            lambda core: down_total.at[:, pl.ds(pl.multiple_of(core * 128, 128), 128)],
            lambda core: down_own.at[pl.ds(pl.multiple_of(core * 384, 128), 384)],
        )

        def keep_first(spot, value):
            rows_in = tokens_[spot].astype(F32)
            through, gain_part = norm_back(rows_in, gains_[0:1, 0:2048], value)
            input_out[spot] = (back_[spot] + through).astype(BF16)
            gain_part = jnp.sum(gain_part, axis=0, keepdims=True)
            gain_sums["first"] = gain_sums.get("first", 0.0) + gain_part

        first_sum.finish(keep_first)
        input_turn = Turn(net, [(input_out, input_own)])
        input_turn.start()
        flat = jnp.concatenate(
            [gain_sums["first"], second_gain_[...], gain_sums["query"], gain_sums["key"]], axis=1
        )
        entry = lax.broadcasted_iota(jnp.int32, (128, GAINS), 1)
        past = entry - owner_starts((128, GAINS), 0)
        owned = jnp.where((past >= 0) & (past < OWN_GAINS), flat, 0.0)
        column = (column_of(entry) == lax.broadcasted_iota(jnp.int32, (128, GAINS), 0)).astype(F32)
        gain_rows[...] = lax.dot_general(
            owned, column, (((1,), (1,)), ((), ())),
            precision=lax.Precision.HIGHEST, preferred_element_type=F32,
        ).reshape(128, 1, 128)
        gains_steps = GainsSum(net, gain_rows, gains_own, gain_land).steps()
        next(gains_steps)
        output_sum.forward()
        next(gains_steps)
        qkv_sum.forward()
        next(gains_steps)
        output_sum.gather()
        next(gains_steps)
        qkv_sum.gather()
        next(gains_steps)
        output_sum.finish(output_total)
        qkv_sum.finish(qkv_total)
        weights = Turn(net, [(qkv_total, qkv_own), (output_total, output_own)])
        weights.start()
        for copy in halves:
            if isinstance(copy, tuple):
                net.arrive(copy[0], copy[1], "core")
            else:
                copy.wait()
        block_turn.wait()
        input_turn.wait()
        weights.wait()

    copies = (
        RowsGather.COPIES + 2 * RowsSum.COPIES + 5 * PlaneSum.COPIES + 3 + 2 + 2 + 4 + 10
    )
    locals_ = 2 + 7 + 3 + 4
    return Kernel(
        2, copies, locals_, CORE_PARTNER + X_PARTNERS + FAR_X + PLANE_PARTNERS + TURN_PARTNERS
    )(
        body,
        [
            (low, VMEM), (back, VMEM), (residual, VMEM), (tokens, VMEM), (gains, VMEM),
            (second_gain, VMEM), (heads, VMEM), (raw, VMEM), (attended, VMEM), (totals, VMEM),
            (cosine, VMEM), (sine, VMEM), (lengths, VMEM), (qkv, HBM), (output, HBM),
            (normed, HBM), (mlp, HBM), (gate, HBM), (up, HBM), (down, HBM),
        ],
        [
            (shape((128, 2048)), HBM),
            (shape((128, 2048)), HBM),
            (shape((128, 512)), HBM),
            (shape((256, 128)), HBM),
            (shape((128, 768)), HBM),
            (shape((128, 768)), HBM),
            (shape((768, 128)), HBM),
            (shape((1, 1, 128), F32), VMEM),
        ],
        (
            pltpu.VMEM((1024, 2048), BF16),
            pltpu.VMEM((1024, 2048), BF16),
            pltpu.VMEM((2048, 512), BF16),
            pltpu.VMEM((256, 2048), BF16),
            pltpu.VMEM((2048, 768), BF16),
            pltpu.VMEM((2048, 768), BF16),
            pltpu.VMEM((768, 2048), BF16),
            pltpu.VMEM((2048, 512), BF16),
            pltpu.VMEM((256, 2048), BF16),
            pltpu.VMEM((1024, 256), BF16),
            pltpu.VMEM((1024, 256), BF16),
            pltpu.VMEM((1024, 128), F32),
            pltpu.VMEM((1024, 128), F32),
            pltpu.VMEM((1024, 512), BF16),
            pltpu.VMEM((128, 2048), BF16),
            pltpu.VMEM((128, 2048), BF16),
            pltpu.VMEM((128, 512), BF16),
            pltpu.VMEM((256, 128), BF16),
            pltpu.VMEM((256, 384), BF16),
            pltpu.VMEM((256, 384), BF16),
            pltpu.VMEM((384, 256), BF16),
            pltpu.VMEM((128, 1, 128), F32),
            pltpu.VMEM((3, 43, 1, 128), F32),
        )
        + ROWS_SCRATCH * 2
        + plane_scratch(256, 384) * 2
        + plane_scratch(384, 256)
        + plane_scratch(128, 512)
        + plane_scratch(256, 128),
    )


def step_rates(total_tokens):
    root_tokens = math.sqrt(total_tokens)
    narrow = MODEL_WIDTH ** (-0.5)
    return (
        narrow / (2.0 * root_tokens),
        narrow / (2.0 * root_tokens),
        (QUERY_HEADS * HEAD_SIZE // 128) ** (-0.5) / (0.24 * root_tokens),
        narrow / (0.7 * root_tokens),
        FF ** (-0.5) / (1.2 * root_tokens),
        0.025 / root_tokens,
    )


def body(tokens, cotangent, doc_lengths, *state):
    masters, moments, averages = state[0:6], state[6:12], state[12:18]
    query_weight, key_value_weight, output_weight, gateup_weight, down_weight, norm_gains = masters
    qkv_own = jnp.concatenate(
        [query_weight, key_value_weight[0], key_value_weight[1]], axis=1
    ).astype(BF16)
    lengths = jnp.pad(doc_lengths, ((0, 7), (0, 124)))
    cosine, sine = rope_tables()
    (
        residual, tokens_here, cotangent_here, normed, raw, heads, attended, totals,
        cosine, sine, qkv, output, gate, up, down_piece, cotangent_all, gains, lengths,
    ) = attention_forward(
        tokens,
        cotangent,
        qkv_own,
        output_weight.astype(BF16),
        jnp.pad(norm_gains, (0, 128 - OWN_GAINS)).reshape(1, 1, 128),
        lengths,
        jnp.asarray(cosine),
        jnp.asarray(sine),
        gateup_weight[0].astype(BF16),
        gateup_weight[1].astype(BF16),
        down_weight.astype(BF16),
    )
    back, low, second_gain, mlp, gate_grad, up_grad, down_grad = feed_forward(
        residual, cotangent_here, gains, cotangent_all, gate, up, down_piece
    )
    block_out, input_grad, qkv_total, output_total, gate_total, up_total, down_total, gains_total = (
        attention_backward(
            low, back, residual, tokens_here, gains, second_gain, heads, raw, attended, totals,
            cosine, sine, lengths, qkv, output, normed, mlp, gate_grad, up_grad, down_grad,
        )
    )
    gradients = (
        qkv_total[:, :256].astype(F32),
        jnp.stack([qkv_total[:, 256:384], qkv_total[:, 384:]]).astype(F32),
        output_total.astype(F32),
        jnp.stack([gate_total, up_total]).astype(F32),
        down_total.astype(F32),
        gains_total.reshape(128)[:OWN_GAINS],
    )
    updated = []
    velocity = []
    smoothed = []
    for master, gradient, moment, average, rate in zip(
        masters, gradients, moments, averages, step_rates(GROUP_TOK * 16)
    ):
        moment_next = MOMENTUM * moment + gradient
        master_next = master - rate * (gradient + MOMENTUM * moment_next)
        updated.append(master_next)
        velocity.append(moment_next)
        smoothed.append(AVERAGING * average + (1.0 - AVERAGING) * master_next)
    return (block_out, input_grad, *updated, *velocity, *smoothed)


def solution(mesh):
    parted = Mesh(mesh.devices.reshape(GRID), AXES)
    data = ("z", "ylo", "core")
    tensor = ("yhi", "x")
    rows = P(AXES, None)
    by_rows = P(data, tensor)
    pair = P(None, data, tensor)
    by_columns = P(tensor, data)
    flat = P(AXES)
    weights = (by_rows, pair, by_columns, pair, by_columns, flat)
    return jax.shard_map(
        body,
        mesh=parted,
        in_specs=(rows, rows, P(data, None)) + weights * 3,
        out_specs=(rows, rows) + weights * 3,
        check_vma=False,
    )
```

```python
import math

import jax
import jax.numpy as jnp
import numpy as np
from jax import lax
from jax.experimental import pallas as pl
from jax.experimental.pallas import tpu as pltpu
from jax.sharding import Mesh
from jax.sharding import PartitionSpec as P

MODEL_WIDTH = 2048
QUERY_HEADS = 16
HEAD_SIZE = 128
FF = 6144
GROUP_TOK = 1024
GAINS = 4352
OWN_GAINS = 34
EPSILON = 1e-06
MOMENTUM = 0.9
AVERAGING = 0.5
ROPE_BASE = 1000000.0
SCALE = HEAD_SIZE ** (-0.5)

AXES = ("z", "ylo", "core", "yhi", "x")
GRID = (4, 2, 2, 2, 4)
RING = 4
BF16 = jnp.bfloat16
F32 = jnp.float32
HBM = pl.ANY
VMEM = pltpu.VMEM


class Place:
    def __init__(self):
        self.x = lax.axis_index("x")
        self.z = lax.axis_index("z")
        self.core = lax.axis_index("core")
        self.yhi = lax.axis_index("yhi")
        self.ylo = lax.axis_index("ylo")
        self.y = self.yhi * 2 + self.ylo
        self.native = self.core == self.yhi
        at = {"x": self.x, "y": self.y, "z": self.z}
        self.steps = {
            (axis, by): lax.rem(here + by, RING) if by else here
            for axis, here in at.items()
            for by in range(RING)
        }
        self.devices = {
            "core": {"core": 1 - self.core},
            "turn": {"core": 1 - self.core, "yhi": 1 - self.yhi},
        }
        for (axis, by), there in self.steps.items():
            self.devices[axis, by] = (
                {"yhi": lax.div(there, 2), "ylo": lax.rem(there, 2)}
                if axis == "y"
                else {axis: there}
            )

    def step(self, axis, by):
        return self.steps[axis, by % RING]

    def device(self, axis, by=1):
        return self.devices[axis] if axis in ("core", "turn") else self.devices[axis, by % RING]


class Local:
    def __init__(self, refs, sems, index):
        self.refs, self.sems, self.index = refs, sems, index

    def copy(self):
        source, target = self.refs()
        return pltpu.make_async_copy(source, target, self.sems.at[self.index])

    def start(self):
        self.copy().start()

    def wait(self):
        self.copy().wait()


class Net:
    def __init__(self, place, partners, send_sems, recv_sems, local_sems):
        self.place, self.partners = place, partners
        self.send_sems, self.recv_sems, self.local_sems = send_sems, recv_sems, local_sems
        self.leaving, self.arriving, self.local_count = 0, 0, 0
        self.waits = []

    def greet(self):
        barrier = pltpu.get_barrier_semaphore()
        for axis, by in self.partners:
            pl.semaphore_signal(
                barrier,
                inc=1,
                device_id=self.place.device(axis, by),
                device_id_type=pl.DeviceIdType.MESH,
            )

    def enter(self):
        pl.semaphore_wait(pltpu.get_barrier_semaphore(), len(self.partners))

    def out(self):
        self.leaving += 1
        return self.leaving - 1

    def into(self):
        self.arriving += 1
        return self.arriving - 1

    def local_number(self):
        self.local_count += 1
        return self.local_count - 1

    def copy(self, source, target, out, into, axis="core", by=1):
        return pltpu.make_async_remote_copy(
            src_ref=source,
            dst_ref=target,
            send_sem=self.send_sems.at[out],
            recv_sem=self.recv_sems.at[into],
            device_id=self.place.device(axis, by),
            device_id_type=pl.DeviceIdType.MESH,
        )

    def send(self, refs, out, into, axis, by=1):
        self.copy(*refs(), out, into, axis, by).start()

    def here(self, into, view):
        self.copy(view, view, 0, into).wait_recv()

    def gone(self, out, view):
        self.copy(view, view, out, 0).wait_send()

    def later(self, wait):
        self.waits.append(wait)

    def finish(self):
        for wait in self.waits:
            wait()

    def local(self, refs):
        copy = Local(refs, self.local_sems, self.local_number())
        copy.start()
        return copy


def staged(count, compute, before=None, after=None):
    def do(acts, n):
        for at, act in (acts or {}).items():

            @pl.when(n == at)
            def _():
                act()

    def step(n, carry):
        do(before, n)
        compute(n)
        do(after, n)
        return carry

    lax.fori_loop(0, count, step, 0)


class RowsGather:
    OUT, INTO, LOCALS = 1, 7, 2

    def __init__(self, net, own, whole):
        self.net, self.own, self.whole = net, own, whole
        self.rows = own.shape[0]
        self.half = self.rows // 2
        place = net.place
        self.me, self.other = place.core, 1 - place.core
        self.spots = {k: place.step("x", k) for k in (0, 1, -1, 2)}
        self.out = net.out()
        self.first, self.second, self.third = net.into(), net.into(), net.into()
        self.shared = {k: net.into() for k in (0, 1, -1, 2)}
        self.kept = []
        net.later(self.gone)

    def block(self, core, k, part):
        start = (self.spots[k] * 2 + core) * self.rows + part * self.half
        return self.whole.at[pl.ds(pl.multiple_of(start, self.half), self.half)]

    def mine(self, k, part):
        return self.block(self.me, k, part)

    def piece(self, part):
        return self.own.at[pl.ds(part * self.half, self.half)]

    def share(self, k, part):
        refs = lambda: (self.piece(part) if k == 0 else self.mine(k, part), self.mine(k, part))
        self.net.send(refs, self.out, self.shared[k], "core")

    def both(self):
        return self.whole.at[pl.ds(0, self.rows)]

    def start(self, parts=(0, 1)):
        for part in parts:
            refs = lambda part=part: (self.piece(part), self.mine(0, part))
            first, second = (1, -1) if part == 0 else (-1, 1)
            self.net.send(refs, self.out, self.first, "x", first)
            self.net.send(refs, self.out, self.second, "x", second)
            self.share(0, part)
            self.kept.append(self.net.local(refs))

    def near_first(self):
        self.net.here(self.first, self.both())
        self.net.send(lambda: (self.mine(-1, 0),) * 2, self.out, self.third, "x", 1)
        self.net.send(lambda: (self.mine(1, 1),) * 2, self.out, self.third, "x", -1)
        self.share(-1, 0)
        self.share(1, 1)

    def near_second(self):
        self.net.here(self.second, self.both())
        self.share(-1, 1)
        self.share(1, 0)

    def far(self):
        self.net.here(self.third, self.both())
        self.share(2, 0)
        self.share(2, 1)

    def here(self, k):
        if k == 0:
            for copy in self.kept:
                copy.wait()
        self.net.here(self.shared[k], self.both())

    def gone(self):
        if self.out is not None:
            self.net.gone(self.out, self.whole.at[pl.ds(0, 7 * self.rows)])
            self.out = None


class RowsSum:
    OUT, INTO = 2, 6

    def __init__(self, net, whole, landed, land):
        self.net, self.whole, self.landed, self.land = net, whole, landed, land
        self.half = landed.shape[2]
        place = net.place
        self.me, self.other = place.core, 1 - place.core
        self.spots = {k: place.step("x", k) for k in (0, 1, -1, 2)}
        self.over, self.along = net.out(), net.out()
        self.given = {k: net.into() for k in (0, 1, -1, 2)}
        self.through, self.last = net.into(), net.into()
        net.later(self.passed)
        net.later(lambda: net.gone(self.along, self.land))

    def block(self, core, k, part):
        start = ((self.spots[k] * 2 + core) * 2 + part) * self.half
        return self.whole.at[pl.ds(pl.multiple_of(start, self.half), self.half)]

    def own(self, k, part):
        return self.landed.at[k % RING, part]

    def pass_over(self, k):
        for part in range(2):
            refs = lambda part=part: (self.block(self.other, k, part), self.own(k, part))
            self.net.send(refs, self.over, self.given[k], "core")

    def passed(self):
        if self.over is not None:
            self.net.gone(self.over, self.landed)
            self.over = None

    def combine(self, k):
        self.net.here(self.given[k], self.landed.at[k % RING])
        for part in range(2):
            here = self.own(k, part)
            here[...] = here[...] + self.block(self.me, k, part)[...]

    def along_x(self, refs, into, by):
        self.net.send(refs, self.along, into, "x", by)

    def start_far(self):
        self.along_x(lambda: (self.own(2, 0), self.land.at[0]), self.through, 1)
        self.along_x(lambda: (self.own(2, 1), self.land.at[1]), self.through, -1)

    def start_right(self):
        self.along_x(lambda: (self.own(1, 1), self.land.at[3]), self.last, 1)

    def start_left(self):
        self.along_x(lambda: (self.own(-1, 0), self.land.at[4]), self.last, -1)

    def forward(self):
        land = self.land
        self.net.here(self.through, land.at[pl.ds(0, 2)])
        land[0] = land[0] + self.own(1, 0)[...]
        self.along_x(lambda: (land.at[0], land.at[2]), self.last, 1)
        land[1] = land[1] + self.own(-1, 1)[...]
        self.along_x(lambda: (land.at[1], land.at[5]), self.last, -1)

    def finish(self, keep):
        land = self.land
        self.net.here(self.last, land.at[pl.ds(2, 4)])
        for part in range(2):
            total = self.own(0, part)[...].astype(F32) + land[2 + part].astype(F32)
            keep(pl.ds(part * self.half, self.half), total + land[4 + part].astype(F32))


ROWS_SCRATCH = (pltpu.VMEM((4, 2, 64, 2048), BF16), pltpu.VMEM((6, 64, 2048), BF16))


class PlaneGather:
    OUT, INTO, LOCALS = 1, 12, 1

    def __init__(self, net, own, whole, spot):
        self.net, self.own, self.whole, self.spot = net, own, whole, spot
        self.rows = own.shape[0]
        self.half = self.rows // 2
        self.width = own.shape[1]
        self.out = net.out()
        self.first = [net.into() for _ in range(2)]
        self.rings = {(color, i): net.into() for color in range(2) for i in (0, 1, -1, -2)}
        self.last = [net.into() for _ in range(2)]
        net.later(lambda: net.gone(self.out, whole.at[pl.ds(0, whole.shape[0] // 16 * 15)]))

    def view(self, color, i, j, part=None):
        place = self.net.place
        first, second = self.axes(color)
        a, b = place.step(first, i), place.step(second, j)
        row, columns = self.spot(a, b) if color == 0 else self.spot(b, a)
        start = row + color * self.half
        if part is None:
            return self.whole.at[pl.ds(pl.multiple_of(start, self.half), self.half), columns]
        size = self.half // 2
        return self.whole.at[pl.ds(pl.multiple_of(start + part * size, size), size), columns]

    def bytes_of(self, halves):
        return self.whole.at[pl.ds(0, halves * self.half), pl.ds(0, self.width)]

    @staticmethod
    def axes(color):
        return ("z", "y") if color == 0 else ("y", "z")

    def mine(self, color):
        return self.own.at[pl.ds(color * self.half, self.half)]

    def ring(self, color, i):
        axis = self.axes(color)[1]
        refs = lambda: (
            self.mine(color) if i == 0 else self.view(color, i, 0), self.view(color, i, 0)
        )
        for by in (1, -1):
            self.net.send(refs, self.out, self.rings[color, i], axis, by)

    def start(self):
        for color in range(2):
            axis = self.axes(color)[0]
            refs = lambda color=color: (self.mine(color), self.view(color, 0, 0))
            for by in (1, -1, 2):
                self.net.send(refs, self.out, self.first[color], axis, by)
        for color in range(2):
            self.ring(color, 0)
        self.kept = self.net.local(self.place_here)

    def place_here(self):
        row, columns = self.spot(self.net.place.z, self.net.place.y)
        return self.own, self.whole.at[pl.ds(pl.multiple_of(row, self.rows), self.rows), columns]

    def spread(self):
        for color in range(2):
            self.net.here(self.first[color], self.bytes_of(3) if self.fits(3) else self.thin(3))
        for i in (-1, 1, -2):
            for color in range(2):
                self.ring(color, i)

    def fits(self, halves):
        return halves * self.half <= self.whole.shape[0]

    def thin(self, halves):
        return self.whole.at[pl.ds(0, self.half), pl.ds(0, halves * self.width)]

    def forward(self, steps=(0, 1, -1, -2)):
        for i in steps:
            for color in range(2):
                axis = self.axes(color)[1]
                self.net.here(self.rings[color, i], self.bytes_of(2))
                for j, part, by in ((-1, 0, 1), (1, 1, -1)):
                    refs = lambda color=color, i=i, j=j, part=part: (
                        self.view(color, i, j, part),
                    ) * 2
                    self.net.send(refs, self.out, self.last[color], axis, by)

    def here(self):
        for color in range(2):
            self.net.here(self.last[color], self.bytes_of(4) if self.fits(4) else self.thin(4))
        self.kept.wait()


class PlaneSum:
    OUT, INTO = 2, 18

    def __init__(self, net, whole, spot, land, last):
        self.net, self.whole, self.spot, self.land, self.last = net, whole, spot, land, last
        self.size = land.shape[3]
        self.ring_out, self.last_out = net.out(), net.out()
        ways = [(color, k) for color in range(2) for k in range(RING)]
        self.through = {way: net.into() for way in ways}
        self.sides = {way: net.into() for way in ways}
        self.ends = [net.into() for _ in range(2)]
        net.later(lambda: net.gone(self.ring_out, land))
        net.later(lambda: net.gone(self.last_out, last))

    @staticmethod
    def axes(color):
        return ("y", "z") if color == 0 else ("z", "y")

    def own(self, color, n, k, part):
        place = self.net.place
        first, second = self.axes(color)
        a, b = place.step(first, n), place.step(second, k)
        row, columns = self.spot(b, a) if color == 0 else self.spot(a, b)
        start = row + (color * 2 + part) * self.size
        return self.whole.at[pl.ds(pl.multiple_of(start, self.size), self.size), columns]

    def slot(self, color, k, n):
        return self.land.at[color, k % RING, n]

    def end(self, color, k, part):
        return self.last.at[color, k % RING - 1, part]

    def start(self):
        for k in (2, 1, -1, 0):
            for color in range(2):
                axis = self.axes(color)[0]
                through, sides = self.through[color, k % RING], self.sides[color, k % RING]
                for n, part, slot, into, by in (
                    (2, 0, 0, through, 1), (2, 1, 1, through, -1),
                    (1, 1, 3, sides, 1), (-1, 0, 4, sides, -1),
                ):
                    refs = lambda color=color, k=k, n=n, part=part, slot=slot: (
                        self.own(color, n, k, part), self.slot(color, k, slot)
                    )
                    self.net.send(refs, self.ring_out, into, axis, by)

    def forward(self, steps=(2, 1, -1, 0)):
        for k in steps:
            for color in range(2):
                axis = self.axes(color)[0]
                sides = self.sides[color, k % RING]
                self.net.here(
                    self.through[color, k % RING], self.land.at[color, k % RING, pl.ds(0, 2)]
                )
                for slot, n, part, target, by in ((0, 1, 0, 2, 1), (1, -1, 1, 5, -1)):
                    here = self.slot(color, k, slot)
                    here[...] = here[...] + self.own(color, n, k, part)[...]
                    refs = lambda color=color, k=k, slot=slot, target=target: (
                        self.slot(color, k, slot), self.slot(color, k, target)
                    )
                    self.net.send(refs, self.ring_out, sides, axis, by)

    def gather(self, steps=(2, 1, -1, 0)):
        for k in steps:
            for color in range(2):
                second = self.axes(color)[1]
                self.net.here(
                    self.sides[color, k % RING], self.land.at[color, k % RING, pl.ds(2, 4)]
                )
                for part in range(2):
                    here = self.slot(color, k, 2 + part)
                    total = self.own(color, 0, k, part)[...].astype(F32) + here[...].astype(F32)
                    total = total + self.slot(color, k, 4 + part)[...].astype(F32)
                    here[...] = total.astype(BF16)
                    if k != 0:
                        refs = lambda color=color, k=k, part=part: (
                            self.slot(color, k, 2 + part), self.end(color, k, part)
                        )
                        self.net.send(refs, self.last_out, self.ends[color], second, k)

    def finish(self, total):
        for color in range(2):
            self.net.here(self.ends[color], self.last.at[color])
            for part in range(2):
                value = self.slot(color, 0, 2 + part)[...].astype(F32)
                for k in (1, -1, 2):
                    value = value + self.end(color, k, part)[...].astype(F32)
                start = (color * 2 + part) * self.size
                total[pl.ds(start, self.size)] = value.astype(total.dtype)


def plane_scratch(rows, columns):
    return (
        pltpu.VMEM((2, 4, 6, rows // 4, columns), BF16),
        pltpu.VMEM((2, 3, 2, rows // 4, columns), BF16),
    )


class Turn:
    def __init__(self, net, pairs):
        self.net = net
        self.pairs = [
            (source, target, net.out(), net.into(), net.local_number()) for source, target in pairs
        ]

    def copies(self):
        return [self.net.copy(a, b, out, into, "turn") for a, b, out, into, _ in self.pairs]

    def kept(self):
        sems = self.net.local_sems
        return [pltpu.make_async_copy(a, b, sems.at[index]) for a, b, _, _, index in self.pairs]

    def both(self, act):
        @pl.when(jnp.logical_not(self.net.place.native))
        def _():
            for copy in self.copies():
                act(copy)

        @pl.when(self.net.place.native)
        def _():
            for copy in self.kept():
                act(copy)

    def start(self):
        self.both(lambda copy: copy.start())

    def wait(self):
        self.both(lambda copy: copy.wait())


class Give:
    def __init__(self, net, refs, there):
        self.net, self.there = net, there
        self.out, self.into = net.out(), net.into()
        net.send(refs, self.out, self.into, "core")
        net.later(lambda: net.gone(self.out, refs()[0]))

    def wait(self):
        self.net.here(self.into, self.there())


def parts_of(source, target, count):
    rows = source.shape[0] // count
    spots = [pl.ds(part * rows, rows) for part in range(count)]
    return [(source.at[spot], target.at[spot]) for spot in spots]


class GainsGather:
    OUT, INTO, LOCALS = 1, 4, 1

    def __init__(self, net, own, whole):
        self.net, self.own, self.whole = net, own, whole
        self.out = net.out()
        self.into = [net.into() for _ in range(4)]
        net.later(lambda: net.gone(self.out, whole.at[pl.ds(0, 127)]))

    def rows(self, z, y, x, core, count):
        start = ((z * RING + y) * RING + x) * 2 + core
        return self.whole.at[pl.ds(start if count == 1 else pl.multiple_of(start, count), count)]

    def spot(self, axis, by):
        place = self.net.place
        if axis == "core":
            return self.rows(place.z, place.y, place.x, (place.core + by) % 2, 1)
        if axis == "x":
            return self.rows(place.z, place.y, place.step("x", by), 0, 2)
        if axis == "y":
            return self.rows(place.z, place.step("y", by), 0, 0, 8)
        return self.rows(place.step("z", by), 0, 0, 0, 32)

    def steps(self):
        net = self.net
        net.local(lambda: (self.own, self.spot("core", 0))).wait()
        for into, axis, count in zip(self.into, ("core", "x", "y", "z"), (1, 2, 8, 32)):
            ways = (1,) if axis == "core" else (1, -1, 2)
            for by in ways:
                net.send(lambda: (self.spot(axis, 0),) * 2, self.out, into, axis, by)
            yield
            net.here(into, self.whole.at[pl.ds(0, count * len(ways))])
        yield


class GainsSum(GainsGather):
    def __init__(self, net, whole, total, land):
        super().__init__(net, None, whole)
        self.total, self.land = total, land

    def steps(self):
        net, land = self.net, self.land
        first = 0
        for into, axis, count in zip(self.into, ("z", "y", "x", "core"), (32, 8, 2, 1)):
            ways = (1,) if axis == "core" else (1, -1, 2)
            spots = [pl.ds(first + n * count, count) for n in range(len(ways))]
            for spot, by in zip(spots, ways):
                refs = lambda spot=spot, by=by: (self.spot(axis, by), land.at[spot])
                net.send(refs, self.out, into, axis, by)
            yield
            net.here(into, land.at[pl.ds(first, count * len(ways))])
            value = self.spot(axis, 0)[...]
            for spot in spots:
                value = value + land[spot]
            if axis == "core":
                self.total[...] = value
            else:
                self.spot(axis, 0)[...] = value
            first += count * len(ways)
        yield


class Kernel:
    def __init__(self, number, plans, gives, turns, locals_, partners):
        self.number, self.partners = number, partners
        extra = gives + turns
        self.sems = (
            sum(plan.OUT for plan in plans) + extra,
            sum(plan.INTO for plan in plans) + extra,
            sum(getattr(plan, "LOCALS", 0) for plan in plans) + turns + locals_,
        )

    def __call__(self, body, arrays, outs, scratch=()):
        n_in, n_out, n_scratch = len(arrays), len(outs), len(scratch)

        def kernel(*refs):
            net = Net(Place(), self.partners, *refs[n_in + n_out + n_scratch :])
            net.greet()
            body(
                net,
                refs[:n_in],
                refs[n_in : n_in + n_out],
                refs[n_in + n_out : n_in + n_out + n_scratch],
            )
            net.finish()
            assert (net.leaving, net.arriving, net.local_count) == self.sems, (
                net.leaving, net.arriving, net.local_count, self.sems,
            )

        return pl.pallas_call(
            kernel,
            out_shape=[shape for shape, _ in outs],
            in_specs=[pl.BlockSpec(memory_space=space) for _, space in arrays],
            out_specs=[pl.BlockSpec(memory_space=space) for _, space in outs],
            scratch_shapes=[*scratch] + [pltpu.SemaphoreType.DMA((n,)) for n in self.sems],
            compiler_params=pltpu.CompilerParams(
                collective_id=self.number, has_side_effects=True, vmem_limit_bytes=61 * 2**20
            ),
            name="links_%d" % self.number,
        )(*[array for array, _ in arrays])


CORE_PARTNER = (("core", 1),)
X_PARTNERS = (("x", 1), ("x", -1))
FAR_X = (("x", 2),)
PLANE_PARTNERS = (("y", 1), ("y", -1), ("y", 2), ("z", 1), ("z", -1), ("z", 2))
TURN_PARTNERS = (("turn", 1),)


def shape(dims, dtype=BF16):
    return jax.ShapeDtypeStruct(dims, dtype)


def attention_spot(z, y):
    piece = z * 4 + lax.rem(y, 2) * 2 + lax.div(y, 2)
    return piece * 128


def rows_spot(z, y):
    return attention_spot(z, y), pl.ds(0, 512)


def output_spot(z, y):
    return 0, pl.ds(pl.multiple_of(attention_spot(z, y), 128), 128)


def gateup_spot(z, y):
    columns = pl.ds(pl.multiple_of(lax.div(y, 2) * 384, 128), 384)
    return (z * 2 + lax.rem(y, 2)) * 256, columns


def down_spot(z, y):
    columns = pl.ds(pl.multiple_of((z * 2 + lax.rem(y, 2)) * 256, 128), 256)
    return lax.div(y, 2) * 384, columns


def nn(left, right):
    return lax.dot_general(left, right, (((1,), (0,)), ((), ())), preferred_element_type=F32)


def nt(left, right):
    return lax.dot_general(left, right, (((1,), (1,)), ((), ())), preferred_element_type=F32)


def tn(left, right):
    return lax.dot_general(left, right, (((0,), (0,)), ((), ())), preferred_element_type=F32)


def exact(left, right):
    return lax.dot_general(
        left, right, (((1,), (0,)), ((), ())),
        precision=lax.Precision.HIGHEST, preferred_element_type=F32,
    )


def inverse_root(rows):
    return lax.rsqrt(jnp.mean(rows * rows, axis=-1, keepdims=True) + EPSILON)


def norm_back(rows, gain, upstream):
    root = inverse_root(rows)
    weighted = upstream * gain
    meant = jnp.mean(weighted * rows, axis=-1, keepdims=True)
    return root * weighted - rows * (root * root * root * meant), upstream * rows * root


def rope_tables():
    halves = np.arange(HEAD_SIZE // 2, dtype=np.float64)
    angles = np.arange(GROUP_TOK)[:, None] * ROPE_BASE ** (-2.0 * halves / HEAD_SIZE)[None, :]
    angles = np.concatenate([angles, angles], axis=1)
    return np.cos(angles).astype(np.float32), np.sin(angles).astype(np.float32)


def owner_starts(dims, axis):
    row = lax.broadcasted_iota(jnp.int32, dims, axis)
    z, y, x, core = row >> 5, (row >> 3) & 3, (row >> 1) & 3, row & 1
    return (z * 32 + (y & 1) * 16 + core * 8 + (y >> 1) * 4 + x) * OWN_GAINS


def column_of(entry):
    return entry - jnp.floor((entry.astype(F32) + 0.5) * (1.0 / OWN_GAINS)).astype(jnp.int32) * OWN_GAINS


def gains_flat(rows):
    entry = lax.broadcasted_iota(jnp.int32, (128, GAINS), 1)
    past = entry - owner_starts((128, GAINS), 0)
    owner = ((past >= 0) & (past < OWN_GAINS)).astype(F32)
    columns = lax.dot_general(
        rows, owner, (((0,), (0,)), ((), ())),
        precision=lax.Precision.HIGHEST, preferred_element_type=F32,
    )
    place = lax.broadcasted_iota(jnp.int32, (128, GAINS), 0)
    return jnp.sum(jnp.where(column_of(entry) == place, columns, 0.0), axis=0, keepdims=True)


class Documents:
    def __init__(self, lengths):
        lengths = [lengths[0:1, n : n + 1] for n in range(4)]
        self.ends = [lengths[0], lengths[0] + lengths[1], lengths[0] + lengths[1] + lengths[2]]

    def pick(self, place, values):
        value = jnp.where(place >= self.ends[0], values[1], values[0])
        value = jnp.where(place >= self.ends[1], values[2], value)
        return jnp.where(place >= self.ends[2], values[3], value)

    def first(self, place):
        zero = jnp.zeros_like(self.ends[0])
        return self.pick(place, [zero] + self.ends)


def allowed_pairs(documents, first_row, rows, keys):
    query = lax.broadcasted_iota(jnp.int32, (rows, 1), 0) + first_row
    key = lax.broadcasted_iota(jnp.int32, (rows, keys), 1)
    return (key >= documents.first(query)) & (key <= query)


def unit_off(n):
    return lax.rem(n + lax.div(n, 2), 4) + 2 * lax.div(n, 3)


class Units:
    ORDER = (0, 1, -1, 2)

    def __init__(self, place):
        self.x = place.x

    def chip(self, n):
        return lax.rem(self.x + unit_off(n), RING)

    def rows(self, n):
        return pl.ds(pl.multiple_of(self.chip(n) * 256, 256), 256)

    def true_rows(self, n, core):
        return pl.ds(pl.multiple_of((core * RING + self.chip(n)) * 128, 128), 128)


def own_half(length, core):
    return pl.ds(pl.multiple_of(core * length, 128), length)


def attention_forward(
    tokens, cotangent, query, keyval, output, gateup, down, gains, lengths, cosine, sine
):
    def body(net, ins, outs, work):
        (
            tokens_, cotangent_, query_, keyval_, output_, gateup_, down_, gains_, lengths_,
            cosine_, sine_,
        ) = ins
        (
            residual_, tokens_here, cotangent_here, normed_, raw_, heads_, attended_, totals_,
            cosine_out, sine_out, qkv_out, output_out, gate_out, up_out, down_piece,
            cotangent_all, flat_, lengths_out,
        ) = outs
        (
            gathered, normed, qkv_w, output_w, qkv_cast, output_cast, qkv_piece, output_piece,
            gains_row, gains_rows, lengths_mine, lengths_there, gate_cast, up_cast, down_cast,
            gate_piece, up_piece, terms, landed, land,
        ) = work
        place = net.place
        units = Units(place)
        mine, theirs = place.core, 1 - place.core

        qkv_cast[:, 0:256] = query_[...].astype(BF16)
        qkv_cast[:, 256:384] = keyval_[0].astype(BF16)
        qkv_cast[:, 384:512] = keyval_[1].astype(BF16)
        output_cast[...] = output_[...].astype(BF16)
        gains_row[0] = jnp.zeros((1, 128), F32)
        gains_row[0, 0:1, 0:OWN_GAINS] = gains_[...]
        lengths_mine[...] = jnp.zeros((8, 128), jnp.int32)
        lengths_mine[0:1, 0:4] = lengths_[...]
        net.enter()
        qkv_turn = Turn(net, [(qkv_cast, qkv_piece)])
        output_turn = Turn(net, [(output_cast, output_piece)])
        rows = [Turn(net, [pair]) for pair in parts_of(tokens_, tokens_here, 2)]
        upstream = Turn(net, parts_of(cotangent_, cotangent_here, 2))
        qkv_turn.start()
        for part in rows:
            part.start()
        qkv_gather = PlaneGather(net, qkv_piece, qkv_w, rows_spot)
        output_gather = PlaneGather(net, output_piece, output_w, output_spot)
        gate_gather = PlaneGather(net, gate_piece, gate_out, gateup_spot)
        up_gather = PlaneGather(net, up_piece, up_out, gateup_spot)
        gather = RowsGather(net, tokens_here, gathered)
        later = RowsGather(net, cotangent_here, cotangent_all)
        length_copy = Give(net, lambda: (lengths_mine, lengths_there), lambda: lengths_there)
        gains_steps = GainsGather(net, gains_row, gains_rows).steps()
        next(gains_steps)

        halves = []
        for n, (cast, piece) in enumerate(((gate_cast, gate_piece), (up_cast, up_piece))):
            spot = own_half(128, mine)
            piece[spot] = gateup_[n, :, own_half(384, mine)].astype(BF16)
            cast[...] = gateup_[n, :, own_half(384, theirs)].astype(BF16)
            halves.append(Give(
                net,
                lambda cast=cast, piece=piece: (cast, piece.at[own_half(128, mine)]),
                lambda piece=piece: piece.at[own_half(128, theirs)],
            ))
        down_piece[:, own_half(128, mine)] = down_[own_half(384, mine)].astype(BF16)
        down_cast[...] = down_[own_half(384, theirs)].astype(BF16)
        halves.append(Give(
            net,
            lambda: (down_cast, down_piece.at[:, own_half(128, mine)]),
            lambda: down_piece.at[:, own_half(128, theirs)],
        ))

        qkv_turn.wait()
        qkv_gather.start()
        output_turn.start()
        for n, part in enumerate(rows):
            part.wait()
            gather.start((n,))
        upstream.start()
        next(gains_steps)

        length_copy.wait()
        lengths_out[...] = jnp.where(place.native, lengths_mine[...], lengths_there[...])
        documents = Documents(lengths_out[...])
        zero = jnp.zeros((1, 1), jnp.int32)
        starts = [zero] + documents.ends
        everywhere = lax.broadcasted_iota(jnp.int32, (1, GROUP_TOK), 1)
        hits = jnp.concatenate(
            [(everywhere == start).astype(F32) for start in starts] * 2, axis=0
        )
        start_cosine = exact(hits, cosine_[...])
        start_sine = exact(hits, sine_[...])
        sign = jnp.where(lax.broadcasted_iota(jnp.int32, (1, HEAD_SIZE), 1) < 64, -1.0, 1.0)

        def table(n):
            spot = pl.ds(pl.multiple_of(n * 256, 256), 256)
            where = lax.broadcasted_iota(jnp.int32, (256, 1), 0) + n * 256
            cosine_by = documents.pick(where, [start_cosine[n : n + 1] for n in range(4)])
            sine_by = documents.pick(where, [start_sine[n : n + 1] for n in range(4)])
            cosine_out[spot] = cosine_[spot] * cosine_by + sine_[spot] * sine_by
            sine_out[spot] = (sine_[spot] * cosine_by - cosine_[spot] * sine_by) * sign

        staged(4, table)
        qkv_gather.spread()
        output_turn.wait()
        output_gather.start()
        next(gains_steps)
        gather.near_first()
        for half in halves:
            half.wait()
        next(gains_steps)
        qkv_gather.forward()
        output_gather.spread()
        gate_gather.start()
        next(gains_steps)
        flat_[...] = gains_flat(gains_rows[...].reshape(128, 128))
        gain_query = flat_[0:1, 4096:4224]
        gain_key = flat_[0:1, 4224:4352]

        def normalize(n):
            rows_in = gathered[units.rows(n)].astype(F32)
            normed[units.rows(n)] = (
                rows_in * inverse_root(rows_in) * flat_[0:1, 0:2048]
            ).astype(BF16)

        def near():
            gather.near_second()
            gather.here(1)

        def far():
            gather.far()
            output_gather.forward()
            up_gather.start()
            upstream.wait()
            later.start()
            gather.here(2)

        staged(4, normalize, {
            0: lambda: gather.here(0), 1: near, 2: lambda: gather.here(-1), 3: far,
        })
        qkv_gather.here()
        stores = [net.local(lambda: (normed, normed_)), net.local(lambda: (qkv_w, qkv_out))]

        def project(n):
            parts = nn(normed[units.rows(n)], qkv_w[...])
            for core in range(2):
                spot = units.true_rows(n, core)
                part = parts[core * 128 : core * 128 + 128]
                raw_[spot] = part[:, 0:384]
                heads_[spot, 384:512] = part[:, 384:512].astype(BF16)
                for head in range(3):
                    columns = slice(head * 128, head * 128 + 128)
                    value = part[:, columns]
                    value = value * inverse_root(value) * (gain_key if head == 2 else gain_query)
                    turned = value * cosine_out[spot] + pltpu.roll(value, 64, 1) * sine_out[spot]
                    heads_[spot, columns] = turned.astype(BF16)

        staged(4, project)
        gate_gather.spread()

        def attend(block):
            keys = 256 * (block + 1)
            spot = slice(block * 256, block * 256 + 256)

            def one(head):
                columns = own_half(128, head)
                scores = nt(heads_[spot, columns], heads_[0:keys, 256:384])
                allowed = allowed_pairs(documents, block * 256, 256, keys)
                scores = jnp.where(allowed, scores, -1e30)
                highest = jnp.max(scores, axis=-1, keepdims=True)
                weights_ = jnp.exp((scores - highest) * SCALE)
                summed = jnp.sum(weights_, axis=-1, keepdims=True)
                probability = (weights_ * (1.0 / summed)).astype(BF16)
                attended_[spot, columns] = nn(probability, heads_[0:keys, 384:512]).astype(BF16)
                totals_[spot, columns] = jnp.broadcast_to(
                    highest * SCALE + jnp.log(summed), (256, 128)
                )

            staged(2, one)

        attend(0)
        attend(1)
        later.near_first()
        up_gather.spread()
        attend(2)
        output_gather.here()
        stores.append(net.local(lambda: (output_w, output_out)))
        attend(3)
        sums = RowsSum(net, terms, landed, land)

        def out(n):
            n = 3 - n
            own = jnp.concatenate(
                [attended_[units.true_rows(n, 0)], attended_[units.true_rows(n, 1)]], axis=0
            )
            terms[units.rows(n)] = nn(own, output_w[...]).astype(BF16)

        def passed(k, ready=None, go=None):
            def act():
                sums.pass_over(k)
                if ready is not None:
                    sums.combine(ready)
                    go()

            return act

        later.near_second()
        staged(4, out, None, {
            0: passed(2),
            1: passed(-1, 2, sums.start_far),
            2: passed(1, -1, sums.start_left),
            3: passed(0, 1, sums.start_right),
        })
        later.far()
        gate_gather.forward()
        sums.combine(0)
        sums.forward()
        up_gather.forward()
        for k in (0, 1, -1, 2):
            later.here(k)

        def keep(spot, value):
            residual_[spot] = value + tokens_here[spot].astype(F32)

        sums.finish(keep)
        gate_gather.here()
        up_gather.here()
        for store in stores:
            store.wait()

    plans = (GainsGather,) + 4 * (PlaneGather,) + 2 * (RowsGather,) + (RowsSum,)
    return Kernel(
        0, plans, 4, 6, 3, CORE_PARTNER + X_PARTNERS + FAR_X + PLANE_PARTNERS + TURN_PARTNERS
    )(
        body,
        [
            (tokens, VMEM), (cotangent, VMEM), (query, VMEM), (keyval, VMEM), (output, VMEM),
            (gateup, VMEM), (down, VMEM), (gains, VMEM), (lengths, VMEM),
            (cosine, VMEM), (sine, VMEM),
        ],
        [
            (shape((128, 2048), F32), VMEM),
            (shape((128, 2048)), VMEM),
            (shape((128, 2048)), VMEM),
            (shape((1024, 2048)), HBM),
            (shape((1024, 384), F32), VMEM),
            (shape((1024, 512)), VMEM),
            (shape((1024, 256)), VMEM),
            (shape((1024, 256), F32), VMEM),
            (shape((1024, 128), F32), VMEM),
            (shape((1024, 128), F32), VMEM),
            (shape((2048, 512)), HBM),
            (shape((256, 2048)), HBM),
            (shape((2048, 768)), HBM),
            (shape((2048, 768)), HBM),
            (shape((384, 256)), VMEM),
            (shape((1024, 2048)), HBM),
            (shape((1, GAINS), F32), VMEM),
            (shape((8, 128), jnp.int32), VMEM),
        ],
        (
            pltpu.VMEM((1024, 2048), BF16),
            pltpu.VMEM((1024, 2048), BF16),
            pltpu.VMEM((2048, 512), BF16),
            pltpu.VMEM((256, 2048), BF16),
            pltpu.VMEM((128, 512), BF16),
            pltpu.VMEM((256, 128), BF16),
            pltpu.VMEM((128, 512), BF16),
            pltpu.VMEM((256, 128), BF16),
            pltpu.VMEM((1, 1, 128), F32),
            pltpu.VMEM((128, 1, 128), F32),
            pltpu.VMEM((8, 128), jnp.int32),
            pltpu.VMEM((8, 128), jnp.int32),
            pltpu.VMEM((128, 384), BF16),
            pltpu.VMEM((128, 384), BF16),
            pltpu.VMEM((384, 128), BF16),
            pltpu.VMEM((256, 384), BF16),
            pltpu.VMEM((256, 384), BF16),
            pltpu.VMEM((1024, 2048), BF16),
        )
        + ROWS_SCRATCH,
    )


def feed_forward(residual, cotangent, gains, cotangent_all, gate, up, down):
    def body(net, ins, outs, work):
        residual_, cotangent_, gains_, cotangent_all_, gate_, up_, down_ = ins
        back_, low_, gain_grad_, mlp_, gate_grad_, up_grad_, down_grad_ = outs
        (
            second_low, second, upstream, gate_w, up_w, down_w, hidden, gate_low, up_low, terms,
            mlp, gate_g, up_g, down_g, landed, land,
        ) = work
        place = net.place
        units = Units(place)
        gain = gains_[0:1, 2048:4096]
        rows = residual_[...]
        second_low[...] = (rows * inverse_root(rows) * gain).astype(BF16)
        loads = [
            net.local(lambda: (gate_, gate_w)),
            net.local(lambda: (up_, up_w)),
            net.local(lambda: (cotangent_all_, upstream)),
        ]
        net.enter()
        gather = RowsGather(net, second_low, second)
        gather.start()
        down_gather = PlaneGather(net, down_, down_w, down_spot)
        down_gather.start()
        sums = RowsSum(net, terms, landed, land)

        def forth(n):
            spot = units.rows(n)
            gate_value = nn(second[spot], gate_w[...])
            upward = nn(second[spot], up_w[...])
            sigmoid = 1.0 / (1.0 + jnp.exp(-gate_value))
            active = gate_value * sigmoid
            hidden[spot] = (active * upward).astype(BF16)
            gate_low[spot] = (upward * (sigmoid + active * (1.0 - sigmoid))).astype(BF16)
            up_low[spot] = active.astype(BF16)

        def begin():
            loads[0].wait()
            loads[1].wait()
            gather.here(0)

        def near():
            gather.near_first()
            down_gather.spread()
            gather.near_second()
            gather.here(1)

        def far():
            down_gather.forward()
            gather.far()
            gather.here(2)

        staged(4, forth, {0: begin, 1: near, 2: lambda: gather.here(-1), 3: far})
        down_gather.here()

        def back(n):
            spot = units.rows(3 - n)
            hidden_grad = nt(upstream[spot], down_w[...])
            gate_low[spot] = (hidden_grad * gate_low[spot].astype(F32)).astype(BF16)
            up_low[spot] = (hidden_grad * up_low[spot].astype(F32)).astype(BF16)
            terms[spot] = (nt(gate_low[spot], gate_w[...]) + nt(up_low[spot], up_w[...])).astype(
                BF16
            )

        def passed(k, ready=None, go=None):
            def act():
                sums.pass_over(k)
                if ready is not None:
                    sums.combine(ready)
                    go()

            return act

        loads[2].wait()
        staged(4, back, None, {
            0: passed(2),
            1: passed(-1, 2, sums.start_far),
            2: passed(1, -1, sums.start_left),
            3: passed(0, 1, sums.start_right),
        })
        def down_grad(n):
            columns = own_half(256, n)
            down_g[columns] = tn(hidden[:, columns], upstream[...]).astype(BF16)

        staged(3, down_grad, None, {2: lambda: (sums.combine(0), sums.forward())})
        stores = [net.local(lambda: (down_g, down_grad_))]

        def weight_grad(low, target):
            def one(n):
                columns = own_half(256, n)
                target[columns] = tn(second[:, columns], low[...]).astype(BF16)

            return one

        staged(8, weight_grad(gate_low, gate_g))
        stores.append(net.local(lambda: (gate_g, gate_grad_)))
        gain_parts = []

        def keep(spot, value):
            through, gain_part = norm_back(residual_[spot], gain, value)
            through = through + cotangent_[spot].astype(F32)
            back_[spot] = through
            low_[spot] = through.astype(BF16)
            gain_parts.append(jnp.sum(gain_part, axis=0, keepdims=True))

        def through(n):
            spot = units.rows(n)
            mlp[spot] = nn(hidden[spot], down_w[...]).astype(BF16)

        staged(4, through)
        stores.append(net.local(lambda: (mlp, mlp_)))
        staged(8, weight_grad(up_low, up_g))
        stores.append(net.local(lambda: (up_g, up_grad_)))
        sums.finish(keep)
        gain_grad_[...] = gain_parts[0] + gain_parts[1]
        for store in stores:
            store.wait()

    plans = (RowsGather, RowsSum, PlaneGather)
    return Kernel(1, plans, 0, 0, 3 + 4, CORE_PARTNER + X_PARTNERS + PLANE_PARTNERS)(
        body,
        [
            (residual, VMEM), (cotangent, VMEM), (gains, VMEM),
            (cotangent_all, HBM), (gate, HBM), (up, HBM), (down, VMEM),
        ],
        [
            (shape((128, 2048), F32), VMEM),
            (shape((128, 2048)), VMEM),
            (shape((1, 2048), F32), VMEM),
            (shape((1024, 2048)), HBM),
            (shape((2048, 768)), HBM),
            (shape((2048, 768)), HBM),
            (shape((768, 2048)), HBM),
        ],
        (
            pltpu.VMEM((128, 2048), BF16),
            pltpu.VMEM((1024, 2048), BF16),
            pltpu.VMEM((1024, 2048), BF16),
            pltpu.VMEM((2048, 768), BF16),
            pltpu.VMEM((2048, 768), BF16),
            pltpu.VMEM((768, 2048), BF16),
            pltpu.VMEM((1024, 768), BF16),
            pltpu.VMEM((1024, 768), BF16),
            pltpu.VMEM((1024, 768), BF16),
            pltpu.VMEM((1024, 2048), BF16),
            pltpu.VMEM((1024, 2048), BF16),
            pltpu.VMEM((2048, 768), BF16),
            pltpu.VMEM((2048, 768), BF16),
            pltpu.VMEM((768, 2048), BF16),
        )
        + ROWS_SCRATCH,
    )


def attention_backward(
    low, back, residual, tokens, gains, second_gain, heads, raw, attended, totals, cosine, sine,
    lengths, qkv, output, normed, mlp, gate, up, down,
):
    def body(net, ins, outs, work):
        (
            low_, back_, residual_, tokens_, gains_, second_gain_, heads_, raw_, attended_, totals_,
            cosine_, sine_, lengths_, qkv_, output_, normed_, mlp_, gate_, up_, down_,
        ) = ins
        (
            block_own, input_own, qkv_own, output_own, gate_own, up_own, down_own, gains_own,
        ) = outs
        (
            rows, terms, qkv_w, output_w, gate_g, up_g, down_g, qkv_g, output_g,
            attended_rows, attended_grad, key_sum, value_sum, parts,
            block_out, input_out, qkv_total, output_total, gate_total, up_total, down_total,
            gain_rows, gain_land,
            mlp_landed, mlp_land, first_landed, first_land,
            gate_land, gate_last, up_land, up_last, down_land, down_last,
            qkv_land, qkv_last, output_land, output_last,
        ) = work
        place = net.place
        units = Units(place)
        mine, theirs = place.core, 1 - place.core
        loads = {
            name: net.local(lambda source=source, target=target: (source, target))
            for name, source, target in (
                ("gate", gate_, gate_g), ("up", up_, up_g), ("output", output_, output_w),
                ("down", down_, down_g), ("mlp", mlp_, terms), ("qkv", qkv_, qkv_w),
            )
        }
        gather = RowsGather(net, low_, rows)
        gate_sum = PlaneSum(net, gate_g, gateup_spot, gate_land, gate_last)
        up_sum = PlaneSum(net, up_g, gateup_spot, up_land, up_last)
        down_sum = PlaneSum(net, down_g, down_spot, down_land, down_last)
        qkv_sum = PlaneSum(net, qkv_g, rows_spot, qkv_land, qkv_last)
        output_sum = PlaneSum(net, output_g, output_spot, output_land, output_last)
        mlp_sum = RowsSum(net, terms, mlp_landed, mlp_land)
        first_sum = RowsSum(net, terms, first_landed, first_land)

        def same_order(n):
            for core in range(2):
                start = pl.multiple_of(units.chip(n) * 256 + core * 128, 128)
                attended_rows[pl.ds(start, 128)] = attended_[units.true_rows(n, core)]

        staged(4, same_order)
        key_sum[...] = jnp.zeros_like(key_sum)
        value_sum[...] = jnp.zeros_like(value_sum)
        net.enter()
        gather.start()
        loads["gate"].wait()
        gate_sum.start()
        loads["up"].wait()
        up_sum.start()
        loads["output"].wait()

        halves = []

        def exchange(cut, there):
            halves.append(net.local(lambda: (cut(mine), there(mine))))
            halves.append(
                Give(net, lambda: (cut(theirs), there(mine)), lambda: there(theirs))
            )

        def enter(n):
            grad = nt(rows[units.rows(n)], output_w[...]).astype(BF16)
            for core in range(2):
                attended_grad[units.true_rows(n, core)] = grad[core * 128 : core * 128 + 128]

        def near():
            loads["down"].wait()
            down_sum.start()
            loads["mlp"].wait()
            for k in (2, 1, -1, 0):
                mlp_sum.pass_over(k)
            gather.near_first()
            gather.near_second()
            for k in (2, 1, -1, 0):
                mlp_sum.combine(k)
            gather.here(1)

        def far():
            gather.far()
            mlp_sum.start_far()
            mlp_sum.start_right()
            mlp_sum.start_left()
            gather.here(2)

        staged(4, enter, {0: lambda: gather.here(0), 1: near, 2: lambda: gather.here(-1), 3: far})

        def output_grad(n):
            columns = own_half(512, n)
            output_g[:, columns] = tn(attended_rows[...], rows[:, columns]).astype(BF16)

        staged(4, output_grad)
        output_sum.start()
        gate_sum.forward()
        gather.gone()
        loads["normed"] = net.local(lambda: (normed_, rows))

        documents = Documents(lengths_[...])
        gain_query, gain_key = gains_[0:1, 4096:4224], gains_[0:1, 4224:4352]

        def through_rope(value, spot, raw_part, gain):
            value = value * cosine_[spot] + pltpu.roll(value * sine_[spot], 64, 1)
            through, gain_part = norm_back(raw_part, gain, value)
            return through.astype(BF16), jnp.sum(gain_part, axis=0, keepdims=True)

        def attend(block, gain_sum):
            keys = 256 * (block + 1)
            spot = slice(block * 256, block * 256 + 256)

            def one(head, gain_sum):
                columns = own_half(128, head)
                query, upstream = heads_[spot, columns], attended_grad[spot, columns]
                key, value = heads_[0:keys, 256:384], heads_[0:keys, 384:512]
                scores = nt(query, key) * SCALE
                total = totals_[spot, columns][:, 0:1]
                allowed = allowed_pairs(documents, block * 256, 256, keys)
                probability = jnp.where(allowed, jnp.exp(scores - total), 0.0)
                prob_grad = nt(upstream, value)
                centre = jnp.sum(probability * prob_grad, axis=-1, keepdims=True)
                score_grad = (probability * (prob_grad - centre)).astype(BF16)
                value_sum[0:keys] += tn(probability.astype(BF16), upstream)
                key_sum[0:keys] += tn(score_grad, query)
                query_grad = nn(score_grad, key) * SCALE
                through, gain_part = through_rope(query_grad, spot, raw_[spot, columns], gain_query)
                for n in range(2):
                    true = block * 2 + n
                    start = ((true % RING) * 2 + true // RING) * 128
                    parts[start : start + 128, columns] = through[n * 128 : n * 128 + 128]
                return gain_sum + gain_part

            return lax.fori_loop(0, 2, one, gain_sum)

        query_gain = attend(3, jnp.zeros((1, 128), F32))
        up_sum.forward()
        mlp_sum.forward()
        query_gain = attend(2, query_gain)
        down_sum.forward()
        query_gain = attend(1, query_gain)
        query_gain = attend(0, query_gain)
        gate_sum.gather()

        def keep_block(spot, value):
            block_out[spot] = (residual_[spot] + value).astype(BF16)

        def key_back(true, gain_sum):
            spot = pl.ds(pl.multiple_of(true * 128, 128), 128)
            start = (lax.rem(true, RING) * 2 + lax.div(true, RING)) * 128
            through, gain_part = through_rope(
                key_sum[spot] * SCALE, spot, raw_[spot, 256:384], gain_key
            )
            here = pl.ds(pl.multiple_of(start, 128), 128)
            parts[here, 256:384] = through
            parts[here, 384:512] = value_sum[spot].astype(BF16)
            return gain_sum + gain_part

        key_gain = lax.fori_loop(0, 8, key_back, jnp.zeros((1, 128), F32))
        mlp_sum.passed()
        loads["qkv"].wait()

        def out(n):
            spot = units.rows(3 - n)
            terms[spot] = nt(parts[spot], qkv_w[...]).astype(BF16)

        def passed(k, ready=None, go=None):
            def act():
                first_sum.pass_over(k)
                if ready is not None:
                    first_sum.combine(ready)
                    go()

            return act

        staged(4, out, None, {
            0: passed(2),
            1: passed(-1, 2, first_sum.start_far),
            2: passed(1, -1, first_sum.start_left),
            3: passed(0, 1, first_sum.start_right),
        })
        loads["normed"].wait()

        def qkv_grad(n):
            columns = own_half(256, n)
            qkv_g[columns] = tn(rows[:, columns], parts[...]).astype(BF16)

        staged(8, qkv_grad, None, {3: lambda: (first_sum.combine(0), first_sum.forward())})
        qkv_sum.start()
        up_sum.gather()
        output_sum.forward()
        down_sum.gather()
        mlp_sum.finish(keep_block)
        block_turn = Turn(net, parts_of(block_out, block_own, 2))
        block_turn.start()
        gate_sum.finish(gate_total)
        output_sum.gather()
        qkv_sum.forward()
        up_sum.finish(up_total)
        for source, target in ((gate_total, gate_own), (up_total, up_own)):
            exchange(
                lambda core, source=source: source.at[own_half(128, core)],
                lambda core, target=target: target.at[:, own_half(384, core)],
            )

        gain_parts = []
        turns = []

        def keep_first(spot, value):
            rows_in = tokens_[spot].astype(F32)
            through, gain_part = norm_back(rows_in, gains_[0:1, 0:2048], value)
            input_out[spot] = (back_[spot] + through).astype(BF16)
            gain_parts.append(jnp.sum(gain_part, axis=0, keepdims=True))
            turns.append(Turn(net, [(input_out.at[spot], input_own.at[spot])]))
            turns[-1].start()

        first_sum.finish(keep_first)
        flat = jnp.concatenate(
            [gain_parts[0] + gain_parts[1], second_gain_[...], query_gain, key_gain], axis=1
        )
        entry = lax.broadcasted_iota(jnp.int32, (128, GAINS), 1)
        past = entry - owner_starts((128, GAINS), 0)
        owned = jnp.where((past >= 0) & (past < OWN_GAINS), flat, 0.0)
        column = (column_of(entry) == lax.broadcasted_iota(jnp.int32, (128, GAINS), 0)).astype(F32)
        gain_rows[...] = lax.dot_general(
            owned, column, (((1,), (1,)), ((), ())),
            precision=lax.Precision.HIGHEST, preferred_element_type=F32,
        ).reshape(128, 1, 128)
        gains_steps = GainsSum(net, gain_rows, gains_own, gain_land).steps()
        next(gains_steps)
        down_sum.finish(down_total)
        exchange(
            lambda core: down_total.at[:, own_half(128, core)],
            lambda core: down_own.at[own_half(384, core)],
        )
        output_sum.finish(output_total)
        output_turn = Turn(net, [(output_total, output_own)])
        output_turn.start()
        next(gains_steps)
        qkv_sum.gather()
        next(gains_steps)
        next(gains_steps)
        qkv_sum.finish(qkv_total)
        qkv_turn = Turn(net, [(qkv_total, qkv_own)])
        qkv_turn.start()
        next(gains_steps)
        for copy in halves:
            copy.wait()
        for turn in (block_turn, output_turn, *turns, qkv_turn):
            turn.wait()

    plans = (RowsGather,) + 2 * (RowsSum,) + 5 * (PlaneSum,) + (GainsSum,)
    return Kernel(
        2, plans, 3, 6, 7 + 3 - 1, CORE_PARTNER + X_PARTNERS + FAR_X + PLANE_PARTNERS + TURN_PARTNERS
    )(
        body,
        [
            (low, VMEM), (back, VMEM), (residual, VMEM), (tokens, VMEM), (gains, VMEM),
            (second_gain, VMEM), (heads, VMEM), (raw, VMEM), (attended, VMEM), (totals, VMEM),
            (cosine, VMEM), (sine, VMEM), (lengths, VMEM), (qkv, HBM),
            (output, HBM), (normed, HBM), (mlp, HBM), (gate, HBM), (up, HBM), (down, HBM),
        ],
        [
            (shape((128, 2048)), VMEM),
            (shape((128, 2048)), VMEM),
            (shape((128, 512)), VMEM),
            (shape((256, 128)), VMEM),
            (shape((128, 768)), VMEM),
            (shape((128, 768)), VMEM),
            (shape((768, 128)), VMEM),
            (shape((1, 1, 128), F32), VMEM),
        ],
        (
            pltpu.VMEM((1024, 2048), BF16),
            pltpu.VMEM((1024, 2048), BF16),
            pltpu.VMEM((2048, 512), BF16),
            pltpu.VMEM((256, 2048), BF16),
            pltpu.VMEM((2048, 768), BF16),
            pltpu.VMEM((2048, 768), BF16),
            pltpu.VMEM((768, 2048), BF16),
            pltpu.VMEM((2048, 512), BF16),
            pltpu.VMEM((256, 2048), BF16),
            pltpu.VMEM((1024, 256), BF16),
            pltpu.VMEM((1024, 256), BF16),
            pltpu.VMEM((1024, 128), F32),
            pltpu.VMEM((1024, 128), F32),
            pltpu.VMEM((1024, 512), BF16),
            pltpu.VMEM((128, 2048), BF16),
            pltpu.VMEM((128, 2048), BF16),
            pltpu.VMEM((128, 512), BF16),
            pltpu.VMEM((256, 128), BF16),
            pltpu.VMEM((256, 384), BF16),
            pltpu.VMEM((256, 384), BF16),
            pltpu.VMEM((384, 256), BF16),
            pltpu.VMEM((128, 1, 128), F32),
            pltpu.VMEM((127, 1, 128), F32),
        )
        + ROWS_SCRATCH * 2
        + plane_scratch(256, 384) * 2
        + plane_scratch(384, 256)
        + plane_scratch(128, 512)
        + plane_scratch(256, 128),
    )


def step_rates(total_tokens):
    root_tokens = math.sqrt(total_tokens)
    narrow = MODEL_WIDTH ** (-0.5)
    return (
        narrow / (2.0 * root_tokens),
        narrow / (2.0 * root_tokens),
        (QUERY_HEADS * HEAD_SIZE // 128) ** (-0.5) / (0.24 * root_tokens),
        narrow / (0.7 * root_tokens),
        FF ** (-0.5) / (1.2 * root_tokens),
        0.025 / root_tokens,
    )


def update(rows, gradients, state):
    rates = step_rates(GROUP_TOK * 16)

    def kernel(*refs):
        block_, input_, qkv_, output_, gate_, up_, down_, gains_ = refs[:8]
        masters, moments, averages = refs[8:14], refs[14:20], refs[20:26]
        outs = refs[26:]
        outs[0][...] = block_[...]
        outs[1][...] = input_[...]

        def one(n, gradient, spot):
            gradient = gradient.astype(F32)
            moment = MOMENTUM * moments[n][spot] + gradient
            master = masters[n][spot] - rates[n] * (gradient + MOMENTUM * moment)
            outs[2 + n][spot] = master
            outs[8 + n][spot] = moment
            outs[14 + n][spot] = AVERAGING * averages[n][spot] + (1.0 - AVERAGING) * master

        one(0, qkv_[:, 0:256], ...)
        one(1, qkv_[:, 256:384], 0)
        one(1, qkv_[:, 384:512], 1)
        one(2, output_[...], ...)
        one(3, gate_[...], 0)
        one(3, up_[...], 1)
        one(4, down_[...], ...)
        one(5, gains_[0, 0:1, 0:OWN_GAINS], ...)

    outs = [shape(a.shape, a.dtype) for a in rows]
    outs += [shape(a.shape, F32) for a in state]
    arrays = (*rows, *gradients, *state)
    return pl.pallas_call(
        kernel,
        out_shape=outs,
        in_specs=[pl.BlockSpec(memory_space=VMEM)] * len(arrays),
        out_specs=[pl.BlockSpec(memory_space=VMEM)] * len(outs),
        compiler_params=pltpu.CompilerParams(vmem_limit_bytes=61 * 2**20),
        name="update",
    )(*arrays)


def body(tokens, cotangent, doc_lengths, *state):
    query_weight, key_value_weight, output_weight, gateup_weight, down_weight, norm_gains = state[:6]
    cosine, sine = rope_tables()
    (
        residual, tokens_here, cotangent_here, normed, raw, heads, attended, totals,
        cosine, sine, qkv, output, gate, up, down_piece, cotangent_all, gains, lengths,
    ) = attention_forward(
        tokens, cotangent, query_weight, key_value_weight, output_weight, gateup_weight,
        down_weight, norm_gains.reshape(1, OWN_GAINS), doc_lengths,
        jnp.asarray(cosine), jnp.asarray(sine),
    )
    back, low, second_gain, mlp, gate_grad, up_grad, down_grad = feed_forward(
        residual, cotangent_here, gains, cotangent_all, gate, up, down_piece
    )
    block_out, input_grad, *gradients = attention_backward(
        low, back, residual, tokens_here, gains, second_gain, heads, raw, attended, totals,
        cosine, sine, lengths, qkv, output, normed, mlp, gate_grad, up_grad, down_grad,
    )
    state = [a.reshape(1, OWN_GAINS) if a.ndim == 1 else a for a in state]
    outs = update((block_out, input_grad), gradients, state)
    return tuple(a.reshape(OWN_GAINS) if a.shape == (1, OWN_GAINS) else a for a in outs)


def solution(mesh):
    parted = Mesh(mesh.devices.reshape(GRID), AXES)
    data = ("z", "ylo", "core")
    tensor = ("yhi", "x")
    rows = P(AXES, None)
    by_rows = P(data, tensor)
    pair = P(None, data, tensor)
    by_columns = P(tensor, data)
    flat = P(AXES)
    weights = (by_rows, pair, by_columns, pair, by_columns, flat)
    return jax.shard_map(
        body,
        mesh=parted,
        in_specs=(rows, rows, P(data, None)) + weights * 3,
        out_specs=(rows, rows) + weights * 3,
        check_vma=False,
    )
```

```python
import math

import jax
import jax.numpy as jnp
import numpy as np
from jax import lax
from jax.experimental import pallas as pl
from jax.experimental.pallas import tpu as pltpu
from jax.sharding import Mesh
from jax.sharding import PartitionSpec as P

MODEL_WIDTH = 2048
QUERY_HEADS = 16
HEAD_SIZE = 128
FF = 6144
GROUP_TOK = 1024
GAINS = 4352
OWN_GAINS = 34
EPSILON = 1e-06
MOMENTUM = 0.9
AVERAGING = 0.5
ROPE_BASE = 1000000.0
SCALE = HEAD_SIZE ** (-0.5)

AXES = ("z", "ylo", "core", "yhi", "x")
GRID = (4, 2, 2, 2, 4)
RING = 4
BF16 = jnp.bfloat16
F32 = jnp.float32
HBM = pl.ANY
VMEM = pltpu.VMEM


class Place:
    def __init__(self):
        self.x = lax.axis_index("x")
        self.z = lax.axis_index("z")
        self.core = lax.axis_index("core")
        self.yhi = lax.axis_index("yhi")
        self.ylo = lax.axis_index("ylo")
        self.y = self.yhi * 2 + self.ylo
        self.native = self.core == self.yhi
        at = {"x": self.x, "y": self.y, "z": self.z}
        self.steps = {
            (axis, by): lax.rem(here + by, RING) if by else here
            for axis, here in at.items()
            for by in range(RING)
        }
        self.devices = {
            "core": {"core": 1 - self.core},
            "turn": {"core": 1 - self.core, "yhi": 1 - self.yhi},
        }
        for (axis, by), there in self.steps.items():
            self.devices[axis, by] = (
                {"yhi": lax.div(there, 2), "ylo": lax.rem(there, 2)}
                if axis == "y"
                else {axis: there}
            )

    def step(self, axis, by):
        return self.steps[axis, by % RING]

    def device(self, axis, by=1):
        return self.devices[axis] if axis in ("core", "turn") else self.devices[axis, by % RING]


class Local:
    def __init__(self, refs, sems, index):
        self.refs, self.sems, self.index = refs, sems, index

    def copy(self):
        source, target = self.refs()
        return pltpu.make_async_copy(source, target, self.sems.at[self.index])

    def start(self):
        self.copy().start()

    def wait(self):
        self.copy().wait()


class Net:
    def __init__(self, place, partners, send_sems, recv_sems, local_sems):
        self.place, self.partners = place, partners
        self.send_sems, self.recv_sems, self.local_sems = send_sems, recv_sems, local_sems
        self.leaving, self.arriving, self.local_count = 0, 0, 0
        self.waits = []

    def greet(self):
        barrier = pltpu.get_barrier_semaphore()
        for axis, by in self.partners:
            pl.semaphore_signal(
                barrier,
                inc=1,
                device_id=self.place.device(axis, by),
                device_id_type=pl.DeviceIdType.MESH,
            )

    def enter(self):
        pl.semaphore_wait(pltpu.get_barrier_semaphore(), len(self.partners))

    def out(self):
        self.leaving += 1
        return self.leaving - 1

    def into(self):
        self.arriving += 1
        return self.arriving - 1

    def local_number(self):
        self.local_count += 1
        return self.local_count - 1

    def copy(self, source, target, out, into, axis="core", by=1):
        return pltpu.make_async_remote_copy(
            src_ref=source,
            dst_ref=target,
            send_sem=self.send_sems.at[out],
            recv_sem=self.recv_sems.at[into],
            device_id=self.place.device(axis, by),
            device_id_type=pl.DeviceIdType.MESH,
        )

    def send(self, refs, out, into, axis, by=1):
        self.copy(*refs(), out, into, axis, by).start()

    def here(self, into, view):
        self.copy(view, view, 0, into).wait_recv()

    def gone(self, out, view):
        self.copy(view, view, out, 0).wait_send()

    def later(self, wait):
        self.waits.append(wait)

    def finish(self):
        for wait in self.waits:
            wait()

    def local(self, refs):
        copy = Local(refs, self.local_sems, self.local_number())
        copy.start()
        return copy


def at_step(acts, n):
    for at, act in (acts or {}).items():

        @pl.when(n == at)
        def _():
            act()


def staged(count, compute, before=None, after=None):
    def step(n, carry):
        at_step(before, n)
        compute(n)
        at_step(after, n)
        return carry

    lax.fori_loop(0, count, step, 0)


class RowsGather:
    OUT, INTO, LOCALS = 1, 7, 2

    def __init__(self, net, own, whole):
        self.net, self.own, self.whole = net, own, whole
        self.rows = own.shape[0]
        self.half = self.rows // 2
        place = net.place
        self.me, self.other = place.core, 1 - place.core
        self.spots = {k: place.step("x", k) for k in (0, 1, -1, 2)}
        self.out = net.out()
        self.first, self.second, self.third = net.into(), net.into(), net.into()
        self.shared = {k: net.into() for k in (0, 1, -1, 2)}
        self.kept = []
        net.later(self.gone)

    def block(self, core, k, part):
        start = (self.spots[k] * 2 + core) * self.rows + part * self.half
        return self.whole.at[pl.ds(pl.multiple_of(start, self.half), self.half)]

    def mine(self, k, part):
        return self.block(self.me, k, part)

    def piece(self, part):
        return self.own.at[pl.ds(part * self.half, self.half)]

    def share(self, k, part):
        refs = lambda: (self.piece(part) if k == 0 else self.mine(k, part), self.mine(k, part))
        self.net.send(refs, self.out, self.shared[k], "core")

    def both(self):
        return self.whole.at[pl.ds(0, self.rows)]

    def start(self, parts=(0, 1)):
        for part in parts:
            refs = lambda part=part: (self.piece(part), self.mine(0, part))
            first, second = (1, -1) if part == 0 else (-1, 1)
            self.net.send(refs, self.out, self.first, "x", first)
            self.net.send(refs, self.out, self.second, "x", second)
            self.share(0, part)
            self.kept.append(self.net.local(refs))

    def near_first(self):
        self.net.here(self.first, self.both())
        self.net.send(lambda: (self.mine(-1, 0),) * 2, self.out, self.third, "x", 1)
        self.net.send(lambda: (self.mine(1, 1),) * 2, self.out, self.third, "x", -1)
        self.share(-1, 0)
        self.share(1, 1)

    def near_second(self):
        self.net.here(self.second, self.both())
        self.share(-1, 1)
        self.share(1, 0)

    def far(self):
        self.net.here(self.third, self.both())
        self.share(2, 0)
        self.share(2, 1)

    def here(self, k):
        if k == 0:
            for copy in self.kept:
                copy.wait()
        self.net.here(self.shared[k], self.both())

    def gone(self):
        if self.out is not None:
            self.net.gone(self.out, self.whole.at[pl.ds(0, 7 * self.rows)])
            self.out = None


class RowsSum:
    OUT, INTO = 2, 6

    def __init__(self, net, whole, landed, land):
        self.net, self.whole, self.landed, self.land = net, whole, landed, land
        self.half = landed.shape[2]
        place = net.place
        self.me, self.other = place.core, 1 - place.core
        self.spots = {k: place.step("x", k) for k in (0, 1, -1, 2)}
        self.over, self.along = net.out(), net.out()
        self.given = {k: net.into() for k in (0, 1, -1, 2)}
        self.through, self.last = net.into(), net.into()
        net.later(self.passed)
        net.later(self.departed)

    def block(self, core, k, part):
        start = ((self.spots[k] * 2 + core) * 2 + part) * self.half
        return self.whole.at[pl.ds(pl.multiple_of(start, self.half), self.half)]

    def own(self, k, part):
        return self.landed.at[k % RING, part]

    def pass_over(self, k):
        for part in range(2):
            refs = lambda part=part: (self.block(self.other, k, part), self.own(k, part))
            self.net.send(refs, self.over, self.given[k], "core")

    def passed(self):
        if self.over is not None:
            self.net.gone(self.over, self.landed)
            self.over = None

    def departed(self):
        if self.along is not None:
            self.net.gone(self.along, self.land)
            self.along = None

    def combine(self, k):
        self.net.here(self.given[k], self.landed.at[k % RING])
        for part in range(2):
            here = self.own(k, part)
            here[...] = here[...] + self.block(self.me, k, part)[...]

    def along_x(self, refs, into, by):
        self.net.send(refs, self.along, into, "x", by)

    def start_far(self):
        self.along_x(lambda: (self.own(2, 0), self.land.at[0]), self.through, 1)
        self.along_x(lambda: (self.own(2, 1), self.land.at[1]), self.through, -1)

    def start_right(self):
        self.along_x(lambda: (self.own(1, 1), self.land.at[3]), self.last, 1)

    def start_left(self):
        self.along_x(lambda: (self.own(-1, 0), self.land.at[4]), self.last, -1)

    def forward(self):
        land = self.land
        self.net.here(self.through, land.at[pl.ds(0, 2)])
        land[0] = land[0] + self.own(1, 0)[...]
        self.along_x(lambda: (land.at[0], land.at[2]), self.last, 1)
        land[1] = land[1] + self.own(-1, 1)[...]
        self.along_x(lambda: (land.at[1], land.at[5]), self.last, -1)

    def finish(self, keep):
        land = self.land
        self.net.here(self.last, land.at[pl.ds(2, 4)])
        for part in range(2):
            total = self.own(0, part)[...].astype(F32) + land[2 + part].astype(F32)
            keep(pl.ds(part * self.half, self.half), total + land[4 + part].astype(F32))


ROWS_SCRATCH = (pltpu.VMEM((4, 2, 64, 2048), BF16), pltpu.VMEM((6, 64, 2048), BF16))


class PlaneGather:
    OUT, INTO, LOCALS = 1, 12, 1

    def __init__(self, net, own, whole, spot):
        self.net, self.own, self.whole, self.spot = net, own, whole, spot
        self.rows = own.shape[0]
        self.half = self.rows // 2
        self.width = own.shape[1]
        self.out = net.out()
        self.first = [net.into() for _ in range(2)]
        self.rings = {(color, i): net.into() for color in range(2) for i in (0, 1, -1, -2)}
        self.last = [net.into() for _ in range(2)]
        net.later(self.gone)

    def gone(self):
        if self.out is not None:
            rows = self.whole.shape[0] // 16 * 15
            self.net.gone(self.out, self.whole.at[pl.ds(0, rows)])
            self.out = None

    def view(self, color, i, j, part=None):
        place = self.net.place
        first, second = self.axes(color)
        a, b = place.step(first, i), place.step(second, j)
        row, columns = self.spot(a, b) if color == 0 else self.spot(b, a)
        start = row + color * self.half
        if part is None:
            return self.whole.at[pl.ds(pl.multiple_of(start, self.half), self.half), columns]
        size = self.half // 2
        return self.whole.at[pl.ds(pl.multiple_of(start + part * size, size), size), columns]

    def bytes_of(self, halves):
        return self.whole.at[pl.ds(0, halves * self.half), pl.ds(0, self.width)]

    @staticmethod
    def axes(color):
        return ("z", "y") if color == 0 else ("y", "z")

    def mine(self, color):
        return self.own.at[pl.ds(color * self.half, self.half)]

    def ring(self, color, i):
        axis = self.axes(color)[1]
        refs = lambda: (
            self.mine(color) if i == 0 else self.view(color, i, 0), self.view(color, i, 0)
        )
        for by in (1, -1):
            self.net.send(refs, self.out, self.rings[color, i], axis, by)

    def start(self):
        for color in range(2):
            axis = self.axes(color)[0]
            refs = lambda color=color: (self.mine(color), self.view(color, 0, 0))
            for by in (1, -1, 2):
                self.net.send(refs, self.out, self.first[color], axis, by)
        for color in range(2):
            self.ring(color, 0)
        self.kept = self.net.local(self.place_here)

    def place_here(self):
        row, columns = self.spot(self.net.place.z, self.net.place.y)
        return self.own, self.whole.at[pl.ds(pl.multiple_of(row, self.rows), self.rows), columns]

    def spread(self):
        for color in range(2):
            self.net.here(self.first[color], self.bytes_of(3) if self.fits(3) else self.thin(3))
        for i in (-1, 1, -2):
            for color in range(2):
                self.ring(color, i)

    def fits(self, halves):
        return halves * self.half <= self.whole.shape[0]

    def thin(self, halves):
        return self.whole.at[pl.ds(0, self.half), pl.ds(0, halves * self.width)]

    def forward(self, steps=(0, 1, -1, -2)):
        for i in steps:
            for color in range(2):
                axis = self.axes(color)[1]
                self.net.here(self.rings[color, i], self.bytes_of(2))
                for j, part, by in ((-1, 0, 1), (1, 1, -1)):
                    refs = lambda color=color, i=i, j=j, part=part: (
                        self.view(color, i, j, part),
                    ) * 2
                    self.net.send(refs, self.out, self.last[color], axis, by)

    def here(self):
        for color in range(2):
            self.net.here(self.last[color], self.bytes_of(4) if self.fits(4) else self.thin(4))
        self.kept.wait()


class PlaneSum:
    OUT, INTO = 2, 18

    def __init__(self, net, whole, spot, land, last):
        self.net, self.whole, self.spot, self.land, self.last = net, whole, spot, land, last
        self.size = land.shape[3]
        self.ring_out, self.last_out = net.out(), net.out()
        ways = [(color, k) for color in range(2) for k in range(RING)]
        self.through = {way: net.into() for way in ways}
        self.sides = {way: net.into() for way in ways}
        self.ends = [net.into() for _ in range(2)]
        net.later(lambda: net.gone(self.ring_out, land))
        net.later(lambda: net.gone(self.last_out, last))

    @staticmethod
    def axes(color):
        return ("y", "z") if color == 0 else ("z", "y")

    def own(self, color, n, k, part):
        place = self.net.place
        first, second = self.axes(color)
        a, b = place.step(first, n), place.step(second, k)
        row, columns = self.spot(b, a) if color == 0 else self.spot(a, b)
        start = row + (color * 2 + part) * self.size
        return self.whole.at[pl.ds(pl.multiple_of(start, self.size), self.size), columns]

    def slot(self, color, k, n):
        return self.land.at[color, k % RING, n]

    def end(self, color, k, part):
        return self.last.at[color, k % RING - 1, part]

    def start(self):
        for k in (2, 1, -1, 0):
            for color in range(2):
                axis = self.axes(color)[0]
                through, sides = self.through[color, k % RING], self.sides[color, k % RING]
                for n, part, slot, into, by in (
                    (2, 0, 0, through, 1), (2, 1, 1, through, -1),
                    (1, 1, 3, sides, 1), (-1, 0, 4, sides, -1),
                ):
                    refs = lambda color=color, k=k, n=n, part=part, slot=slot: (
                        self.own(color, n, k, part), self.slot(color, k, slot)
                    )
                    self.net.send(refs, self.ring_out, into, axis, by)

    def forward(self, steps=(2, 1, -1, 0)):
        for k in steps:
            for color in range(2):
                axis = self.axes(color)[0]
                sides = self.sides[color, k % RING]
                self.net.here(
                    self.through[color, k % RING], self.land.at[color, k % RING, pl.ds(0, 2)]
                )
                for slot, n, part, target, by in ((0, 1, 0, 2, 1), (1, -1, 1, 5, -1)):
                    here = self.slot(color, k, slot)
                    here[...] = here[...] + self.own(color, n, k, part)[...]
                    refs = lambda color=color, k=k, slot=slot, target=target: (
                        self.slot(color, k, slot), self.slot(color, k, target)
                    )
                    self.net.send(refs, self.ring_out, sides, axis, by)

    def gather(self, steps=(2, 1, -1, 0)):
        for k in steps:
            for color in range(2):
                second = self.axes(color)[1]
                self.net.here(
                    self.sides[color, k % RING], self.land.at[color, k % RING, pl.ds(2, 4)]
                )
                for part in range(2):
                    here = self.slot(color, k, 2 + part)
                    total = self.own(color, 0, k, part)[...].astype(F32) + here[...].astype(F32)
                    total = total + self.slot(color, k, 4 + part)[...].astype(F32)
                    here[...] = total.astype(BF16)
                    if k != 0:
                        refs = lambda color=color, k=k, part=part: (
                            self.slot(color, k, 2 + part), self.end(color, k, part)
                        )
                        self.net.send(refs, self.last_out, self.ends[color], second, k)

    def finish(self, total):
        for color in range(2):
            self.net.here(self.ends[color], self.last.at[color])
            for part in range(2):
                value = self.slot(color, 0, 2 + part)[...].astype(F32)
                for k in (1, -1, 2):
                    value = value + self.end(color, k, part)[...].astype(F32)
                start = (color * 2 + part) * self.size
                total[pl.ds(start, self.size)] = value.astype(total.dtype)


def plane_scratch(rows, columns):
    return (
        pltpu.VMEM((2, 4, 6, rows // 4, columns), BF16),
        pltpu.VMEM((2, 3, 2, rows // 4, columns), BF16),
    )


class Turn:
    def __init__(self, net, pairs):
        self.net = net
        self.pairs = [
            (source, target, net.out(), net.into(), net.local_number()) for source, target in pairs
        ]

    def copies(self):
        return [self.net.copy(a, b, out, into, "turn") for a, b, out, into, _ in self.pairs]

    def kept(self):
        sems = self.net.local_sems
        return [pltpu.make_async_copy(a, b, sems.at[index]) for a, b, _, _, index in self.pairs]

    def both(self, act):
        @pl.when(jnp.logical_not(self.net.place.native))
        def _():
            for copy in self.copies():
                act(copy)

        @pl.when(self.net.place.native)
        def _():
            for copy in self.kept():
                act(copy)

    def start(self):
        self.both(lambda copy: copy.start())

    def wait(self):
        self.both(lambda copy: copy.wait())


class Give:
    def __init__(self, net, refs, there):
        self.net, self.there = net, there
        self.out, self.into = net.out(), net.into()
        net.send(refs, self.out, self.into, "core")
        net.later(lambda: net.gone(self.out, refs()[0]))

    def wait(self):
        self.net.here(self.into, self.there())


def parts_of(source, target, count):
    rows = source.shape[0] // count
    spots = [pl.ds(part * rows, rows) for part in range(count)]
    return [(source.at[spot], target.at[spot]) for spot in spots]


class GainsGather:
    OUT, INTO, LOCALS = 1, 4, 1

    def __init__(self, net, own, whole):
        self.net, self.own, self.whole = net, own, whole
        self.out = net.out()
        self.into = [net.into() for _ in range(4)]
        net.later(lambda: net.gone(self.out, whole.at[pl.ds(0, 127)]))

    def rows(self, z, y, x, core, count):
        start = ((z * RING + y) * RING + x) * 2 + core
        return self.whole.at[pl.ds(start if count == 1 else pl.multiple_of(start, count), count)]

    def spot(self, axis, by):
        place = self.net.place
        if axis == "core":
            return self.rows(place.z, place.y, place.x, (place.core + by) % 2, 1)
        if axis == "x":
            return self.rows(place.z, place.y, place.step("x", by), 0, 2)
        if axis == "y":
            return self.rows(place.z, place.step("y", by), 0, 0, 8)
        return self.rows(place.step("z", by), 0, 0, 0, 32)

    def steps(self):
        net = self.net
        net.local(lambda: (self.own, self.spot("core", 0))).wait()
        for into, axis, count in zip(self.into, ("core", "x", "y", "z"), (1, 2, 8, 32)):
            ways = (1,) if axis == "core" else (1, -1, 2)
            for by in ways:
                net.send(lambda axis=axis: (self.spot(axis, 0),) * 2, self.out, into, axis, by)
            yield
            net.here(into, self.whole.at[pl.ds(0, count * len(ways))])
        yield


class GainsSum(GainsGather):
    def __init__(self, net, whole, total, land):
        super().__init__(net, None, whole)
        self.total, self.land = total, land

    def steps(self):
        net, land = self.net, self.land
        first = 0
        for into, axis, count in zip(self.into, ("z", "y", "x", "core"), (32, 8, 2, 1)):
            ways = (1,) if axis == "core" else (1, -1, 2)
            spots = [pl.ds(first + n * count, count) for n in range(len(ways))]
            for spot, by in zip(spots, ways):
                refs = lambda axis=axis, spot=spot, by=by: (self.spot(axis, by), land.at[spot])
                net.send(refs, self.out, into, axis, by)
            yield
            net.here(into, land.at[pl.ds(first, count * len(ways))])
            value = self.spot(axis, 0)[...]
            for spot in spots:
                value = value + land[spot]
            if axis == "core":
                self.total[...] = value
            else:
                self.spot(axis, 0)[...] = value
            first += count * len(ways)
        yield


class Kernel:
    def __init__(self, number, plans, gives, turns, locals_, partners):
        self.number, self.partners = number, partners
        extra = gives + turns
        self.sems = (
            sum(plan.OUT for plan in plans) + extra,
            sum(plan.INTO for plan in plans) + extra,
            sum(getattr(plan, "LOCALS", 0) for plan in plans) + turns + locals_,
        )

    def __call__(self, body, arrays, outs, scratch=()):
        n_in, n_out, n_scratch = len(arrays), len(outs), len(scratch)

        def kernel(*refs):
            net = Net(Place(), self.partners, *refs[n_in + n_out + n_scratch :])
            net.greet()
            body(
                net,
                refs[:n_in],
                refs[n_in : n_in + n_out],
                refs[n_in + n_out : n_in + n_out + n_scratch],
            )
            net.finish()
            assert (net.leaving, net.arriving, net.local_count) == self.sems, (
                net.leaving, net.arriving, net.local_count, self.sems,
            )

        return pl.pallas_call(
            kernel,
            out_shape=[shape for shape, _ in outs],
            in_specs=[pl.BlockSpec(memory_space=space) for _, space in arrays],
            out_specs=[pl.BlockSpec(memory_space=space) for _, space in outs],
            scratch_shapes=[*scratch] + [pltpu.SemaphoreType.DMA((n,)) for n in self.sems],
            compiler_params=pltpu.CompilerParams(
                collective_id=self.number, has_side_effects=True, vmem_limit_bytes=62 * 2**20
            ),
            name="links_%d" % self.number,
        )(*[array for array, _ in arrays])


CORE_PARTNER = (("core", 1),)
X_PARTNERS = (("x", 1), ("x", -1))
FAR_X = (("x", 2),)
PLANE_PARTNERS = (("y", 1), ("y", -1), ("y", 2), ("z", 1), ("z", -1), ("z", 2))
TURN_PARTNERS = (("turn", 1),)


def shape(dims, dtype=BF16):
    return jax.ShapeDtypeStruct(dims, dtype)


def attention_spot(z, y):
    piece = z * 4 + lax.rem(y, 2) * 2 + lax.div(y, 2)
    return piece * 128


def rows_spot(z, y):
    return attention_spot(z, y), pl.ds(0, 512)


def output_spot(z, y):
    return 0, pl.ds(pl.multiple_of(attention_spot(z, y), 128), 128)


def gateup_spot(z, y):
    columns = pl.ds(pl.multiple_of(lax.div(y, 2) * 384, 128), 384)
    return (z * 2 + lax.rem(y, 2)) * 256, columns


def down_spot(z, y):
    columns = pl.ds(pl.multiple_of((z * 2 + lax.rem(y, 2)) * 256, 128), 256)
    return lax.div(y, 2) * 384, columns


def nn(left, right):
    return lax.dot_general(left, right, (((1,), (0,)), ((), ())), preferred_element_type=F32)


def nt(left, right):
    return lax.dot_general(left, right, (((1,), (1,)), ((), ())), preferred_element_type=F32)


def tn(left, right):
    return lax.dot_general(left, right, (((0,), (0,)), ((), ())), preferred_element_type=F32)


def exact(left, right):
    return lax.dot_general(
        left, right, (((1,), (0,)), ((), ())),
        precision=lax.Precision.HIGHEST, preferred_element_type=F32,
    )


def inverse_root(rows):
    return lax.rsqrt(jnp.mean(rows * rows, axis=-1, keepdims=True) + EPSILON)


def norm_back(rows, gain, upstream):
    root = inverse_root(rows)
    weighted = upstream * gain
    meant = jnp.mean(weighted * rows, axis=-1, keepdims=True)
    return root * weighted - rows * (root * root * root * meant), upstream * rows * root


def rope_tables():
    halves = np.arange(HEAD_SIZE // 2, dtype=np.float64)
    angles = np.arange(GROUP_TOK)[:, None] * ROPE_BASE ** (-2.0 * halves / HEAD_SIZE)[None, :]
    angles = np.concatenate([angles, angles], axis=1)
    return np.cos(angles).astype(np.float32), np.sin(angles).astype(np.float32)


def owner_starts(dims, axis):
    row = lax.broadcasted_iota(jnp.int32, dims, axis)
    z, y, x, core = row >> 5, (row >> 3) & 3, (row >> 1) & 3, row & 1
    return (z * 32 + (y & 1) * 16 + core * 8 + (y >> 1) * 4 + x) * OWN_GAINS


def column_of(entry):
    return entry - jnp.floor((entry.astype(F32) + 0.5) * (1.0 / OWN_GAINS)).astype(jnp.int32) * OWN_GAINS


def gains_flat(rows):
    entry = lax.broadcasted_iota(jnp.int32, (128, GAINS), 1)
    past = entry - owner_starts((128, GAINS), 0)
    owner = ((past >= 0) & (past < OWN_GAINS)).astype(F32)
    columns = lax.dot_general(
        rows, owner, (((0,), (0,)), ((), ())),
        precision=lax.Precision.HIGHEST, preferred_element_type=F32,
    )
    place = lax.broadcasted_iota(jnp.int32, (128, GAINS), 0)
    return jnp.sum(jnp.where(column_of(entry) == place, columns, 0.0), axis=0, keepdims=True)


class Documents:
    def __init__(self, lengths):
        lengths = [lengths[0:1, n : n + 1] for n in range(4)]
        self.ends = [lengths[0], lengths[0] + lengths[1], lengths[0] + lengths[1] + lengths[2]]

    def pick(self, place, values):
        value = jnp.where(place >= self.ends[0], values[1], values[0])
        value = jnp.where(place >= self.ends[1], values[2], value)
        return jnp.where(place >= self.ends[2], values[3], value)

    def first(self, place):
        zero = jnp.zeros_like(self.ends[0])
        return self.pick(place, [zero] + self.ends)


def allowed_pairs(documents, first_row, rows, keys):
    query = lax.broadcasted_iota(jnp.int32, (rows, 1), 0) + first_row
    key = lax.broadcasted_iota(jnp.int32, (rows, keys), 1)
    return (key >= documents.first(query)) & (key <= query)


def unit_off(n):
    return lax.rem(n + lax.div(n, 2), 4) + 2 * lax.div(n, 3)


class Units:
    ORDER = (0, 1, -1, 2)

    def __init__(self, place):
        self.x = place.x

    def chip(self, n):
        return lax.rem(self.x + unit_off(n), RING)

    def rows(self, n):
        return pl.ds(pl.multiple_of(self.chip(n) * 256, 256), 256)

    def true_rows(self, n, core):
        return pl.ds(pl.multiple_of((core * RING + self.chip(n)) * 128, 128), 128)


def own_half(length, core):
    return pl.ds(pl.multiple_of(core * length, 128), length)


def attention_forward(
    tokens, cotangent, query, keyval, output, gateup, down, gains, lengths, cosine, sine
):
    def body(net, ins, outs, work):
        (
            tokens_, cotangent_, query_, keyval_, output_, gateup_, down_, gains_, lengths_,
            cosine_, sine_,
        ) = ins
        (
            residual_, tokens_here, normed_, raw_, heads_, attended_, totals_,
            cosine_out, sine_out, qkv_out, output_out, gate_out, up_out, down_piece,
            cotangent_all, flat_, lengths_out,
        ) = outs
        (
            gathered, normed, qkv_w, output_w, qkv_cast, output_cast, qkv_piece, output_piece,
            gains_row, gains_rows, lengths_mine, lengths_there, gate_cast, up_cast, down_cast,
            gate_piece, up_piece, cotangent_here, terms, landed, land,
        ) = work
        place = net.place
        units = Units(place)
        mine, theirs = place.core, 1 - place.core

        qkv_cast[:, 0:256] = query_[...].astype(BF16)
        qkv_cast[:, 256:384] = keyval_[0].astype(BF16)
        qkv_cast[:, 384:512] = keyval_[1].astype(BF16)
        output_cast[...] = output_[...].astype(BF16)
        gains_row[0] = jnp.zeros((1, 128), F32)
        gains_row[0, 0:1, 0:OWN_GAINS] = gains_[...]
        lengths_mine[...] = jnp.zeros((8, 128), jnp.int32)
        lengths_mine[0:1, 0:4] = lengths_[...]
        net.enter()
        qkv_turn = Turn(net, [(qkv_cast, qkv_piece)])
        output_turn = Turn(net, [(output_cast, output_piece)])
        rows = [Turn(net, [pair]) for pair in parts_of(tokens_, tokens_here, 2)]
        upstream = Turn(net, parts_of(cotangent_, cotangent_here, 2))
        qkv_turn.start()
        for part in rows:
            part.start()
        qkv_gather = PlaneGather(net, qkv_piece, qkv_w, rows_spot)
        output_gather = PlaneGather(net, output_piece, output_w, output_spot)
        gate_gather = PlaneGather(net, gate_piece, gate_out, gateup_spot)
        up_gather = PlaneGather(net, up_piece, up_out, gateup_spot)
        gather = RowsGather(net, tokens_here, gathered)
        later = RowsGather(net, cotangent_here, cotangent_all)
        length_copy = Give(net, lambda: (lengths_mine, lengths_there), lambda: lengths_there)
        gains_steps = GainsGather(net, gains_row, gains_rows).steps()
        next(gains_steps)

        halves = []
        for n, (cast, piece) in enumerate(((gate_cast, gate_piece), (up_cast, up_piece))):
            spot = own_half(128, mine)
            piece[spot] = gateup_[n, :, own_half(384, mine)].astype(BF16)
            cast[...] = gateup_[n, :, own_half(384, theirs)].astype(BF16)
            halves.append(Give(
                net,
                lambda cast=cast, piece=piece: (cast, piece.at[own_half(128, mine)]),
                lambda piece=piece: piece.at[own_half(128, theirs)],
            ))
        down_piece[:, own_half(128, mine)] = down_[own_half(384, mine)].astype(BF16)
        down_cast[...] = down_[own_half(384, theirs)].astype(BF16)
        halves.append(Give(
            net,
            lambda: (down_cast, down_piece.at[:, own_half(128, mine)]),
            lambda: down_piece.at[:, own_half(128, theirs)],
        ))

        qkv_turn.wait()
        qkv_gather.start()
        output_turn.start()
        for n, part in enumerate(rows):
            part.wait()
            gather.start((n,))
        upstream.start()
        next(gains_steps)

        length_copy.wait()
        lengths_out[...] = jnp.where(place.native, lengths_mine[...], lengths_there[...])
        documents = Documents(lengths_out[...])
        zero = jnp.zeros((1, 1), jnp.int32)
        starts = [zero] + documents.ends
        everywhere = lax.broadcasted_iota(jnp.int32, (1, GROUP_TOK), 1)
        hits = jnp.concatenate(
            [(everywhere == start).astype(F32) for start in starts] * 2, axis=0
        )
        start_cosine = exact(hits, cosine_[...])
        start_sine = exact(hits, sine_[...])
        sign = jnp.where(lax.broadcasted_iota(jnp.int32, (1, HEAD_SIZE), 1) < 64, -1.0, 1.0)

        def table(n):
            spot = pl.ds(pl.multiple_of(n * 256, 256), 256)
            where = lax.broadcasted_iota(jnp.int32, (256, 1), 0) + n * 256
            cosine_by = documents.pick(where, [start_cosine[n : n + 1] for n in range(4)])
            sine_by = documents.pick(where, [start_sine[n : n + 1] for n in range(4)])
            cosine_out[spot] = cosine_[spot] * cosine_by + sine_[spot] * sine_by
            sine_out[spot] = (sine_[spot] * cosine_by - cosine_[spot] * sine_by) * sign

        staged(4, table)
        qkv_gather.spread()
        output_turn.wait()
        output_gather.start()
        next(gains_steps)
        gather.near_first()
        for half in halves:
            half.wait()
        next(gains_steps)
        qkv_gather.forward()
        output_gather.spread()
        gate_gather.start()
        next(gains_steps)
        flat_[...] = gains_flat(gains_rows[...].reshape(128, 128))
        gain_query = flat_[0:1, 4096:4224]
        gain_key = flat_[0:1, 4224:4352]

        def normalize(n):
            rows_in = gathered[units.rows(n)].astype(F32)
            normed[units.rows(n)] = (
                rows_in * inverse_root(rows_in) * flat_[0:1, 0:2048]
            ).astype(BF16)

        def near():
            gather.near_second()
            gather.here(1)

        def far():
            gather.far()
            output_gather.forward()
            up_gather.start()
            upstream.wait()
            later.start()
            gather.here(2)

        staged(4, normalize, {
            0: lambda: gather.here(0), 1: near, 2: lambda: gather.here(-1), 3: far,
        })
        qkv_gather.here()
        stores = [net.local(lambda: (normed, normed_)), net.local(lambda: (qkv_w, qkv_out))]

        def project(n):
            parts = nn(normed[units.rows(n)], qkv_w[...])
            for core in range(2):
                spot = units.true_rows(n, core)
                part = parts[core * 128 : core * 128 + 128]
                raw_[spot] = part[:, 0:384]
                heads_[spot, 384:512] = part[:, 384:512].astype(BF16)
                for head in range(3):
                    columns = slice(head * 128, head * 128 + 128)
                    value = part[:, columns]
                    value = value * inverse_root(value) * (gain_key if head == 2 else gain_query)
                    turned = value * cosine_out[spot] + pltpu.roll(value, 64, 1) * sine_out[spot]
                    heads_[spot, columns] = turned.astype(BF16)

        staged(4, project)
        gate_gather.spread()

        def attend(block):
            keys = 256 * (block + 1)
            spot = slice(block * 256, block * 256 + 256)

            def one(head):
                columns = own_half(128, head)
                scores = nt(heads_[spot, columns], heads_[0:keys, 256:384])
                allowed = allowed_pairs(documents, block * 256, 256, keys)
                scores = jnp.where(allowed, scores, -1e30)
                highest = jnp.max(scores, axis=-1, keepdims=True)
                weights_ = jnp.exp((scores - highest) * SCALE)
                summed = jnp.sum(weights_, axis=-1, keepdims=True)
                probability = (weights_ * (1.0 / summed)).astype(BF16)
                attended_[spot, columns] = nn(probability, heads_[0:keys, 384:512]).astype(BF16)
                lane = lax.broadcasted_iota(jnp.int32, (1, 128), 1)
                ours = (lane >= head * 64) & (lane < head * 64 + 64)
                totals_[spot] = jnp.where(ours, highest * SCALE + jnp.log(summed), totals_[spot])

            staged(2, one)

        attend(0)
        attend(1)
        later.near_first()
        up_gather.spread()
        attend(2)
        output_gather.here()
        stores.append(net.local(lambda: (output_w, output_out)))
        attend(3)
        sums = RowsSum(net, terms, landed, land)

        def out(n):
            n = 3 - n
            own = jnp.concatenate(
                [attended_[units.true_rows(n, 0)], attended_[units.true_rows(n, 1)]], axis=0
            )
            terms[units.rows(n)] = nn(own, output_w[...]).astype(BF16)

        def passed(k, ready=None, go=None):
            def act():
                sums.pass_over(k)
                if ready is not None:
                    sums.combine(ready)
                    go()

            return act

        later.near_second()
        staged(4, out, None, {
            0: passed(2),
            1: passed(-1, 2, sums.start_far),
            2: passed(1, -1, sums.start_left),
            3: passed(0, 1, sums.start_right),
        })
        later.far()
        gate_gather.forward()
        sums.combine(0)
        sums.forward()
        up_gather.forward()
        for k in (0, 1, -1, 2):
            later.here(k)

        def keep(spot, value):
            residual_[spot] = value + tokens_here[spot].astype(F32)

        sums.finish(keep)
        gate_gather.here()
        up_gather.here()
        for store in stores:
            store.wait()

    plans = (GainsGather,) + 4 * (PlaneGather,) + 2 * (RowsGather,) + (RowsSum,)
    return Kernel(
        0, plans, 4, 6, 3, CORE_PARTNER + X_PARTNERS + FAR_X + PLANE_PARTNERS + TURN_PARTNERS
    )(
        body,
        [
            (tokens, VMEM), (cotangent, VMEM), (query, VMEM), (keyval, VMEM), (output, VMEM),
            (gateup, VMEM), (down, VMEM), (gains, VMEM), (lengths, VMEM),
            (cosine, VMEM), (sine, VMEM),
        ],
        [
            (shape((128, 2048), F32), VMEM),
            (shape((128, 2048)), VMEM),
            (shape((1024, 2048)), HBM),
            (shape((1024, 384), F32), VMEM),
            (shape((1024, 512)), VMEM),
            (shape((1024, 256)), VMEM),
            (shape((1024, 128), F32), VMEM),
            (shape((1024, 128), F32), VMEM),
            (shape((1024, 128), F32), VMEM),
            (shape((2048, 512)), HBM),
            (shape((256, 2048)), HBM),
            (shape((2048, 768)), HBM),
            (shape((2048, 768)), HBM),
            (shape((384, 256)), VMEM),
            (shape((1024, 2048)), HBM),
            (shape((1, GAINS), F32), VMEM),
            (shape((8, 128), jnp.int32), VMEM),
        ],
        (
            pltpu.VMEM((1024, 2048), BF16),
            pltpu.VMEM((1024, 2048), BF16),
            pltpu.VMEM((2048, 512), BF16),
            pltpu.VMEM((256, 2048), BF16),
            pltpu.VMEM((128, 512), BF16),
            pltpu.VMEM((256, 128), BF16),
            pltpu.VMEM((128, 512), BF16),
            pltpu.VMEM((256, 128), BF16),
            pltpu.VMEM((1, 1, 128), F32),
            pltpu.VMEM((128, 1, 128), F32),
            pltpu.VMEM((8, 128), jnp.int32),
            pltpu.VMEM((8, 128), jnp.int32),
            pltpu.VMEM((128, 384), BF16),
            pltpu.VMEM((128, 384), BF16),
            pltpu.VMEM((384, 128), BF16),
            pltpu.VMEM((256, 384), BF16),
            pltpu.VMEM((256, 384), BF16),
            pltpu.VMEM((128, 2048), BF16),
            pltpu.VMEM((1024, 2048), BF16),
        )
        + ROWS_SCRATCH,
    )


def layer_backward(
    residual, tokens, gains, lengths, down, cotangent_all, gate, up, heads, raw, attended,
    totals, cosine, sine, qkv, output, normed,
):
    def body(net, ins, outs, work):
        (
            residual_, tokens_, gains_, lengths_, down_, cotangent_all_, gate_, up_,
            heads_, raw_, attended_, totals_, cosine_, sine_, qkv_, output_, normed_,
        ) = ins
        (
            block_own, input_own, qkv_own, output_own, gate_own, up_own, down_own, gains_own,
        ) = outs
        (
            low, second, upstream, qkv_w, output_w, gate_w, up_w, down_w, hidden, gate_low, up_low,
            terms, back_rows, raw_here, totals_here, cosine_here, sine_here, key_sum, value_sum,
            own_out, qkv_total, output_total, gate_total, up_total, down_total,
            gain_rows, gain_land, first_gain, flat, landed, land, mlp_landed, mlp_land,
            gate_land, gate_last, up_land, up_last, down_land, down_last,
            qkv_land, qkv_last, output_land, output_last, free,
        ) = work
        place = net.place
        units = Units(place)
        mine, theirs = place.core, 1 - place.core

        def load(source, target):
            return net.local(lambda: (source, target))

        loads = {
            "gate": load(gate_, gate_w),
            "up": load(up_, up_w),
            "upstream": load(cotangent_all_, upstream),
            "output": load(output_, output_w),
            "qkv": load(qkv_, qkv_w),
            "raw": load(raw_, raw_here),
            "totals": load(totals_, totals_here),
            "cosine": load(cosine_, cosine_here),
            "sine": load(sine_, sine_here),
        }
        second_gain = gains_[0:1, 2048:4096]

        def second_norm(n):
            spot = pl.ds(pl.multiple_of(n * 64, 64), 64)
            rows = residual_[spot]
            low[spot] = (rows * inverse_root(rows) * second_gain).astype(BF16)

        staged(2, second_norm)
        net.enter()
        gather = RowsGather(net, low, second)
        gather.start()
        down_gather = PlaneGather(net, down_, down_w, down_spot)
        down_gather.start()
        sums = RowsSum(net, terms, landed, land)
        mlp_sum = RowsSum(net, terms, mlp_landed, mlp_land)
        first_sum = RowsSum(net, terms, landed, land)
        last_gather = RowsGather(net, low, upstream)
        gate_sum = PlaneSum(net, gate_w, gateup_spot, gate_land, gate_last)
        up_sum = PlaneSum(net, up_w, gateup_spot, up_land, up_last)
        down_sum = PlaneSum(net, down_w, down_spot, down_land, down_last)
        qkv_sum = PlaneSum(net, qkv_w, rows_spot, qkv_land, qkv_last)
        output_sum = PlaneSum(net, output_w, output_spot, output_land, output_last)

        def forth(n):
            spot = units.rows(n)
            gate_value = nn(second[spot], gate_w[...])
            upward = nn(second[spot], up_w[...])
            sigmoid = 1.0 / (1.0 + jnp.exp(-gate_value))
            active = gate_value * sigmoid
            hidden[spot] = (active * upward).astype(BF16)
            gate_low[spot] = (upward * (sigmoid + active * (1.0 - sigmoid))).astype(BF16)
            up_low[spot] = active.astype(BF16)

        def back(n):
            spot = units.rows(3 - n)
            hidden_grad = nt(upstream[spot], down_w[...])
            gate_low[spot] = (hidden_grad * gate_low[spot].astype(F32)).astype(BF16)
            up_low[spot] = (hidden_grad * up_low[spot].astype(F32)).astype(BF16)
            terms[spot] = (nt(gate_low[spot], gate_w[...]) + nt(up_low[spot], up_w[...])).astype(
                BF16
            )

        def handed(to, k, ready=None, go=None):
            def act():
                to.pass_over(k)
                if ready is not None:
                    to.combine(ready)
                    go()

            return act

        def in_turn(to):
            return {
                0: handed(to, 2),
                1: handed(to, -1, 2, to.start_far),
                2: handed(to, 1, -1, to.start_left),
                3: handed(to, 0, 1, to.start_right),
            }

        def begin():
            for name in ("gate", "up", "upstream"):
                loads[name].wait()
            gather.here(0)

        def near():
            gather.near_first()
            down_gather.spread()
            gather.near_second()
            gather.here(1)

        def far():
            down_gather.forward()
            gather.far()
            gather.here(2)

        staged(4, forth, {0: begin, 1: near, 2: lambda: gather.here(-1), 3: far})
        down_gather.here()
        staged(4, back, None, in_turn(sums))
        sums.combine(0)
        sums.passed()
        down_gather.gone()

        def through(n):
            spot = units.rows(n)
            terms[spot] = nn(hidden[spot], down_w[...]).astype(BF16)

        staged(4, through, None, {0: sums.forward})

        def down_grad(n):
            columns = own_half(256, n)
            down_w[columns] = tn(hidden[:, columns], upstream[...]).astype(BF16)

        staged(3, down_grad)
        for axis, by in CORE_PARTNER + X_PARTNERS:
            pl.semaphore_signal(
                free, inc=1, device_id=place.device(axis, by), device_id_type=pl.DeviceIdType.MESH
            )
        down_sum.start()
        gather.gone()
        gain_parts = []

        def own_rows(spot):
            start = (place.x * 2 + place.core) * 128 + spot.start
            return pl.ds(pl.multiple_of(start, 64), 64)

        def keep(spot, value):
            through_, gain_part = norm_back(residual_[spot], second_gain, value)
            through_ = through_ + upstream[own_rows(spot)].astype(F32)
            back_rows[spot] = through_
            low[spot] = through_.astype(BF16)
            gain_parts.append(jnp.sum(gain_part, axis=0, keepdims=True))

        sums.finish(keep)
        sums.departed()
        pl.semaphore_wait(free, 3)
        last_gather.start()

        def weight_grad(low_grad, target):
            def one(n):
                columns = own_half(256, n)
                target[columns] = tn(second[:, columns], low_grad[...]).astype(BF16)

            return one

        staged(8, weight_grad(gate_low, gate_w))
        gate_sum.start()
        last_gather.near_first()
        staged(8, weight_grad(up_low, up_w))
        up_sum.start()
        heads_cols, attended_cols = hidden.at[:, 0:512], hidden.at[:, 512:768]
        parts, attended_grad = gate_low.at[:, 0:512], gate_low.at[:, 512:768]
        attended_rows = up_low.at[:, 0:256]
        loads["heads"] = load(heads_, heads_cols)
        loads["attended"] = load(attended_, attended_cols)
        loads["normed"] = load(normed_, second)
        for k in (2, 1, -1, 0):
            mlp_sum.pass_over(k)
        last_gather.near_second()
        down_sum.forward()
        loads["output"].wait()

        def enter(n):
            grad = nt(upstream[units.rows(n)], output_w[...]).astype(BF16)
            for core in range(2):
                attended_grad[units.true_rows(n, core)] = grad[core * 128 : core * 128 + 128]

        def combined():
            last_gather.here(1)
            for k in (2, 1, -1, 0):
                mlp_sum.combine(k)

        def last_far():
            last_gather.far()
            mlp_sum.start_far()
            mlp_sum.start_right()
            mlp_sum.start_left()
            last_gather.here(2)

        staged(4, enter, {
            0: lambda: last_gather.here(0), 1: combined, 2: lambda: last_gather.here(-1), 3: last_far,
        })
        loads["heads"].wait()
        loads["attended"].wait()

        def same_order(n):
            for core in range(2):
                start = pl.multiple_of(units.chip(n) * 256 + core * 128, 128)
                attended_rows[pl.ds(start, 128)] = attended_cols[units.true_rows(n, core)]

        staged(4, same_order)

        def output_grad(n):
            columns = own_half(512, n)
            output_w[:, columns] = tn(attended_rows[...], upstream[:, columns]).astype(BF16)

        staged(4, output_grad)
        output_sum.start()
        gate_sum.forward()
        key_sum[...] = jnp.zeros_like(key_sum)
        value_sum[...] = jnp.zeros_like(value_sum)
        for name in ("raw", "totals", "cosine", "sine"):
            loads[name].wait()
        documents = Documents(lengths_[...])
        gain_query, gain_key = gains_[0:1, 4096:4224], gains_[0:1, 4224:4352]

        def through_rope(value, spot, raw_part, gain):
            value = value * cosine_here[spot] + pltpu.roll(value * sine_here[spot], 64, 1)
            through_, gain_part = norm_back(raw_part, gain, value)
            return through_.astype(BF16), jnp.sum(gain_part, axis=0, keepdims=True)

        def attend(block, gain_sum):
            keys = 256 * (block + 1)
            spot = slice(block * 256, block * 256 + 256)

            def one(head, gain_sum):
                columns = own_half(128, head)
                query = hidden[spot, columns]
                upward = gate_low[spot, pl.ds(pl.multiple_of(512 + head * 128, 128), 128)]
                key, value = hidden[0:keys, 256:384], hidden[0:keys, 384:512]
                scores = nt(query, key) * SCALE
                total = jnp.where(head == 0, totals_here[spot, 0:1], totals_here[spot, 64:65])
                allowed = allowed_pairs(documents, block * 256, 256, keys)
                probability = jnp.where(allowed, jnp.exp(scores - total), 0.0)
                prob_grad = nt(upward, value)
                centre = jnp.sum(probability * prob_grad, axis=-1, keepdims=True)
                score_grad = (probability * (prob_grad - centre)).astype(BF16)
                value_sum[0:keys] += tn(probability.astype(BF16), upward)
                key_sum[0:keys] += tn(score_grad, query)
                query_grad = nn(score_grad, key) * SCALE
                through_, gain_part = through_rope(
                    query_grad, spot, raw_here[spot, columns], gain_query
                )
                for n in range(2):
                    true = block * 2 + n
                    start = ((true % RING) * 2 + true // RING) * 128
                    gate_low[start : start + 128, columns] = through_[n * 128 : n * 128 + 128]
                return gain_sum + gain_part

            return lax.fori_loop(0, 2, one, gain_sum)

        query_gain = attend(3, jnp.zeros((1, 128), F32))
        down_sum.gather()
        query_gain = attend(2, query_gain)
        mlp_sum.forward()
        query_gain = attend(1, query_gain)
        query_gain = attend(0, query_gain)
        up_sum.forward()

        def key_back(true, gain_sum):
            spot = pl.ds(pl.multiple_of(true * 128, 128), 128)
            start = (lax.rem(true, RING) * 2 + lax.div(true, RING)) * 128
            through_, gain_part = through_rope(
                key_sum[spot] * SCALE, spot, raw_here[spot, 256:384], gain_key
            )
            here = pl.ds(pl.multiple_of(start, 128), 128)
            gate_low[here, 256:384] = through_
            gate_low[here, 384:512] = value_sum[spot].astype(BF16)
            return gain_sum + gain_part

        key_gain = lax.fori_loop(0, 8, key_back, jnp.zeros((1, 128), F32))
        mlp_sum.passed()
        last_gather.gone()
        loads["tokens"] = load(tokens_, low)
        loads["qkv"].wait()
        loads["normed"].wait()
        first_gain[...] = jnp.zeros_like(first_gain)

        def out(n):
            spot = units.rows(3 - n)
            value = nt(parts[spot], qkv_w[...])
            terms[spot] = value.astype(BF16)
            part = jnp.sum(value * second[spot].astype(F32), axis=0, keepdims=True)
            first_gain[...] += part

        staged(4, out, None, in_turn(first_sum))
        gate_sum.gather()

        def qkv_grad(n):
            columns = own_half(256, n)
            qkv_w[columns] = tn(second[:, columns], parts[...]).astype(BF16)

        staged(8, qkv_grad, None, {3: lambda: (first_sum.combine(0), first_sum.forward())})
        qkv_sum.start()
        flat[...] = jnp.concatenate(
            [first_gain[...] / gains_[0:1, 0:2048], gain_parts[0] + gain_parts[1], query_gain, key_gain],
            axis=1,
        )

        def to_rows(n, total):
            entry = lax.broadcasted_iota(jnp.int32, (128, 256), 1) + n * 256
            past = entry - owner_starts((128, 256), 0)
            here = flat[0:1, own_half(256, n)]
            owned = jnp.where((past >= 0) & (past < OWN_GAINS), here, 0.0)
            place_ = lax.broadcasted_iota(jnp.int32, (128, 256), 0)
            column = (column_of(entry) == place_).astype(F32)
            return total + lax.dot_general(
                owned, column, (((1,), (1,)), ((), ())),
                precision=lax.Precision.HIGHEST, preferred_element_type=F32,
            )

        rows_of = lax.fori_loop(0, GAINS // 256, to_rows, jnp.zeros((128, 128), F32))
        gain_rows[...] = rows_of.reshape(128, 1, 128)
        gains_steps = GainsSum(net, gain_rows, gains_own, gain_land).steps()
        next(gains_steps)
        output_sum.forward()

        def keep_block(spot, value):
            own_out[spot] = (residual_[spot] + value).astype(BF16)

        mlp_sum.finish(keep_block)
        block_turn = Turn(net, parts_of(own_out, block_own, 2))
        block_turn.start()
        next(gains_steps)

        halves = []

        def exchange(cut, there):
            halves.append(net.local(lambda: (cut(mine), there(mine))))
            halves.append(
                Give(net, lambda: (cut(theirs), there(mine)), lambda: there(theirs))
            )

        down_sum.finish(down_total)
        exchange(
            lambda core: down_total.at[:, own_half(128, core)],
            lambda core: down_own.at[own_half(384, core)],
        )
        up_sum.gather()
        next(gains_steps)
        output_sum.gather()
        qkv_sum.forward()
        next(gains_steps)
        gate_sum.finish(gate_total)
        exchange(
            lambda core: gate_total.at[own_half(128, core)],
            lambda core: gate_own.at[:, own_half(384, core)],
        )
        turns = []
        block_turn.wait()
        loads["tokens"].wait()

        def keep_first(spot, value):
            rows_in = low[spot].astype(F32)
            through_, _ = norm_back(rows_in, gains_[0:1, 0:2048], value)
            own_out[spot] = (back_rows[spot] + through_).astype(BF16)
            turns.append(Turn(net, [(own_out.at[spot], input_own.at[spot])]))
            turns[-1].start()

        first_sum.finish(keep_first)
        up_sum.finish(up_total)
        exchange(
            lambda core: up_total.at[own_half(128, core)],
            lambda core: up_own.at[:, own_half(384, core)],
        )
        output_sum.finish(output_total)
        output_turn = Turn(net, [(output_total, output_own)])
        output_turn.start()
        qkv_sum.gather()
        next(gains_steps)
        qkv_sum.finish(qkv_total)
        qkv_turn = Turn(net, [(qkv_total, qkv_own)])
        qkv_turn.start()
        for copy in halves:
            copy.wait()
        for turn in (output_turn, *turns, qkv_turn):
            turn.wait()

    plans = (
        2 * (RowsGather,) + 3 * (RowsSum,) + (PlaneGather,) + 5 * (PlaneSum,) + (GainsSum,)
    )
    return Kernel(
        1, plans, 3, 6, 13 + 3 - 1, CORE_PARTNER + X_PARTNERS + FAR_X + PLANE_PARTNERS + TURN_PARTNERS
    )(
        body,
        [
            (residual, VMEM), (tokens, HBM), (gains, VMEM), (lengths, VMEM),
            (down, VMEM), (cotangent_all, HBM), (gate, HBM), (up, HBM), (heads, HBM), (raw, HBM),
            (attended, HBM), (totals, HBM), (cosine, HBM), (sine, HBM), (qkv, HBM), (output, HBM),
            (normed, HBM),
        ],
        [
            (shape((128, 2048)), HBM),
            (shape((128, 2048)), HBM),
            (shape((128, 512)), VMEM),
            (shape((256, 128)), VMEM),
            (shape((128, 768)), HBM),
            (shape((128, 768)), HBM),
            (shape((768, 128)), HBM),
            (shape((1, 1, 128), F32), VMEM),
        ],
        (
            pltpu.VMEM((128, 2048), BF16),
            pltpu.VMEM((1024, 2048), BF16),
            pltpu.VMEM((1024, 2048), BF16),
            pltpu.VMEM((2048, 512), BF16),
            pltpu.VMEM((256, 2048), BF16),
            pltpu.VMEM((2048, 768), BF16),
            pltpu.VMEM((2048, 768), BF16),
            pltpu.VMEM((768, 2048), BF16),
            pltpu.VMEM((1024, 768), BF16),
            pltpu.VMEM((1024, 768), BF16),
            pltpu.VMEM((1024, 768), BF16),
            pltpu.VMEM((1024, 2048), BF16),
            pltpu.VMEM((128, 2048), F32),
            pltpu.VMEM((1024, 384), F32),
            pltpu.VMEM((1024, 128), F32),
            pltpu.VMEM((1024, 128), F32),
            pltpu.VMEM((1024, 128), F32),
            pltpu.VMEM((1024, 128), F32),
            pltpu.VMEM((1024, 128), F32),
            pltpu.VMEM((128, 2048), BF16),
            pltpu.VMEM((128, 512), BF16),
            pltpu.VMEM((256, 128), BF16),
            pltpu.VMEM((256, 384), BF16),
            pltpu.VMEM((256, 384), BF16),
            pltpu.VMEM((384, 256), BF16),
            pltpu.VMEM((128, 1, 128), F32),
            pltpu.VMEM((127, 1, 128), F32),
            pltpu.VMEM((1, 2048), F32),
            pltpu.VMEM((1, GAINS), F32),
        )
        + ROWS_SCRATCH * 2
        + plane_scratch(256, 384) * 2
        + plane_scratch(384, 256)
        + plane_scratch(128, 512)
        + plane_scratch(256, 128)
        + (pltpu.SemaphoreType.REGULAR,),
    )


def step_rates(total_tokens):
    root_tokens = math.sqrt(total_tokens)
    narrow = MODEL_WIDTH ** (-0.5)
    return (
        narrow / (2.0 * root_tokens),
        narrow / (2.0 * root_tokens),
        (QUERY_HEADS * HEAD_SIZE // 128) ** (-0.5) / (0.24 * root_tokens),
        narrow / (0.7 * root_tokens),
        FF ** (-0.5) / (1.2 * root_tokens),
        0.025 / root_tokens,
    )


def update(rows, gradients, state):
    rates = step_rates(GROUP_TOK * 16)

    def kernel(*refs):
        block_, input_, qkv_, output_, gate_, up_, down_, gains_ = refs[:8]
        masters, moments, averages = refs[8:14], refs[14:20], refs[20:26]
        outs = refs[26:]
        outs[0][...] = block_[...]
        outs[1][...] = input_[...]

        def one(n, gradient, spot):
            gradient = gradient.astype(F32)
            moment = MOMENTUM * moments[n][spot] + gradient
            master = masters[n][spot] - rates[n] * (gradient + MOMENTUM * moment)
            outs[2 + n][spot] = master
            outs[8 + n][spot] = moment
            outs[14 + n][spot] = AVERAGING * averages[n][spot] + (1.0 - AVERAGING) * master

        one(0, qkv_[:, 0:256], ...)
        one(1, qkv_[:, 256:384], 0)
        one(1, qkv_[:, 384:512], 1)
        one(2, output_[...], ...)
        one(3, gate_[...], 0)
        one(3, up_[...], 1)
        one(4, down_[...], ...)
        one(5, gains_[0, 0:1, 0:OWN_GAINS], ...)

    outs = [shape(a.shape, a.dtype) for a in rows]
    outs += [shape(a.shape, F32) for a in state]
    arrays = (*rows, *gradients, *state)
    return pl.pallas_call(
        kernel,
        out_shape=outs,
        in_specs=[pl.BlockSpec(memory_space=VMEM)] * len(arrays),
        out_specs=[pl.BlockSpec(memory_space=VMEM)] * len(outs),
        compiler_params=pltpu.CompilerParams(vmem_limit_bytes=61 * 2**20),
        name="update",
    )(*arrays)


def body(tokens, cotangent, doc_lengths, *state):
    query_weight, key_value_weight, output_weight, gateup_weight, down_weight, norm_gains = state[:6]
    cosine, sine = rope_tables()
    (
        residual, tokens_here, normed, raw, heads, attended, totals,
        cosine, sine, qkv, output, gate, up, down, cotangent_all, gains, lengths,
    ) = attention_forward(
        tokens, cotangent, query_weight, key_value_weight, output_weight, gateup_weight,
        down_weight, norm_gains.reshape(1, OWN_GAINS), doc_lengths,
        jnp.asarray(cosine), jnp.asarray(sine),
    )
    block_out, input_grad, *gradients = layer_backward(
        residual, tokens_here, gains, lengths, down, cotangent_all, gate, up,
        heads, raw, attended, totals, cosine, sine, qkv, output, normed,
    )
    state = [a.reshape(1, OWN_GAINS) if a.ndim == 1 else a for a in state]
    outs = update((block_out, input_grad), gradients, state)
    return tuple(a.reshape(OWN_GAINS) if a.shape == (1, OWN_GAINS) else a for a in outs)


def solution(mesh):
    parted = Mesh(mesh.devices.reshape(GRID), AXES)
    data = ("z", "ylo", "core")
    tensor = ("yhi", "x")
    rows = P(AXES, None)
    by_rows = P(data, tensor)
    pair = P(None, data, tensor)
    by_columns = P(tensor, data)
    flat = P(AXES)
    weights = (by_rows, pair, by_columns, pair, by_columns, flat)
    return jax.shard_map(
        body,
        mesh=parted,
        in_specs=(rows, rows, P(data, None)) + weights * 3,
        out_specs=(rows, rows) + weights * 3,
        check_vma=False,
    )
```

```python
import math

import jax
import jax.numpy as jnp
import numpy as np
from jax import lax
from jax.experimental import pallas as pl
from jax.experimental.pallas import tpu as pltpu
from jax.sharding import Mesh
from jax.sharding import PartitionSpec as P

MODEL_WIDTH = 2048
QUERY_HEADS = 16
HEAD_SIZE = 128
FF = 6144
GROUP_TOK = 1024
GAINS = 4352
OWN_GAINS = 34
EPSILON = 1e-06
MOMENTUM = 0.9
AVERAGING = 0.5
ROPE_BASE = 1000000.0
SCALE = HEAD_SIZE ** (-0.5)

AXES = ("z", "ylo", "core", "yhi", "x")
GRID = (4, 2, 2, 2, 4)
RING = 4
BF16 = jnp.bfloat16
F32 = jnp.float32
HBM = pl.ANY
VMEM = pltpu.VMEM


class Place:
    def __init__(self):
        self.x = lax.axis_index("x")
        self.z = lax.axis_index("z")
        self.core = lax.axis_index("core")
        self.yhi = lax.axis_index("yhi")
        self.ylo = lax.axis_index("ylo")
        self.y = self.yhi * 2 + self.ylo
        self.native = self.core == self.yhi
        at = {"x": self.x, "y": self.y, "z": self.z}
        self.steps = {
            (axis, by): lax.rem(here + by, RING) if by else here
            for axis, here in at.items()
            for by in range(RING)
        }
        self.devices = {
            "core": {"core": 1 - self.core},
            "turn": {"core": 1 - self.core, "yhi": 1 - self.yhi},
        }
        for (axis, by), there in self.steps.items():
            self.devices[axis, by] = (
                {"yhi": lax.div(there, 2), "ylo": lax.rem(there, 2)}
                if axis == "y"
                else {axis: there}
            )

    def step(self, axis, by):
        return self.steps[axis, by % RING]

    def device(self, axis, by=1):
        return self.devices[axis] if axis in ("core", "turn") else self.devices[axis, by % RING]


class Local:
    def __init__(self, refs, sems, index):
        self.refs, self.sems, self.index = refs, sems, index

    def copy(self):
        source, target = self.refs()
        return pltpu.make_async_copy(source, target, self.sems.at[self.index])

    def start(self):
        self.copy().start()

    def wait(self):
        self.copy().wait()


class Net:
    def __init__(self, place, partners, send_sems, recv_sems, local_sems):
        self.place, self.partners = place, partners
        self.send_sems, self.recv_sems, self.local_sems = send_sems, recv_sems, local_sems
        self.leaving, self.arriving, self.local_count = 0, 0, 0
        self.waits = []

    def greet(self):
        barrier = pltpu.get_barrier_semaphore()
        for axis, by in self.partners:
            pl.semaphore_signal(
                barrier,
                inc=1,
                device_id=self.place.device(axis, by),
                device_id_type=pl.DeviceIdType.MESH,
            )

    def enter(self):
        pl.semaphore_wait(pltpu.get_barrier_semaphore(), len(self.partners))

    def out(self):
        self.leaving += 1
        return self.leaving - 1

    def into(self):
        self.arriving += 1
        return self.arriving - 1

    def local_number(self):
        self.local_count += 1
        return self.local_count - 1

    def copy(self, source, target, out, into, axis="core", by=1):
        return pltpu.make_async_remote_copy(
            src_ref=source,
            dst_ref=target,
            send_sem=self.send_sems.at[out],
            recv_sem=self.recv_sems.at[into],
            device_id=self.place.device(axis, by),
            device_id_type=pl.DeviceIdType.MESH,
        )

    def send(self, refs, out, into, axis, by=1):
        self.copy(*refs(), out, into, axis, by).start()

    def here(self, into, view):
        self.copy(view, view, 0, into).wait_recv()

    def gone(self, out, view):
        self.copy(view, view, out, 0).wait_send()

    def later(self, wait):
        self.waits.append(wait)

    def finish(self):
        for wait in self.waits:
            wait()

    def local(self, refs):
        copy = Local(refs, self.local_sems, self.local_number())
        copy.start()
        return copy


def at_step(acts, n):
    for at, act in (acts or {}).items():

        @pl.when(n == at)
        def _():
            act()


def staged(count, compute, before=None, after=None):
    def step(n, carry):
        at_step(before, n)
        compute(n)
        at_step(after, n)
        return carry

    lax.fori_loop(0, count, step, 0)


class RowsGather:
    OUT, INTO, LOCALS = 1, 7, 2

    def __init__(self, net, own, whole):
        self.net, self.own, self.whole = net, own, whole
        self.rows = own.shape[0]
        self.half = self.rows // 2
        place = net.place
        self.me, self.other = place.core, 1 - place.core
        self.spots = {k: place.step("x", k) for k in (0, 1, -1, 2)}
        self.out = net.out()
        self.first, self.second, self.third = net.into(), net.into(), net.into()
        self.shared = {k: net.into() for k in (0, 1, -1, 2)}
        self.kept = []
        net.later(self.gone)

    def block(self, core, k, part):
        start = (self.spots[k] * 2 + core) * self.rows + part * self.half
        return self.whole.at[pl.ds(pl.multiple_of(start, self.half), self.half)]

    def mine(self, k, part):
        return self.block(self.me, k, part)

    def piece(self, part):
        return self.own.at[pl.ds(part * self.half, self.half)]

    def share(self, k, part):
        refs = lambda: (self.piece(part) if k == 0 else self.mine(k, part), self.mine(k, part))
        self.net.send(refs, self.out, self.shared[k], "core")

    def both(self):
        return self.whole.at[pl.ds(0, self.rows)]

    def start(self, parts=(0, 1)):
        for part in parts:
            refs = lambda part=part: (self.piece(part), self.mine(0, part))
            first, second = (1, -1) if part == 0 else (-1, 1)
            self.net.send(refs, self.out, self.first, "x", first)
            self.net.send(refs, self.out, self.second, "x", second)
            self.share(0, part)
            self.kept.append(self.net.local(refs))

    def near_first(self):
        self.net.here(self.first, self.both())
        self.net.send(lambda: (self.mine(-1, 0),) * 2, self.out, self.third, "x", 1)
        self.net.send(lambda: (self.mine(1, 1),) * 2, self.out, self.third, "x", -1)
        self.share(-1, 0)
        self.share(1, 1)

    def near_second(self):
        self.net.here(self.second, self.both())
        self.share(-1, 1)
        self.share(1, 0)

    def far(self):
        self.net.here(self.third, self.both())
        self.share(2, 0)
        self.share(2, 1)

    def here(self, k):
        if k == 0:
            for copy in self.kept:
                copy.wait()
        self.net.here(self.shared[k], self.both())

    def gone(self):
        if self.out is not None:
            self.net.gone(self.out, self.whole.at[pl.ds(0, 7 * self.rows)])
            self.out = None


class RowsSum:
    OUT, INTO = 2, 6

    def __init__(self, net, whole, landed, land, share=0, shares=1):
        self.net, self.whole, self.landed, self.land = net, whole, landed, land
        self.share, self.shares = share, shares
        self.half = landed.shape[2]
        place = net.place
        self.me, self.other = place.core, 1 - place.core
        self.spots = {k: place.step("x", k) for k in (0, 1, -1, 2)}
        self.over, self.along = net.out(), net.out()
        self.given = {k: net.into() for k in (0, 1, -1, 2)}
        self.through, self.last = net.into(), net.into()
        net.later(self.passed)
        net.later(self.departed)

    def block(self, core, k, part):
        block = (self.spots[k] * 2 + core) * self.shares + self.share
        start = (block * 2 + part) * self.half
        return self.whole.at[pl.ds(pl.multiple_of(start, self.half), self.half)]

    def own(self, k, part):
        return self.landed.at[k % RING, part]

    def pass_over(self, k):
        for part in range(2):
            refs = lambda part=part: (self.block(self.other, k, part), self.own(k, part))
            self.net.send(refs, self.over, self.given[k], "core")

    def passed(self):
        if self.over is not None:
            self.net.gone(self.over, self.landed)
            self.over = None

    def departed(self):
        if self.along is not None:
            self.net.gone(self.along, self.land)
            self.along = None

    def combine(self, k):
        self.net.here(self.given[k], self.landed.at[k % RING])
        for part in range(2):
            here = self.own(k, part)
            here[...] = here[...] + self.block(self.me, k, part)[...]

    def along_x(self, refs, into, by):
        self.net.send(refs, self.along, into, "x", by)

    def start_far(self):
        self.along_x(lambda: (self.own(2, 0), self.land.at[0]), self.through, 1)
        self.along_x(lambda: (self.own(2, 1), self.land.at[1]), self.through, -1)

    def start_right(self):
        self.along_x(lambda: (self.own(1, 1), self.land.at[3]), self.last, 1)

    def start_left(self):
        self.along_x(lambda: (self.own(-1, 0), self.land.at[4]), self.last, -1)

    def forward(self):
        land = self.land
        self.net.here(self.through, land.at[pl.ds(0, 2)])
        land[0] = land[0] + self.own(1, 0)[...]
        self.along_x(lambda: (land.at[0], land.at[2]), self.last, 1)
        land[1] = land[1] + self.own(-1, 1)[...]
        self.along_x(lambda: (land.at[1], land.at[5]), self.last, -1)

    def finish(self, keep):
        land = self.land
        self.net.here(self.last, land.at[pl.ds(2, 4)])
        for part in range(2):
            total = self.own(0, part)[...].astype(F32) + land[2 + part].astype(F32)
            keep(pl.ds(part * self.half, self.half), total + land[4 + part].astype(F32))


ROWS_SCRATCH = (pltpu.VMEM((4, 2, 64, 2048), BF16), pltpu.VMEM((6, 64, 2048), BF16))


class PlaneGather:
    OUT, INTO, LOCALS = 1, 12, 1

    def __init__(self, net, own, whole, spot):
        self.net, self.own, self.whole, self.spot = net, own, whole, spot
        self.rows = own.shape[0]
        self.half = self.rows // 2
        self.width = own.shape[1]
        self.out = net.out()
        self.first = [net.into() for _ in range(2)]
        self.rings = {(color, i): net.into() for color in range(2) for i in (0, 1, -1, -2)}
        self.last = [net.into() for _ in range(2)]
        net.later(self.gone)

    def gone(self):
        if self.out is not None:
            rows = self.whole.shape[0] // 16 * 15
            self.net.gone(self.out, self.whole.at[pl.ds(0, rows)])
            self.out = None

    def view(self, color, i, j, part=None):
        place = self.net.place
        first, second = self.axes(color)
        a, b = place.step(first, i), place.step(second, j)
        row, columns = self.spot(a, b) if color == 0 else self.spot(b, a)
        start = row + color * self.half
        if part is None:
            return self.whole.at[pl.ds(pl.multiple_of(start, self.half), self.half), columns]
        size = self.half // 2
        return self.whole.at[pl.ds(pl.multiple_of(start + part * size, size), size), columns]

    def bytes_of(self, halves):
        return self.whole.at[pl.ds(0, halves * self.half), pl.ds(0, self.width)]

    @staticmethod
    def axes(color):
        return ("z", "y") if color == 0 else ("y", "z")

    def mine(self, color):
        return self.own.at[pl.ds(color * self.half, self.half)]

    def ring(self, color, i):
        axis = self.axes(color)[1]
        refs = lambda: (
            self.mine(color) if i == 0 else self.view(color, i, 0), self.view(color, i, 0)
        )
        for by in (1, -1):
            self.net.send(refs, self.out, self.rings[color, i], axis, by)

    def start(self):
        for color in range(2):
            axis = self.axes(color)[0]
            refs = lambda color=color: (self.mine(color), self.view(color, 0, 0))
            for by in (1, -1, 2):
                self.net.send(refs, self.out, self.first[color], axis, by)
        for color in range(2):
            self.ring(color, 0)
        self.kept = self.net.local(self.place_here)

    def place_here(self):
        row, columns = self.spot(self.net.place.z, self.net.place.y)
        return self.own, self.whole.at[pl.ds(pl.multiple_of(row, self.rows), self.rows), columns]

    def spread(self):
        for color in range(2):
            self.net.here(self.first[color], self.bytes_of(3) if self.fits(3) else self.thin(3))
        for i in (-1, 1, -2):
            for color in range(2):
                self.ring(color, i)

    def fits(self, halves):
        return halves * self.half <= self.whole.shape[0]

    def thin(self, halves):
        return self.whole.at[pl.ds(0, self.half), pl.ds(0, halves * self.width)]

    def forward(self, steps=(0, 1, -1, -2)):
        for i in steps:
            for color in range(2):
                axis = self.axes(color)[1]
                self.net.here(self.rings[color, i], self.bytes_of(2))
                for j, part, by in ((-1, 0, 1), (1, 1, -1)):
                    refs = lambda color=color, i=i, j=j, part=part: (
                        self.view(color, i, j, part),
                    ) * 2
                    self.net.send(refs, self.out, self.last[color], axis, by)

    def here(self):
        for color in range(2):
            self.net.here(self.last[color], self.bytes_of(4) if self.fits(4) else self.thin(4))
        self.kept.wait()


class PlaneSum:
    OUT, INTO = 2, 18

    def __init__(self, net, whole, spot, land, last):
        self.net, self.whole, self.spot, self.land, self.last = net, whole, spot, land, last
        self.size = land.shape[3]
        self.ring_out, self.last_out = net.out(), net.out()
        ways = [(color, k) for color in range(2) for k in range(RING)]
        self.through = {way: net.into() for way in ways}
        self.sides = {way: net.into() for way in ways}
        self.ends = [net.into() for _ in range(2)]
        net.later(lambda: net.gone(self.ring_out, land))
        net.later(lambda: net.gone(self.last_out, last))

    @staticmethod
    def axes(color):
        return ("y", "z") if color == 0 else ("z", "y")

    def own(self, color, n, k, part):
        place = self.net.place
        first, second = self.axes(color)
        a, b = place.step(first, n), place.step(second, k)
        row, columns = self.spot(b, a) if color == 0 else self.spot(a, b)
        start = row + (color * 2 + part) * self.size
        return self.whole.at[pl.ds(pl.multiple_of(start, self.size), self.size), columns]

    def slot(self, color, k, n):
        return self.land.at[color, k % RING, n]

    def end(self, color, k, part):
        return self.last.at[color, k % RING - 1, part]

    def start(self):
        for k in (2, 1, -1, 0):
            for color in range(2):
                axis = self.axes(color)[0]
                through, sides = self.through[color, k % RING], self.sides[color, k % RING]
                for n, part, slot, into, by in (
                    (2, 0, 0, through, 1), (2, 1, 1, through, -1),
                    (1, 1, 3, sides, 1), (-1, 0, 4, sides, -1),
                ):
                    refs = lambda color=color, k=k, n=n, part=part, slot=slot: (
                        self.own(color, n, k, part), self.slot(color, k, slot)
                    )
                    self.net.send(refs, self.ring_out, into, axis, by)

    def forward(self, steps=(2, 1, -1, 0)):
        for k in steps:
            for color in range(2):
                axis = self.axes(color)[0]
                sides = self.sides[color, k % RING]
                self.net.here(
                    self.through[color, k % RING], self.land.at[color, k % RING, pl.ds(0, 2)]
                )
                for slot, n, part, target, by in ((0, 1, 0, 2, 1), (1, -1, 1, 5, -1)):
                    here = self.slot(color, k, slot)
                    here[...] = here[...] + self.own(color, n, k, part)[...]
                    refs = lambda color=color, k=k, slot=slot, target=target: (
                        self.slot(color, k, slot), self.slot(color, k, target)
                    )
                    self.net.send(refs, self.ring_out, sides, axis, by)

    def gather(self, steps=(2, 1, -1, 0)):
        for k in steps:
            for color in range(2):
                second = self.axes(color)[1]
                self.net.here(
                    self.sides[color, k % RING], self.land.at[color, k % RING, pl.ds(2, 4)]
                )
                for part in range(2):
                    here = self.slot(color, k, 2 + part)
                    total = self.own(color, 0, k, part)[...].astype(F32) + here[...].astype(F32)
                    total = total + self.slot(color, k, 4 + part)[...].astype(F32)
                    here[...] = total.astype(BF16)
                    if k != 0:
                        refs = lambda color=color, k=k, part=part: (
                            self.slot(color, k, 2 + part), self.end(color, k, part)
                        )
                        self.net.send(refs, self.last_out, self.ends[color], second, k)

    def finish(self, total):
        for color in range(2):
            self.net.here(self.ends[color], self.last.at[color])
            for part in range(2):
                value = self.slot(color, 0, 2 + part)[...].astype(F32)
                for k in (1, -1, 2):
                    value = value + self.end(color, k, part)[...].astype(F32)
                start = (color * 2 + part) * self.size
                total[pl.ds(start, self.size)] = value.astype(total.dtype)


def plane_scratch(rows, columns):
    return (
        pltpu.VMEM((2, 4, 6, rows // 4, columns), BF16),
        pltpu.VMEM((2, 3, 2, rows // 4, columns), BF16),
    )


class Turn:
    def __init__(self, net, pairs):
        self.net = net
        self.pairs = [
            (source, target, net.out(), net.into(), net.local_number()) for source, target in pairs
        ]

    def copies(self):
        return [self.net.copy(a, b, out, into, "turn") for a, b, out, into, _ in self.pairs]

    def kept(self):
        sems = self.net.local_sems
        return [pltpu.make_async_copy(a, b, sems.at[index]) for a, b, _, _, index in self.pairs]

    def both(self, act):
        @pl.when(jnp.logical_not(self.net.place.native))
        def _():
            for copy in self.copies():
                act(copy)

        @pl.when(self.net.place.native)
        def _():
            for copy in self.kept():
                act(copy)

    def start(self):
        self.both(lambda copy: copy.start())

    def wait(self):
        self.both(lambda copy: copy.wait())


class Give:
    def __init__(self, net, refs, there):
        self.net, self.there = net, there
        self.out, self.into = net.out(), net.into()
        net.send(refs, self.out, self.into, "core")
        net.later(lambda: net.gone(self.out, refs()[0]))

    def wait(self):
        self.net.here(self.into, self.there())


def parts_of(source, target, count):
    rows = source.shape[0] // count
    spots = [pl.ds(part * rows, rows) for part in range(count)]
    return [(source.at[spot], target.at[spot]) for spot in spots]


class GainsGather:
    OUT, INTO, LOCALS = 1, 4, 1

    def __init__(self, net, own, whole):
        self.net, self.own, self.whole = net, own, whole
        self.out = net.out()
        self.into = [net.into() for _ in range(4)]
        net.later(lambda: net.gone(self.out, whole.at[pl.ds(0, 127)]))

    def rows(self, z, y, x, core, count):
        start = ((z * RING + y) * RING + x) * 2 + core
        return self.whole.at[pl.ds(start if count == 1 else pl.multiple_of(start, count), count)]

    def spot(self, axis, by):
        place = self.net.place
        if axis == "core":
            return self.rows(place.z, place.y, place.x, (place.core + by) % 2, 1)
        if axis == "x":
            return self.rows(place.z, place.y, place.step("x", by), 0, 2)
        if axis == "y":
            return self.rows(place.z, place.step("y", by), 0, 0, 8)
        return self.rows(place.step("z", by), 0, 0, 0, 32)

    def steps(self):
        net = self.net
        net.local(lambda: (self.own, self.spot("core", 0))).wait()
        for into, axis, count in zip(self.into, ("core", "x", "y", "z"), (1, 2, 8, 32)):
            ways = (1,) if axis == "core" else (1, -1, 2)
            for by in ways:
                net.send(lambda axis=axis: (self.spot(axis, 0),) * 2, self.out, into, axis, by)
            yield
            net.here(into, self.whole.at[pl.ds(0, count * len(ways))])
        yield


class GainsSum(GainsGather):
    def __init__(self, net, whole, total, land):
        super().__init__(net, None, whole)
        self.total, self.land = total, land

    def steps(self):
        net, land = self.net, self.land
        first = 0
        for into, axis, count in zip(self.into, ("z", "y", "x", "core"), (32, 8, 2, 1)):
            ways = (1,) if axis == "core" else (1, -1, 2)
            spots = [pl.ds(first + n * count, count) for n in range(len(ways))]
            for spot, by in zip(spots, ways):
                refs = lambda axis=axis, spot=spot, by=by: (self.spot(axis, by), land.at[spot])
                net.send(refs, self.out, into, axis, by)
            yield
            net.here(into, land.at[pl.ds(first, count * len(ways))])
            value = self.spot(axis, 0)[...]
            for spot in spots:
                value = value + land[spot]
            if axis == "core":
                self.total[...] = value
            else:
                self.spot(axis, 0)[...] = value
            first += count * len(ways)
        yield


class Kernel:
    def __init__(self, number, plans, gives, turns, locals_, partners):
        self.number, self.partners = number, partners
        extra = gives + turns
        self.sems = (
            sum(plan.OUT for plan in plans) + extra,
            sum(plan.INTO for plan in plans) + extra,
            sum(getattr(plan, "LOCALS", 0) for plan in plans) + turns + locals_,
        )

    def __call__(self, body, arrays, outs, scratch=()):
        n_in, n_out, n_scratch = len(arrays), len(outs), len(scratch)

        def kernel(*refs):
            net = Net(Place(), self.partners, *refs[n_in + n_out + n_scratch :])
            net.greet()
            body(
                net,
                refs[:n_in],
                refs[n_in : n_in + n_out],
                refs[n_in + n_out : n_in + n_out + n_scratch],
            )
            net.finish()
            assert (net.leaving, net.arriving, net.local_count) == self.sems, (
                net.leaving, net.arriving, net.local_count, self.sems,
            )

        return pl.pallas_call(
            kernel,
            out_shape=[shape for shape, _ in outs],
            in_specs=[pl.BlockSpec(memory_space=space) for _, space in arrays],
            out_specs=[pl.BlockSpec(memory_space=space) for _, space in outs],
            scratch_shapes=[*scratch] + [pltpu.SemaphoreType.DMA((n,)) for n in self.sems],
            compiler_params=pltpu.CompilerParams(
                collective_id=self.number, has_side_effects=True, vmem_limit_bytes=62 * 2**20
            ),
            name="links_%d" % self.number,
        )(*[array for array, _ in arrays])


CORE_PARTNER = (("core", 1),)
X_PARTNERS = (("x", 1), ("x", -1))
FAR_X = (("x", 2),)
PLANE_PARTNERS = (("y", 1), ("y", -1), ("y", 2), ("z", 1), ("z", -1), ("z", 2))
TURN_PARTNERS = (("turn", 1),)


def shape(dims, dtype=BF16):
    return jax.ShapeDtypeStruct(dims, dtype)


def attention_spot(z, y):
    piece = z * 4 + lax.rem(y, 2) * 2 + lax.div(y, 2)
    return piece * 128


def rows_spot(z, y):
    return attention_spot(z, y), pl.ds(0, 512)


def output_spot(z, y):
    return 0, pl.ds(pl.multiple_of(attention_spot(z, y), 128), 128)


def gateup_spot(z, y):
    columns = pl.ds(pl.multiple_of(lax.div(y, 2) * 384, 128), 384)
    return (z * 2 + lax.rem(y, 2)) * 256, columns


def down_spot(z, y):
    columns = pl.ds(pl.multiple_of((z * 2 + lax.rem(y, 2)) * 256, 128), 256)
    return lax.div(y, 2) * 384, columns


def nn(left, right):
    return lax.dot_general(left, right, (((1,), (0,)), ((), ())), preferred_element_type=F32)


def nt(left, right):
    return lax.dot_general(left, right, (((1,), (1,)), ((), ())), preferred_element_type=F32)


def tn(left, right):
    return lax.dot_general(left, right, (((0,), (0,)), ((), ())), preferred_element_type=F32)


def exact(left, right):
    return lax.dot_general(
        left, right, (((1,), (0,)), ((), ())),
        precision=lax.Precision.HIGHEST, preferred_element_type=F32,
    )


def inverse_root(rows):
    return lax.rsqrt(jnp.mean(rows * rows, axis=-1, keepdims=True) + EPSILON)


def norm_back(rows, gain, upstream):
    root = inverse_root(rows)
    weighted = upstream * gain
    meant = jnp.mean(weighted * rows, axis=-1, keepdims=True)
    return root * weighted - rows * (root * root * root * meant), upstream * rows * root


def rope_tables():
    halves = np.arange(HEAD_SIZE // 2, dtype=np.float64)
    angles = np.arange(GROUP_TOK)[:, None] * ROPE_BASE ** (-2.0 * halves / HEAD_SIZE)[None, :]
    angles = np.concatenate([angles, angles], axis=1)
    return np.cos(angles).astype(np.float32), np.sin(angles).astype(np.float32)


def owner_starts(dims, axis):
    row = lax.broadcasted_iota(jnp.int32, dims, axis)
    z, y, x, core = row >> 5, (row >> 3) & 3, (row >> 1) & 3, row & 1
    return (z * 32 + (y & 1) * 16 + core * 8 + (y >> 1) * 4 + x) * OWN_GAINS


def column_of(entry):
    return entry - jnp.floor((entry.astype(F32) + 0.5) * (1.0 / OWN_GAINS)).astype(jnp.int32) * OWN_GAINS


def gains_flat(rows):
    entry = lax.broadcasted_iota(jnp.int32, (128, GAINS), 1)
    past = entry - owner_starts((128, GAINS), 0)
    owner = ((past >= 0) & (past < OWN_GAINS)).astype(F32)
    columns = lax.dot_general(
        rows, owner, (((0,), (0,)), ((), ())),
        precision=lax.Precision.HIGHEST, preferred_element_type=F32,
    )
    place = lax.broadcasted_iota(jnp.int32, (128, GAINS), 0)
    return jnp.sum(jnp.where(column_of(entry) == place, columns, 0.0), axis=0, keepdims=True)


class Documents:
    def __init__(self, lengths):
        lengths = [lengths[0:1, n : n + 1] for n in range(4)]
        self.ends = [lengths[0], lengths[0] + lengths[1], lengths[0] + lengths[1] + lengths[2]]

    def pick(self, place, values):
        value = jnp.where(place >= self.ends[0], values[1], values[0])
        value = jnp.where(place >= self.ends[1], values[2], value)
        return jnp.where(place >= self.ends[2], values[3], value)

    def first(self, place):
        zero = jnp.zeros_like(self.ends[0])
        return self.pick(place, [zero] + self.ends)


def allowed_pairs(documents, first_row, rows, keys):
    query = lax.broadcasted_iota(jnp.int32, (rows, 1), 0) + first_row
    key = lax.broadcasted_iota(jnp.int32, (rows, keys), 1)
    return (key >= documents.first(query)) & (key <= query)


def unit_off(n):
    return lax.rem(n + lax.div(n, 2), 4) + 2 * lax.div(n, 3)


class Units:
    ORDER = (0, 1, -1, 2)

    def __init__(self, place):
        self.x = place.x

    def chip(self, n):
        return lax.rem(self.x + unit_off(n), RING)

    def rows(self, n):
        return pl.ds(pl.multiple_of(self.chip(n) * 256, 256), 256)

    def true_rows(self, n, core):
        return pl.ds(pl.multiple_of((core * RING + self.chip(n)) * 128, 128), 128)


def own_half(length, core):
    return pl.ds(pl.multiple_of(core * length, 128), length)


def attention_forward(
    tokens, cotangent, query, keyval, output, gateup, down, gains, lengths, cosine, sine
):
    def body(net, ins, outs, work):
        (
            tokens_, cotangent_, query_, keyval_, output_, gateup_, down_, gains_, lengths_,
            cosine_, sine_,
        ) = ins
        (
            residual_, tokens_here, normed_, raw_, heads_, attended_, totals_,
            cosine_out, sine_out, qkv_out, output_out, gate_out, up_out, down_piece,
            cotangent_all, flat_, lengths_out,
        ) = outs
        (
            gathered, normed, qkv_w, output_w, qkv_cast, output_cast, qkv_piece, output_piece,
            gains_row, gains_rows, lengths_mine, lengths_there, gate_cast, up_cast, down_cast,
            gate_piece, up_piece, cotangent_here, terms, landed, land,
        ) = work
        place = net.place
        units = Units(place)
        mine, theirs = place.core, 1 - place.core

        qkv_cast[:, 0:256] = query_[...].astype(BF16)
        qkv_cast[:, 256:384] = keyval_[0].astype(BF16)
        qkv_cast[:, 384:512] = keyval_[1].astype(BF16)
        output_cast[...] = output_[...].astype(BF16)
        gains_row[0] = jnp.zeros((1, 128), F32)
        gains_row[0, 0:1, 0:OWN_GAINS] = gains_[...]
        lengths_mine[...] = jnp.zeros((8, 128), jnp.int32)
        lengths_mine[0:1, 0:4] = lengths_[...]
        net.enter()
        qkv_turn = Turn(net, [(qkv_cast, qkv_piece)])
        output_turn = Turn(net, [(output_cast, output_piece)])
        rows = [Turn(net, [pair]) for pair in parts_of(tokens_, tokens_here, 2)]
        upstream = Turn(net, parts_of(cotangent_, cotangent_here, 2))
        qkv_turn.start()
        for part in rows:
            part.start()
        qkv_gather = PlaneGather(net, qkv_piece, qkv_w, rows_spot)
        output_gather = PlaneGather(net, output_piece, output_w, output_spot)
        gate_gather = PlaneGather(net, gate_piece, gate_out, gateup_spot)
        up_gather = PlaneGather(net, up_piece, up_out, gateup_spot)
        gather = RowsGather(net, tokens_here, gathered)
        later = RowsGather(net, cotangent_here, cotangent_all)
        length_copy = Give(net, lambda: (lengths_mine, lengths_there), lambda: lengths_there)
        gains_steps = GainsGather(net, gains_row, gains_rows).steps()
        next(gains_steps)

        halves = []
        for n, (cast, piece) in enumerate(((gate_cast, gate_piece), (up_cast, up_piece))):
            spot = own_half(128, mine)
            piece[spot] = gateup_[n, :, own_half(384, mine)].astype(BF16)
            cast[...] = gateup_[n, :, own_half(384, theirs)].astype(BF16)
            halves.append(Give(
                net,
                lambda cast=cast, piece=piece: (cast, piece.at[own_half(128, mine)]),
                lambda piece=piece: piece.at[own_half(128, theirs)],
            ))
        down_piece[:, own_half(128, mine)] = down_[own_half(384, mine)].astype(BF16)
        down_cast[...] = down_[own_half(384, theirs)].astype(BF16)
        halves.append(Give(
            net,
            lambda: (down_cast, down_piece.at[:, own_half(128, mine)]),
            lambda: down_piece.at[:, own_half(128, theirs)],
        ))

        qkv_turn.wait()
        qkv_gather.start()
        output_turn.start()
        for n, part in enumerate(rows):
            part.wait()
            gather.start((n,))
        upstream.start()
        next(gains_steps)

        length_copy.wait()
        lengths_out[...] = jnp.where(place.native, lengths_mine[...], lengths_there[...])
        documents = Documents(lengths_out[...])
        zero = jnp.zeros((1, 1), jnp.int32)
        starts = [zero] + documents.ends
        everywhere = lax.broadcasted_iota(jnp.int32, (1, GROUP_TOK), 1)
        hits = jnp.concatenate(
            [(everywhere == start).astype(F32) for start in starts] * 2, axis=0
        )
        start_cosine = exact(hits, cosine_[...])
        start_sine = exact(hits, sine_[...])
        sign = jnp.where(lax.broadcasted_iota(jnp.int32, (1, HEAD_SIZE), 1) < 64, -1.0, 1.0)

        def table(n):
            spot = pl.ds(pl.multiple_of(n * 256, 256), 256)
            where = lax.broadcasted_iota(jnp.int32, (256, 1), 0) + n * 256
            cosine_by = documents.pick(where, [start_cosine[n : n + 1] for n in range(4)])
            sine_by = documents.pick(where, [start_sine[n : n + 1] for n in range(4)])
            cosine_out[spot] = cosine_[spot] * cosine_by + sine_[spot] * sine_by
            sine_out[spot] = (sine_[spot] * cosine_by - cosine_[spot] * sine_by) * sign

        staged(4, table)
        qkv_gather.spread()
        output_turn.wait()
        output_gather.start()
        next(gains_steps)
        gather.near_first()
        for half in halves:
            half.wait()
        next(gains_steps)
        qkv_gather.forward()
        output_gather.spread()
        gate_gather.start()
        next(gains_steps)
        flat_[...] = gains_flat(gains_rows[...].reshape(128, 128))
        gain_query = flat_[0:1, 4096:4224]
        gain_key = flat_[0:1, 4224:4352]

        def normalize(n):
            rows_in = gathered[units.rows(n)].astype(F32)
            normed[units.rows(n)] = (
                rows_in * inverse_root(rows_in) * flat_[0:1, 0:2048]
            ).astype(BF16)

        def near():
            gather.near_second()
            gather.here(1)

        def far():
            gather.far()
            output_gather.forward()
            up_gather.start()
            upstream.wait()
            later.start()
            gather.here(2)

        staged(4, normalize, {
            0: lambda: gather.here(0), 1: near, 2: lambda: gather.here(-1), 3: far,
        })
        qkv_gather.here()
        stores = [net.local(lambda: (normed, normed_)), net.local(lambda: (qkv_w, qkv_out))]

        def project(n):
            parts = nn(normed[units.rows(n)], qkv_w[...])
            for core in range(2):
                spot = units.true_rows(n, core)
                part = parts[core * 128 : core * 128 + 128]
                raw_[spot] = part[:, 0:384]
                heads_[spot, 384:512] = part[:, 384:512].astype(BF16)
                for head in range(3):
                    columns = slice(head * 128, head * 128 + 128)
                    value = part[:, columns]
                    value = value * inverse_root(value) * (gain_key if head == 2 else gain_query)
                    turned = value * cosine_out[spot] + pltpu.roll(value, 64, 1) * sine_out[spot]
                    heads_[spot, columns] = turned.astype(BF16)

        staged(4, project)
        gate_gather.spread()

        def attend(block):
            keys = 256 * (block + 1)
            spot = slice(block * 256, block * 256 + 256)

            def one(head):
                columns = own_half(128, head)
                scores = nt(heads_[spot, columns], heads_[0:keys, 256:384])
                allowed = allowed_pairs(documents, block * 256, 256, keys)
                scores = jnp.where(allowed, scores, -1e30)
                highest = jnp.max(scores, axis=-1, keepdims=True)
                weights_ = jnp.exp((scores - highest) * SCALE)
                summed = jnp.sum(weights_, axis=-1, keepdims=True)
                probability = (weights_ * (1.0 / summed)).astype(BF16)
                attended_[spot, columns] = nn(probability, heads_[0:keys, 384:512]).astype(BF16)
                lane = lax.broadcasted_iota(jnp.int32, (1, 128), 1)
                ours = (lane >= head * 64) & (lane < head * 64 + 64)
                totals_[spot] = jnp.where(ours, highest * SCALE + jnp.log(summed), totals_[spot])

            staged(2, one)

        attend(0)
        attend(1)
        later.near_first()
        up_gather.spread()
        attend(2)
        output_gather.here()
        stores.append(net.local(lambda: (output_w, output_out)))
        attend(3)
        sums = RowsSum(net, terms, landed, land)

        def out(n):
            n = 3 - n
            own = jnp.concatenate(
                [attended_[units.true_rows(n, 0)], attended_[units.true_rows(n, 1)]], axis=0
            )
            terms[units.rows(n)] = nn(own, output_w[...]).astype(BF16)

        def passed(k, ready=None, go=None):
            def act():
                sums.pass_over(k)
                if ready is not None:
                    sums.combine(ready)
                    go()

            return act

        later.near_second()
        staged(4, out, None, {
            0: passed(2),
            1: passed(-1, 2, sums.start_far),
            2: passed(1, -1, sums.start_left),
            3: passed(0, 1, sums.start_right),
        })
        later.far()
        gate_gather.forward()
        sums.combine(0)
        sums.forward()
        up_gather.forward()
        for k in (0, 1, -1, 2):
            later.here(k)

        def keep(spot, value):
            residual_[spot] = value + tokens_here[spot].astype(F32)

        sums.finish(keep)
        gate_gather.here()
        up_gather.here()
        for store in stores:
            store.wait()

    plans = (GainsGather,) + 4 * (PlaneGather,) + 2 * (RowsGather,) + (RowsSum,)
    return Kernel(
        0, plans, 4, 6, 3, CORE_PARTNER + X_PARTNERS + FAR_X + PLANE_PARTNERS + TURN_PARTNERS
    )(
        body,
        [
            (tokens, VMEM), (cotangent, VMEM), (query, VMEM), (keyval, VMEM), (output, VMEM),
            (gateup, VMEM), (down, VMEM), (gains, VMEM), (lengths, VMEM),
            (cosine, VMEM), (sine, VMEM),
        ],
        [
            (shape((128, 2048), F32), VMEM),
            (shape((128, 2048)), VMEM),
            (shape((1024, 2048)), HBM),
            (shape((1024, 384), F32), VMEM),
            (shape((1024, 512)), VMEM),
            (shape((1024, 256)), VMEM),
            (shape((1024, 128), F32), VMEM),
            (shape((1024, 128), F32), VMEM),
            (shape((1024, 128), F32), VMEM),
            (shape((2048, 512)), HBM),
            (shape((256, 2048)), HBM),
            (shape((2048, 768)), HBM),
            (shape((2048, 768)), HBM),
            (shape((384, 256)), VMEM),
            (shape((1024, 2048)), HBM),
            (shape((1, GAINS), F32), VMEM),
            (shape((8, 128), jnp.int32), VMEM),
        ],
        (
            pltpu.VMEM((1024, 2048), BF16),
            pltpu.VMEM((1024, 2048), BF16),
            pltpu.VMEM((2048, 512), BF16),
            pltpu.VMEM((256, 2048), BF16),
            pltpu.VMEM((128, 512), BF16),
            pltpu.VMEM((256, 128), BF16),
            pltpu.VMEM((128, 512), BF16),
            pltpu.VMEM((256, 128), BF16),
            pltpu.VMEM((1, 1, 128), F32),
            pltpu.VMEM((128, 1, 128), F32),
            pltpu.VMEM((8, 128), jnp.int32),
            pltpu.VMEM((8, 128), jnp.int32),
            pltpu.VMEM((128, 384), BF16),
            pltpu.VMEM((128, 384), BF16),
            pltpu.VMEM((384, 128), BF16),
            pltpu.VMEM((256, 384), BF16),
            pltpu.VMEM((256, 384), BF16),
            pltpu.VMEM((128, 2048), BF16),
            pltpu.VMEM((1024, 2048), BF16),
        )
        + ROWS_SCRATCH,
    )


def layer_backward(
    residual, tokens, gains, lengths, down, cotangent_all, gate, up, heads, raw, attended,
    totals, cosine, sine, qkv, output, normed,
):
    def body(net, ins, outs, work):
        (
            residual_, tokens_, gains_, lengths_, down_, cotangent_all_, gate_, up_,
            heads_, raw_, attended_, totals_, cosine_, sine_, qkv_, output_, normed_,
        ) = ins
        (
            block_own, input_own, qkv_own, output_own, gate_own, up_own, down_own, gains_own,
        ) = outs
        (
            low, second, upstream, qkv_w, output_w, gate_w, up_w, down_w, hidden, gate_low, up_low,
            terms, back_rows, raw_here, totals_here, cosine_here, sine_here, key_sum, value_sum,
            own_out, qkv_total, output_total, gate_total, up_total, down_total,
            gain_rows, gain_land, first_gain, query_gain, flat, landed, land,
            gate_land, gate_last, up_land, up_last, down_land, down_last,
            qkv_land, qkv_last, output_land, output_last, free,
            early_landed, early_land, late_landed, late_land,
        ) = work
        share_landed, share_land = (early_landed, late_landed), (early_land, late_land)
        place = net.place
        units = Units(place)
        mine, theirs = place.core, 1 - place.core

        def load(source, target):
            return net.local(lambda: (source, target))

        loads = {
            "gate": load(gate_, gate_w),
            "up": load(up_, up_w),
            "upstream": load(cotangent_all_, upstream),
            "output": load(output_, output_w),
            "qkv": load(qkv_, qkv_w),
            "raw": load(raw_, raw_here),
            "totals": load(totals_, totals_here),
            "cosine": load(cosine_, cosine_here),
            "sine": load(sine_, sine_here),
        }
        second_gain = gains_[0:1, 2048:4096]

        def second_norm(n):
            spot = pl.ds(pl.multiple_of(n * 64, 64), 64)
            rows = residual_[spot]
            low[spot] = (rows * inverse_root(rows) * second_gain).astype(BF16)

        staged(2, second_norm)
        net.enter()
        gather = RowsGather(net, low, second)
        gather.start()
        down_gather = PlaneGather(net, down_, down_w, down_spot)
        down_gather.start()
        sums = RowsSum(net, terms, landed, land)
        mlp_sum = RowsSum(net, second, landed, land)
        first_sums = [
            RowsSum(
                net, upstream, share_landed[share], share_land[share], share, 2,
            )
            for share in range(2)
        ]
        last_gather = RowsGather(net, low, terms)
        gate_sum = PlaneSum(net, gate_w, gateup_spot, gate_land, gate_last)
        up_sum = PlaneSum(net, up_w, gateup_spot, up_land, up_last)
        down_sum = PlaneSum(net, down_w, down_spot, down_land, down_last)
        qkv_sum = PlaneSum(net, qkv_w, rows_spot, qkv_land, qkv_last)
        output_sum = PlaneSum(net, output_w, output_spot, output_land, output_last)

        def forth(n):
            spot = units.rows(n)
            gate_value = nn(second[spot], gate_w[...])
            upward = nn(second[spot], up_w[...])
            sigmoid = 1.0 / (1.0 + jnp.exp(-gate_value))
            active = gate_value * sigmoid
            hidden[spot] = (active * upward).astype(BF16)
            gate_low[spot] = (upward * (sigmoid + active * (1.0 - sigmoid))).astype(BF16)
            up_low[spot] = active.astype(BF16)

        between = {
            1: lambda: (sums.combine(2), sums.start_far()),
            2: lambda: (sums.combine(-1), sums.start_left()),
            3: lambda: (sums.combine(1), sums.start_right()),
        }

        def back(n):
            spot = units.rows(3 - n)
            hidden_grad = nt(upstream[spot], down_w[...])
            gate_low[spot] = (hidden_grad * gate_low[spot].astype(F32)).astype(BF16)
            up_low[spot] = (hidden_grad * up_low[spot].astype(F32)).astype(BF16)
            at_step(between, n)
            terms[spot] = (nt(gate_low[spot], gate_w[...]) + nt(up_low[spot], up_w[...])).astype(
                BF16
            )

        def begin():
            for name in ("gate", "up", "upstream"):
                loads[name].wait()
            gather.here(0)

        def near():
            gather.near_first()
            down_gather.spread()
            gather.near_second()
            gather.here(1)

        def far():
            down_gather.forward()
            gather.far()
            gather.here(2)

        staged(4, forth, {0: begin, 1: near, 2: lambda: gather.here(-1), 3: far})
        down_gather.here()
        staged(4, back, None, {
            0: lambda: sums.pass_over(2), 1: lambda: sums.pass_over(-1),
            2: lambda: sums.pass_over(1), 3: lambda: sums.pass_over(0),
        })
        sums.combine(0)
        sums.passed()
        for axis, by in CORE_PARTNER + X_PARTNERS:
            pl.semaphore_signal(
                free, inc=1, device_id=place.device(axis, by), device_id_type=pl.DeviceIdType.MESH
            )
        sums.forward()
        gain_parts = []

        def weight_grad(low_grad, target):
            def one(n):
                columns = own_half(256, n)
                target[columns] = tn(second[:, columns], low_grad[...]).astype(BF16)

            return one

        staged(8, weight_grad(gate_low, gate_w))
        gate_sum.start()
        staged(8, weight_grad(up_low, up_w))
        up_sum.start()
        gather.gone()
        down_gather.gone()

        def own_rows(spot):
            start = (place.x * 2 + place.core) * 128 + spot.start
            return pl.ds(pl.multiple_of(start, 64), 64)

        def keep(spot, value):
            through_, gain_part = norm_back(residual_[spot], second_gain, value)
            through_ = through_ + upstream[own_rows(spot)].astype(F32)
            back_rows[spot] = through_
            low[spot] = through_.astype(BF16)
            gain_parts.append(jnp.sum(gain_part, axis=0, keepdims=True))

        sums.finish(keep)
        sums.departed()
        pl.semaphore_wait(free, 3)
        last_gather.start()

        def through(n):
            spot = units.rows(n)
            second[spot] = nn(hidden[spot], down_w[...]).astype(BF16)

        staged(4, through)

        def down_grad(n):
            columns = own_half(256, n)
            down_w[columns] = tn(hidden[:, columns], upstream[...]).astype(BF16)

        staged(3, down_grad)
        down_sum.start()
        last_gather.near_first()
        heads_cols, attended_cols = hidden.at[:, 0:512], hidden.at[:, 512:768]
        parts, attended_grad = gate_low.at[:, 0:512], gate_low.at[:, 512:768]
        attended_rows = up_low.at[:, 0:256]
        loads["heads"] = load(heads_, heads_cols)
        loads["attended"] = load(attended_, attended_cols)
        gate_sum.forward()
        loads["output"].wait()
        key_sum[...] = jnp.zeros_like(key_sum)
        value_sum[...] = jnp.zeros_like(value_sum)
        query_gain[...] = jnp.zeros_like(query_gain)
        for name in ("heads", "raw", "totals", "cosine", "sine"):
            loads[name].wait()
        documents = Documents(lengths_[...])
        gain_query, gain_key = gains_[0:1, 4096:4224], gains_[0:1, 4224:4352]

        def through_rope(value, cosine_part, sine_part, raw_part, gain):
            value = value * cosine_part + pltpu.roll(value * sine_part, 64, 1)
            through_, gain_part = norm_back(raw_part, gain, value)
            return through_.astype(BF16), jnp.sum(gain_part, axis=0, keepdims=True)

        def twice(value):
            return jnp.concatenate([value, value], axis=0)

        def both_heads(ref, spot, first):
            return jnp.concatenate(
                [ref[spot, first : first + 128], ref[spot, first + 128 : first + 256]], axis=0
            )

        def attend(n, core):
            spot = units.true_rows(n, core)
            keys = 512 * (core + 1)
            query = both_heads(hidden, spot, 0)
            upward = both_heads(gate_low, spot, 512)
            key, value = hidden[0:keys, 256:384], hidden[0:keys, 384:512]
            scores = nt(query, key) * SCALE
            total = jnp.concatenate([totals_here[spot, 0:1], totals_here[spot, 64:65]], axis=0)
            allowed = allowed_pairs(documents, spot.start, 128, keys)
            probability = jnp.where(twice(allowed), jnp.exp(scores - total), 0.0)
            prob_grad = nt(upward, value)
            centre = jnp.sum(probability * prob_grad, axis=-1, keepdims=True)
            score_grad = (probability * (prob_grad - centre)).astype(BF16)
            value_sum[0:keys] += tn(probability.astype(BF16), upward)
            key_sum[0:keys] += tn(score_grad, query)
            query_grad = nn(score_grad, key) * SCALE
            through_, gain_part = through_rope(
                query_grad, twice(cosine_here[spot]), twice(sine_here[spot]),
                both_heads(raw_here, spot, 0), gain_query,
            )
            here = pl.ds(pl.multiple_of(units.chip(n) * 256 + core * 128, 128), 128)
            gate_low[here, 0:128] = through_[0:128]
            gate_low[here, 128:256] = through_[128:256]
            query_gain[...] += gain_part

        def enter(n):
            grad = nt(terms[units.rows(n)], output_w[...]).astype(BF16)
            for core in range(2):
                attended_grad[units.true_rows(n, core)] = grad[core * 128 : core * 128 + 128]
            for core in range(2):
                attend(n, core)

        def own_here():
            last_gather.here(0)
            for k in (2, 1, -1, 0):
                mlp_sum.pass_over(k)

        def combined():
            last_gather.near_second()
            last_gather.here(1)
            for k in (2, 1, -1, 0):
                mlp_sum.combine(k)

        def last_far():
            up_sum.forward()
            last_gather.far()
            mlp_sum.start_far()
            mlp_sum.start_right()
            mlp_sum.start_left()
            last_gather.here(2)

        staged(4, enter, {
            0: own_here, 1: combined, 2: lambda: last_gather.here(-1), 3: last_far,
        })
        mlp_sum.passed()
        loads["normed"] = load(normed_, second)
        loads["attended"].wait()

        def same_order(n):
            for core in range(2):
                start = pl.multiple_of(units.chip(n) * 256 + core * 128, 128)
                attended_rows[pl.ds(start, 128)] = attended_cols[units.true_rows(n, core)]

        staged(4, same_order)

        def output_grad(n):
            columns = own_half(512, n)
            output_w[:, columns] = tn(attended_rows[...], terms[:, columns]).astype(BF16)

        staged(4, output_grad)
        output_sum.start()
        gate_sum.gather()
        down_sum.forward()
        mlp_sum.forward()
        def key_back(true, gain_sum):
            spot = pl.ds(pl.multiple_of(true * 128, 128), 128)
            start = (lax.rem(true, RING) * 2 + lax.div(true, RING)) * 128
            through_, gain_part = through_rope(
                key_sum[spot] * SCALE, cosine_here[spot], sine_here[spot],
                raw_here[spot, 256:384], gain_key,
            )
            here = pl.ds(pl.multiple_of(start, 128), 128)
            gate_low[here, 256:384] = through_
            gate_low[here, 384:512] = value_sum[spot].astype(BF16)
            return gain_sum + gain_part

        key_gain = lax.fori_loop(0, 8, key_back, jnp.zeros((1, 128), F32))
        last_gather.gone()
        loads["tokens"] = load(tokens_, low)
        loads["qkv"].wait()
        loads["normed"].wait()
        up_sum.gather()
        first_gain[...] = jnp.zeros_like(first_gain)

        def out(n):
            spot = units.rows(3 - n)
            value = nt(parts[spot], qkv_w[...])
            upstream[spot] = value.astype(BF16)
            part = jnp.sum(value * second[spot].astype(F32), axis=0, keepdims=True)
            first_gain[...] += part

        early, late = first_sums

        def give(k):
            for one in first_sums:
                one.pass_over(k)

        staged(4, out, None, {
            0: lambda: give(2),
            1: lambda: (give(-1), early.combine(2), early.start_far()),
            2: lambda: (give(1), early.combine(-1), early.start_left()),
            3: lambda: (give(0), early.combine(1), early.start_right()),
        })
        output_sum.forward()

        def keep_block(spot, value):
            own_out[spot] = (residual_[spot] + value).astype(BF16)

        mlp_sum.finish(keep_block)
        block_turn = Turn(net, parts_of(own_out, block_own, 2))
        block_turn.start()

        def qkv_grad(n):
            columns = own_half(256, n)
            qkv_w[columns] = tn(second[:, columns], parts[...]).astype(BF16)

        staged(8, qkv_grad, None, {
            1: lambda: (late.combine(2), late.start_far(), early.combine(0)),
            3: lambda: (early.forward(), late.combine(-1), late.start_left()),
            5: lambda: (late.combine(1), late.start_right(), late.combine(0)),
        })
        qkv_sum.start()
        flat[...] = jnp.concatenate(
            [first_gain[...] / gains_[0:1, 0:2048], gain_parts[0] + gain_parts[1], query_gain[...], key_gain],
            axis=1,
        )

        def to_rows(n, total):
            entry = lax.broadcasted_iota(jnp.int32, (128, 256), 1) + n * 256
            past = entry - owner_starts((128, 256), 0)
            here = flat[0:1, own_half(256, n)]
            owned = jnp.where((past >= 0) & (past < OWN_GAINS), here, 0.0)
            place_ = lax.broadcasted_iota(jnp.int32, (128, 256), 0)
            column = (column_of(entry) == place_).astype(F32)
            return total + lax.dot_general(
                owned, column, (((1,), (1,)), ((), ())),
                precision=lax.Precision.HIGHEST, preferred_element_type=F32,
            )

        rows_of = lax.fori_loop(0, GAINS // 256, to_rows, jnp.zeros((128, 128), F32))
        gain_rows[...] = rows_of.reshape(128, 1, 128)
        late.forward()
        gains_steps = GainsSum(net, gain_rows, gains_own, gain_land).steps()
        next(gains_steps)

        halves = []

        def exchange(cut, there):
            halves.append(net.local(lambda: (cut(mine), there(mine))))
            halves.append(
                Give(net, lambda: (cut(theirs), there(mine)), lambda: there(theirs))
            )

        output_sum.gather()
        qkv_sum.forward()
        next(gains_steps)
        down_sum.gather()
        gate_sum.finish(gate_total)
        exchange(
            lambda core: gate_total.at[own_half(128, core)],
            lambda core: gate_own.at[:, own_half(384, core)],
        )
        output_sum.finish(output_total)
        output_turn = Turn(net, [(output_total, output_own)])
        output_turn.start()
        next(gains_steps)
        turns = []
        block_turn.wait()
        loads["tokens"].wait()

        def ended(share):
            def keep_first(spot, value):
                spot = pl.ds(64 * share + spot.start, 32)
                through_, _ = norm_back(low[spot].astype(F32), gains_[0:1, 0:2048], value)
                own_out[spot] = (back_rows[spot] + through_).astype(BF16)

            first_sums[share].finish(keep_first)
            spot = pl.ds(64 * share, 64)
            turns.append(Turn(net, [(own_out.at[spot], input_own.at[spot])]))
            turns[-1].start()

        ended(0)
        qkv_sum.gather()
        next(gains_steps)
        ended(1)
        qkv_sum.finish(qkv_total)
        qkv_turn = Turn(net, [(qkv_total, qkv_own)])
        qkv_turn.start()
        up_sum.finish(up_total)
        exchange(
            lambda core: up_total.at[own_half(128, core)],
            lambda core: up_own.at[:, own_half(384, core)],
        )
        down_sum.finish(down_total)
        exchange(
            lambda core: down_total.at[:, own_half(128, core)],
            lambda core: down_own.at[own_half(384, core)],
        )
        next(gains_steps)
        for copy in halves:
            copy.wait()
        for turn in (output_turn, *turns, qkv_turn):
            turn.wait()

    plans = (
        2 * (RowsGather,) + 4 * (RowsSum,) + (PlaneGather,) + 5 * (PlaneSum,) + (GainsSum,)
    )
    return Kernel(
        1, plans, 3, 6, 13 + 3 - 1, CORE_PARTNER + X_PARTNERS + FAR_X + PLANE_PARTNERS + TURN_PARTNERS
    )(
        body,
        [
            (residual, VMEM), (tokens, HBM), (gains, VMEM), (lengths, VMEM),
            (down, VMEM), (cotangent_all, HBM), (gate, HBM), (up, HBM), (heads, HBM), (raw, HBM),
            (attended, HBM), (totals, HBM), (cosine, HBM), (sine, HBM), (qkv, HBM), (output, HBM),
            (normed, HBM),
        ],
        [
            (shape((128, 2048)), HBM),
            (shape((128, 2048)), HBM),
            (shape((128, 512)), VMEM),
            (shape((256, 128)), VMEM),
            (shape((128, 768)), HBM),
            (shape((128, 768)), HBM),
            (shape((768, 128)), HBM),
            (shape((1, 1, 128), F32), VMEM),
        ],
        (
            pltpu.VMEM((128, 2048), BF16),
            pltpu.VMEM((1024, 2048), BF16),
            pltpu.VMEM((1024, 2048), BF16),
            pltpu.VMEM((2048, 512), BF16),
            pltpu.VMEM((256, 2048), BF16),
            pltpu.VMEM((2048, 768), BF16),
            pltpu.VMEM((2048, 768), BF16),
            pltpu.VMEM((768, 2048), BF16),
            pltpu.VMEM((1024, 768), BF16),
            pltpu.VMEM((1024, 768), BF16),
            pltpu.VMEM((1024, 768), BF16),
            pltpu.VMEM((1024, 2048), BF16),
            pltpu.VMEM((128, 2048), F32),
            pltpu.VMEM((1024, 384), F32),
            pltpu.VMEM((1024, 128), F32),
            pltpu.VMEM((1024, 128), F32),
            pltpu.VMEM((1024, 128), F32),
            pltpu.VMEM((1024, 128), F32),
            pltpu.VMEM((1024, 128), F32),
            pltpu.VMEM((128, 2048), BF16),
            pltpu.VMEM((128, 512), BF16),
            pltpu.VMEM((256, 128), BF16),
            pltpu.VMEM((256, 384), BF16),
            pltpu.VMEM((256, 384), BF16),
            pltpu.VMEM((384, 256), BF16),
            pltpu.VMEM((128, 1, 128), F32),
            pltpu.VMEM((127, 1, 128), F32),
            pltpu.VMEM((1, 2048), F32),
            pltpu.VMEM((1, 128), F32),
            pltpu.VMEM((1, GAINS), F32),
        )
        + ROWS_SCRATCH
        + plane_scratch(256, 384) * 2
        + plane_scratch(384, 256)
        + plane_scratch(128, 512)
        + plane_scratch(256, 128)
        + (pltpu.SemaphoreType.REGULAR,)
        + (pltpu.VMEM((4, 2, 32, 2048), BF16), pltpu.VMEM((6, 32, 2048), BF16)) * 2,
    )


def step_rates(total_tokens):
    root_tokens = math.sqrt(total_tokens)
    narrow = MODEL_WIDTH ** (-0.5)
    return (
        narrow / (2.0 * root_tokens),
        narrow / (2.0 * root_tokens),
        (QUERY_HEADS * HEAD_SIZE // 128) ** (-0.5) / (0.24 * root_tokens),
        narrow / (0.7 * root_tokens),
        FF ** (-0.5) / (1.2 * root_tokens),
        0.025 / root_tokens,
    )


def update(rows, gradients, state):
    rates = step_rates(GROUP_TOK * 16)

    def kernel(*refs):
        block_, input_, qkv_, output_, gate_, up_, down_, gains_ = refs[:8]
        masters, moments, averages = refs[8:14], refs[14:20], refs[20:26]
        outs = refs[26:]
        outs[0][...] = block_[...]
        outs[1][...] = input_[...]

        def one(n, gradient, spot):
            gradient = gradient.astype(F32)
            moment = MOMENTUM * moments[n][spot] + gradient
            master = masters[n][spot] - rates[n] * (gradient + MOMENTUM * moment)
            outs[2 + n][spot] = master
            outs[8 + n][spot] = moment
            outs[14 + n][spot] = AVERAGING * averages[n][spot] + (1.0 - AVERAGING) * master

        one(0, qkv_[:, 0:256], ...)
        one(1, qkv_[:, 256:384], 0)
        one(1, qkv_[:, 384:512], 1)
        one(2, output_[...], ...)
        one(3, gate_[...], 0)
        one(3, up_[...], 1)
        one(4, down_[...], ...)
        one(5, gains_[0, 0:1, 0:OWN_GAINS], ...)

    outs = [shape(a.shape, a.dtype) for a in rows]
    outs += [shape(a.shape, F32) for a in state]
    arrays = (*rows, *gradients, *state)
    return pl.pallas_call(
        kernel,
        out_shape=outs,
        in_specs=[pl.BlockSpec(memory_space=VMEM)] * len(arrays),
        out_specs=[pl.BlockSpec(memory_space=VMEM)] * len(outs),
        compiler_params=pltpu.CompilerParams(vmem_limit_bytes=61 * 2**20),
        name="update",
    )(*arrays)


def body(tokens, cotangent, doc_lengths, *state):
    query_weight, key_value_weight, output_weight, gateup_weight, down_weight, norm_gains = state[:6]
    cosine, sine = rope_tables()
    (
        residual, tokens_here, normed, raw, heads, attended, totals,
        cosine, sine, qkv, output, gate, up, down, cotangent_all, gains, lengths,
    ) = attention_forward(
        tokens, cotangent, query_weight, key_value_weight, output_weight, gateup_weight,
        down_weight, norm_gains.reshape(1, OWN_GAINS), doc_lengths,
        jnp.asarray(cosine), jnp.asarray(sine),
    )
    block_out, input_grad, *gradients = layer_backward(
        residual, tokens_here, gains, lengths, down, cotangent_all, gate, up,
        heads, raw, attended, totals, cosine, sine, qkv, output, normed,
    )
    state = [a.reshape(1, OWN_GAINS) if a.ndim == 1 else a for a in state]
    outs = update((block_out, input_grad), gradients, state)
    return tuple(a.reshape(OWN_GAINS) if a.shape == (1, OWN_GAINS) else a for a in outs)


def solution(mesh):
    parted = Mesh(mesh.devices.reshape(GRID), AXES)
    data = ("z", "ylo", "core")
    tensor = ("yhi", "x")
    rows = P(AXES, None)
    by_rows = P(data, tensor)
    pair = P(None, data, tensor)
    by_columns = P(tensor, data)
    flat = P(AXES)
    weights = (by_rows, pair, by_columns, pair, by_columns, flat)
    return jax.shard_map(
        body,
        mesh=parted,
        in_specs=(rows, rows, P(data, None)) + weights * 3,
        out_specs=(rows, rows) + weights * 3,
        check_vma=False,
    )
```

```python
import math

import jax
import jax.numpy as jnp
import numpy as np
from jax import lax
from jax.experimental import pallas as pl
from jax.experimental.pallas import tpu as pltpu
from jax.sharding import Mesh
from jax.sharding import PartitionSpec as P

MODEL_WIDTH = 2048
QUERY_HEADS = 16
HEAD_SIZE = 128
FF = 6144
GROUP_TOK = 1024
GAINS = 4352
OWN_GAINS = 34
EPSILON = 1e-06
MOMENTUM = 0.9
AVERAGING = 0.5
ROPE_BASE = 1000000.0
SCALE = HEAD_SIZE ** (-0.5)

AXES = ("z", "ylo", "core", "yhi", "x")
GRID = (4, 2, 2, 2, 4)
RING = 4
BF16 = jnp.bfloat16
F32 = jnp.float32
HBM = pl.ANY
VMEM = pltpu.VMEM


class Place:
    def __init__(self):
        self.x = lax.axis_index("x")
        self.z = lax.axis_index("z")
        self.core = lax.axis_index("core")
        self.yhi = lax.axis_index("yhi")
        self.ylo = lax.axis_index("ylo")
        self.y = self.yhi * 2 + self.ylo
        self.native = self.core == self.yhi
        at = {"x": self.x, "y": self.y, "z": self.z}
        self.steps = {
            (axis, by): lax.rem(here + by, RING) if by else here
            for axis, here in at.items()
            for by in range(RING)
        }
        self.devices = {
            "core": {"core": 1 - self.core},
            "turn": {"core": 1 - self.core, "yhi": 1 - self.yhi},
        }
        for (axis, by), there in self.steps.items():
            self.devices[axis, by] = (
                {"yhi": lax.div(there, 2), "ylo": lax.rem(there, 2)}
                if axis == "y"
                else {axis: there}
            )

    def step(self, axis, by):
        return self.steps[axis, by % RING]

    def device(self, axis, by=1):
        return self.devices[axis] if axis in ("core", "turn") else self.devices[axis, by % RING]


class Local:
    def __init__(self, refs, sems, index):
        self.refs, self.sems, self.index = refs, sems, index

    def copy(self):
        source, target = self.refs()
        return pltpu.make_async_copy(source, target, self.sems.at[self.index])

    def start(self):
        self.copy().start()

    def wait(self):
        self.copy().wait()


class Net:
    def __init__(self, place, partners, send_sems, recv_sems, local_sems):
        self.place, self.partners = place, partners
        self.send_sems, self.recv_sems, self.local_sems = send_sems, recv_sems, local_sems
        self.leaving, self.arriving, self.local_count = 0, 0, 0
        self.waits = []

    def greet(self):
        barrier = pltpu.get_barrier_semaphore()
        for axis, by in self.partners:
            pl.semaphore_signal(
                barrier,
                inc=1,
                device_id=self.place.device(axis, by),
                device_id_type=pl.DeviceIdType.MESH,
            )

    def enter(self):
        pl.semaphore_wait(pltpu.get_barrier_semaphore(), len(self.partners))

    def out(self):
        self.leaving += 1
        return self.leaving - 1

    def into(self):
        self.arriving += 1
        return self.arriving - 1

    def local_number(self):
        self.local_count += 1
        return self.local_count - 1

    def copy(self, source, target, out, into, axis="core", by=1):
        return pltpu.make_async_remote_copy(
            src_ref=source,
            dst_ref=target,
            send_sem=self.send_sems.at[out],
            recv_sem=self.recv_sems.at[into],
            device_id=self.place.device(axis, by),
            device_id_type=pl.DeviceIdType.MESH,
        )

    def send(self, refs, out, into, axis, by=1):
        self.copy(*refs(), out, into, axis, by).start()

    def here(self, into, view):
        self.copy(view, view, 0, into).wait_recv()

    def gone(self, out, view):
        self.copy(view, view, out, 0).wait_send()

    def later(self, wait):
        self.waits.append(wait)

    def finish(self):
        for wait in self.waits:
            wait()

    def local(self, refs):
        copy = Local(refs, self.local_sems, self.local_number())
        copy.start()
        return copy


def at_step(acts, n):
    for at, act in (acts or {}).items():

        @pl.when(n == at)
        def _():
            act()


def staged(count, compute, before=None, after=None):
    def step(n, carry):
        at_step(before, n)
        compute(n)
        at_step(after, n)
        return carry

    lax.fori_loop(0, count, step, 0)


class RowsGather:
    OUT, INTO, LOCALS = 1, 7, 2

    def __init__(self, net, own, whole):
        self.net, self.own, self.whole = net, own, whole
        self.rows = own.shape[0]
        self.half = self.rows // 2
        place = net.place
        self.me, self.other = place.core, 1 - place.core
        self.spots = {k: place.step("x", k) for k in (0, 1, -1, 2)}
        self.out = net.out()
        self.first, self.second, self.third = net.into(), net.into(), net.into()
        self.shared = {k: net.into() for k in (0, 1, -1, 2)}
        self.kept = []
        net.later(self.gone)

    def block(self, core, k, part):
        start = (self.spots[k] * 2 + core) * self.rows + part * self.half
        return self.whole.at[pl.ds(pl.multiple_of(start, self.half), self.half)]

    def mine(self, k, part):
        return self.block(self.me, k, part)

    def piece(self, part):
        return self.own.at[pl.ds(part * self.half, self.half)]

    def share(self, k, part):
        refs = lambda: (self.piece(part) if k == 0 else self.mine(k, part), self.mine(k, part))
        self.net.send(refs, self.out, self.shared[k], "core")

    def both(self):
        return self.whole.at[pl.ds(0, self.rows)]

    def start(self, parts=(0, 1)):
        for part in parts:
            refs = lambda part=part: (self.piece(part), self.mine(0, part))
            first, second = (1, -1) if part == 0 else (-1, 1)
            self.net.send(refs, self.out, self.first, "x", first)
            self.net.send(refs, self.out, self.second, "x", second)
            self.share(0, part)
            self.kept.append(self.net.local(refs))

    def near_first(self):
        self.net.here(self.first, self.both())
        self.net.send(lambda: (self.mine(-1, 0),) * 2, self.out, self.third, "x", 1)
        self.net.send(lambda: (self.mine(1, 1),) * 2, self.out, self.third, "x", -1)
        self.share(-1, 0)
        self.share(1, 1)

    def near_second(self):
        self.net.here(self.second, self.both())
        self.share(-1, 1)
        self.share(1, 0)

    def far(self):
        self.net.here(self.third, self.both())
        self.share(2, 0)
        self.share(2, 1)

    def here(self, k):
        if k == 0:
            for copy in self.kept:
                copy.wait()
        self.net.here(self.shared[k], self.both())

    def gone(self):
        if self.out is not None:
            self.net.gone(self.out, self.whole.at[pl.ds(0, 7 * self.rows)])
            self.out = None


class RowsSum:
    OUT, INTO = 2, 6

    def __init__(self, net, whole, landed, land, share=0, shares=1):
        self.net, self.whole, self.landed, self.land = net, whole, landed, land
        self.share, self.shares = share, shares
        self.half = landed.shape[2]
        place = net.place
        self.me, self.other = place.core, 1 - place.core
        self.spots = {k: place.step("x", k) for k in (0, 1, -1, 2)}
        self.over, self.along = net.out(), net.out()
        self.given = {k: net.into() for k in (0, 1, -1, 2)}
        self.through, self.last = net.into(), net.into()
        net.later(self.passed)
        net.later(self.departed)

    def block(self, core, k, part):
        block = (self.spots[k] * 2 + core) * self.shares + self.share
        start = (block * 2 + part) * self.half
        return self.whole.at[pl.ds(pl.multiple_of(start, self.half), self.half)]

    def own(self, k, part):
        return self.landed.at[k % RING, part]

    def pass_over(self, k):
        for part in range(2):
            refs = lambda part=part: (self.block(self.other, k, part), self.own(k, part))
            self.net.send(refs, self.over, self.given[k], "core")

    def passed(self):
        if self.over is not None:
            self.net.gone(self.over, self.landed)
            self.over = None

    def departed(self):
        if self.along is not None:
            self.net.gone(self.along, self.land)
            self.along = None

    def combine(self, k):
        self.net.here(self.given[k], self.landed.at[k % RING])
        for part in range(2):
            here = self.own(k, part)
            here[...] = here[...] + self.block(self.me, k, part)[...]

    def along_x(self, refs, into, by):
        self.net.send(refs, self.along, into, "x", by)

    def start_far(self):
        self.along_x(lambda: (self.own(2, 0), self.land.at[0]), self.through, 1)
        self.along_x(lambda: (self.own(2, 1), self.land.at[1]), self.through, -1)

    def start_right(self):
        self.along_x(lambda: (self.own(1, 1), self.land.at[3]), self.last, 1)

    def start_left(self):
        self.along_x(lambda: (self.own(-1, 0), self.land.at[4]), self.last, -1)

    def forward(self):
        land = self.land
        self.net.here(self.through, land.at[pl.ds(0, 2)])
        land[0] = land[0] + self.own(1, 0)[...]
        self.along_x(lambda: (land.at[0], land.at[2]), self.last, 1)
        land[1] = land[1] + self.own(-1, 1)[...]
        self.along_x(lambda: (land.at[1], land.at[5]), self.last, -1)

    def finish(self, keep):
        land = self.land
        self.net.here(self.last, land.at[pl.ds(2, 4)])
        for part in range(2):
            total = self.own(0, part)[...].astype(F32) + land[2 + part].astype(F32)
            keep(pl.ds(part * self.half, self.half), total + land[4 + part].astype(F32))


ROWS_SCRATCH = (pltpu.VMEM((4, 2, 64, 2048), BF16), pltpu.VMEM((6, 64, 2048), BF16))


class PlaneGather:
    OUT, INTO, LOCALS = 1, 12, 1

    def __init__(self, net, own, whole, spot, first_rows=None):
        self.net, self.own, self.whole, self.spot = net, own, whole, spot
        self.rows = own.shape[0]
        first_rows = self.rows // 2 if first_rows is None else first_rows
        self.sizes, self.starts = (first_rows, self.rows - first_rows), (0, first_rows)
        self.width = own.shape[1]
        self.out = net.out()
        self.first = [net.into() for _ in range(2)]
        self.rings = {(color, i): net.into() for color in range(2) for i in (0, 1, -1, -2)}
        self.last = [net.into() for _ in range(2)]
        net.later(self.gone)

    def gone(self):
        if self.out is not None:
            rows = self.whole.shape[0] // 16 * 15
            self.net.gone(self.out, self.whole.at[pl.ds(0, rows)])
            self.out = None

    def view(self, color, i, j, part=None):
        place = self.net.place
        first, second = self.axes(color)
        a, b = place.step(first, i), place.step(second, j)
        row, columns = self.spot(a, b) if color == 0 else self.spot(b, a)
        start, size = row + self.starts[color], self.sizes[color]
        if part is not None:
            size //= 2
            start = start + part * size
        return self.whole.at[pl.ds(pl.multiple_of(start, math.gcd(size, self.rows)), size), columns]

    def bytes_of(self, color, count):
        size = self.sizes[color]
        if count * size <= self.whole.shape[0]:
            return self.whole.at[pl.ds(0, count * size), pl.ds(0, self.width)]
        return self.whole.at[pl.ds(0, size), pl.ds(0, count * self.width)]

    @staticmethod
    def axes(color):
        return ("z", "y") if color == 0 else ("y", "z")

    def mine(self, color):
        return self.own.at[pl.ds(self.starts[color], self.sizes[color])]

    def ring(self, color, i):
        axis = self.axes(color)[1]
        refs = lambda: (
            self.mine(color) if i == 0 else self.view(color, i, 0), self.view(color, i, 0)
        )
        for by in (1, -1):
            self.net.send(refs, self.out, self.rings[color, i], axis, by)

    def start(self):
        for color in range(2):
            axis = self.axes(color)[0]
            refs = lambda color=color: (self.mine(color), self.view(color, 0, 0))
            for by in (1, -1, 2):
                self.net.send(refs, self.out, self.first[color], axis, by)
        for color in range(2):
            self.ring(color, 0)
        self.kept = self.net.local(self.place_here)

    def place_here(self):
        row, columns = self.spot(self.net.place.z, self.net.place.y)
        return self.own, self.whole.at[pl.ds(pl.multiple_of(row, self.rows), self.rows), columns]

    def spread(self):
        for color in range(2):
            self.net.here(self.first[color], self.bytes_of(color, 3))
        for i in (-1, 1, -2):
            for color in range(2):
                self.ring(color, i)

    def forward(self, steps=(0, 1, -1, -2)):
        for i in steps:
            for color in range(2):
                axis = self.axes(color)[1]
                self.net.here(self.rings[color, i], self.bytes_of(color, 2))
                for j, part, by in ((-1, 0, 1), (1, 1, -1)):
                    refs = lambda color=color, i=i, j=j, part=part: (
                        self.view(color, i, j, part),
                    ) * 2
                    self.net.send(refs, self.out, self.last[color], axis, by)

    def here(self):
        for color in range(2):
            self.net.here(self.last[color], self.bytes_of(color, 4))
        self.kept.wait()


class PlaneSum:
    OUT, INTO = 4, 18

    def __init__(self, net, whole, spot, scratch):
        self.net, self.whole, self.spot = net, whole, spot
        self.land, self.last = scratch[0:2], scratch[2:4]
        self.sizes = [land.shape[2] for land in self.land]
        self.starts = (0, 2 * self.sizes[0])
        self.ring_out, self.last_out = (net.out(), net.out()), (net.out(), net.out())
        ways = [(color, k) for color in range(2) for k in range(RING)]
        self.through = {way: net.into() for way in ways}
        self.sides = {way: net.into() for way in ways}
        self.ends = [net.into() for _ in range(2)]
        for color in range(2):
            net.later(lambda color=color: net.gone(self.ring_out[color], self.land[color]))
            net.later(lambda color=color: net.gone(self.last_out[color], self.last[color]))

    @staticmethod
    def axes(color):
        return ("y", "z") if color == 0 else ("z", "y")

    def own(self, color, n, k, part):
        place = self.net.place
        first, second = self.axes(color)
        a, b = place.step(first, n), place.step(second, k)
        row, columns = self.spot(b, a) if color == 0 else self.spot(a, b)
        size = self.sizes[color]
        start = row + self.starts[color] + part * size
        return self.whole.at[pl.ds(pl.multiple_of(start, math.gcd(size, 128)), size), columns]

    def slot(self, color, k, n):
        return self.land[color].at[k % RING, n]

    def end(self, color, k, part):
        return self.last[color].at[k % RING - 1, part]

    def start(self):
        for k in (2, 1, -1, 0):
            for color in range(2):
                axis = self.axes(color)[0]
                through, sides = self.through[color, k % RING], self.sides[color, k % RING]
                for n, part, slot, into, by in (
                    (2, 0, 0, through, 1), (2, 1, 1, through, -1),
                    (1, 1, 3, sides, 1), (-1, 0, 4, sides, -1),
                ):
                    refs = lambda color=color, k=k, n=n, part=part, slot=slot: (
                        self.own(color, n, k, part), self.slot(color, k, slot)
                    )
                    self.net.send(refs, self.ring_out[color], into, axis, by)

    def forward(self, steps=(2, 1, -1, 0)):
        for k in steps:
            for color in range(2):
                axis = self.axes(color)[0]
                sides = self.sides[color, k % RING]
                self.net.here(
                    self.through[color, k % RING], self.land[color].at[k % RING, pl.ds(0, 2)]
                )
                for slot, n, part, target, by in ((0, 1, 0, 2, 1), (1, -1, 1, 5, -1)):
                    here = self.slot(color, k, slot)
                    here[...] = here[...] + self.own(color, n, k, part)[...]
                    refs = lambda color=color, k=k, slot=slot, target=target: (
                        self.slot(color, k, slot), self.slot(color, k, target)
                    )
                    self.net.send(refs, self.ring_out[color], sides, axis, by)

    def gather(self, steps=(2, 1, -1, 0)):
        for k in steps:
            for color in range(2):
                second = self.axes(color)[1]
                self.net.here(
                    self.sides[color, k % RING], self.land[color].at[k % RING, pl.ds(2, 4)]
                )
                for part in range(2):
                    here = self.slot(color, k, 2 + part)
                    total = self.own(color, 0, k, part)[...].astype(F32) + here[...].astype(F32)
                    total = total + self.slot(color, k, 4 + part)[...].astype(F32)
                    here[...] = total.astype(BF16)
                    if k != 0:
                        refs = lambda color=color, k=k, part=part: (
                            self.slot(color, k, 2 + part), self.end(color, k, part)
                        )
                        self.net.send(refs, self.last_out[color], self.ends[color], second, k)

    def finish(self, total):
        for color in range(2):
            self.net.here(self.ends[color], self.last[color])
            for part in range(2):
                value = self.slot(color, 0, 2 + part)[...].astype(F32)
                for k in (1, -1, 2):
                    value = value + self.end(color, k, part)[...].astype(F32)
                start = self.starts[color] + part * self.sizes[color]
                total[pl.ds(start, self.sizes[color])] = value.astype(total.dtype)


def plane_scratch(rows, columns, first_rows=None):
    first_rows = rows // 2 if first_rows is None else first_rows
    parts = (first_rows // 2, (rows - first_rows) // 2)
    return tuple(
        pltpu.VMEM((*dims, part, columns), BF16) for dims in ((4, 6), (3, 2)) for part in parts
    )


class Turn:
    def __init__(self, net, pairs):
        self.net = net
        self.pairs = [
            (source, target, net.out(), net.into(), net.local_number()) for source, target in pairs
        ]

    def copies(self):
        return [self.net.copy(a, b, out, into, "turn") for a, b, out, into, _ in self.pairs]

    def kept(self):
        sems = self.net.local_sems
        return [pltpu.make_async_copy(a, b, sems.at[index]) for a, b, _, _, index in self.pairs]

    def both(self, act):
        @pl.when(jnp.logical_not(self.net.place.native))
        def _():
            for copy in self.copies():
                act(copy)

        @pl.when(self.net.place.native)
        def _():
            for copy in self.kept():
                act(copy)

    def start(self):
        self.both(lambda copy: copy.start())

    def wait(self):
        self.both(lambda copy: copy.wait())


class Give:
    def __init__(self, net, refs, there):
        self.net, self.there = net, there
        self.out, self.into = net.out(), net.into()
        net.send(refs, self.out, self.into, "core")
        net.later(lambda: net.gone(self.out, refs()[0]))

    def wait(self):
        self.net.here(self.into, self.there())


def parts_of(source, target, count):
    rows = source.shape[0] // count
    spots = [pl.ds(part * rows, rows) for part in range(count)]
    return [(source.at[spot], target.at[spot]) for spot in spots]


class GainsGather:
    OUT, INTO, LOCALS = 1, 4, 1

    def __init__(self, net, own, whole):
        self.net, self.own, self.whole = net, own, whole
        self.out = net.out()
        self.into = [net.into() for _ in range(4)]
        net.later(lambda: net.gone(self.out, whole.at[pl.ds(0, 127)]))

    def rows(self, z, y, x, core, count):
        start = ((z * RING + y) * RING + x) * 2 + core
        return self.whole.at[pl.ds(start if count == 1 else pl.multiple_of(start, count), count)]

    def spot(self, axis, by):
        place = self.net.place
        if axis == "core":
            return self.rows(place.z, place.y, place.x, (place.core + by) % 2, 1)
        if axis == "x":
            return self.rows(place.z, place.y, place.step("x", by), 0, 2)
        if axis == "y":
            return self.rows(place.z, place.step("y", by), 0, 0, 8)
        return self.rows(place.step("z", by), 0, 0, 0, 32)

    def steps(self):
        net = self.net
        net.local(lambda: (self.own, self.spot("core", 0))).wait()
        for into, axis, count in zip(self.into, ("core", "x", "y", "z"), (1, 2, 8, 32)):
            ways = (1,) if axis == "core" else (1, -1, 2)
            for by in ways:
                net.send(lambda axis=axis: (self.spot(axis, 0),) * 2, self.out, into, axis, by)
            yield
            net.here(into, self.whole.at[pl.ds(0, count * len(ways))])
        yield


class GainsSum(GainsGather):
    def __init__(self, net, whole, total, land):
        super().__init__(net, None, whole)
        self.total, self.land = total, land

    def steps(self):
        net, land = self.net, self.land
        first = 0
        for into, axis, count in zip(self.into, ("z", "y", "x", "core"), (32, 8, 2, 1)):
            ways = (1,) if axis == "core" else (1, -1, 2)
            spots = [pl.ds(first + n * count, count) for n in range(len(ways))]
            for spot, by in zip(spots, ways):
                refs = lambda axis=axis, spot=spot, by=by: (self.spot(axis, by), land.at[spot])
                net.send(refs, self.out, into, axis, by)
            yield
            net.here(into, land.at[pl.ds(first, count * len(ways))])
            value = self.spot(axis, 0)[...]
            for spot in spots:
                value = value + land[spot]
            if axis == "core":
                self.total[...] = value
            else:
                self.spot(axis, 0)[...] = value
            first += count * len(ways)
        yield


class Kernel:
    def __init__(self, number, plans, gives, turns, locals_, partners):
        self.number, self.partners = number, partners
        extra = gives + turns
        self.sems = (
            sum(plan.OUT for plan in plans) + extra,
            sum(plan.INTO for plan in plans) + extra,
            sum(getattr(plan, "LOCALS", 0) for plan in plans) + turns + locals_,
        )

    def __call__(self, body, arrays, outs, scratch=()):
        n_in, n_out, n_scratch = len(arrays), len(outs), len(scratch)

        def kernel(*refs):
            net = Net(Place(), self.partners, *refs[n_in + n_out + n_scratch :])
            net.greet()
            body(
                net,
                refs[:n_in],
                refs[n_in : n_in + n_out],
                refs[n_in + n_out : n_in + n_out + n_scratch],
            )
            net.finish()
            assert (net.leaving, net.arriving, net.local_count) == self.sems, (
                net.leaving, net.arriving, net.local_count, self.sems,
            )

        return pl.pallas_call(
            kernel,
            out_shape=[shape for shape, _ in outs],
            in_specs=[pl.BlockSpec(memory_space=space) for _, space in arrays],
            out_specs=[pl.BlockSpec(memory_space=space) for _, space in outs],
            scratch_shapes=[*scratch] + [pltpu.SemaphoreType.DMA((n,)) for n in self.sems],
            compiler_params=pltpu.CompilerParams(
                collective_id=self.number, has_side_effects=True, vmem_limit_bytes=62 * 2**20
            ),
            name="links_%d" % self.number,
        )(*[array for array, _ in arrays])


CORE_PARTNER = (("core", 1),)
X_PARTNERS = (("x", 1), ("x", -1))
FAR_X = (("x", 2),)
PLANE_PARTNERS = (("y", 1), ("y", -1), ("y", 2), ("z", 1), ("z", -1), ("z", 2))
TURN_PARTNERS = (("turn", 1),)


def shape(dims, dtype=BF16):
    return jax.ShapeDtypeStruct(dims, dtype)


def attention_spot(z, y):
    piece = z * 4 + lax.rem(y, 2) * 2 + lax.div(y, 2)
    return piece * 128


def rows_spot(z, y):
    return attention_spot(z, y), pl.ds(0, 512)


def output_spot(z, y):
    return 0, pl.ds(pl.multiple_of(attention_spot(z, y), 128), 128)


def gateup_spot(z, y):
    columns = pl.ds(pl.multiple_of(lax.div(y, 2) * 384, 128), 384)
    return (z * 2 + lax.rem(y, 2)) * 256, columns


def down_spot(z, y):
    columns = pl.ds(pl.multiple_of((z * 2 + lax.rem(y, 2)) * 256, 128), 256)
    return lax.div(y, 2) * 384, columns


def nn(left, right):
    return lax.dot_general(left, right, (((1,), (0,)), ((), ())), preferred_element_type=F32)


def nt(left, right):
    return lax.dot_general(left, right, (((1,), (1,)), ((), ())), preferred_element_type=F32)


def tn(left, right):
    return lax.dot_general(left, right, (((0,), (0,)), ((), ())), preferred_element_type=F32)


def exact(left, right):
    return lax.dot_general(
        left, right, (((1,), (0,)), ((), ())),
        precision=lax.Precision.HIGHEST, preferred_element_type=F32,
    )


def inverse_root(rows):
    return lax.rsqrt(jnp.mean(rows * rows, axis=-1, keepdims=True) + EPSILON)


def norm_back(rows, gain, upstream):
    root = inverse_root(rows)
    weighted = upstream * gain
    meant = jnp.mean(weighted * rows, axis=-1, keepdims=True)
    return root * weighted - rows * (root * root * root * meant), upstream * rows * root


def rope_tables():
    halves = np.arange(HEAD_SIZE // 2, dtype=np.float64)
    angles = np.arange(GROUP_TOK)[:, None] * ROPE_BASE ** (-2.0 * halves / HEAD_SIZE)[None, :]
    angles = np.concatenate([angles, angles], axis=1)
    return np.cos(angles).astype(np.float32), np.sin(angles).astype(np.float32)


def owner_starts(dims, axis):
    row = lax.broadcasted_iota(jnp.int32, dims, axis)
    z, y, x, core = row >> 5, (row >> 3) & 3, (row >> 1) & 3, row & 1
    return (z * 32 + (y & 1) * 16 + core * 8 + (y >> 1) * 4 + x) * OWN_GAINS


def column_of(entry):
    return entry - jnp.floor((entry.astype(F32) + 0.5) * (1.0 / OWN_GAINS)).astype(jnp.int32) * OWN_GAINS


def gains_flat(rows):
    entry = lax.broadcasted_iota(jnp.int32, (128, GAINS), 1)
    past = entry - owner_starts((128, GAINS), 0)
    owner = ((past >= 0) & (past < OWN_GAINS)).astype(F32)
    columns = lax.dot_general(
        rows, owner, (((0,), (0,)), ((), ())),
        precision=lax.Precision.HIGHEST, preferred_element_type=F32,
    )
    place = lax.broadcasted_iota(jnp.int32, (128, GAINS), 0)
    return jnp.sum(jnp.where(column_of(entry) == place, columns, 0.0), axis=0, keepdims=True)


class Documents:
    def __init__(self, lengths):
        lengths = [lengths[0:1, n : n + 1] for n in range(4)]
        self.ends = [lengths[0], lengths[0] + lengths[1], lengths[0] + lengths[1] + lengths[2]]

    def pick(self, place, values):
        value = jnp.where(place >= self.ends[0], values[1], values[0])
        value = jnp.where(place >= self.ends[1], values[2], value)
        return jnp.where(place >= self.ends[2], values[3], value)

    def first(self, place):
        zero = jnp.zeros_like(self.ends[0])
        return self.pick(place, [zero] + self.ends)


def allowed_pairs(documents, first_row, rows, keys):
    query = lax.broadcasted_iota(jnp.int32, (rows, 1), 0) + first_row
    key = lax.broadcasted_iota(jnp.int32, (rows, keys), 1)
    return (key >= documents.first(query)) & (key <= query)


def unit_off(n):
    return lax.rem(n + lax.div(n, 2), 4) + 2 * lax.div(n, 3)


class Units:
    ORDER = (0, 1, -1, 2)

    def __init__(self, place):
        self.x = place.x

    def chip(self, n):
        return lax.rem(self.x + unit_off(n), RING)

    def rows(self, n):
        return pl.ds(pl.multiple_of(self.chip(n) * 256, 256), 256)

    def true_rows(self, n, core):
        return pl.ds(pl.multiple_of((core * RING + self.chip(n)) * 128, 128), 128)


def own_half(length, core):
    return pl.ds(pl.multiple_of(core * length, 128), length)


def attention_forward(
    tokens, cotangent, query, keyval, output, gateup, down, gains, lengths, cosine, sine
):
    def body(net, ins, outs, work):
        (
            tokens_, cotangent_, query_, keyval_, output_, gateup_, down_, gains_, lengths_,
            cosine_, sine_,
        ) = ins
        (
            residual_, tokens_here, normed_, raw_hbm, heads_hbm, attended_hbm, totals_hbm,
            cosine_hbm, sine_hbm, qkv_out, output_out, gate_out, up_out, down_piece,
            cotangent_all, flat_, lengths_out,
        ) = outs
        (
            gathered, normed, qkv_w, output_w, qkv_cast, output_cast, qkv_piece, output_piece,
            gains_row, gains_rows, lengths_mine, lengths_there, gate_cast, up_cast, down_cast,
            gate_piece, up_piece, cotangent_here, terms, raw_, heads_, attended_, totals_,
            cosine_out, sine_out, landed, land,
        ) = work
        place = net.place
        units = Units(place)
        mine, theirs = place.core, 1 - place.core

        qkv_cast[:, 0:256] = query_[...].astype(BF16)
        qkv_cast[:, 256:384] = keyval_[0].astype(BF16)
        qkv_cast[:, 384:512] = keyval_[1].astype(BF16)
        output_cast[...] = output_[...].astype(BF16)
        gains_row[0] = jnp.zeros((1, 128), F32)
        gains_row[0, 0:1, 0:OWN_GAINS] = gains_[...]
        lengths_mine[...] = jnp.zeros((8, 128), jnp.int32)
        lengths_mine[0:1, 0:4] = lengths_[...]
        net.enter()
        qkv_turn = Turn(net, [(qkv_cast, qkv_piece)])
        output_turn = Turn(net, [(output_cast, output_piece)])
        rows = [Turn(net, [pair]) for pair in parts_of(tokens_, tokens_here, 2)]
        upstream = Turn(net, parts_of(cotangent_, cotangent_here, 2))
        qkv_turn.start()
        for part in rows:
            part.start()
        qkv_gather = PlaneGather(net, qkv_piece, qkv_w, rows_spot, 32)
        output_gather = PlaneGather(net, output_piece, output_w, output_spot, 64)
        gate_gather = PlaneGather(net, gate_piece, gate_out, gateup_spot)
        up_gather = PlaneGather(net, up_piece, up_out, gateup_spot)
        gather = RowsGather(net, tokens_here, gathered)
        later = RowsGather(net, cotangent_here, cotangent_all)
        length_copy = Give(net, lambda: (lengths_mine, lengths_there), lambda: lengths_there)
        gains_steps = GainsGather(net, gains_row, gains_rows).steps()
        next(gains_steps)

        halves = []
        for n, (cast, piece) in enumerate(((gate_cast, gate_piece), (up_cast, up_piece))):
            spot = own_half(128, mine)
            piece[spot] = gateup_[n, :, own_half(384, mine)].astype(BF16)
            cast[...] = gateup_[n, :, own_half(384, theirs)].astype(BF16)
            halves.append(Give(
                net,
                lambda cast=cast, piece=piece: (cast, piece.at[own_half(128, mine)]),
                lambda piece=piece: piece.at[own_half(128, theirs)],
            ))
        down_piece[:, own_half(128, mine)] = down_[own_half(384, mine)].astype(BF16)
        down_cast[...] = down_[own_half(384, theirs)].astype(BF16)
        halves.append(Give(
            net,
            lambda: (down_cast, down_piece.at[:, own_half(128, mine)]),
            lambda: down_piece.at[:, own_half(128, theirs)],
        ))

        qkv_turn.wait()
        qkv_gather.start()
        output_turn.start()
        for n, part in enumerate(rows):
            part.wait()
            gather.start((n,))
        upstream.start()
        next(gains_steps)

        length_copy.wait()
        lengths_out[...] = jnp.where(place.native, lengths_mine[...], lengths_there[...])
        documents = Documents(lengths_out[...])
        zero = jnp.zeros((1, 1), jnp.int32)
        starts = [zero] + documents.ends
        everywhere = lax.broadcasted_iota(jnp.int32, (1, GROUP_TOK), 1)
        hits = jnp.concatenate(
            [(everywhere == start).astype(F32) for start in starts] * 2, axis=0
        )
        start_cosine = exact(hits, cosine_[...])
        start_sine = exact(hits, sine_[...])
        sign = jnp.where(lax.broadcasted_iota(jnp.int32, (1, HEAD_SIZE), 1) < 64, -1.0, 1.0)

        def table(n):
            spot = pl.ds(pl.multiple_of(n * 256, 256), 256)
            where = lax.broadcasted_iota(jnp.int32, (256, 1), 0) + n * 256
            cosine_by = documents.pick(where, [start_cosine[n : n + 1] for n in range(4)])
            sine_by = documents.pick(where, [start_sine[n : n + 1] for n in range(4)])
            cosine_out[spot] = cosine_[spot] * cosine_by + sine_[spot] * sine_by
            sine_out[spot] = (sine_[spot] * cosine_by - cosine_[spot] * sine_by) * sign

        staged(4, table)
        qkv_gather.spread()
        output_turn.wait()
        output_gather.start()
        next(gains_steps)
        gather.near_first()
        for half in halves:
            half.wait()
        next(gains_steps)
        qkv_gather.forward()
        output_gather.spread()
        gate_gather.start()
        next(gains_steps)
        flat_[...] = gains_flat(gains_rows[...].reshape(128, 128))
        gain_query = flat_[0:1, 4096:4224]
        gain_key = flat_[0:1, 4224:4352]

        def normalize(n):
            rows_in = gathered[units.rows(n)].astype(F32)
            normed[units.rows(n)] = (
                rows_in * inverse_root(rows_in) * flat_[0:1, 0:2048]
            ).astype(BF16)

        def near():
            gather.near_second()
            gather.here(1)

        def far():
            gather.far()
            output_gather.forward()
            up_gather.start()
            upstream.wait()
            later.start()
            gather.here(2)

        staged(4, normalize, {
            0: lambda: gather.here(0), 1: near, 2: lambda: gather.here(-1), 3: far,
        })
        qkv_gather.here()
        stores = [net.local(lambda: (normed, normed_)), net.local(lambda: (qkv_w, qkv_out))]

        def project(n):
            parts = nn(normed[units.rows(n)], qkv_w[...])
            for core in range(2):
                spot = units.true_rows(n, core)
                part = parts[core * 128 : core * 128 + 128]
                raw_[spot] = part[:, 0:384]
                heads_[spot, 384:512] = part[:, 384:512].astype(BF16)
                for head in range(3):
                    columns = slice(head * 128, head * 128 + 128)
                    value = part[:, columns]
                    value = value * inverse_root(value) * (gain_key if head == 2 else gain_query)
                    turned = value * cosine_out[spot] + pltpu.roll(value, 64, 1) * sine_out[spot]
                    heads_[spot, columns] = turned.astype(BF16)

        staged(4, project)
        gate_gather.spread()

        def attend(block):
            keys = 256 * (block + 1)
            spot = slice(block * 256, block * 256 + 256)

            def one(head):
                columns = own_half(128, head)
                scores = nt(heads_[spot, columns], heads_[0:keys, 256:384])
                allowed = allowed_pairs(documents, block * 256, 256, keys)
                scores = jnp.where(allowed, scores, -1e30)
                highest = jnp.max(scores, axis=-1, keepdims=True)
                weights_ = jnp.exp((scores - highest) * SCALE)
                summed = jnp.sum(weights_, axis=-1, keepdims=True)
                probability = (weights_ * (1.0 / summed)).astype(BF16)
                attended_[spot, columns] = nn(probability, heads_[0:keys, 384:512]).astype(BF16)
                lane = lax.broadcasted_iota(jnp.int32, (1, 128), 1)
                ours = (lane >= head * 64) & (lane < head * 64 + 64)
                totals_[spot] = jnp.where(ours, highest * SCALE + jnp.log(summed), totals_[spot])

            staged(2, one)

        attend(0)
        attend(1)
        attend(2)
        output_gather.here()
        stores.append(net.local(lambda: (output_w, output_out)))
        attend(3)
        later.near_first()
        up_gather.spread()
        sums = RowsSum(net, terms, landed, land)

        def out(n):
            n = 3 - n
            own = jnp.concatenate(
                [attended_[units.true_rows(n, 0)], attended_[units.true_rows(n, 1)]], axis=0
            )
            terms[units.rows(n)] = nn(own, output_w[...]).astype(BF16)

        def passed(k, ready=None, go=None):
            def act():
                sums.pass_over(k)
                if ready is not None:
                    sums.combine(ready)
                    go()

            return act

        staged(4, out, None, {
            0: passed(2),
            1: passed(-1, 2, sums.start_far),
            2: passed(1, -1, sums.start_left),
            3: passed(0, 1, sums.start_right),
        })
        for source, target in (
            (raw_, raw_hbm), (heads_, heads_hbm), (attended_, attended_hbm),
            (totals_, totals_hbm), (cosine_out, cosine_hbm), (sine_out, sine_hbm),
        ):
            stores.append(net.local(lambda source=source, target=target: (source, target)))
        sums.combine(0)
        sums.forward()
        later.near_second()
        gate_gather.forward()
        later.far()
        up_gather.forward()
        for k in (0, 1, -1, 2):
            later.here(k)

        def keep(spot, value):
            residual_[spot] = value + tokens_here[spot].astype(F32)

        sums.finish(keep)
        gate_gather.here()
        up_gather.here()
        for store in stores:
            store.wait()

    plans = (GainsGather,) + 4 * (PlaneGather,) + 2 * (RowsGather,) + (RowsSum,)
    return Kernel(
        0, plans, 4, 6, 9, CORE_PARTNER + X_PARTNERS + FAR_X + PLANE_PARTNERS + TURN_PARTNERS
    )(
        body,
        [
            (tokens, VMEM), (cotangent, VMEM), (query, VMEM), (keyval, VMEM), (output, VMEM),
            (gateup, VMEM), (down, VMEM), (gains, VMEM), (lengths, VMEM),
            (cosine, VMEM), (sine, VMEM),
        ],
        [
            (shape((128, 2048), F32), VMEM),
            (shape((128, 2048)), VMEM),
            (shape((1024, 2048)), HBM),
            (shape((1024, 384), F32), HBM),
            (shape((1024, 512)), HBM),
            (shape((1024, 256)), HBM),
            (shape((1024, 128), F32), HBM),
            (shape((1024, 128), F32), HBM),
            (shape((1024, 128), F32), HBM),
            (shape((2048, 512)), HBM),
            (shape((256, 2048)), HBM),
            (shape((2048, 768)), HBM),
            (shape((2048, 768)), HBM),
            (shape((384, 256)), VMEM),
            (shape((1024, 2048)), HBM),
            (shape((1, GAINS), F32), VMEM),
            (shape((8, 128), jnp.int32), VMEM),
        ],
        (
            pltpu.VMEM((1024, 2048), BF16),
            pltpu.VMEM((1024, 2048), BF16),
            pltpu.VMEM((2048, 512), BF16),
            pltpu.VMEM((256, 2048), BF16),
            pltpu.VMEM((128, 512), BF16),
            pltpu.VMEM((256, 128), BF16),
            pltpu.VMEM((128, 512), BF16),
            pltpu.VMEM((256, 128), BF16),
            pltpu.VMEM((1, 1, 128), F32),
            pltpu.VMEM((128, 1, 128), F32),
            pltpu.VMEM((8, 128), jnp.int32),
            pltpu.VMEM((8, 128), jnp.int32),
            pltpu.VMEM((128, 384), BF16),
            pltpu.VMEM((128, 384), BF16),
            pltpu.VMEM((384, 128), BF16),
            pltpu.VMEM((256, 384), BF16),
            pltpu.VMEM((256, 384), BF16),
            pltpu.VMEM((128, 2048), BF16),
            pltpu.VMEM((1024, 2048), BF16),
            pltpu.VMEM((1024, 384), F32),
            pltpu.VMEM((1024, 512), BF16),
            pltpu.VMEM((1024, 256), BF16),
            pltpu.VMEM((1024, 128), F32),
            pltpu.VMEM((1024, 128), F32),
            pltpu.VMEM((1024, 128), F32),
        )
        + ROWS_SCRATCH,
    )


def layer_backward(
    residual, tokens, gains, lengths, down, cotangent_all, gate, up, heads, raw, attended,
    totals, cosine, sine, qkv, output, normed,
):
    def body(net, ins, outs, work):
        (
            residual_, tokens_, gains_, lengths_, down_, cotangent_all_, gate_, up_,
            heads_, raw_, attended_, totals_, cosine_, sine_, qkv_, output_, normed_,
        ) = ins
        (
            block_own, input_own, qkv_own, output_own, gate_own, up_own, down_own, gains_own,
        ) = outs
        (
            low, second, upstream, qkv_w, output_w, gate_w, up_w, down_w, hidden, gate_low, up_low,
            terms, back_rows, raw_here, totals_here, cosine_here, sine_here, key_sum, value_sum,
            own_out, qkv_total, output_total, gate_total, up_total, down_total,
            gain_rows, gain_land, first_gain, query_gain, flat, landed, land,
            *planes, free,
            early_landed, early_land, late_landed, late_land,
        ) = work
        share_landed, share_land = (early_landed, late_landed), (early_land, late_land)
        place = net.place
        units = Units(place)
        mine, theirs = place.core, 1 - place.core

        def load(source, target):
            return net.local(lambda: (source, target))

        loads = {
            "gate": load(gate_, gate_w),
            "up": load(up_, up_w),
            "upstream": load(cotangent_all_, upstream),
            "output": load(output_, output_w),
            "qkv": load(qkv_, qkv_w),
            "raw": load(raw_, raw_here),
            "totals": load(totals_, totals_here),
            "cosine": load(cosine_, cosine_here),
            "sine": load(sine_, sine_here),
        }
        second_gain = gains_[0:1, 2048:4096]

        def second_norm(n):
            spot = pl.ds(pl.multiple_of(n * 64, 64), 64)
            rows = residual_[spot]
            low[spot] = (rows * inverse_root(rows) * second_gain).astype(BF16)

        staged(2, second_norm)
        net.enter()
        gather = RowsGather(net, low, second)
        gather.start()
        down_gather = PlaneGather(net, down_, down_w, down_spot)
        down_gather.start()
        sums = RowsSum(net, terms, landed, land)
        mlp_sum = RowsSum(net, second, landed, land)
        first_sums = [
            RowsSum(
                net, upstream, share_landed[share], share_land[share], share, 2,
            )
            for share in range(2)
        ]
        last_gather = RowsGather(net, low, terms)
        gate_sum = PlaneSum(net, gate_w, gateup_spot, planes[0:4])
        up_sum = PlaneSum(net, up_w, gateup_spot, planes[4:8])
        down_sum = PlaneSum(net, down_w, down_spot, planes[8:12])
        qkv_sum = PlaneSum(net, qkv_w, rows_spot, planes[12:16])
        output_sum = PlaneSum(net, output_w, output_spot, planes[16:20])

        def forth(n):
            spot = units.rows(n)
            gate_value = nn(second[spot], gate_w[...])
            upward = nn(second[spot], up_w[...])
            sigmoid = 1.0 / (1.0 + jnp.exp(-gate_value))
            active = gate_value * sigmoid
            hidden[spot] = (active * upward).astype(BF16)
            gate_low[spot] = (upward * (sigmoid + active * (1.0 - sigmoid))).astype(BF16)
            up_low[spot] = active.astype(BF16)

        between = {
            1: lambda: (sums.combine(2), sums.start_far()),
            2: lambda: (sums.combine(-1), sums.start_left()),
            3: lambda: (sums.combine(1), sums.start_right()),
        }

        def back(n):
            spot = units.rows(3 - n)
            hidden_grad = nt(upstream[spot], down_w[...])
            gate_low[spot] = (hidden_grad * gate_low[spot].astype(F32)).astype(BF16)
            up_low[spot] = (hidden_grad * up_low[spot].astype(F32)).astype(BF16)
            at_step(between, n)
            terms[spot] = (nt(gate_low[spot], gate_w[...]) + nt(up_low[spot], up_w[...])).astype(
                BF16
            )

        def begin():
            for name in ("gate", "up", "upstream"):
                loads[name].wait()
            gather.here(0)

        def near():
            gather.near_first()
            down_gather.spread()
            gather.near_second()
            gather.here(1)

        def far():
            down_gather.forward()
            gather.far()
            gather.here(2)

        staged(4, forth, {0: begin, 1: near, 2: lambda: gather.here(-1), 3: far})
        down_gather.here()
        staged(4, back, None, {
            0: lambda: sums.pass_over(2), 1: lambda: sums.pass_over(-1),
            2: lambda: sums.pass_over(1), 3: lambda: sums.pass_over(0),
        })
        sums.combine(0)
        sums.passed()
        for axis, by in CORE_PARTNER + X_PARTNERS:
            pl.semaphore_signal(
                free, inc=1, device_id=place.device(axis, by), device_id_type=pl.DeviceIdType.MESH
            )
        sums.forward()
        gain_parts = []

        def weight_grad(low_grad, target):
            def one(n):
                columns = own_half(256, n)
                target[columns] = tn(second[:, columns], low_grad[...]).astype(BF16)

            return one

        staged(8, weight_grad(gate_low, gate_w))
        gate_sum.start()
        staged(8, weight_grad(up_low, up_w))
        up_sum.start()
        gather.gone()
        down_gather.gone()

        def own_rows(spot):
            start = (place.x * 2 + place.core) * 128 + spot.start
            return pl.ds(pl.multiple_of(start, 64), 64)

        def keep(spot, value):
            through_, gain_part = norm_back(residual_[spot], second_gain, value)
            through_ = through_ + upstream[own_rows(spot)].astype(F32)
            back_rows[spot] = through_
            low[spot] = through_.astype(BF16)
            gain_parts.append(jnp.sum(gain_part, axis=0, keepdims=True))

        sums.finish(keep)
        sums.departed()
        pl.semaphore_wait(free, 3)
        last_gather.start()

        def through(n):
            spot = units.rows(n)
            second[spot] = nn(hidden[spot], down_w[...]).astype(BF16)

        staged(4, through)

        def down_grad(n):
            columns = own_half(256, n)
            down_w[columns] = tn(hidden[:, columns], upstream[...]).astype(BF16)

        staged(3, down_grad)
        down_sum.start()
        last_gather.near_first()
        heads_cols, attended_cols = hidden.at[:, 0:512], hidden.at[:, 512:768]
        parts, attended_grad = gate_low.at[:, 0:512], gate_low.at[:, 512:768]
        attended_rows = up_low.at[:, 0:256]
        loads["heads"] = load(heads_, heads_cols)
        loads["attended"] = load(attended_, attended_cols)
        gate_sum.forward()
        loads["output"].wait()
        key_sum[...] = jnp.zeros_like(key_sum)
        value_sum[...] = jnp.zeros_like(value_sum)
        query_gain[...] = jnp.zeros_like(query_gain)
        for name in ("heads", "raw", "totals", "cosine", "sine"):
            loads[name].wait()
        documents = Documents(lengths_[...])
        gain_query, gain_key = gains_[0:1, 4096:4224], gains_[0:1, 4224:4352]

        def through_rope(value, cosine_part, sine_part, raw_part, gain):
            value = value * cosine_part + pltpu.roll(value * sine_part, 64, 1)
            through_, gain_part = norm_back(raw_part, gain, value)
            return through_.astype(BF16), jnp.sum(gain_part, axis=0, keepdims=True)

        def twice(value):
            return jnp.concatenate([value, value], axis=0)

        def both_heads(ref, spot, first):
            return jnp.concatenate(
                [ref[spot, first : first + 128], ref[spot, first + 128 : first + 256]], axis=0
            )

        def attend(n, core):
            spot = units.true_rows(n, core)
            keys = 512 * (core + 1)
            query = both_heads(hidden, spot, 0)
            upward = both_heads(gate_low, spot, 512)
            key, value = hidden[0:keys, 256:384], hidden[0:keys, 384:512]
            scores = nt(query, key) * SCALE
            total = jnp.concatenate([totals_here[spot, 0:1], totals_here[spot, 64:65]], axis=0)
            allowed = allowed_pairs(documents, spot.start, 128, keys)
            probability = jnp.where(twice(allowed), jnp.exp(scores - total), 0.0)
            prob_grad = nt(upward, value)
            centre = jnp.sum(probability * prob_grad, axis=-1, keepdims=True)
            score_grad = (probability * (prob_grad - centre)).astype(BF16)
            value_sum[0:keys] += tn(probability.astype(BF16), upward)
            key_sum[0:keys] += tn(score_grad, query)
            query_grad = nn(score_grad, key) * SCALE
            through_, gain_part = through_rope(
                query_grad, twice(cosine_here[spot]), twice(sine_here[spot]),
                both_heads(raw_here, spot, 0), gain_query,
            )
            here = pl.ds(pl.multiple_of(units.chip(n) * 256 + core * 128, 128), 128)
            gate_low[here, 0:128] = through_[0:128]
            gate_low[here, 128:256] = through_[128:256]
            query_gain[...] += gain_part

        def enter(n):
            grad = nt(terms[units.rows(n)], output_w[...]).astype(BF16)
            for core in range(2):
                attended_grad[units.true_rows(n, core)] = grad[core * 128 : core * 128 + 128]
            for core in range(2):
                attend(n, core)

        def own_here():
            last_gather.here(0)
            for k in (2, 1, -1, 0):
                mlp_sum.pass_over(k)

        def combined():
            last_gather.near_second()
            last_gather.here(1)
            for k in (2, 1, -1, 0):
                mlp_sum.combine(k)

        def last_far():
            up_sum.forward()
            last_gather.far()
            mlp_sum.start_far()
            mlp_sum.start_right()
            mlp_sum.start_left()
            last_gather.here(2)

        staged(4, enter, {
            0: own_here, 1: combined, 2: lambda: last_gather.here(-1), 3: last_far,
        })
        mlp_sum.passed()
        loads["normed"] = load(normed_, second)
        loads["attended"].wait()

        def same_order(n):
            for core in range(2):
                start = pl.multiple_of(units.chip(n) * 256 + core * 128, 128)
                attended_rows[pl.ds(start, 128)] = attended_cols[units.true_rows(n, core)]

        staged(4, same_order)

        def output_grad(n):
            columns = own_half(512, n)
            output_w[:, columns] = tn(attended_rows[...], terms[:, columns]).astype(BF16)

        staged(4, output_grad)
        output_sum.start()
        gate_sum.gather()
        down_sum.forward()
        mlp_sum.forward()
        def key_back(true, gain_sum):
            spot = pl.ds(pl.multiple_of(true * 128, 128), 128)
            start = (lax.rem(true, RING) * 2 + lax.div(true, RING)) * 128
            through_, gain_part = through_rope(
                key_sum[spot] * SCALE, cosine_here[spot], sine_here[spot],
                raw_here[spot, 256:384], gain_key,
            )
            here = pl.ds(pl.multiple_of(start, 128), 128)
            gate_low[here, 256:384] = through_
            gate_low[here, 384:512] = value_sum[spot].astype(BF16)
            return gain_sum + gain_part

        key_gain = lax.fori_loop(0, 8, key_back, jnp.zeros((1, 128), F32))
        last_gather.gone()
        loads["tokens"] = load(tokens_, low)
        loads["qkv"].wait()
        loads["normed"].wait()
        up_sum.gather()
        first_gain[...] = jnp.zeros_like(first_gain)

        def out(n):
            spot = units.rows(3 - n)
            value = nt(parts[spot], qkv_w[...])
            upstream[spot] = value.astype(BF16)
            part = jnp.sum(value * second[spot].astype(F32), axis=0, keepdims=True)
            first_gain[...] += part

        early, late = first_sums

        def give(k):
            for one in first_sums:
                one.pass_over(k)

        staged(4, out, None, {
            0: lambda: give(2),
            1: lambda: (give(-1), early.combine(2), early.start_far()),
            2: lambda: (give(1), early.combine(-1), early.start_left()),
            3: lambda: (give(0), early.combine(1), early.start_right()),
        })
        output_sum.forward()

        def keep_block(spot, value):
            own_out[spot] = (residual_[spot] + value).astype(BF16)

        mlp_sum.finish(keep_block)
        block_turn = Turn(net, parts_of(own_out, block_own, 2))
        block_turn.start()

        def qkv_grad(n):
            columns = own_half(256, n)
            qkv_w[columns] = tn(second[:, columns], parts[...]).astype(BF16)

        staged(8, qkv_grad, None, {
            1: lambda: (late.combine(2), late.start_far(), early.combine(0)),
            3: lambda: (early.forward(), late.combine(-1), late.start_left()),
            5: lambda: (late.combine(1), late.start_right(), late.combine(0)),
        })
        qkv_sum.start()
        flat[...] = jnp.concatenate(
            [first_gain[...] / gains_[0:1, 0:2048], gain_parts[0] + gain_parts[1], query_gain[...], key_gain],
            axis=1,
        )

        def to_rows(n, total):
            entry = lax.broadcasted_iota(jnp.int32, (128, 256), 1) + n * 256
            past = entry - owner_starts((128, 256), 0)
            here = flat[0:1, own_half(256, n)]
            owned = jnp.where((past >= 0) & (past < OWN_GAINS), here, 0.0)
            place_ = lax.broadcasted_iota(jnp.int32, (128, 256), 0)
            column = (column_of(entry) == place_).astype(F32)
            return total + lax.dot_general(
                owned, column, (((1,), (1,)), ((), ())),
                precision=lax.Precision.HIGHEST, preferred_element_type=F32,
            )

        rows_of = lax.fori_loop(0, GAINS // 256, to_rows, jnp.zeros((128, 128), F32))
        gain_rows[...] = rows_of.reshape(128, 1, 128)
        late.forward()
        gains_steps = GainsSum(net, gain_rows, gains_own, gain_land).steps()
        next(gains_steps)

        halves = []

        def exchange(cut, there):
            halves.append(net.local(lambda: (cut(mine), there(mine))))
            halves.append(
                Give(net, lambda: (cut(theirs), there(mine)), lambda: there(theirs))
            )

        output_sum.gather()
        qkv_sum.forward()
        next(gains_steps)
        down_sum.gather()
        gate_sum.finish(gate_total)
        exchange(
            lambda core: gate_total.at[own_half(128, core)],
            lambda core: gate_own.at[:, own_half(384, core)],
        )
        output_sum.finish(output_total)
        output_turn = Turn(net, [(output_total, output_own)])
        output_turn.start()
        next(gains_steps)
        turns = []
        block_turn.wait()
        loads["tokens"].wait()

        def ended(share):
            def keep_first(spot, value):
                spot = pl.ds(64 * share + spot.start, 32)
                through_, _ = norm_back(low[spot].astype(F32), gains_[0:1, 0:2048], value)
                own_out[spot] = (back_rows[spot] + through_).astype(BF16)

            first_sums[share].finish(keep_first)
            spot = pl.ds(64 * share, 64)
            turns.append(Turn(net, [(own_out.at[spot], input_own.at[spot])]))
            turns[-1].start()

        ended(0)
        qkv_sum.gather()
        next(gains_steps)
        ended(1)
        qkv_sum.finish(qkv_total)
        qkv_turn = Turn(net, [(qkv_total, qkv_own)])
        qkv_turn.start()
        up_sum.finish(up_total)
        exchange(
            lambda core: up_total.at[own_half(128, core)],
            lambda core: up_own.at[:, own_half(384, core)],
        )
        down_sum.finish(down_total)
        exchange(
            lambda core: down_total.at[:, own_half(128, core)],
            lambda core: down_own.at[own_half(384, core)],
        )
        next(gains_steps)
        for copy in halves:
            copy.wait()
        for turn in (output_turn, *turns, qkv_turn):
            turn.wait()

    plans = (
        2 * (RowsGather,) + 4 * (RowsSum,) + (PlaneGather,) + 5 * (PlaneSum,) + (GainsSum,)
    )
    return Kernel(
        1, plans, 3, 6, 13 + 3 - 1, CORE_PARTNER + X_PARTNERS + FAR_X + PLANE_PARTNERS + TURN_PARTNERS
    )(
        body,
        [
            (residual, VMEM), (tokens, HBM), (gains, VMEM), (lengths, VMEM),
            (down, VMEM), (cotangent_all, HBM), (gate, HBM), (up, HBM), (heads, HBM), (raw, HBM),
            (attended, HBM), (totals, HBM), (cosine, HBM), (sine, HBM), (qkv, HBM), (output, HBM),
            (normed, HBM),
        ],
        [
            (shape((128, 2048)), HBM),
            (shape((128, 2048)), HBM),
            (shape((128, 512)), VMEM),
            (shape((256, 128)), VMEM),
            (shape((128, 768)), HBM),
            (shape((128, 768)), HBM),
            (shape((768, 128)), HBM),
            (shape((1, 1, 128), F32), VMEM),
        ],
        (
            pltpu.VMEM((128, 2048), BF16),
            pltpu.VMEM((1024, 2048), BF16),
            pltpu.VMEM((1024, 2048), BF16),
            pltpu.VMEM((2048, 512), BF16),
            pltpu.VMEM((256, 2048), BF16),
            pltpu.VMEM((2048, 768), BF16),
            pltpu.VMEM((2048, 768), BF16),
            pltpu.VMEM((768, 2048), BF16),
            pltpu.VMEM((1024, 768), BF16),
            pltpu.VMEM((1024, 768), BF16),
            pltpu.VMEM((1024, 768), BF16),
            pltpu.VMEM((1024, 2048), BF16),
            pltpu.VMEM((128, 2048), F32),
            pltpu.VMEM((1024, 384), F32),
            pltpu.VMEM((1024, 128), F32),
            pltpu.VMEM((1024, 128), F32),
            pltpu.VMEM((1024, 128), F32),
            pltpu.VMEM((1024, 128), F32),
            pltpu.VMEM((1024, 128), F32),
            pltpu.VMEM((128, 2048), BF16),
            pltpu.VMEM((128, 512), BF16),
            pltpu.VMEM((256, 128), BF16),
            pltpu.VMEM((256, 384), BF16),
            pltpu.VMEM((256, 384), BF16),
            pltpu.VMEM((384, 256), BF16),
            pltpu.VMEM((128, 1, 128), F32),
            pltpu.VMEM((127, 1, 128), F32),
            pltpu.VMEM((1, 2048), F32),
            pltpu.VMEM((1, 128), F32),
            pltpu.VMEM((1, GAINS), F32),
        )
        + ROWS_SCRATCH
        + plane_scratch(256, 384) * 2
        + plane_scratch(384, 256)
        + plane_scratch(128, 512, 32)
        + plane_scratch(256, 128, 64)
        + (pltpu.SemaphoreType.REGULAR,)
        + (pltpu.VMEM((4, 2, 32, 2048), BF16), pltpu.VMEM((6, 32, 2048), BF16)) * 2,
    )


def step_rates(total_tokens):
    root_tokens = math.sqrt(total_tokens)
    narrow = MODEL_WIDTH ** (-0.5)
    return (
        narrow / (2.0 * root_tokens),
        narrow / (2.0 * root_tokens),
        (QUERY_HEADS * HEAD_SIZE // 128) ** (-0.5) / (0.24 * root_tokens),
        narrow / (0.7 * root_tokens),
        FF ** (-0.5) / (1.2 * root_tokens),
        0.025 / root_tokens,
    )


def update(rows, gradients, state):
    rates = step_rates(GROUP_TOK * 16)

    def kernel(*refs):
        block_, input_, qkv_, output_, gate_, up_, down_, gains_ = refs[:8]
        masters, moments, averages = refs[8:14], refs[14:20], refs[20:26]
        outs = refs[26:]
        outs[0][...] = block_[...]
        outs[1][...] = input_[...]

        def one(n, gradient, spot):
            gradient = gradient.astype(F32)
            moment = MOMENTUM * moments[n][spot] + gradient
            master = masters[n][spot] - rates[n] * (gradient + MOMENTUM * moment)
            outs[2 + n][spot] = master
            outs[8 + n][spot] = moment
            outs[14 + n][spot] = AVERAGING * averages[n][spot] + (1.0 - AVERAGING) * master

        one(0, qkv_[:, 0:256], ...)
        one(1, qkv_[:, 256:384], 0)
        one(1, qkv_[:, 384:512], 1)
        one(2, output_[...], ...)
        one(3, gate_[...], 0)
        one(3, up_[...], 1)
        one(4, down_[...], ...)
        one(5, gains_[0, 0:1, 0:OWN_GAINS], ...)

    outs = [shape(a.shape, a.dtype) for a in rows]
    outs += [shape(a.shape, F32) for a in state]
    arrays = (*rows, *gradients, *state)
    return pl.pallas_call(
        kernel,
        out_shape=outs,
        in_specs=[pl.BlockSpec(memory_space=VMEM)] * len(arrays),
        out_specs=[pl.BlockSpec(memory_space=VMEM)] * len(outs),
        compiler_params=pltpu.CompilerParams(vmem_limit_bytes=61 * 2**20),
        name="update",
    )(*arrays)


def body(tokens, cotangent, doc_lengths, *state):
    query_weight, key_value_weight, output_weight, gateup_weight, down_weight, norm_gains = state[:6]
    cosine, sine = rope_tables()
    (
        residual, tokens_here, normed, raw, heads, attended, totals,
        cosine, sine, qkv, output, gate, up, down, cotangent_all, gains, lengths,
    ) = attention_forward(
        tokens, cotangent, query_weight, key_value_weight, output_weight, gateup_weight,
        down_weight, norm_gains.reshape(1, OWN_GAINS), doc_lengths,
        jnp.asarray(cosine), jnp.asarray(sine),
    )
    block_out, input_grad, *gradients = layer_backward(
        residual, tokens_here, gains, lengths, down, cotangent_all, gate, up,
        heads, raw, attended, totals, cosine, sine, qkv, output, normed,
    )
    state = [a.reshape(1, OWN_GAINS) if a.ndim == 1 else a for a in state]
    outs = update((block_out, input_grad), gradients, state)
    return tuple(a.reshape(OWN_GAINS) if a.shape == (1, OWN_GAINS) else a for a in outs)


def solution(mesh):
    parted = Mesh(mesh.devices.reshape(GRID), AXES)
    data = ("z", "ylo", "core")
    tensor = ("yhi", "x")
    rows = P(AXES, None)
    by_rows = P(data, tensor)
    pair = P(None, data, tensor)
    by_columns = P(tensor, data)
    flat = P(AXES)
    weights = (by_rows, pair, by_columns, pair, by_columns, flat)
    return jax.shard_map(
        body,
        mesh=parted,
        in_specs=(rows, rows, P(data, None)) + weights * 3,
        out_specs=(rows, rows) + weights * 3,
        check_vma=False,
    )
```

```python
import math

import jax
import jax.numpy as jnp
import numpy as np
from jax import lax
from jax.experimental import pallas as pl
from jax.experimental.pallas import tpu as pltpu
from jax.sharding import Mesh
from jax.sharding import PartitionSpec as P

MODEL_WIDTH = 2048
QUERY_HEADS = 16
HEAD_SIZE = 128
FF = 6144
GROUP_TOK = 1024
GAINS = 4352
OWN_GAINS = 34
EPSILON = 1e-06
MOMENTUM = 0.9
AVERAGING = 0.5
ROPE_BASE = 1000000.0
SCALE = HEAD_SIZE ** (-0.5)

AXES = ("z", "ylo", "core", "yhi", "x")
GRID = (4, 2, 2, 2, 4)
RING = 4
BF16 = jnp.bfloat16
F32 = jnp.float32
HBM = pl.ANY
VMEM = pltpu.VMEM


class Place:
    def __init__(self):
        self.x = lax.axis_index("x")
        self.z = lax.axis_index("z")
        self.core = lax.axis_index("core")
        self.yhi = lax.axis_index("yhi")
        self.ylo = lax.axis_index("ylo")
        self.y = self.yhi * 2 + self.ylo
        self.native = self.core == self.yhi
        at = {"x": self.x, "y": self.y, "z": self.z}
        self.steps = {
            (axis, by): lax.rem(here + by, RING) if by else here
            for axis, here in at.items()
            for by in range(RING)
        }
        self.devices = {
            "core": {"core": 1 - self.core},
            "turn": {"core": 1 - self.core, "yhi": 1 - self.yhi},
        }
        for (axis, by), there in self.steps.items():
            self.devices[axis, by] = (
                {"yhi": lax.div(there, 2), "ylo": lax.rem(there, 2)}
                if axis == "y"
                else {axis: there}
            )

    def step(self, axis, by):
        return self.steps[axis, by % RING]

    def device(self, axis, by=1):
        return self.devices[axis] if axis in ("core", "turn") else self.devices[axis, by % RING]


class Local:
    def __init__(self, refs, sems, index):
        self.refs, self.sems, self.index = refs, sems, index

    def copy(self):
        source, target = self.refs()
        return pltpu.make_async_copy(source, target, self.sems.at[self.index])

    def start(self):
        self.copy().start()

    def wait(self):
        self.copy().wait()


class Net:
    def __init__(self, place, partners, send_sems, recv_sems, local_sems):
        self.place, self.partners = place, partners
        self.send_sems, self.recv_sems, self.local_sems = send_sems, recv_sems, local_sems
        self.leaving, self.arriving, self.local_count = 0, 0, 0
        self.waits = []

    def greet(self):
        barrier = pltpu.get_barrier_semaphore()
        for axis, by in self.partners:
            pl.semaphore_signal(
                barrier,
                inc=1,
                device_id=self.place.device(axis, by),
                device_id_type=pl.DeviceIdType.MESH,
            )

    def enter(self):
        pl.semaphore_wait(pltpu.get_barrier_semaphore(), len(self.partners))

    def out(self):
        self.leaving += 1
        return self.leaving - 1

    def into(self):
        self.arriving += 1
        return self.arriving - 1

    def local_number(self):
        self.local_count += 1
        return self.local_count - 1

    def copy(self, source, target, out, into, axis="core", by=1):
        return pltpu.make_async_remote_copy(
            src_ref=source,
            dst_ref=target,
            send_sem=self.send_sems.at[out],
            recv_sem=self.recv_sems.at[into],
            device_id=self.place.device(axis, by),
            device_id_type=pl.DeviceIdType.MESH,
        )

    def send(self, refs, out, into, axis, by=1):
        self.copy(*refs(), out, into, axis, by).start()

    def here(self, into, view):
        self.copy(view, view, 0, into).wait_recv()

    def gone(self, out, view):
        self.copy(view, view, out, 0).wait_send()

    def later(self, wait):
        self.waits.append(wait)

    def finish(self):
        for wait in self.waits:
            wait()

    def local(self, refs):
        copy = Local(refs, self.local_sems, self.local_number())
        copy.start()
        return copy


def at_step(acts, n):
    for at, act in (acts or {}).items():

        @pl.when(n == at)
        def _():
            act()


def staged(count, compute, before=None, after=None):
    def step(n, carry):
        at_step(before, n)
        compute(n)
        at_step(after, n)
        return carry

    lax.fori_loop(0, count, step, 0)


class RowsGather:
    OUT, INTO, LOCALS = 1, 7, 2

    def __init__(self, net, own, whole):
        self.net, self.own, self.whole = net, own, whole
        self.rows = own.shape[0]
        self.half = self.rows // 2
        place = net.place
        self.me, self.other = place.core, 1 - place.core
        self.spots = {k: place.step("x", k) for k in (0, 1, -1, 2)}
        self.out = net.out()
        self.first, self.second, self.third = net.into(), net.into(), net.into()
        self.shared = {k: net.into() for k in (0, 1, -1, 2)}
        self.kept = []
        net.later(self.gone)

    def block(self, core, k, part):
        start = (self.spots[k] * 2 + core) * self.rows + part * self.half
        return self.whole.at[pl.ds(pl.multiple_of(start, self.half), self.half)]

    def mine(self, k, part):
        return self.block(self.me, k, part)

    def piece(self, part):
        return self.own.at[pl.ds(part * self.half, self.half)]

    def share(self, k, part):
        refs = lambda: (self.piece(part) if k == 0 else self.mine(k, part), self.mine(k, part))
        self.net.send(refs, self.out, self.shared[k], "core")

    def both(self):
        return self.whole.at[pl.ds(0, self.rows)]

    def start(self, parts=(0, 1)):
        for part in parts:
            refs = lambda part=part: (self.piece(part), self.mine(0, part))
            first, second = (1, -1) if part == 0 else (-1, 1)
            self.net.send(refs, self.out, self.first, "x", first)
            self.net.send(refs, self.out, self.second, "x", second)
            self.share(0, part)
            self.kept.append(self.net.local(refs))

    def near_first(self):
        self.net.here(self.first, self.both())
        self.net.send(lambda: (self.mine(-1, 0),) * 2, self.out, self.third, "x", 1)
        self.net.send(lambda: (self.mine(1, 1),) * 2, self.out, self.third, "x", -1)
        self.share(-1, 0)
        self.share(1, 1)

    def near_second(self):
        self.net.here(self.second, self.both())
        self.share(-1, 1)
        self.share(1, 0)

    def far(self):
        self.net.here(self.third, self.both())
        self.share(2, 0)
        self.share(2, 1)

    def here(self, k):
        if k == 0:
            for copy in self.kept:
                copy.wait()
        self.net.here(self.shared[k], self.both())

    def gone(self):
        if self.out is not None:
            self.net.gone(self.out, self.whole.at[pl.ds(0, 7 * self.rows)])
            self.out = None


class RowsSum:
    OUT, INTO = 2, 6

    def __init__(self, net, whole, landed, land, share=0, shares=1):
        self.net, self.whole, self.landed, self.land = net, whole, landed, land
        self.share, self.shares = share, shares
        self.half = landed.shape[2]
        place = net.place
        self.me, self.other = place.core, 1 - place.core
        self.spots = {k: place.step("x", k) for k in (0, 1, -1, 2)}
        self.over, self.along = net.out(), net.out()
        self.given = {k: net.into() for k in (0, 1, -1, 2)}
        self.through, self.last = net.into(), net.into()
        net.later(self.passed)
        net.later(self.departed)

    def block(self, core, k, part):
        block = (self.spots[k] * 2 + core) * self.shares + self.share
        start = (block * 2 + part) * self.half
        return self.whole.at[pl.ds(pl.multiple_of(start, self.half), self.half)]

    def own(self, k, part):
        return self.landed.at[k % RING, part]

    def pass_over(self, k):
        for part in range(2):
            refs = lambda part=part: (self.block(self.other, k, part), self.own(k, part))
            self.net.send(refs, self.over, self.given[k], "core")

    def passed(self):
        if self.over is not None:
            self.net.gone(self.over, self.landed)
            self.over = None

    def departed(self):
        if self.along is not None:
            self.net.gone(self.along, self.land)
            self.along = None

    def combine(self, k):
        self.net.here(self.given[k], self.landed.at[k % RING])
        for part in range(2):
            here = self.own(k, part)
            here[...] = here[...] + self.block(self.me, k, part)[...]

    def along_x(self, refs, into, by):
        self.net.send(refs, self.along, into, "x", by)

    def start_far(self):
        self.along_x(lambda: (self.own(2, 0), self.land.at[0]), self.through, 1)
        self.along_x(lambda: (self.own(2, 1), self.land.at[1]), self.through, -1)

    def start_right(self):
        self.along_x(lambda: (self.own(1, 1), self.land.at[3]), self.last, 1)

    def start_left(self):
        self.along_x(lambda: (self.own(-1, 0), self.land.at[4]), self.last, -1)

    def forward(self):
        land = self.land
        self.net.here(self.through, land.at[pl.ds(0, 2)])
        land[0] = land[0] + self.own(1, 0)[...]
        self.along_x(lambda: (land.at[0], land.at[2]), self.last, 1)
        land[1] = land[1] + self.own(-1, 1)[...]
        self.along_x(lambda: (land.at[1], land.at[5]), self.last, -1)

    def finish(self, keep):
        land = self.land
        self.net.here(self.last, land.at[pl.ds(2, 4)])
        for part in range(2):
            total = self.own(0, part)[...].astype(F32) + land[2 + part].astype(F32)
            keep(pl.ds(part * self.half, self.half), total + land[4 + part].astype(F32))


ROWS_SCRATCH = (pltpu.VMEM((4, 2, 64, 2048), BF16), pltpu.VMEM((6, 64, 2048), BF16))


class PlaneGather:
    OUT, INTO, LOCALS = 1, 12, 1

    def __init__(self, net, own, whole, spot, first_rows=None):
        self.net, self.own, self.whole, self.spot = net, own, whole, spot
        self.rows = own.shape[0]
        first_rows = self.rows // 2 if first_rows is None else first_rows
        self.sizes, self.starts = (first_rows, self.rows - first_rows), (0, first_rows)
        self.width = own.shape[1]
        self.out = net.out()
        self.first = [net.into() for _ in range(2)]
        self.rings = {(color, i): net.into() for color in range(2) for i in (0, 1, -1, -2)}
        self.last = [net.into() for _ in range(2)]
        net.later(self.gone)

    def gone(self):
        if self.out is not None:
            rows = self.whole.shape[0] // 16 * 15
            self.net.gone(self.out, self.whole.at[pl.ds(0, rows)])
            self.out = None

    def view(self, color, i, j, part=None):
        place = self.net.place
        first, second = self.axes(color)
        a, b = place.step(first, i), place.step(second, j)
        row, columns = self.spot(a, b) if color == 0 else self.spot(b, a)
        start, size = row + self.starts[color], self.sizes[color]
        if part is not None:
            size //= 2
            start = start + part * size
        return self.whole.at[pl.ds(pl.multiple_of(start, math.gcd(size, self.rows)), size), columns]

    def bytes_of(self, color, count):
        size = self.sizes[color]
        if count * size <= self.whole.shape[0]:
            return self.whole.at[pl.ds(0, count * size), pl.ds(0, self.width)]
        return self.whole.at[pl.ds(0, size), pl.ds(0, count * self.width)]

    @staticmethod
    def axes(color):
        return ("z", "y") if color == 0 else ("y", "z")

    def mine(self, color):
        return self.own.at[pl.ds(self.starts[color], self.sizes[color])]

    def ring(self, color, i):
        axis = self.axes(color)[1]
        refs = lambda: (
            self.mine(color) if i == 0 else self.view(color, i, 0), self.view(color, i, 0)
        )
        for by in (1, -1):
            self.net.send(refs, self.out, self.rings[color, i], axis, by)

    def start(self):
        for color in range(2):
            axis = self.axes(color)[0]
            refs = lambda color=color: (self.mine(color), self.view(color, 0, 0))
            for by in (1, -1, 2):
                self.net.send(refs, self.out, self.first[color], axis, by)
        for color in range(2):
            self.ring(color, 0)
        self.kept = self.net.local(self.place_here)

    def place_here(self):
        row, columns = self.spot(self.net.place.z, self.net.place.y)
        return self.own, self.whole.at[pl.ds(pl.multiple_of(row, self.rows), self.rows), columns]

    def spread(self):
        for color in range(2):
            self.net.here(self.first[color], self.bytes_of(color, 3))
        for i in (-1, 1, -2):
            for color in range(2):
                self.ring(color, i)

    def forward(self, steps=(0, 1, -1, -2)):
        for i in steps:
            for color in range(2):
                axis = self.axes(color)[1]
                self.net.here(self.rings[color, i], self.bytes_of(color, 2))
                for j, part, by in ((-1, 0, 1), (1, 1, -1)):
                    refs = lambda color=color, i=i, j=j, part=part: (
                        self.view(color, i, j, part),
                    ) * 2
                    self.net.send(refs, self.out, self.last[color], axis, by)

    def here(self):
        for color in range(2):
            self.net.here(self.last[color], self.bytes_of(color, 4))
        self.kept.wait()


class PlaneSum:
    OUT, INTO = 4, 18

    def __init__(self, net, whole, spot, scratch):
        self.net, self.whole, self.spot = net, whole, spot
        self.land, self.last = scratch[0:2], scratch[2:4]
        self.sizes = [land.shape[2] for land in self.land]
        self.starts = (0, 2 * self.sizes[0])
        self.ring_out, self.last_out = (net.out(), net.out()), (net.out(), net.out())
        ways = [(color, k) for color in range(2) for k in range(RING)]
        self.through = {way: net.into() for way in ways}
        self.sides = {way: net.into() for way in ways}
        self.ends = [net.into() for _ in range(2)]
        for color in range(2):
            net.later(lambda color=color: net.gone(self.ring_out[color], self.land[color]))
            net.later(lambda color=color: net.gone(self.last_out[color], self.last[color]))

    @staticmethod
    def axes(color):
        return ("y", "z") if color == 0 else ("z", "y")

    def own(self, color, n, k, part):
        place = self.net.place
        first, second = self.axes(color)
        a, b = place.step(first, n), place.step(second, k)
        row, columns = self.spot(b, a) if color == 0 else self.spot(a, b)
        size = self.sizes[color]
        start = row + self.starts[color] + part * size
        return self.whole.at[pl.ds(pl.multiple_of(start, math.gcd(size, 128)), size), columns]

    def slot(self, color, k, n):
        return self.land[color].at[k % RING, n]

    def end(self, color, k, part):
        return self.last[color].at[k % RING - 1, part]

    def start(self):
        for k in (2, 1, -1, 0):
            for color in range(2):
                axis = self.axes(color)[0]
                through, sides = self.through[color, k % RING], self.sides[color, k % RING]
                for n, part, slot, into, by in (
                    (2, 0, 0, through, 1), (2, 1, 1, through, -1),
                    (1, 1, 3, sides, 1), (-1, 0, 4, sides, -1),
                ):
                    refs = lambda color=color, k=k, n=n, part=part, slot=slot: (
                        self.own(color, n, k, part), self.slot(color, k, slot)
                    )
                    self.net.send(refs, self.ring_out[color], into, axis, by)

    def forward(self, steps=(2, 1, -1, 0)):
        for k in steps:
            for color in range(2):
                axis = self.axes(color)[0]
                sides = self.sides[color, k % RING]
                self.net.here(
                    self.through[color, k % RING], self.land[color].at[k % RING, pl.ds(0, 2)]
                )
                for slot, n, part, target, by in ((0, 1, 0, 2, 1), (1, -1, 1, 5, -1)):
                    here = self.slot(color, k, slot)
                    here[...] = here[...] + self.own(color, n, k, part)[...]
                    refs = lambda color=color, k=k, slot=slot, target=target: (
                        self.slot(color, k, slot), self.slot(color, k, target)
                    )
                    self.net.send(refs, self.ring_out[color], sides, axis, by)

    def gather(self, steps=(2, 1, -1, 0)):
        for k in steps:
            for color in range(2):
                second = self.axes(color)[1]
                self.net.here(
                    self.sides[color, k % RING], self.land[color].at[k % RING, pl.ds(2, 4)]
                )
                for part in range(2):
                    here = self.slot(color, k, 2 + part)
                    total = self.own(color, 0, k, part)[...].astype(F32) + here[...].astype(F32)
                    total = total + self.slot(color, k, 4 + part)[...].astype(F32)
                    here[...] = total.astype(BF16)
                    if k != 0:
                        refs = lambda color=color, k=k, part=part: (
                            self.slot(color, k, 2 + part), self.end(color, k, part)
                        )
                        self.net.send(refs, self.last_out[color], self.ends[color], second, k)

    def finish(self, total):
        for color in range(2):
            self.net.here(self.ends[color], self.last[color])
            for part in range(2):
                value = self.slot(color, 0, 2 + part)[...].astype(F32)
                for k in (1, -1, 2):
                    value = value + self.end(color, k, part)[...].astype(F32)
                start = self.starts[color] + part * self.sizes[color]
                total[pl.ds(start, self.sizes[color])] = value.astype(total.dtype)


def plane_scratch(rows, columns, first_rows=None):
    first_rows = rows // 2 if first_rows is None else first_rows
    parts = (first_rows // 2, (rows - first_rows) // 2)
    return tuple(
        pltpu.VMEM((*dims, part, columns), BF16) for dims in ((4, 6), (3, 2)) for part in parts
    )


class Turn:
    def __init__(self, net, pairs):
        self.net = net
        self.pairs = [
            (source, target, net.out(), net.into(), net.local_number()) for source, target in pairs
        ]

    def copies(self):
        return [self.net.copy(a, b, out, into, "turn") for a, b, out, into, _ in self.pairs]

    def kept(self):
        sems = self.net.local_sems
        return [pltpu.make_async_copy(a, b, sems.at[index]) for a, b, _, _, index in self.pairs]

    def both(self, act):
        @pl.when(jnp.logical_not(self.net.place.native))
        def _():
            for copy in self.copies():
                act(copy)

        @pl.when(self.net.place.native)
        def _():
            for copy in self.kept():
                act(copy)

    def start(self):
        self.both(lambda copy: copy.start())

    def wait(self):
        self.both(lambda copy: copy.wait())


class Give:
    def __init__(self, net, refs, there):
        self.net, self.there = net, there
        self.out, self.into = net.out(), net.into()
        net.send(refs, self.out, self.into, "core")
        net.later(lambda: net.gone(self.out, refs()[0]))

    def wait(self):
        self.net.here(self.into, self.there())


def parts_of(source, target, count):
    rows = source.shape[0] // count
    spots = [pl.ds(part * rows, rows) for part in range(count)]
    return [(source.at[spot], target.at[spot]) for spot in spots]


class GainsGather:
    OUT, INTO, LOCALS = 1, 4, 1

    def __init__(self, net, own, whole):
        self.net, self.own, self.whole = net, own, whole
        self.out = net.out()
        self.into = [net.into() for _ in range(4)]
        net.later(lambda: net.gone(self.out, whole.at[pl.ds(0, 127)]))

    def rows(self, z, y, x, core, count):
        start = ((z * RING + y) * RING + x) * 2 + core
        return self.whole.at[pl.ds(start if count == 1 else pl.multiple_of(start, count), count)]

    def spot(self, axis, by):
        place = self.net.place
        if axis == "core":
            return self.rows(place.z, place.y, place.x, (place.core + by) % 2, 1)
        if axis == "x":
            return self.rows(place.z, place.y, place.step("x", by), 0, 2)
        if axis == "y":
            return self.rows(place.z, place.step("y", by), 0, 0, 8)
        return self.rows(place.step("z", by), 0, 0, 0, 32)

    def steps(self):
        net = self.net
        net.local(lambda: (self.own, self.spot("core", 0))).wait()
        for into, axis, count in zip(self.into, ("core", "x", "y", "z"), (1, 2, 8, 32)):
            ways = (1,) if axis == "core" else (1, -1, 2)
            for by in ways:
                net.send(lambda axis=axis: (self.spot(axis, 0),) * 2, self.out, into, axis, by)
            yield
            net.here(into, self.whole.at[pl.ds(0, count * len(ways))])
        yield


class GainsSum(GainsGather):
    def __init__(self, net, whole, total, land):
        super().__init__(net, None, whole)
        self.total, self.land = total, land

    def steps(self):
        net, land = self.net, self.land
        first = 0
        for into, axis, count in zip(self.into, ("z", "y", "x", "core"), (32, 8, 2, 1)):
            ways = (1,) if axis == "core" else (1, -1, 2)
            spots = [pl.ds(first + n * count, count) for n in range(len(ways))]
            for spot, by in zip(spots, ways):
                refs = lambda axis=axis, spot=spot, by=by: (self.spot(axis, by), land.at[spot])
                net.send(refs, self.out, into, axis, by)
            yield
            net.here(into, land.at[pl.ds(first, count * len(ways))])
            value = self.spot(axis, 0)[...]
            for spot in spots:
                value = value + land[spot]
            if axis == "core":
                self.total[...] = value
            else:
                self.spot(axis, 0)[...] = value
            first += count * len(ways)
        yield


class Kernel:
    def __init__(self, number, plans, gives, turns, locals_, partners):
        self.number, self.partners = number, partners
        extra = gives + turns
        self.sems = (
            sum(plan.OUT for plan in plans) + extra,
            sum(plan.INTO for plan in plans) + extra,
            sum(getattr(plan, "LOCALS", 0) for plan in plans) + turns + locals_,
        )

    def __call__(self, body, arrays, outs, scratch=()):
        n_in, n_out, n_scratch = len(arrays), len(outs), len(scratch)

        def kernel(*refs):
            net = Net(Place(), self.partners, *refs[n_in + n_out + n_scratch :])
            net.greet()
            body(
                net,
                refs[:n_in],
                refs[n_in : n_in + n_out],
                refs[n_in + n_out : n_in + n_out + n_scratch],
            )
            net.finish()
            assert (net.leaving, net.arriving, net.local_count) == self.sems, (
                net.leaving, net.arriving, net.local_count, self.sems,
            )

        return pl.pallas_call(
            kernel,
            out_shape=[shape for shape, _ in outs],
            in_specs=[pl.BlockSpec(memory_space=space) for _, space in arrays],
            out_specs=[pl.BlockSpec(memory_space=space) for _, space in outs],
            scratch_shapes=[*scratch] + [pltpu.SemaphoreType.DMA((n,)) for n in self.sems],
            compiler_params=pltpu.CompilerParams(
                collective_id=self.number, has_side_effects=True, vmem_limit_bytes=62 * 2**20
            ),
            name="links_%d" % self.number,
        )(*[array for array, _ in arrays])


CORE_PARTNER = (("core", 1),)
X_PARTNERS = (("x", 1), ("x", -1))
FAR_X = (("x", 2),)
PLANE_PARTNERS = (("y", 1), ("y", -1), ("y", 2), ("z", 1), ("z", -1), ("z", 2))
TURN_PARTNERS = (("turn", 1),)


def shape(dims, dtype=BF16):
    return jax.ShapeDtypeStruct(dims, dtype)


def attention_spot(z, y):
    piece = z * 4 + lax.rem(y, 2) * 2 + lax.div(y, 2)
    return piece * 128


def rows_spot(z, y):
    return attention_spot(z, y), pl.ds(0, 512)


def output_spot(z, y):
    return 0, pl.ds(pl.multiple_of(attention_spot(z, y), 128), 128)


def gateup_spot(z, y):
    columns = pl.ds(pl.multiple_of(lax.div(y, 2) * 384, 128), 384)
    return (z * 2 + lax.rem(y, 2)) * 256, columns


def down_spot(z, y):
    columns = pl.ds(pl.multiple_of((z * 2 + lax.rem(y, 2)) * 256, 128), 256)
    return lax.div(y, 2) * 384, columns


def nn(left, right):
    return lax.dot_general(left, right, (((1,), (0,)), ((), ())), preferred_element_type=F32)


def nt(left, right):
    return lax.dot_general(left, right, (((1,), (1,)), ((), ())), preferred_element_type=F32)


def tn(left, right):
    return lax.dot_general(left, right, (((0,), (0,)), ((), ())), preferred_element_type=F32)


def exact(left, right):
    return lax.dot_general(
        left, right, (((1,), (0,)), ((), ())),
        precision=lax.Precision.HIGHEST, preferred_element_type=F32,
    )


def inverse_root(rows):
    return lax.rsqrt(jnp.mean(rows * rows, axis=-1, keepdims=True) + EPSILON)


def norm_back(rows, gain, upstream):
    root = inverse_root(rows)
    weighted = upstream * gain
    meant = jnp.mean(weighted * rows, axis=-1, keepdims=True)
    return root * weighted - rows * (root * root * root * meant), upstream * rows * root


def rope_tables():
    halves = np.arange(HEAD_SIZE // 2, dtype=np.float64)
    angles = np.arange(GROUP_TOK)[:, None] * ROPE_BASE ** (-2.0 * halves / HEAD_SIZE)[None, :]
    angles = np.concatenate([angles, angles], axis=1)
    return np.cos(angles).astype(np.float32), np.sin(angles).astype(np.float32)


def owner_starts(dims, axis):
    row = lax.broadcasted_iota(jnp.int32, dims, axis)
    z, y, x, core = row >> 5, (row >> 3) & 3, (row >> 1) & 3, row & 1
    return (z * 32 + (y & 1) * 16 + core * 8 + (y >> 1) * 4 + x) * OWN_GAINS


def column_of(entry):
    return entry - jnp.floor((entry.astype(F32) + 0.5) * (1.0 / OWN_GAINS)).astype(jnp.int32) * OWN_GAINS


def gains_flat(rows):
    entry = lax.broadcasted_iota(jnp.int32, (128, GAINS), 1)
    past = entry - owner_starts((128, GAINS), 0)
    owner = ((past >= 0) & (past < OWN_GAINS)).astype(F32)
    columns = lax.dot_general(
        rows, owner, (((0,), (0,)), ((), ())),
        precision=lax.Precision.HIGHEST, preferred_element_type=F32,
    )
    place = lax.broadcasted_iota(jnp.int32, (128, GAINS), 0)
    return jnp.sum(jnp.where(column_of(entry) == place, columns, 0.0), axis=0, keepdims=True)


class Documents:
    def __init__(self, lengths):
        lengths = [lengths[0:1, n : n + 1] for n in range(4)]
        self.ends = [lengths[0], lengths[0] + lengths[1], lengths[0] + lengths[1] + lengths[2]]

    def pick(self, place, values):
        value = jnp.where(place >= self.ends[0], values[1], values[0])
        value = jnp.where(place >= self.ends[1], values[2], value)
        return jnp.where(place >= self.ends[2], values[3], value)

    def first(self, place):
        zero = jnp.zeros_like(self.ends[0])
        return self.pick(place, [zero] + self.ends)


def allowed_pairs(documents, first_row, rows, keys):
    query = lax.broadcasted_iota(jnp.int32, (rows, 1), 0) + first_row
    key = lax.broadcasted_iota(jnp.int32, (rows, keys), 1)
    return (key >= documents.first(query)) & (key <= query)


def unit_off(n):
    return lax.rem(n + lax.div(n, 2), 4) + 2 * lax.div(n, 3)


class Units:
    ORDER = (0, 1, -1, 2)

    def __init__(self, place):
        self.x = place.x

    def chip(self, n):
        return lax.rem(self.x + unit_off(n), RING)

    def rows(self, n):
        return pl.ds(pl.multiple_of(self.chip(n) * 256, 256), 256)

    def true_rows(self, n, core):
        return pl.ds(pl.multiple_of((core * RING + self.chip(n)) * 128, 128), 128)


def own_half(length, core):
    return pl.ds(pl.multiple_of(core * length, 128), length)


def attention_forward(
    tokens, cotangent, query, keyval, output, gateup, down, gains, lengths, cosine, sine
):
    def body(net, ins, outs, work):
        (
            tokens_, cotangent_, query_, keyval_, output_, gateup_in, down_in, gains_, lengths_,
            cosine_in, sine_in,
        ) = ins
        (
            residual_, tokens_here, normed_, raw_hbm, heads_hbm, attended_hbm, totals_hbm,
            cosine_hbm, sine_hbm, qkv_out, output_out, gate_out, up_out, down_piece,
            cotangent_all, flat_, lengths_out,
        ) = outs
        (
            gathered, normed, qkv_w, output_w, qkv_cast, output_cast, qkv_piece, output_piece,
            gains_row, gains_rows, lengths_mine, lengths_there, gate_cast, up_cast, down_cast,
            gate_piece, up_piece, cotangent_here, terms, raw_, heads_, attended_, totals_,
            cosine_out, sine_out, gateup_, down_, cosine_, sine_, landed, land,
        ) = work
        place = net.place
        units = Units(place)
        mine, theirs = place.core, 1 - place.core

        loads = [
            net.local(lambda source=source, target=target: (source, target))
            for source, target in (
                (gateup_in, gateup_), (down_in, down_), (cosine_in, cosine_), (sine_in, sine_),
            )
        ]
        qkv_cast[:, 0:256] = query_[...].astype(BF16)
        qkv_cast[:, 256:384] = keyval_[0].astype(BF16)
        qkv_cast[:, 384:512] = keyval_[1].astype(BF16)
        output_cast[...] = output_[...].astype(BF16)
        gains_row[0] = jnp.zeros((1, 128), F32)
        gains_row[0, 0:1, 0:OWN_GAINS] = gains_[...]
        lengths_mine[...] = jnp.zeros((8, 128), jnp.int32)
        lengths_mine[0:1, 0:4] = lengths_[...]
        net.enter()
        qkv_turn = Turn(net, [(qkv_cast, qkv_piece)])
        output_turn = Turn(net, [(output_cast, output_piece)])
        rows = [Turn(net, [pair]) for pair in parts_of(tokens_, tokens_here, 2)]
        upstream = Turn(net, parts_of(cotangent_, cotangent_here, 2))
        qkv_turn.start()
        for part in rows:
            part.start()
        qkv_gather = PlaneGather(net, qkv_piece, qkv_w, rows_spot, 32)
        output_gather = PlaneGather(net, output_piece, output_w, output_spot, 64)
        gate_gather = PlaneGather(net, gate_piece, gate_out, gateup_spot)
        up_gather = PlaneGather(net, up_piece, up_out, gateup_spot)
        gather = RowsGather(net, tokens_here, gathered)
        later = RowsGather(net, cotangent_here, cotangent_all)
        length_copy = Give(net, lambda: (lengths_mine, lengths_there), lambda: lengths_there)
        gains_steps = GainsGather(net, gains_row, gains_rows).steps()
        next(gains_steps)

        for load in loads:
            load.wait()
        halves = []
        for n, (cast, piece) in enumerate(((gate_cast, gate_piece), (up_cast, up_piece))):
            spot = own_half(128, mine)
            piece[spot] = gateup_[n, :, own_half(384, mine)].astype(BF16)
            cast[...] = gateup_[n, :, own_half(384, theirs)].astype(BF16)
            halves.append(Give(
                net,
                lambda cast=cast, piece=piece: (cast, piece.at[own_half(128, mine)]),
                lambda piece=piece: piece.at[own_half(128, theirs)],
            ))
        down_piece[:, own_half(128, mine)] = down_[own_half(384, mine)].astype(BF16)
        down_cast[...] = down_[own_half(384, theirs)].astype(BF16)
        halves.append(Give(
            net,
            lambda: (down_cast, down_piece.at[:, own_half(128, mine)]),
            lambda: down_piece.at[:, own_half(128, theirs)],
        ))

        qkv_turn.wait()
        qkv_gather.start()
        output_turn.start()
        for n, part in enumerate(rows):
            part.wait()
            gather.start((n,))
        upstream.start()
        next(gains_steps)

        length_copy.wait()
        lengths_out[...] = jnp.where(place.native, lengths_mine[...], lengths_there[...])
        documents = Documents(lengths_out[...])
        zero = jnp.zeros((1, 1), jnp.int32)
        starts = [zero] + documents.ends
        everywhere = lax.broadcasted_iota(jnp.int32, (1, GROUP_TOK), 1)
        hits = jnp.concatenate(
            [(everywhere == start).astype(F32) for start in starts] * 2, axis=0
        )
        start_cosine = exact(hits, cosine_[...])
        start_sine = exact(hits, sine_[...])
        sign = jnp.where(lax.broadcasted_iota(jnp.int32, (1, HEAD_SIZE), 1) < 64, -1.0, 1.0)

        def table(n):
            spot = pl.ds(pl.multiple_of(n * 256, 256), 256)
            where = lax.broadcasted_iota(jnp.int32, (256, 1), 0) + n * 256
            cosine_by = documents.pick(where, [start_cosine[n : n + 1] for n in range(4)])
            sine_by = documents.pick(where, [start_sine[n : n + 1] for n in range(4)])
            cosine_out[spot] = cosine_[spot] * cosine_by + sine_[spot] * sine_by
            sine_out[spot] = (sine_[spot] * cosine_by - cosine_[spot] * sine_by) * sign

        staged(4, table)
        qkv_gather.spread()
        output_turn.wait()
        output_gather.start()
        next(gains_steps)
        gather.near_first()
        for half in halves:
            half.wait()
        next(gains_steps)
        qkv_gather.forward()
        output_gather.spread()
        gate_gather.start()
        next(gains_steps)
        flat_[...] = gains_flat(gains_rows[...].reshape(128, 128))
        gain_query = flat_[0:1, 4096:4224]
        gain_key = flat_[0:1, 4224:4352]

        def normalize(n):
            rows_in = gathered[units.rows(n)].astype(F32)
            normed[units.rows(n)] = (
                rows_in * inverse_root(rows_in) * flat_[0:1, 0:2048]
            ).astype(BF16)

        def near():
            gather.near_second()
            gather.here(1)

        def far():
            gather.far()
            output_gather.forward()
            up_gather.start()
            upstream.wait()
            later.start()
            gather.here(2)

        staged(4, normalize, {
            0: lambda: gather.here(0), 1: near, 2: lambda: gather.here(-1), 3: far,
        })
        qkv_gather.here()
        stores = [net.local(lambda: (normed, normed_)), net.local(lambda: (qkv_w, qkv_out))]

        def project(n):
            parts = nn(normed[units.rows(n)], qkv_w[...])
            for core in range(2):
                spot = units.true_rows(n, core)
                part = parts[core * 128 : core * 128 + 128]
                raw_[spot] = part[:, 0:384]
                heads_[spot, 384:512] = part[:, 384:512].astype(BF16)
                for head in range(3):
                    columns = slice(head * 128, head * 128 + 128)
                    value = part[:, columns]
                    value = value * inverse_root(value) * (gain_key if head == 2 else gain_query)
                    turned = value * cosine_out[spot] + pltpu.roll(value, 64, 1) * sine_out[spot]
                    heads_[spot, columns] = turned.astype(BF16)

        staged(4, project)
        gate_gather.spread()

        def attend(block):
            keys = 256 * (block + 1)
            spot = slice(block * 256, block * 256 + 256)

            def one(head):
                columns = own_half(128, head)
                scores = nt(heads_[spot, columns], heads_[0:keys, 256:384])
                allowed = allowed_pairs(documents, block * 256, 256, keys)
                scores = jnp.where(allowed, scores, -1e30)
                highest = jnp.max(scores, axis=-1, keepdims=True)
                weights_ = jnp.exp((scores - highest) * SCALE)
                summed = jnp.sum(weights_, axis=-1, keepdims=True)
                probability = (weights_ * (1.0 / summed)).astype(BF16)
                attended_[spot, columns] = nn(probability, heads_[0:keys, 384:512]).astype(BF16)
                lane = lax.broadcasted_iota(jnp.int32, (1, 128), 1)
                ours = (lane >= head * 64) & (lane < head * 64 + 64)
                totals_[spot] = jnp.where(ours, highest * SCALE + jnp.log(summed), totals_[spot])

            staged(2, one)

        attend(0)
        attend(1)
        attend(2)
        output_gather.here()
        stores.append(net.local(lambda: (output_w, output_out)))
        attend(3)
        later.near_first()
        up_gather.spread()
        sums = RowsSum(net, terms, landed, land)

        def out(n):
            n = 3 - n
            own = jnp.concatenate(
                [attended_[units.true_rows(n, 0)], attended_[units.true_rows(n, 1)]], axis=0
            )
            terms[units.rows(n)] = nn(own, output_w[...]).astype(BF16)

        def passed(k, ready=None, go=None):
            def act():
                sums.pass_over(k)
                if ready is not None:
                    sums.combine(ready)
                    go()

            return act

        staged(4, out, None, {
            0: passed(2),
            1: passed(-1, 2, sums.start_far),
            2: passed(1, -1, sums.start_left),
            3: passed(0, 1, sums.start_right),
        })
        for source, target in (
            (raw_, raw_hbm), (heads_, heads_hbm), (attended_, attended_hbm),
            (totals_, totals_hbm), (cosine_out, cosine_hbm), (sine_out, sine_hbm),
        ):
            stores.append(net.local(lambda source=source, target=target: (source, target)))
        sums.combine(0)
        sums.forward()
        later.near_second()
        gate_gather.forward()
        later.far()
        up_gather.forward()
        for k in (0, 1, -1, 2):
            later.here(k)

        def keep(spot, value):
            residual_[spot] = value + tokens_here[spot].astype(F32)

        sums.finish(keep)
        gate_gather.here()
        up_gather.here()
        for store in stores:
            store.wait()

    plans = (GainsGather,) + 4 * (PlaneGather,) + 2 * (RowsGather,) + (RowsSum,)
    return Kernel(
        0, plans, 4, 6, 13, CORE_PARTNER + X_PARTNERS + FAR_X + PLANE_PARTNERS + TURN_PARTNERS
    )(
        body,
        [
            (tokens, VMEM), (cotangent, VMEM), (query, VMEM), (keyval, VMEM), (output, VMEM),
            (gateup, HBM), (down, HBM), (gains, VMEM), (lengths, VMEM),
            (cosine, HBM), (sine, HBM),
        ],
        [
            (shape((128, 2048), F32), VMEM),
            (shape((128, 2048)), VMEM),
            (shape((1024, 2048)), HBM),
            (shape((1024, 384), F32), HBM),
            (shape((1024, 512)), HBM),
            (shape((1024, 256)), HBM),
            (shape((1024, 128), F32), HBM),
            (shape((1024, 128), F32), HBM),
            (shape((1024, 128), F32), HBM),
            (shape((2048, 512)), HBM),
            (shape((256, 2048)), HBM),
            (shape((2048, 768)), HBM),
            (shape((2048, 768)), HBM),
            (shape((384, 256)), VMEM),
            (shape((1024, 2048)), HBM),
            (shape((1, GAINS), F32), VMEM),
            (shape((8, 128), jnp.int32), VMEM),
        ],
        (
            pltpu.VMEM((1024, 2048), BF16),
            pltpu.VMEM((1024, 2048), BF16),
            pltpu.VMEM((2048, 512), BF16),
            pltpu.VMEM((256, 2048), BF16),
            pltpu.VMEM((128, 512), BF16),
            pltpu.VMEM((256, 128), BF16),
            pltpu.VMEM((128, 512), BF16),
            pltpu.VMEM((256, 128), BF16),
            pltpu.VMEM((1, 1, 128), F32),
            pltpu.VMEM((128, 1, 128), F32),
            pltpu.VMEM((8, 128), jnp.int32),
            pltpu.VMEM((8, 128), jnp.int32),
            pltpu.VMEM((128, 384), BF16),
            pltpu.VMEM((128, 384), BF16),
            pltpu.VMEM((384, 128), BF16),
            pltpu.VMEM((256, 384), BF16),
            pltpu.VMEM((256, 384), BF16),
            pltpu.VMEM((128, 2048), BF16),
            pltpu.VMEM((1024, 2048), BF16),
            pltpu.VMEM((1024, 384), F32),
            pltpu.VMEM((1024, 512), BF16),
            pltpu.VMEM((1024, 256), BF16),
            pltpu.VMEM((1024, 128), F32),
            pltpu.VMEM((1024, 128), F32),
            pltpu.VMEM((1024, 128), F32),
            pltpu.VMEM((2, 128, 768), F32),
            pltpu.VMEM((768, 128), F32),
            pltpu.VMEM((1024, 128), F32),
            pltpu.VMEM((1024, 128), F32),
        )
        + ROWS_SCRATCH,
    )


def layer_backward(
    residual, tokens, gains, lengths, down, cotangent_all, gate, up, heads, raw, attended,
    totals, cosine, sine, qkv, output, normed,
):
    def body(net, ins, outs, work):
        (
            residual_, tokens_, gains_, lengths_, down_, cotangent_all_, gate_, up_,
            heads_, raw_, attended_, totals_, cosine_, sine_, qkv_, output_, normed_,
        ) = ins
        (
            block_own, input_own, qkv_own, output_own, gate_own, up_own, down_own, gains_own,
        ) = outs
        (
            low, second, upstream, qkv_w, output_w, gate_w, up_w, down_w, hidden, gate_low, up_low,
            terms, back_rows, raw_here, totals_here, cosine_here, sine_here, key_sum, value_sum,
            own_out, qkv_total, output_total, gate_total, up_total, down_total,
            gain_rows, gain_land, first_gain, query_gain, flat, landed, land,
            *planes, free,
            early_landed, early_land, late_landed, late_land,
        ) = work
        share_landed, share_land = (early_landed, late_landed), (early_land, late_land)
        place = net.place
        units = Units(place)
        mine, theirs = place.core, 1 - place.core

        def load(source, target):
            return net.local(lambda: (source, target))

        loads = {
            "gate": load(gate_, gate_w),
            "up": load(up_, up_w),
            "upstream": load(cotangent_all_, upstream),
            "output": load(output_, output_w),
            "qkv": load(qkv_, qkv_w),
            "raw": load(raw_, raw_here),
            "totals": load(totals_, totals_here),
            "cosine": load(cosine_, cosine_here),
            "sine": load(sine_, sine_here),
        }
        second_gain = gains_[0:1, 2048:4096]

        def second_norm(n):
            spot = pl.ds(pl.multiple_of(n * 64, 64), 64)
            rows = residual_[spot]
            low[spot] = (rows * inverse_root(rows) * second_gain).astype(BF16)

        staged(2, second_norm)
        net.enter()
        gather = RowsGather(net, low, second)
        gather.start()
        down_gather = PlaneGather(net, down_, down_w, down_spot)
        down_gather.start()
        sums = RowsSum(net, terms, landed, land)
        mlp_sum = RowsSum(net, second, landed, land)
        first_sums = [
            RowsSum(
                net, upstream, share_landed[share], share_land[share], share, 2,
            )
            for share in range(2)
        ]
        last_gather = RowsGather(net, low, terms)
        gate_sum = PlaneSum(net, gate_w, gateup_spot, planes[0:4])
        up_sum = PlaneSum(net, up_w, gateup_spot, planes[4:8])
        down_sum = PlaneSum(net, down_w, down_spot, planes[8:12])
        qkv_sum = PlaneSum(net, qkv_w, rows_spot, planes[12:16])
        output_sum = PlaneSum(net, output_w, output_spot, planes[16:20])

        def forth(n):
            spot = units.rows(n)
            gate_value = nn(second[spot], gate_w[...])
            upward = nn(second[spot], up_w[...])
            sigmoid = 1.0 / (1.0 + jnp.exp(-gate_value))
            active = gate_value * sigmoid
            hidden[spot] = (active * upward).astype(BF16)
            gate_low[spot] = (upward * (sigmoid + active * (1.0 - sigmoid))).astype(BF16)
            up_low[spot] = active.astype(BF16)

        between = {
            1: lambda: (sums.combine(2), sums.start_far()),
            2: lambda: (sums.combine(-1), sums.start_left()),
            3: lambda: (sums.combine(1), sums.start_right()),
        }

        def back(n):
            spot = units.rows(3 - n)
            hidden_grad = nt(upstream[spot], down_w[...])
            gate_low[spot] = (hidden_grad * gate_low[spot].astype(F32)).astype(BF16)
            up_low[spot] = (hidden_grad * up_low[spot].astype(F32)).astype(BF16)
            at_step(between, n)
            terms[spot] = (nt(gate_low[spot], gate_w[...]) + nt(up_low[spot], up_w[...])).astype(
                BF16
            )

        def begin():
            for name in ("gate", "up", "upstream"):
                loads[name].wait()
            gather.here(0)

        def near():
            gather.near_first()
            down_gather.spread()
            gather.near_second()
            gather.here(1)

        def far():
            down_gather.forward()
            gather.far()
            gather.here(2)

        staged(4, forth, {0: begin, 1: near, 2: lambda: gather.here(-1), 3: far})
        down_gather.here()
        staged(4, back, None, {
            0: lambda: sums.pass_over(2), 1: lambda: sums.pass_over(-1),
            2: lambda: sums.pass_over(1), 3: lambda: sums.pass_over(0),
        })
        sums.combine(0)
        sums.passed()
        for axis, by in CORE_PARTNER + X_PARTNERS:
            pl.semaphore_signal(
                free, inc=1, device_id=place.device(axis, by), device_id_type=pl.DeviceIdType.MESH
            )
        sums.forward()
        gain_parts = []

        def weight_grad(low_grad, target):
            def one(n):
                columns = own_half(256, n)
                target[columns] = tn(second[:, columns], low_grad[...]).astype(BF16)

            return one

        staged(8, weight_grad(gate_low, gate_w))
        gate_sum.start()
        staged(8, weight_grad(up_low, up_w))
        up_sum.start()
        gather.gone()
        down_gather.gone()

        def own_rows(spot):
            start = (place.x * 2 + place.core) * 128 + spot.start
            return pl.ds(pl.multiple_of(start, 64), 64)

        def keep(spot, value):
            through_, gain_part = norm_back(residual_[spot], second_gain, value)
            through_ = through_ + upstream[own_rows(spot)].astype(F32)
            back_rows[spot] = through_
            low[spot] = through_.astype(BF16)
            gain_parts.append(jnp.sum(gain_part, axis=0, keepdims=True))

        sums.finish(keep)
        sums.departed()
        pl.semaphore_wait(free, 3)
        last_gather.start()

        def through(n):
            spot = units.rows(n)
            second[spot] = nn(hidden[spot], down_w[...]).astype(BF16)

        staged(4, through)

        def down_grad(n):
            columns = own_half(256, n)
            down_w[columns] = tn(hidden[:, columns], upstream[...]).astype(BF16)

        staged(3, down_grad)
        down_sum.start()
        last_gather.near_first()
        heads_cols, attended_cols = hidden.at[:, 0:512], hidden.at[:, 512:768]
        parts, attended_grad = gate_low.at[:, 0:512], gate_low.at[:, 512:768]
        attended_rows = up_low.at[:, 0:256]
        loads["heads"] = load(heads_, heads_cols)
        loads["attended"] = load(attended_, attended_cols)
        gate_sum.forward()
        loads["output"].wait()
        key_sum[...] = jnp.zeros_like(key_sum)
        value_sum[...] = jnp.zeros_like(value_sum)
        query_gain[...] = jnp.zeros_like(query_gain)
        for name in ("heads", "raw", "totals", "cosine", "sine"):
            loads[name].wait()
        documents = Documents(lengths_[...])
        gain_query, gain_key = gains_[0:1, 4096:4224], gains_[0:1, 4224:4352]

        def through_rope(value, cosine_part, sine_part, raw_part, gain):
            value = value * cosine_part + pltpu.roll(value * sine_part, 64, 1)
            through_, gain_part = norm_back(raw_part, gain, value)
            return through_.astype(BF16), jnp.sum(gain_part, axis=0, keepdims=True)

        def twice(value):
            return jnp.concatenate([value, value], axis=0)

        def both_heads(ref, spot, first):
            return jnp.concatenate(
                [ref[spot, first : first + 128], ref[spot, first + 128 : first + 256]], axis=0
            )

        def attend(n, core):
            spot = units.true_rows(n, core)
            keys = 512 * (core + 1)
            query = both_heads(hidden, spot, 0)
            upward = both_heads(gate_low, spot, 512)
            key, value = hidden[0:keys, 256:384], hidden[0:keys, 384:512]
            scores = nt(query, key) * SCALE
            total = jnp.concatenate([totals_here[spot, 0:1], totals_here[spot, 64:65]], axis=0)
            allowed = allowed_pairs(documents, spot.start, 128, keys)
            probability = jnp.where(twice(allowed), jnp.exp(scores - total), 0.0)
            prob_grad = nt(upward, value)
            centre = jnp.sum(probability * prob_grad, axis=-1, keepdims=True)
            score_grad = (probability * (prob_grad - centre)).astype(BF16)
            value_sum[0:keys] += tn(probability.astype(BF16), upward)
            key_sum[0:keys] += tn(score_grad, query)
            query_grad = nn(score_grad, key) * SCALE
            through_, gain_part = through_rope(
                query_grad, twice(cosine_here[spot]), twice(sine_here[spot]),
                both_heads(raw_here, spot, 0), gain_query,
            )
            here = pl.ds(pl.multiple_of(units.chip(n) * 256 + core * 128, 128), 128)
            gate_low[here, 0:128] = through_[0:128]
            gate_low[here, 128:256] = through_[128:256]
            query_gain[...] += gain_part

        def enter(n):
            grad = nt(terms[units.rows(n)], output_w[...]).astype(BF16)
            for core in range(2):
                attended_grad[units.true_rows(n, core)] = grad[core * 128 : core * 128 + 128]
            for core in range(2):
                attend(n, core)

        def own_here():
            last_gather.here(0)
            for k in (2, 1, -1, 0):
                mlp_sum.pass_over(k)

        def combined():
            last_gather.near_second()
            last_gather.here(1)
            for k in (2, 1, -1, 0):
                mlp_sum.combine(k)

        def last_far():
            up_sum.forward()
            last_gather.far()
            mlp_sum.start_far()
            mlp_sum.start_right()
            mlp_sum.start_left()
            last_gather.here(2)

        staged(4, enter, {
            0: own_here, 1: combined, 2: lambda: last_gather.here(-1), 3: last_far,
        })
        mlp_sum.passed()
        loads["normed"] = load(normed_, second)
        loads["attended"].wait()

        def same_order(n):
            for core in range(2):
                start = pl.multiple_of(units.chip(n) * 256 + core * 128, 128)
                attended_rows[pl.ds(start, 128)] = attended_cols[units.true_rows(n, core)]

        staged(4, same_order)

        def output_grad(n):
            columns = own_half(512, n)
            output_w[:, columns] = tn(attended_rows[...], terms[:, columns]).astype(BF16)

        staged(4, output_grad)
        output_sum.start()
        gate_sum.gather()
        down_sum.forward()
        mlp_sum.forward()
        def key_back(true, gain_sum):
            spot = pl.ds(pl.multiple_of(true * 128, 128), 128)
            start = (lax.rem(true, RING) * 2 + lax.div(true, RING)) * 128
            through_, gain_part = through_rope(
                key_sum[spot] * SCALE, cosine_here[spot], sine_here[spot],
                raw_here[spot, 256:384], gain_key,
            )
            here = pl.ds(pl.multiple_of(start, 128), 128)
            gate_low[here, 256:384] = through_
            gate_low[here, 384:512] = value_sum[spot].astype(BF16)
            return gain_sum + gain_part

        key_gain = lax.fori_loop(0, 8, key_back, jnp.zeros((1, 128), F32))
        last_gather.gone()
        loads["tokens"] = load(tokens_, low)
        loads["qkv"].wait()
        loads["normed"].wait()
        up_sum.gather()
        first_gain[...] = jnp.zeros_like(first_gain)

        def out(n):
            spot = units.rows(3 - n)
            value = nt(parts[spot], qkv_w[...])
            upstream[spot] = value.astype(BF16)
            part = jnp.sum(value * second[spot].astype(F32), axis=0, keepdims=True)
            first_gain[...] += part

        early, late = first_sums

        def give(k):
            for one in first_sums:
                one.pass_over(k)

        staged(4, out, None, {
            0: lambda: give(2),
            1: lambda: (give(-1), early.combine(2), early.start_far()),
            2: lambda: (give(1), early.combine(-1), early.start_left()),
            3: lambda: (give(0), early.combine(1), early.start_right()),
        })
        output_sum.forward()

        def keep_block(spot, value):
            own_out[spot] = (residual_[spot] + value).astype(BF16)

        mlp_sum.finish(keep_block)
        block_turn = Turn(net, parts_of(own_out, block_own, 2))
        block_turn.start()

        def qkv_grad(n):
            columns = own_half(256, n)
            qkv_w[columns] = tn(second[:, columns], parts[...]).astype(BF16)

        staged(8, qkv_grad, None, {
            1: lambda: (late.combine(2), late.start_far(), early.combine(0)),
            3: lambda: (early.forward(), late.combine(-1), late.start_left()),
            5: lambda: (late.combine(1), late.start_right(), late.combine(0)),
        })
        qkv_sum.start()
        flat[...] = jnp.concatenate(
            [first_gain[...] / gains_[0:1, 0:2048], gain_parts[0] + gain_parts[1], query_gain[...], key_gain],
            axis=1,
        )

        def to_rows(n, total):
            entry = lax.broadcasted_iota(jnp.int32, (128, 256), 1) + n * 256
            past = entry - owner_starts((128, 256), 0)
            here = flat[0:1, own_half(256, n)]
            owned = jnp.where((past >= 0) & (past < OWN_GAINS), here, 0.0)
            place_ = lax.broadcasted_iota(jnp.int32, (128, 256), 0)
            column = (column_of(entry) == place_).astype(F32)
            return total + lax.dot_general(
                owned, column, (((1,), (1,)), ((), ())),
                precision=lax.Precision.HIGHEST, preferred_element_type=F32,
            )

        rows_of = lax.fori_loop(0, GAINS // 256, to_rows, jnp.zeros((128, 128), F32))
        gain_rows[...] = rows_of.reshape(128, 1, 128)
        late.forward()
        gains_steps = GainsSum(net, gain_rows, gains_own, gain_land).steps()
        next(gains_steps)

        halves = []

        def exchange(cut, there):
            halves.append(net.local(lambda: (cut(mine), there(mine))))
            halves.append(
                Give(net, lambda: (cut(theirs), there(mine)), lambda: there(theirs))
            )

        output_sum.gather()
        qkv_sum.forward()
        next(gains_steps)
        down_sum.gather()
        gate_sum.finish(gate_total)
        exchange(
            lambda core: gate_total.at[own_half(128, core)],
            lambda core: gate_own.at[:, own_half(384, core)],
        )
        output_sum.finish(output_total)
        output_turn = Turn(net, [(output_total, output_own)])
        output_turn.start()
        next(gains_steps)
        turns = []
        block_turn.wait()
        loads["tokens"].wait()

        def ended(share):
            def keep_first(spot, value):
                spot = pl.ds(64 * share + spot.start, 32)
                through_, _ = norm_back(low[spot].astype(F32), gains_[0:1, 0:2048], value)
                own_out[spot] = (back_rows[spot] + through_).astype(BF16)

            first_sums[share].finish(keep_first)
            spot = pl.ds(64 * share, 64)
            turns.append(Turn(net, [(own_out.at[spot], input_own.at[spot])]))
            turns[-1].start()

        ended(0)
        qkv_sum.gather()
        next(gains_steps)
        ended(1)
        qkv_sum.finish(qkv_total)
        qkv_turn = Turn(net, [(qkv_total, qkv_own)])
        qkv_turn.start()
        up_sum.finish(up_total)
        exchange(
            lambda core: up_total.at[own_half(128, core)],
            lambda core: up_own.at[:, own_half(384, core)],
        )
        down_sum.finish(down_total)
        exchange(
            lambda core: down_total.at[:, own_half(128, core)],
            lambda core: down_own.at[own_half(384, core)],
        )
        next(gains_steps)
        for copy in halves:
            copy.wait()
        for turn in (output_turn, *turns, qkv_turn):
            turn.wait()

    plans = (
        2 * (RowsGather,) + 4 * (RowsSum,) + (PlaneGather,) + 5 * (PlaneSum,) + (GainsSum,)
    )
    return Kernel(
        1, plans, 3, 6, 13 + 3 - 1, CORE_PARTNER + X_PARTNERS + FAR_X + PLANE_PARTNERS + TURN_PARTNERS
    )(
        body,
        [
            (residual, VMEM), (tokens, HBM), (gains, VMEM), (lengths, VMEM),
            (down, VMEM), (cotangent_all, HBM), (gate, HBM), (up, HBM), (heads, HBM), (raw, HBM),
            (attended, HBM), (totals, HBM), (cosine, HBM), (sine, HBM), (qkv, HBM), (output, HBM),
            (normed, HBM),
        ],
        [
            (shape((128, 2048)), HBM),
            (shape((128, 2048)), HBM),
            (shape((128, 512)), VMEM),
            (shape((256, 128)), VMEM),
            (shape((128, 768)), HBM),
            (shape((128, 768)), HBM),
            (shape((768, 128)), HBM),
            (shape((1, 1, 128), F32), VMEM),
        ],
        (
            pltpu.VMEM((128, 2048), BF16),
            pltpu.VMEM((1024, 2048), BF16),
            pltpu.VMEM((1024, 2048), BF16),
            pltpu.VMEM((2048, 512), BF16),
            pltpu.VMEM((256, 2048), BF16),
            pltpu.VMEM((2048, 768), BF16),
            pltpu.VMEM((2048, 768), BF16),
            pltpu.VMEM((768, 2048), BF16),
            pltpu.VMEM((1024, 768), BF16),
            pltpu.VMEM((1024, 768), BF16),
            pltpu.VMEM((1024, 768), BF16),
            pltpu.VMEM((1024, 2048), BF16),
            pltpu.VMEM((128, 2048), F32),
            pltpu.VMEM((1024, 384), F32),
            pltpu.VMEM((1024, 128), F32),
            pltpu.VMEM((1024, 128), F32),
            pltpu.VMEM((1024, 128), F32),
            pltpu.VMEM((1024, 128), F32),
            pltpu.VMEM((1024, 128), F32),
            pltpu.VMEM((128, 2048), BF16),
            pltpu.VMEM((128, 512), BF16),
            pltpu.VMEM((256, 128), BF16),
            pltpu.VMEM((256, 384), BF16),
            pltpu.VMEM((256, 384), BF16),
            pltpu.VMEM((384, 256), BF16),
            pltpu.VMEM((128, 1, 128), F32),
            pltpu.VMEM((127, 1, 128), F32),
            pltpu.VMEM((1, 2048), F32),
            pltpu.VMEM((1, 128), F32),
            pltpu.VMEM((1, GAINS), F32),
        )
        + ROWS_SCRATCH
        + plane_scratch(256, 384) * 2
        + plane_scratch(384, 256)
        + plane_scratch(128, 512, 32)
        + plane_scratch(256, 128, 64)
        + (pltpu.SemaphoreType.REGULAR,)
        + (pltpu.VMEM((4, 2, 32, 2048), BF16), pltpu.VMEM((6, 32, 2048), BF16)) * 2,
    )


def step_rates(total_tokens):
    root_tokens = math.sqrt(total_tokens)
    narrow = MODEL_WIDTH ** (-0.5)
    return (
        narrow / (2.0 * root_tokens),
        narrow / (2.0 * root_tokens),
        (QUERY_HEADS * HEAD_SIZE // 128) ** (-0.5) / (0.24 * root_tokens),
        narrow / (0.7 * root_tokens),
        FF ** (-0.5) / (1.2 * root_tokens),
        0.025 / root_tokens,
    )


def update(rows, gradients, state):
    rates = step_rates(GROUP_TOK * 16)

    def kernel(*refs):
        block_, input_, qkv_, output_, gate_, up_, down_, gains_ = refs[:8]
        masters, moments, averages = refs[8:14], refs[14:20], refs[20:26]
        outs = refs[26:]
        outs[0][...] = block_[...]
        outs[1][...] = input_[...]

        def one(n, gradient, spot):
            gradient = gradient.astype(F32)
            moment = MOMENTUM * moments[n][spot] + gradient
            master = masters[n][spot] - rates[n] * (gradient + MOMENTUM * moment)
            outs[2 + n][spot] = master
            outs[8 + n][spot] = moment
            outs[14 + n][spot] = AVERAGING * averages[n][spot] + (1.0 - AVERAGING) * master

        one(0, qkv_[:, 0:256], ...)
        one(1, qkv_[:, 256:384], 0)
        one(1, qkv_[:, 384:512], 1)
        one(2, output_[...], ...)
        one(3, gate_[...], 0)
        one(3, up_[...], 1)
        one(4, down_[...], ...)
        one(5, gains_[0, 0:1, 0:OWN_GAINS], ...)

    outs = [shape(a.shape, a.dtype) for a in rows]
    outs += [shape(a.shape, F32) for a in state]
    arrays = (*rows, *gradients, *state)
    return pl.pallas_call(
        kernel,
        out_shape=outs,
        in_specs=[pl.BlockSpec(memory_space=VMEM)] * len(arrays),
        out_specs=[pl.BlockSpec(memory_space=VMEM)] * len(outs),
        compiler_params=pltpu.CompilerParams(vmem_limit_bytes=61 * 2**20),
        name="update",
    )(*arrays)


def body(tokens, cotangent, doc_lengths, *state):
    query_weight, key_value_weight, output_weight, gateup_weight, down_weight, norm_gains = state[:6]
    cosine, sine = rope_tables()
    (
        residual, tokens_here, normed, raw, heads, attended, totals,
        cosine, sine, qkv, output, gate, up, down, cotangent_all, gains, lengths,
    ) = attention_forward(
        tokens, cotangent, query_weight, key_value_weight, output_weight, gateup_weight,
        down_weight, norm_gains.reshape(1, OWN_GAINS), doc_lengths,
        jnp.asarray(cosine), jnp.asarray(sine),
    )
    block_out, input_grad, *gradients = layer_backward(
        residual, tokens_here, gains, lengths, down, cotangent_all, gate, up,
        heads, raw, attended, totals, cosine, sine, qkv, output, normed,
    )
    state = [a.reshape(1, OWN_GAINS) if a.ndim == 1 else a for a in state]
    outs = update((block_out, input_grad), gradients, state)
    return tuple(a.reshape(OWN_GAINS) if a.shape == (1, OWN_GAINS) else a for a in outs)


def solution(mesh):
    parted = Mesh(mesh.devices.reshape(GRID), AXES)
    data = ("z", "ylo", "core")
    tensor = ("yhi", "x")
    rows = P(AXES, None)
    by_rows = P(data, tensor)
    pair = P(None, data, tensor)
    by_columns = P(tensor, data)
    flat = P(AXES)
    weights = (by_rows, pair, by_columns, pair, by_columns, flat)
    return jax.shard_map(
        body,
        mesh=parted,
        in_specs=(rows, rows, P(data, None)) + weights * 3,
        out_specs=(rows, rows) + weights * 3,
        check_vma=False,
    )
```
